32 devices in a mesh: dom: 8 (over z, x), sub: 4 (over y, core).
Axes of the slice: x: 2, y: 2, z: 4, core: 2. Of those that a mesh axis runs over, the one named last changes fastest.
Arguments:
- adjoint_field: float32 [4096, 5, 512], P(('dom', 'sub')), may hold values from -6 to 6
- metric: float32 [4096, 3, 512], P(('dom', 'sub')), may hold values from 0.5 to 4
- velocity: float32 [4096, 3, 512], P(('dom', 'sub')), may hold values from -2 to 2
- mortar_route: int32 [4096, 1], P(('dom', 'sub')), may hold values from 0 to 7, as said below
- mortar_element: int32 [4096, 1], P(('dom', 'sub')), may hold values from 0 to 127
- face_code: int32 [4096, 1], P(('dom', 'sub')), may hold values from 0 to 7
- hanging: int32 [4096, 1], P(('dom', 'sub')), may hold values 0 or 1
Outputs:
- result: float32 [4096, 5, 512], P(('dom', 'sub'))
The draws below stay inside these ranges and needn't reach their ends.
Inputs may be any that keep to these rules, and one draw needn't show every extreme that they name: `mortar_route`: each element's value is its own device's dom index d or one of d - 2, d - 1, d + 1, d + 2 taken modulo 8. In each aligned block of 128 rows (the elements of one device) no value is named by more than 96 rows, and some value by exactly 96.
All inputs are finite; a program needn't handle non-finite values. No bound on the sum of `hanging` on one device may be relied on, other than what follows from the above.
Results may differ from the reference program's by a relative error of at most 0.00088.
Values may be sent and summed in bfloat16 or wider, within the bound.
No kernel may reach another device: no remote copies, remote signals or barrier semaphores. Data moves between devices by JAX's collectives and lax.ppermute only.
A program may use at most 64 MiB of HBM per device.

```python
import math
import jax
import jax.numpy as jnp
import numpy as np
from jax import lax

NODES = 8
FIELDS = 5
E_DEV = 128
CAP = 96
ELEMS = 4096
N_DOM = 8
N_SUB = 4


def route_block(key, dom_index):
    keys = jax.random.split(key, 5)
    rest = E_DEV - CAP
    first = jax.random.randint(keys[0], (), max(0, rest - 3 * CAP), min(CAP, rest) + 1)
    left_one = rest - first
    second = jax.random.randint(keys[1], (), jnp.maximum(0, left_one - 2 * CAP), jnp.minimum(CAP, left_one) + 1)
    left_two = left_one - second
    third = jax.random.randint(keys[2], (), jnp.maximum(0, left_two - CAP), jnp.minimum(CAP, left_two) + 1)
    fourth = left_two - third
    counts = jnp.stack([jnp.array(CAP, jnp.int32), first.astype(jnp.int32), second.astype(jnp.int32), third.astype(jnp.int32), fourth.astype(jnp.int32)])
    ends = jnp.cumsum(counts)
    labels = jax.random.permutation(keys[3], 5).astype(jnp.int32) - 2
    positions = jnp.arange(E_DEV, dtype=jnp.int32)
    group = jnp.sum((positions[:, None] >= ends[None, :]).astype(jnp.int32), axis=1)
    values = (dom_index + labels[group] + N_DOM) % N_DOM
    order = jax.random.permutation(keys[4], E_DEV)
    return jnp.zeros((E_DEV,), jnp.int32).at[order].set(values.astype(jnp.int32))


def draw_mortar_route(key, part):
    blocks = ELEMS // E_DEV
    keys = jax.random.split(jax.random.fold_in(key, 7), blocks)
    dom_ids = (jnp.arange(blocks, dtype=jnp.int32) // N_SUB).astype(jnp.int32)
    routes = jax.vmap(route_block)(keys, dom_ids)
    return routes.reshape(ELEMS, 1).astype(jnp.int32)


def touch_ends(values, key, smallest, high):
    longest = values.shape.index(max(values.shape))
    spots = []
    for shift in (0, 1):
        where = [jax.random.randint(jax.random.fold_in(key, axis), (), 0, length) for axis, length in enumerate(values.shape)]
        where[longest] = (where[longest] + shift) % values.shape[longest]
        spots.append(tuple(where))
    return values.at[spots[0]].set(smallest).at[spots[1]].set(high)


def block_levels(rng, dims, shards, low, top_value):
    factor_of = 1.0
    for dim, parts in shards:
        heights = jax.random.uniform(jax.random.fold_in(jax.random.fold_in(rng, 6), dim), (parts,), jnp.float32, low / len(shards), top_value / len(shards))
        factor_of = factor_of * jnp.repeat(jnp.exp(heights), dims[dim] // parts).reshape((-1,) + (1,) * (len(dims) - 1 - dim))
    return factor_of


def bell_draw(key, shape, deviation, limit, cuts=(), held_as=jnp.bfloat16):
    entries = jax.random.normal(key, shape, jnp.float32) * deviation
    if len(cuts) > 0:
        entries = block_levels(key, shape, cuts, -0.22, 0.18) * entries
    return jnp.clip(entries, min=-limit, max=limit).astype(held_as)


def setup_inputs(seed: int = 0) -> dict:
    streams_of = jax.random.split(jax.random.key(seed), 8)
    adjoint_field = bell_draw(streams_of[0], (ELEMS, FIELDS, NODES ** 3), 1.0, 6.0, ((0, 32),), jnp.float32)
    metric = jnp.clip(jnp.exp(math.log(4.0) - 2.0794415 * jax.random.uniform(streams_of[1], (ELEMS, 3, NODES ** 3), jnp.float32) ** block_levels(streams_of[1], (ELEMS, 3, NODES ** 3), ((0, 32),), -0.2, 0.2)), 0.5, 4.0)
    velocity = bell_draw(streams_of[2], (ELEMS, 3, NODES ** 3), 0.3, 2.0, ((0, 32),), jnp.float32)
    mortar_route = draw_mortar_route(jax.random.fold_in(streams_of[7], 71), 0)
    mortar_element = touch_ends(jax.random.randint(streams_of[4], (ELEMS, 1), 0, E_DEV), jax.random.fold_in(streams_of[4], 1), 0, E_DEV - 1).astype(jnp.int32)
    face_code = touch_ends(jax.random.randint(streams_of[5], (ELEMS, 1), 0, 8), jax.random.fold_in(streams_of[5], 1), 0, 7).astype(jnp.int32)
    hanging = touch_ends((jax.random.randint(streams_of[6], (ELEMS, 1), 0, 4) < 3).astype(jnp.int32), jax.random.fold_in(streams_of[6], 1), 0, 1)
    return {"adjoint_field": adjoint_field, "metric": metric, "velocity": velocity, "mortar_route": mortar_route, "mortar_element": mortar_element, "face_code": face_code, "hanging": hanging}


gll_nodes = np.array([-1.0, -0.8717401485096066, -0.5917001814331423, -0.2092992179024789, 0.2092992179024789, 0.5917001814331423, 0.8717401485096066, 1.0])
viscosity = 0.005


def legendre_seven(points):
    prev = np.ones(points.shape)
    curr = np.array(points)
    for order in range(1, 7):
        nxt = ((2 * order + 1) * points * curr - order * prev) / (order + 1)
        prev, curr = curr, nxt
    return curr


def diff_matrix():
    values = legendre_seven(gll_nodes)
    result_mat = np.zeros((8, 8))
    for row in range(8):
        for col in range(8):
            if row != col:
                result_mat[row, col] = values[row] / (values[col] * (gll_nodes[row] - gll_nodes[col]))
    result_mat[0, 0] = -14.0
    result_mat[7, 7] = 14.0
    return result_mat


def lagrange_at(points):
    basis = np.ones((8, 8))
    for row in range(8):
        for col in range(8):
            for other in range(8):
                if other != col:
                    basis[row, col] *= (points[row] - gll_nodes[other]) / (gll_nodes[col] - gll_nodes[other])
    return basis


def face_tables():
    halves = [lagrange_at((gll_nodes - 1.0) / 2.0), lagrange_at((gll_nodes + 1.0) / 2.0)]
    perm_mat = np.zeros((64, 64))
    for col in range(64):
        perm_mat[(col % 8) * 8 + col // 8, col] = 1.0
    tables = []
    for code in range(8):
        mat = np.kron(halves[code % 2], halves[(code // 2) % 2])
        if code >= 4:
            mat = mat @ perm_mat
        tables.append(mat)
    return np.stack(tables).astype(np.float32)


def kron_tables():
    dmat = diff_matrix()
    eye_eight = np.eye(8)
    first = np.kron(np.kron(eye_eight, dmat), eye_eight)
    second = np.kron(np.kron(eye_eight, eye_eight), dmat)
    return dmat.astype(np.float32), first.astype(np.float32), second.astype(np.float32)


def fold_faces(fine, codes):
    tables = jnp.asarray(face_tables())
    total = jnp.zeros(fine.shape, jnp.float32)
    for code in range(8):
        mapped = jnp.einsum("efa,ab->efb", fine, tables[code], precision=lax.Precision.HIGHEST)
        total = total + jnp.where((codes == code)[:, :, None], mapped, 0.0)
    return total


def derive(field, dim, mats):
    dmat, first, second = mats
    count = field.shape[0]
    if dim == 0:
        cube = field.reshape(count, 5, 8, 64)
        return jnp.einsum("ai,efip->efap", dmat, cube, precision=lax.Precision.HIGHEST).reshape(count, 5, 512)
    kron_mat = first if dim == 1 else second
    return jnp.einsum("efp,qp->efq", field, kron_mat, precision=lax.Precision.HIGHEST)


def derive_back(field, dim, mats):
    dmat, first, second = mats
    count = field.shape[0]
    if dim == 0:
        cube = field.reshape(count, 5, 8, 64)
        return jnp.einsum("ai,efap->efip", dmat, cube, precision=lax.Precision.HIGHEST).reshape(count, 5, 512)
    kron_mat = first if dim == 1 else second
    return jnp.einsum("efq,qp->efp", field, kron_mat, precision=lax.Precision.HIGHEST)


def apply_adjoint(summed, metric, velocity):
    mats = tuple(jnp.asarray(m) for m in kron_tables())
    total = jnp.zeros(summed.shape, jnp.float32)
    for dim in range(3):
        inner = viscosity * metric[:, dim:dim + 1] * derive(summed, dim, mats) + velocity[:, dim:dim + 1] * summed
        total = total + derive_back(inner, dim, mats)
    return total


def reference(adjoint_field, metric, velocity, mortar_route, mortar_element, face_code, hanging):
    count = adjoint_field.shape[0]
    field_cube = adjoint_field.reshape(count, 5, 8, 8, 8)
    fine = field_cube[:, :, :, 7, :].reshape(count, 5, 64)
    hang_f = hanging.astype(jnp.float32)
    folded = (fold_faces(fine, face_code) * hang_f[:, :, None]).astype(jnp.bfloat16)
    element_ids = jnp.arange(count, dtype=jnp.int32)
    sub_index = (element_ids // E_DEV) % N_SUB
    target = ((mortar_route[:, 0] * N_SUB + sub_index) * E_DEV + mortar_element[:, 0]).astype(jnp.int32)
    mortar = jnp.zeros((count, 5, 64), jnp.float32).at[target].add(folded.astype(jnp.float32))
    keep = (1.0 - hang_f)[:, :, None, None]
    field_cube = field_cube.at[:, :, :, 7, :].set(field_cube[:, :, :, 7, :] * keep)
    field_cube = field_cube.at[:, :, :, 0, :].add(mortar.reshape(count, 5, 8, 8))
    shared = field_cube[:-1, :, 7] + field_cube[1:, :, 0]
    field_cube = field_cube.at[:-1, :, 7].set(shared).at[1:, :, 0].set(shared)
    summed = field_cube.reshape(count // E_DEV, E_DEV, 5, 512)
    metric_b = metric.reshape(count // E_DEV, E_DEV, 3, 512)
    velocity_b = velocity.reshape(count // E_DEV, E_DEV, 3, 512)
    result = lax.map(lambda t: apply_adjoint(t[0], t[1], t[2]), (summed, metric_b, velocity_b))
    return result.reshape(count, 5, 512)
```

```python
import jax
import jax.numpy as jnp
import ml_dtypes
import numpy as np
from jax import lax
from jax.experimental import pallas as pl
from jax.experimental.pallas import tpu as pltpu
from jax.sharding import PartitionSpec as P

gll_nodes = np.array(
    [
        -1.0,
        -0.8717401485096066,
        -0.5917001814331423,
        -0.2092992179024789,
        0.2092992179024789,
        0.5917001814331423,
        0.8717401485096066,
        1.0,
    ]
)
viscosity = 0.005
F32, BF16 = jnp.float32, jnp.bfloat16
E = 128
ANY = pl.BlockSpec(memory_space=pl.ANY)
VM = pl.BlockSpec(memory_space=pltpu.VMEM)
SM = pl.BlockSpec(memory_space=pltpu.SMEM)
LIMIT = 32 * 1024 * 1024


def legendre_seven(points):
    prev = np.ones(points.shape)
    curr = np.array(points)
    for order in range(1, 7):
        nxt = ((2 * order + 1) * points * curr - order * prev) / (order + 1)
        prev, curr = (curr, nxt)
    return curr


def diff_matrix():
    values = legendre_seven(gll_nodes)
    result_mat = np.zeros((8, 8))
    for row in range(8):
        for col in range(8):
            if row != col:
                result_mat[row, col] = values[row] / (
                    values[col] * (gll_nodes[row] - gll_nodes[col])
                )
    result_mat[0, 0] = -14.0
    result_mat[7, 7] = 14.0
    return result_mat


def lagrange_at(points):
    basis = np.ones((8, 8))
    for row in range(8):
        for col in range(8):
            for other in range(8):
                if other != col:
                    basis[row, col] *= (points[row] - gll_nodes[other]) / (
                        gll_nodes[col] - gll_nodes[other]
                    )
    return basis


def face_tables():
    halves = [lagrange_at((gll_nodes - 1.0) / 2.0), lagrange_at((gll_nodes + 1.0) / 2.0)]
    perm_mat = np.zeros((64, 64))
    for col in range(64):
        perm_mat[col % 8 * 8 + col // 8, col] = 1.0
    tables = []
    for code in range(8):
        mat = np.kron(halves[code % 2], halves[code // 2 % 2])
        if code >= 4:
            mat = mat @ perm_mat
        tables.append(mat)
    return np.stack(tables)


def two_parts(mat):
    high = mat.astype(ml_dtypes.bfloat16)
    low = (mat - high.astype(np.float64)).astype(ml_dtypes.bfloat16)
    return high, low


def constants():
    dmat = diff_matrix()
    eye = np.eye(8)
    along_j = np.kron(np.eye(2), np.kron(dmat, eye))
    along_k = np.kron(np.eye(16), dmat)
    along_i = along_j

    def forward(first, second):
        fh, fl = two_parts(viscosity * first.T)
        sh, sl = two_parts(viscosity * second.T)
        top = np.concatenate([fh, sh], 1)
        return np.concatenate([top, top], 0), np.concatenate([fl, sl], 1)

    def backward(first, second):
        fh, fl = two_parts(first)
        sh, sl = two_parts(second)
        return (
            np.concatenate([np.concatenate([fh, fl], 1), np.concatenate([sh, sl], 1)], 0),
            np.concatenate([fh, sh], 0),
        )

    def split_parity(mat):
        vectors = []
        for sign in (1.0, -1.0):
            small = (mat[:4, :4] + sign * mat[:4, ::-1][:, :4]) / 2
            for c in range(2):
                for other in range(2):
                    for swap in (0, 1):
                        vectors.append(
                            np.concatenate(
                                [
                                    np.full(64, small[2 * c + h, 2 * other + (h ^ swap)])
                                    for h in range(2)
                                ]
                            )
                        )
        return np.stack(vectors)

    coef = np.concatenate([split_parity(viscosity * dmat), split_parity(dmat.T)], 0)
    column = np.tile(np.repeat(viscosity * dmat[:, 0], 8), 2)[None]
    coef = np.concatenate([coef, column, np.zeros((7, 128))], 0).astype(np.float32)

    tables = face_tables()
    fold = np.zeros((256, 512), ml_dtypes.bfloat16)
    for code in range(8):
        high, low = two_parts(tables[code])
        for i in range(8):
            for k in range(8):
                c, h = i // 2, i % 2
                spot = (56 + 64 * h + 16 * c + k) % 128
                cols = slice(64 * code, 64 * code + 64)
                fold[spot, cols] = high[8 * i + k]
                fold[(spot + 8) % 128, cols] = high[8 * i + k]
                fold[128 + spot, cols] = low[8 * i + k]

    spread = np.zeros((64, 512))
    place = np.zeros((64, 512))
    for i in range(8):
        for k in range(8):
            place[8 * i + k, 64 * i + k] = 1.0
            for j in range(8):
                spread[8 * i + k, 64 * i + 8 * j + k] = 1.0
    zero = np.zeros((64, 512))

    def pair(mat):
        one = np.concatenate(
            [np.concatenate([mat, zero], 1), np.concatenate([zero, mat], 1)], 0
        )
        return np.concatenate([one, one], 0).astype(ml_dtypes.bfloat16)

    return {
        "fold": fold,
        "forward": forward(along_j, along_k),
        "backward": backward(along_j, along_k),
        "face_forward": forward(along_i, along_k),
        "face_backward": backward(along_i, along_k),
        "spread": pair(spread),
        "place": pair(place),
        "coef": coef,
    }


def iota(dim, shape=(E, 128)):
    return lax.broadcasted_iota(jnp.int32, shape, dim)


def down(row):
    spots = jnp.where(iota(0) == iota(1), row, 0).astype(F32).astype(BF16)
    return jnp.dot(spots, jnp.ones((E, 128), BF16), preferred_element_type=F32)


def dot(a, b):
    return jnp.dot(a, b, preferred_element_type=F32)


def parts_of(x):
    high = x.astype(BF16)
    return high, (x - high.astype(F32)).astype(BF16)


def edge_kernel(hang_ref, low_ref, high_ref, low_out, high_out):
    lane = iota(1, (1, 128)) % 64
    low_out[...] = jnp.zeros((8, 128), F32)
    high_out[...] = jnp.zeros((8, 128), F32)
    low_keep = jnp.where(lane >= 56, 1.0 - hang_ref[0, 0].astype(F32), 1.0)
    high_keep = jnp.where(lane >= 56, 1.0 - hang_ref[0, E - 1].astype(F32), 1.0)
    for f in range(5):
        low_out[f : f + 1] = pltpu.roll(low_ref[f, 0:1] * low_keep, 64, 1)
        high_out[f : f + 1] = pltpu.roll(high_ref[f, 7:8] * high_keep, 64, 1)


def edges_of(adjoint, hang):
    return pl.pallas_call(
        edge_kernel,
        grid=(1,),
        out_shape=[jax.ShapeDtypeStruct((8, 128), F32)] * 2,
        in_specs=[
            SM,
            pl.BlockSpec((5, 8, 128), lambda g: (0, 0, 0)),
            pl.BlockSpec((5, 8, 128), lambda g: (0, E // 8 - 1, 3)),
        ],
        out_specs=[pl.BlockSpec((8, 128), lambda g: (0, 0))] * 2,
        name="edges",
    )(hang, adjoint, adjoint)


def fold_kernel(peers, adj_hbm, route, target, code, hang, fold, *refs):
    outs, own, x, sems = refs[:4], refs[4], refs[5], refs[6]
    copies = [pltpu.make_async_copy(adj_hbm.at[f], x.at[f], sems.at[f]) for f in range(5)]
    for copy in copies:
        copy.start()
    slot = lax.rem(route[...] - lax.axis_index("dom") + 2 + peers, peers)
    spot = slot * E + target[...]
    hit = (iota(0, (5 * E, E)) == spot).astype(F32).astype(BF16)
    lane = iota(1)
    marked = down(jnp.where(hang[...] == 1, code[...], -2)) - (lane // 64).astype(F32)
    odd = lane % 16 >= 8
    group = (lane // 16 + 1) % 4
    faces = []
    for f in range(5):
        copies[f].wait()
        packed = jnp.zeros((E, 128), F32)
        for c in range(4):
            moved = x[f, :, 128 * c : 128 * c + 128]
            if c:
                moved = pltpu.roll(moved, 16 * c, 1)
            packed = jnp.where(odd & (group == c), moved, packed)
        high = packed.astype(BF16)
        high_f = high.astype(F32)
        both = jnp.where(odd, high_f, pltpu.roll(packed - high_f, 8, 1)).astype(BF16)
        mapped = dot(jnp.concatenate([both, high], 1), fold[...])
        total = jnp.zeros((E, 128), F32)
        for q in range(4):
            total = total + jnp.where(
                marked == 2.0 * q, mapped[:, 128 * q : 128 * q + 128], 0.0
            )
        faces.append(total + pltpu.roll(total, 64, 1))
    left = lane < 64
    f01 = jnp.where(left, faces[0], faces[1]).astype(BF16)
    f23 = jnp.where(left, faces[2], faces[3]).astype(BF16)
    f4 = faces[4].astype(BF16)
    rhs = jnp.concatenate([f01, f23, f4], 1)
    for o in range(5):
        ref = (outs[0], outs[1], own, outs[2], outs[3])[o]
        sums = dot(hit[o * E : o * E + E], rhs)
        ref[0:128] = sums[:, 0:128].astype(ref.dtype)
        ref[128:256] = sums[:, 128:256].astype(ref.dtype)
        last = jnp.where(left[:64], sums[:64, 256:384], sums[64:, 256:384])
        ref[256:320] = last.astype(ref.dtype)


def folded_of(adjoint, route, target, code, hang, fold, peers):
    def body(*refs):
        fold_kernel(peers, *refs)

    return pl.pallas_call(
        body,
        out_shape=[jax.ShapeDtypeStruct((320, 128), BF16)] * 4
        + [jax.ShapeDtypeStruct((320, 128), F32)],
        in_specs=[ANY] + [VM] * 5,
        out_specs=[VM] * 5,
        scratch_shapes=[pltpu.VMEM((5, E, 512), F32), pltpu.SemaphoreType.DMA((5,))],
        compiler_params=pltpu.CompilerParams(vmem_limit_bytes=LIMIT),
        name="fold",
    )(adjoint, route, target, code, hang, fold)


def swap(x):
    return pltpu.roll(x, 64, 1)


def along_first(x, coef, base):
    r3, r2 = swap(x[3]), swap(x[2])
    parity = ((x[0] + r3, x[1] + r2), (x[0] - r3, x[1] - r2))
    sums = []
    for s in range(2):
        kept = (parity[s][0], swap(parity[s][0]), parity[s][1], swap(parity[s][1]))
        for c in range(2):
            at = base + 8 * s + 4 * c
            total = coef[at : at + 1] * kept[0]
            for n in range(1, 4):
                total = total + coef[at + n : at + n + 1] * kept[n]
            sums.append(total)
    p0, p1, q0, q1 = sums
    return [p0 + q0, p1 + q1, swap(q1 - p1), swap(q0 - p0)]


def main_kernel(
    adj_hbm, met_hbm, vel_hbm, hang, before, after, wf1, wf2, wb1, wb2, coef,
    out, q_out, plane_out, x_ref, met, vel, sems,
):
    loads = [
        pltpu.make_async_copy(met_hbm, met, sems.at[0]),
        pltpu.make_async_copy(vel_hbm, vel, sems.at[1]),
        pltpu.make_async_copy(adj_hbm, x_ref, sems.at[2]),
    ]
    for copy in loads:
        copy.start()
    lane, row = iota(1), iota(0)
    keep = jnp.where(lane % 64 >= 56, 1.0 - down(hang[...]), 1.0)
    left = lane < 64
    for copy in loads:
        copy.wait()

    for c in range(4):
        at = slice(128 * c, 128 * c + 128)
        w = met[1, :, at] * coef[32:33] + jnp.where(lane % 64 < 8, vel[1, :, at], 0.0)
        high, low = parts_of(w)
        wide = dot(high, wb1[0:128])
        q_out[:, at] = wide[:, :128] + wide[:, 128:] + dot(low, wb2[0:128])

    for n, (ref, d) in enumerate(((met, 0), (met, 2), (vel, 0), (vel, 2))):
        packed = jnp.zeros((E, 128), F32)
        for c in range(4):
            moved = ref[d, :, 128 * c : 128 * c + 128]
            if c:
                moved = pltpu.roll(moved, 16 * c, 1)
            packed = jnp.where((lane // 16) % 4 == c, moved, packed)
        even = jnp.where(left, packed, swap(packed))
        other = jnp.where(left, swap(packed), packed)
        plane_out[n] = jnp.where(lane % 16 < 8, even, pltpu.roll(other, 8, 1))

    def field(f, carry):
        x = [x_ref[f, :, 128 * c : 128 * c + 128] * keep for c in range(4)]
        low_faces = pltpu.roll(swap(x[0]), E - 1, 0)
        high_faces = pltpu.roll(swap(x[3]), 1, 0)
        low_faces = jnp.where(row == E - 1, after[pl.ds(f, 1)], low_faces)
        high_faces = jnp.where(row == 0, before[pl.ds(f, 1)], high_faces)
        x[0] = x[0] + jnp.where(left, high_faces, 0.0)
        x[3] = x[3] + jnp.where(left, 0.0, low_faces)
        g0 = along_first(x, coef, 0)
        inner0 = []
        totals = []
        for c in range(4):
            at = slice(128 * c, 128 * c + 128)
            high, low = parts_of(x[c])
            g = dot(jnp.concatenate([high, low], 1), wf1[...]) + dot(high, wf2[...])
            inner0.append(met[0, :, at] * g0[c] + vel[0, :, at] * x[c])
            in1 = met[1, :, at] * g[:, :128] + vel[1, :, at] * x[c]
            in2 = met[2, :, at] * g[:, 128:] + vel[2, :, at] * x[c]
            high1, low1 = parts_of(in1)
            high2, low2 = parts_of(in2)
            wide = dot(jnp.concatenate([high1, high2], 1), wb1[...])
            totals.append(
                wide[:, :128]
                + wide[:, 128:]
                + dot(jnp.concatenate([low1, low2], 1), wb2[...])
            )
        back = along_first(inner0, coef, 16)
        for c in range(4):
            out[f, :, 128 * c : 128 * c + 128] = totals[c] + back[c]
        return carry

    lax.fori_loop(0, 5, field, 0)


def main_of(adjoint, metric, velocity, hang, before, after, tables):
    return pl.pallas_call(
        main_kernel,
        out_shape=[
            jax.ShapeDtypeStruct((5, E, 512), F32),
            jax.ShapeDtypeStruct((E, 512), F32),
            jax.ShapeDtypeStruct((4, E, 128), F32),
        ],
        in_specs=[ANY] * 3 + [VM] * 8,
        out_specs=[VM] * 3,
        scratch_shapes=[
            pltpu.VMEM((5, E, 512), F32),
            pltpu.VMEM((3, E, 512), F32),
            pltpu.VMEM((3, E, 512), F32),
            pltpu.SemaphoreType.DMA((3,)),
        ],
        compiler_params=pltpu.CompilerParams(vmem_limit_bytes=LIMIT),
        cost_estimate=pl.CostEstimate(
            flops=4_000_000_000, bytes_accessed=6_000_000, transcendentals=0
        ),
        name="inner",
    )(
        adjoint, metric, velocity, hang, before, after,
        *tables["forward"], *tables["backward"], tables["coef"],
    )


def line_kernel(a, b, own, c, d, low_out, high_out):
    def rows(start):
        return sum(
            ref[start : start + 16].astype(F32) for ref in (a, b, own, c, d)
        )

    low_out[...] = jnp.zeros((8, 128), F32)
    high_out[...] = jnp.zeros((8, 128), F32)
    for n, (first, last) in enumerate(((0, 112), (128, 240), (256, 304))):
        low_out[n : n + 1] = pltpu.roll(rows(first)[0:1], 56, 1)
        line = rows(last)[15:16]
        high_out[n : n + 1] = pltpu.roll(swap(line) if n == 2 else line, 72, 1)


def lines_of(parts):
    return pl.pallas_call(
        line_kernel,
        out_shape=[jax.ShapeDtypeStruct((8, 128), F32)] * 2,
        in_specs=[VM] * 5,
        out_specs=[VM] * 2,
        name="lines",
    )(*parts)


def post_kernel(
    a, b, own, c, d, before, after, base, q_ref, plane, wf1, wf2, wb1, wb2,
    spread, place, out_hbm, out, sems,
):
    lane, row = iota(1), iota(0)
    left = lane < 64
    refs = (a, b, own, c, d)
    copies = [pltpu.make_async_copy(out.at[f], out_hbm.at[f], sems.at[f]) for f in range(5)]
    for n in range(3):
        rows = slice(128 * n, min(128 * n + 128, 320))
        m = sum(ref[rows].astype(F32) for ref in refs)
        if n == 2:
            m = jnp.concatenate([m, swap(m)], 0)
        low_lines = pltpu.roll(pltpu.roll(m, 56, 1), E - 1, 0)
        high_lines = pltpu.roll(pltpu.roll(m, 72, 1), 1, 0)
        low_lines = jnp.where(row == E - 1, after[n : n + 1], low_lines)
        high_lines = jnp.where(row == 0, before[n : n + 1], high_lines)
        y = m + jnp.where(lane % 64 < 8, high_lines, 0.0)
        y = y + jnp.where(lane % 64 >= 56, low_lines, 0.0)
        high, low = parts_of(y)
        y_parts = jnp.concatenate([high, low], 1)
        g = dot(y_parts, wf1[...]) + dot(high, wf2[...])
        in0 = plane[0] * g[:, :128] + plane[2] * y
        in2 = plane[1] * g[:, 128:] + plane[3] * y
        high0, low0 = parts_of(in0)
        high2, low2 = parts_of(in2)
        wide = dot(jnp.concatenate([high0, high2], 1), wb1[...])
        r = wide[:, :128] + wide[:, 128:] + dot(jnp.concatenate([low0, low2], 1), wb2[...])
        r_parts = jnp.concatenate(parts_of(r), 1)
        for f in range(2 * n, min(2 * n + 2, 5)):
            for c_at in range(4):
                at = slice(128 * c_at, 128 * c_at + 128)
                cols = slice(512 * (f - 2 * n) + 128 * c_at, 512 * (f - 2 * n) + 128 * c_at + 128)
                out[f, :, at] = (
                    base[f, :, at]
                    + q_ref[:, at] * dot(y_parts, spread[:, cols])
                    + dot(r_parts, place[:, cols])
                )
            copies[f].start()
    for copy in copies:
        copy.wait()


def post_of(parts, before, after, base, q, plane, tables):
    return pl.pallas_call(
        post_kernel,
        out_shape=jax.ShapeDtypeStruct((5, E, 512), F32),
        in_specs=[VM] * 16,
        out_specs=ANY,
        scratch_shapes=[pltpu.VMEM((5, E, 512), F32), pltpu.SemaphoreType.DMA((5,))],
        compiler_params=pltpu.CompilerParams(vmem_limit_bytes=LIMIT),
        name="outer",
    )(
        *parts, before, after, base, q, plane,
        *tables["face_forward"], *tables["face_backward"],
        tables["spread"], tables["place"],
    )


def both_ways(low, high):
    axes = ("dom", "sub")
    count = lax.axis_size(axes)
    forward = [(i, i + 1) for i in range(count - 1)]
    backward = [(i + 1, i) for i in range(count - 1)]
    return lax.ppermute(high, axes, forward), lax.ppermute(low, axes, backward)


def shards(adjoint_field, metric, velocity, mortar_route, mortar_element, face_code, hanging):
    tables = constants()
    peers = lax.axis_size("dom")
    adjoint = jnp.transpose(adjoint_field, (1, 0, 2))
    met = jnp.transpose(metric, (1, 0, 2))
    vel = jnp.transpose(velocity, (1, 0, 2))
    route, target, code, hang = (
        x.reshape(1, E) for x in (mortar_route, mortar_element, face_code, hanging)
    )
    low, high = edges_of(adjoint, hang)
    before, after = both_ways(low, high)
    *sends, own = folded_of(adjoint, route, target, code, hang, tables["fold"], peers)
    got = []
    for send, offset in zip(sends, (-2, -1, 1, 2)):
        pairs = [(i, (i + offset) % peers) for i in range(peers)]
        got.append(lax.ppermute(send, "dom", pairs))
    base, q, plane = main_of(adjoint, met, vel, hang, before, after, tables)
    parts = (got[0], got[1], own, got[2], got[3])
    line_before, line_after = both_ways(*lines_of(parts))
    result = post_of(parts, line_before, line_after, base, q, plane, tables)
    return jnp.transpose(result, (1, 0, 2))


def solution(mesh):
    block = P(("dom", "sub"), None, None)
    flat = P(("dom", "sub"), None)
    return jax.shard_map(
        shards,
        mesh=mesh,
        in_specs=(block, block, block, flat, flat, flat, flat),
        out_specs=block,
        check_vma=False,
    )
```

```python
import jax
import jax.numpy as jnp
import ml_dtypes
import numpy as np
from jax import lax
from jax.experimental import pallas as pl
from jax.experimental.pallas import tpu as pltpu
from jax.sharding import PartitionSpec as P

gll_nodes = np.array(
    [
        -1.0,
        -0.8717401485096066,
        -0.5917001814331423,
        -0.2092992179024789,
        0.2092992179024789,
        0.5917001814331423,
        0.8717401485096066,
        1.0,
    ]
)
viscosity = 0.005
F32, BF16 = jnp.float32, jnp.bfloat16
E = 128
HBM = pl.BlockSpec(memory_space=pltpu.HBM)
VM = pl.BlockSpec(memory_space=pltpu.VMEM)
LIMIT = 32 * 1024 * 1024


def legendre_seven(points):
    prev = np.ones(points.shape)
    curr = np.array(points)
    for order in range(1, 7):
        nxt = ((2 * order + 1) * points * curr - order * prev) / (order + 1)
        prev, curr = (curr, nxt)
    return curr


def diff_matrix():
    values = legendre_seven(gll_nodes)
    result_mat = np.zeros((8, 8))
    for row in range(8):
        for col in range(8):
            if row != col:
                result_mat[row, col] = values[row] / (
                    values[col] * (gll_nodes[row] - gll_nodes[col])
                )
    result_mat[0, 0] = -14.0
    result_mat[7, 7] = 14.0
    return result_mat


def lagrange_at(points):
    basis = np.ones((8, 8))
    for row in range(8):
        for col in range(8):
            for other in range(8):
                if other != col:
                    basis[row, col] *= (points[row] - gll_nodes[other]) / (
                        gll_nodes[col] - gll_nodes[other]
                    )
    return basis


def face_tables():
    halves = [lagrange_at((gll_nodes - 1.0) / 2.0), lagrange_at((gll_nodes + 1.0) / 2.0)]
    perm_mat = np.zeros((64, 64))
    for col in range(64):
        perm_mat[col % 8 * 8 + col // 8, col] = 1.0
    tables = []
    for code in range(8):
        mat = np.kron(halves[code % 2], halves[code // 2 % 2])
        if code >= 4:
            mat = mat @ perm_mat
        tables.append(mat)
    return np.stack(tables)


def two_parts(mat):
    high = mat.astype(ml_dtypes.bfloat16)
    low = (mat - high.astype(np.float64)).astype(ml_dtypes.bfloat16)
    return high, low


def constants():
    dmat = diff_matrix()
    eye = np.eye(8)
    along_j = np.kron(np.eye(2), np.kron(dmat, eye))
    along_k = np.kron(np.eye(16), dmat)

    def forward(first, second):
        fh, fl = two_parts(viscosity * first.T)
        sh, sl = two_parts(viscosity * second.T)
        top = np.concatenate([fh, sh], 1)
        return np.concatenate([top, top], 0), np.concatenate([fl, sl], 1)

    def backward(first, second):
        fh, fl = two_parts(first)
        sh, sl = two_parts(second)
        return (
            np.concatenate([np.concatenate([fh, fl], 1), np.concatenate([sh, sl], 1)], 0),
            np.concatenate([fh, sh], 0),
        )

    def split_parity(mat):
        vectors = []
        for sign in (1.0, -1.0):
            small = (mat[:4, :4] + sign * mat[:4, ::-1][:, :4]) / 2
            for c in range(2):
                for other in range(2):
                    for swap in (0, 1):
                        vectors.append(
                            np.concatenate(
                                [
                                    np.full(64, small[2 * c + h, 2 * other + (h ^ swap)])
                                    for h in range(2)
                                ]
                            )
                        )
        return np.stack(vectors)

    coef = np.concatenate([split_parity(viscosity * dmat), split_parity(dmat.T)], 0)
    column = np.tile(np.repeat(viscosity * dmat[:, 0], 8), 2)[None]
    ends = [
        np.repeat(viscosity * dmat[2 * c : 2 * c + 2, end], 64)[None]
        for end in (0, 7)
        for c in range(4)
    ]
    coef = np.concatenate([coef, column, *ends, np.zeros((7, 128))], 0).astype(np.float32)

    tables = face_tables()
    fold = np.zeros((256, 512), ml_dtypes.bfloat16)
    for code in range(8):
        high, low = two_parts(tables[code])
        for i in range(8):
            for k in range(8):
                c, h = i // 2, i % 2
                spot = (56 + 64 * h + 16 * c + k) % 128
                cols = slice(64 * code, 64 * code + 64)
                fold[spot, cols] = high[8 * i + k]
                fold[(spot + 8) % 128, cols] = high[8 * i + k]
                fold[128 + spot, cols] = low[8 * i + k]

    spread = np.zeros((64, 512))
    place = np.zeros((64, 512))
    for i in range(8):
        for k in range(8):
            place[8 * i + k, 64 * i + k] = 1.0
            for j in range(8):
                spread[8 * i + k, 64 * i + 8 * j + k] = 1.0
    zero = np.zeros((64, 512))

    def pair(mat):
        one = np.concatenate(
            [np.concatenate([mat, zero], 1), np.concatenate([zero, mat], 1)], 0
        )
        return np.concatenate([one, one], 0).astype(ml_dtypes.bfloat16)

    return {
        "fold": fold,
        "forward": forward(along_j, along_k),
        "backward": backward(along_j, along_k),
        "spread": pair(spread),
        "place": pair(place),
        "coef": coef,
    }


def iota(dim, shape=(E, 128)):
    return lax.broadcasted_iota(jnp.int32, shape, dim)


def down(row):
    spots = jnp.where(iota(0) == iota(1), row, 0).astype(F32).astype(BF16)
    return jnp.dot(spots, jnp.ones((E, 128), BF16), preferred_element_type=F32)


def dot(a, b):
    return jnp.dot(a, b, preferred_element_type=F32)


def parts_of(x):
    high = x.astype(BF16)
    return high, (x - high.astype(F32)).astype(BF16)


def fetch(pairs, sems):
    copies = [
        pltpu.make_async_copy(src, dst, sems.at[n]) for n, (src, dst) in enumerate(pairs)
    ]
    for copy in copies:
        copy.start()
    return copies


def fold_kernel(
    route_hbm, target_hbm, code_hbm, hang_hbm, adj_hbm, fold_hbm, faces_out, edges_out,
    ints, x, fold, sems,
):
    peers = lax.axis_size("dom")
    copies = fetch(
        [(ref, ints.at[n]) for n, ref in enumerate((route_hbm, target_hbm, code_hbm, hang_hbm))]
        + [(fold_hbm, fold)]
        + [(adj_hbm.at[f], x.at[f]) for f in range(5)],
        sems,
    )
    for copy in copies[:5]:
        copy.wait()
    route, target, code, hang = (ints[n] for n in range(4))
    lane = iota(1)
    left = lane < 64
    marked = down(jnp.where(hang == 1, code, -2)) - (lane // 64).astype(F32)
    odd = lane % 16 >= 8
    group = (lane // 16 + 1) % 4
    faces = []
    for f in range(5):
        copies[5 + f].wait()
        packed = jnp.zeros((E, 128), F32)
        for c in range(4):
            moved = x[f, :, 128 * c : 128 * c + 128]
            if c:
                moved = pltpu.roll(moved, 16 * c, 1)
            packed = jnp.where(odd & (group == c), moved, packed)
        high = packed.astype(BF16)
        high_f = high.astype(F32)
        both = jnp.where(odd, high_f, pltpu.roll(packed - high_f, 8, 1)).astype(BF16)
        mapped = dot(jnp.concatenate([both, high], 1), fold[...])
        total = jnp.zeros((E, 128), F32)
        for q in range(4):
            total = total + jnp.where(
                marked == 2.0 * q, mapped[:, 128 * q : 128 * q + 128], 0.0
            )
        faces.append(total + pltpu.roll(total, 64, 1))
    f01 = jnp.where(left, faces[0], faces[1]).astype(BF16)
    f23 = jnp.where(left, faces[2], faces[3]).astype(BF16)
    f4 = faces[4].astype(BF16)
    faces_out[0:128] = f01
    faces_out[128:256] = f23
    faces_out[256:320] = jnp.where(left[:64], faces[4][:64], faces[4][64:]).astype(BF16)
    row = iota(0, (16, 128))
    where_to = jnp.where(row == 0, route, jnp.where(row == 1, target, 0))
    faces_out[320:336] = where_to.astype(F32).astype(BF16)

    slot = lax.rem(route - lax.axis_index("dom") + 2 + peers, peers)
    spot = slot * E + target
    wanted = (row // 2) * E + (row % 2) * (E - 1)
    hit = ((spot == wanted) & (row < 10)).astype(F32).astype(BF16)
    sums = dot(hit, jnp.concatenate([f01, f23, f4], 1))
    lines = jnp.zeros((16, 128), F32)
    lane = iota(1, (16, 128))
    for n in range(3):
        part = sums[:, 128 * n : 128 * n + 128]
        part = jnp.where(row % 2 == 1, pltpu.roll(part, 72, 1), part)
        part = jnp.where(lane % 64 < 8, part, 0.0)
        lines = lines + (pltpu.roll(part, 16 * n, 1) if n else part)
    edges_out[...] = lines
    lane = iota(1, (1, 128))
    own = marked[0:1], marked[E - 1 : E]
    for n in range(3):
        first, second = 2 * n, min(2 * n + 1, 4)
        for end, (at, chunk) in enumerate(((0, 0), (E - 1, 3))):
            a = x[first, at : at + 1, 128 * chunk : 128 * chunk + 128]
            b = x[second, at : at + 1, 128 * chunk : 128 * chunk + 128]
            if end == 0:
                b = pltpu.roll(b, 64, 1)
            else:
                a = pltpu.roll(a, 64, 1)
            keep = jnp.where((lane % 64 >= 56) & (own[end] >= -1.5), 0.0, 1.0)
            spot_row = 10 + 3 * end + n
            edges_out[spot_row : spot_row + 1] = jnp.where(lane < 64, a, b) * keep


def folded_of(route, target, code, hang, adjoint, fold):
    return pl.pallas_call(
        fold_kernel,
        out_shape=[
            jax.ShapeDtypeStruct((336, 128), BF16),
            jax.ShapeDtypeStruct((16, 128), F32),
        ],
        in_specs=[HBM] * 6,
        out_specs=[VM] * 2,
        scratch_shapes=[
            pltpu.VMEM((4, 1, E), jnp.int32),
            pltpu.VMEM((5, E, 512), F32),
            pltpu.VMEM((256, 512), BF16),
            pltpu.SemaphoreType.DMA((10,)),
        ],
        compiler_params=pltpu.CompilerParams(vmem_limit_bytes=LIMIT),
        name="fold",
    )(route, target, code, hang, adjoint, fold)


def swap(x):
    return pltpu.roll(x, 64, 1)


def along_first(x, coef, base):
    r3, r2 = swap(x[3]), swap(x[2])
    parity = ((x[0] + r3, x[1] + r2), (x[0] - r3, x[1] - r2))
    sums = []
    for s in range(2):
        kept = (parity[s][0], swap(parity[s][0]), parity[s][1], swap(parity[s][1]))
        for c in range(2):
            at = base + 8 * s + 4 * c
            total = coef[at : at + 1] * kept[0]
            for n in range(1, 4):
                total = total + coef[at + n : at + n + 1] * kept[n]
            sums.append(total)
    p0, p1, q0, q1 = sums
    return [p0 + q0, p1 + q1, swap(q1 - p1), swap(q0 - p0)]


def main_kernel(
    adj_hbm, met_hbm, vel_hbm, hang, wf1, wf2, wb1, wb2, coef,
    out, q_out, plane_out, end_q, end_mv, x_ref, met, vel, sems,
):
    order = (1, 0, 2)
    pairs = [(adj_hbm.at[0], x_ref.at[0])]
    for d in order:
        pairs += [(met_hbm.at[d], met.at[d]), (vel_hbm.at[d], vel.at[d])]
    pairs += [(adj_hbm.at[f], x_ref.at[f]) for f in range(1, 5)]
    copies = fetch(pairs, sems)
    lane, row = iota(1), iota(0)
    keep = jnp.where(lane % 64 >= 56, 1.0 - down(hang[...]), 1.0)
    left = lane < 64
    for copy in copies[:3]:
        copy.wait()

    for c in range(4):
        at = slice(128 * c, 128 * c + 128)
        w = met[1, :, at] * coef[32:33] + jnp.where(lane % 64 < 8, vel[1, :, at], 0.0)
        high, low = parts_of(w)
        wide = dot(high, wb1[0:128])
        q_out[:, at] = wide[:, :128] + wide[:, 128:] + dot(low, wb2[0:128])

    for copy in copies[3:]:
        copy.wait()
    for n, (ref, d) in enumerate(((met, 0), (met, 2), (vel, 0), (vel, 2))):
        packed = jnp.zeros((E, 128), F32)
        for c in range(4):
            moved = ref[d, :, 128 * c : 128 * c + 128]
            if c:
                moved = pltpu.roll(moved, 16 * c, 1)
            packed = jnp.where((lane // 16) % 4 == c, moved, packed)
        even = jnp.where(left, packed, swap(packed))
        other = jnp.where(left, swap(packed), packed)
        plane_out[n] = jnp.where(lane % 16 < 8, even, pltpu.roll(other, 8, 1))

    small_left = iota(1, (8, 128)) < 64
    for end in range(2):
        rows = slice((E - 8) * end, (E - 8) * end + 8)
        w = []
        for c in range(4):
            at = slice(128 * c, 128 * c + 128)
            spot = 33 + 4 * end + c
            term = met[0, rows, at] * coef[spot : spot + 1]
            if c == 3 * end:
                term = term + jnp.where(small_left != (end == 1), vel[0, rows, at], 0.0)
            w.append(term)
        back = along_first(w, coef, 16)
        for c in range(4):
            end_q[end, c] = back[c]
        at = slice(384 * end, 384 * end + 128)
        for n, (ref, d) in enumerate(((met, 1), (met, 2), (vel, 1), (vel, 2))):
            end_mv[end, n] = ref[d, rows, at]

    def field(f, carry):
        x = [x_ref[f, :, 128 * c : 128 * c + 128] * keep for c in range(4)]
        low_faces = pltpu.roll(swap(x[0]), E - 1, 0)
        high_faces = pltpu.roll(swap(x[3]), 1, 0)
        x[0] = x[0] + jnp.where(left & (row > 0), high_faces, 0.0)
        x[3] = x[3] + jnp.where(left | (row == E - 1), 0.0, low_faces)
        g0 = along_first(x, coef, 0)
        inner0 = []
        totals = []
        for c in range(4):
            at = slice(128 * c, 128 * c + 128)
            high, low = parts_of(x[c])
            g = dot(jnp.concatenate([high, low], 1), wf1[...]) + dot(high, wf2[...])
            inner0.append(met[0, :, at] * g0[c] + vel[0, :, at] * x[c])
            in1 = met[1, :, at] * g[:, :128] + vel[1, :, at] * x[c]
            in2 = met[2, :, at] * g[:, 128:] + vel[2, :, at] * x[c]
            high1, low1 = parts_of(in1)
            high2, low2 = parts_of(in2)
            wide = dot(jnp.concatenate([high1, high2], 1), wb1[...])
            totals.append(
                wide[:, :128]
                + wide[:, 128:]
                + dot(jnp.concatenate([low1, low2], 1), wb2[...])
            )
        back = along_first(inner0, coef, 16)
        for c in range(4):
            out[f, :, 128 * c : 128 * c + 128] = totals[c] + back[c]
        return carry

    lax.fori_loop(0, 5, field, 0)


def main_of(adjoint, metric, velocity, hang, tables):
    return pl.pallas_call(
        main_kernel,
        out_shape=[
            jax.ShapeDtypeStruct((5, E, 512), F32),
            jax.ShapeDtypeStruct((E, 512), F32),
            jax.ShapeDtypeStruct((4, E, 128), F32),
            jax.ShapeDtypeStruct((2, 4, 8, 128), F32),
            jax.ShapeDtypeStruct((2, 4, 8, 128), F32),
        ],
        in_specs=[HBM] * 3 + [VM] * 6,
        out_specs=[VM] * 5,
        scratch_shapes=[
            pltpu.VMEM((5, E, 512), F32),
            pltpu.VMEM((3, E, 512), F32),
            pltpu.VMEM((3, E, 512), F32),
            pltpu.SemaphoreType.DMA((11,)),
        ],
        compiler_params=pltpu.CompilerParams(vmem_limit_bytes=LIMIT),
        cost_estimate=pl.CostEstimate(
            flops=4_000_000_000, bytes_accessed=6_000_000, transcendentals=0
        ),
        name="inner",
    )(
        adjoint, metric, velocity, hang,
        *tables["forward"], *tables["backward"], tables["coef"],
    )


def post_kernel(
    faces_hbm, edges_hbm, base, q_ref, plane, end_q, end_mv, wf1, wf2, wb1, wb2,
    spread, place, out_hbm, faces, edges, out, face_sems, edge_sems, out_sems,
):
    dom, sub = lax.axis_index("dom"), lax.axis_index("sub")
    peers, subs = lax.axis_size("dom"), lax.axis_size("sub")
    count = peers * subs
    me = dom * subs + sub
    face_copies = fetch(
        [
            (faces_hbm.at[lax.rem(dom + o - 2 + peers, peers)], faces.at[o])
            for o in range(5)
        ],
        face_sems,
    )
    pairs = []
    for end, step in enumerate((count - 1, 1)):
        other = lax.rem(me + step, count)
        other_dom, other_sub = lax.div(other, subs), lax.rem(other, subs)
        for o in range(5):
            source = lax.rem(other_dom + peers + 2 - o, peers) * subs + other_sub
            pairs.append((edges_hbm.at[source], edges.at[end, o]))
    edge_copies = fetch(pairs, edge_sems)
    out_copies = [
        pltpu.make_async_copy(out.at[f], out_hbm.at[f], out_sems.at[f]) for f in range(5)
    ]
    lane, row = iota(1), iota(0)
    left = lane < 64
    for copy in edge_copies:
        copy.wait()
    exists = ((me > 0).astype(F32), (me < count - 1).astype(F32))

    small_left = iota(1, (1, 128)) < 64
    halo = []
    lines = []
    for end in range(2):
        rows = []
        for n in range(3):
            spot = 10 + 3 * (1 - end) + n
            pair = edges[end, 2, spot : spot + 1] * exists[end]
            turned = pltpu.roll(pair, 64, 1)
            rows.append(jnp.where(small_left, pair, turned))
            rows.append(jnp.where(small_left, turned, pair))
        halo.append(jnp.concatenate(rows + [jnp.zeros((2, 128), F32)], 0))
        r = 1 - end
        total = edges[end, 0, r : r + 1]
        for o in range(1, 5):
            total = total + edges[end, o, 2 * o + r : 2 * o + r + 1]
        lines.append(total * exists[end])
    u = jnp.concatenate(halo, 0)
    mv = [
        jnp.concatenate(
            [
                jnp.broadcast_to(end_mv[0, n, 0:1], (8, 128)),
                jnp.broadcast_to(end_mv[1, n, 7:8], (8, 128)),
            ],
            0,
        )
        for n in range(4)
    ]

    def two_dims(y, m_first, m_second, v_first, v_second):
        high, low = parts_of(y)
        g = dot(jnp.concatenate([high, low], 1), wf1[...]) + dot(high, wf2[...])
        first = m_first * g[:, :128] + v_first * y
        second = m_second * g[:, 128:] + v_second * y
        high1, low1 = parts_of(first)
        high2, low2 = parts_of(second)
        wide = dot(jnp.concatenate([high1, high2], 1), wb1[...])
        return (
            wide[:, :128]
            + wide[:, 128:]
            + dot(jnp.concatenate([low1, low2], 1), wb2[...])
        )

    ends = two_dims(u, *mv)

    for copy in face_copies:
        copy.wait()
    owned = []
    blocks = []
    for o in range(5):
        heads = faces[o, 320:336].astype(F32)
        mine = heads[0:1] == dom.astype(F32)
        owned.append(jnp.where(mine & (heads[1:2] == row.astype(F32)), 1.0, 0.0).astype(BF16))
        last = faces[o, 256:320].astype(F32)
        last = jnp.concatenate(
            [jnp.where(left[:64], last, 0.0), jnp.where(left[:64], 0.0, last)], 0
        ).astype(BF16)
        blocks.append(jnp.concatenate([faces[o, 0:128], faces[o, 128:256], last], 1))
    mortar = dot(jnp.concatenate(owned, 1), jnp.concatenate(blocks, 0))

    for n in range(3):
        m = mortar[:, 128 * n : 128 * n + 128]
        if n == 2:
            m = m + swap(m)
        low_lines = pltpu.roll(pltpu.roll(m, 56, 1), E - 1, 0)
        high_lines = pltpu.roll(pltpu.roll(m, 72, 1), 1, 0)
        after = pltpu.roll(lines[1], 56 - 16 * n, 1)
        before = pltpu.roll(lines[0], 128 - 16 * n, 1) if n else lines[0]
        low_lines = jnp.where(row == E - 1, after, low_lines)
        high_lines = jnp.where(row == 0, before, high_lines)
        y = m + jnp.where(lane % 64 < 8, high_lines, 0.0)
        y = y + jnp.where(lane % 64 >= 56, low_lines, 0.0)
        y_parts = jnp.concatenate(parts_of(y), 1)
        r = two_dims(y, plane[0], plane[1], plane[2], plane[3])
        r_parts = jnp.concatenate(parts_of(r), 1)
        for f in range(2 * n, min(2 * n + 2, 5)):
            for c in range(4):
                at = slice(128 * c, 128 * c + 128)
                start = 512 * (f - 2 * n) + 128 * c
                cols = slice(start, start + 128)
                out[f, :, at] = (
                    base[f, :, at]
                    + q_ref[:, at] * dot(y_parts, spread[:, cols])
                    + dot(r_parts, place[:, cols])
                )
                first = end_q[0, c, 0:1] * halo[0][f : f + 1]
                final = end_q[1, c, 7:8] * halo[1][f : f + 1]
                if c == 0:
                    first = first + jnp.where(small_left, ends[f : f + 1], 0.0)
                if c == 3:
                    final = final + jnp.where(small_left, 0.0, ends[8 + f : 9 + f])
                out[f, 0:1, at] += first
                out[f, E - 1 : E, at] += final
            out_copies[f].start()
    for copy in out_copies:
        copy.wait()


def post_of(faces, edges, parts, tables):
    return pl.pallas_call(
        post_kernel,
        out_shape=jax.ShapeDtypeStruct((5, E, 512), F32),
        in_specs=[HBM] * 2 + [VM] * 11,
        out_specs=HBM,
        scratch_shapes=[
            pltpu.VMEM((5, 336, 128), BF16),
            pltpu.VMEM((2, 5, 16, 128), F32),
            pltpu.VMEM((5, E, 512), F32),
            pltpu.SemaphoreType.DMA((5,)),
            pltpu.SemaphoreType.DMA((10,)),
            pltpu.SemaphoreType.DMA((5,)),
        ],
        compiler_params=pltpu.CompilerParams(vmem_limit_bytes=LIMIT),
        name="outer",
    )(
        faces, edges, *parts, *tables["forward"], *tables["backward"],
        tables["spread"], tables["place"],
    )


def shards(adjoint_field, metric, velocity, mortar_route, mortar_element, face_code, hanging):
    tables = constants()
    adjoint = jnp.transpose(adjoint_field, (1, 0, 2))
    met = jnp.transpose(metric, (1, 0, 2))
    vel = jnp.transpose(velocity, (1, 0, 2))
    route, target, code, hang = (
        x.reshape(1, E) for x in (mortar_route, mortar_element, face_code, hanging)
    )
    faces, edges = folded_of(route, target, code, hang, adjoint, tables["fold"])
    all_faces = lax.all_gather(faces, "dom")
    all_edges = lax.all_gather(edges, ("dom", "sub"))
    parts = main_of(adjoint, met, vel, hang, tables)
    result = post_of(all_faces, all_edges, parts, tables)
    return jnp.transpose(result, (1, 0, 2))


def solution(mesh):
    block = P(("dom", "sub"), None, None)
    flat = P(("dom", "sub"), None)
    return jax.shard_map(
        shards,
        mesh=mesh,
        in_specs=(block, block, block, flat, flat, flat, flat),
        out_specs=block,
        check_vma=False,
    )
```

```python
import jax
import jax.numpy as jnp
import ml_dtypes
import numpy as np
from jax import lax
from jax.experimental import pallas as pl
from jax.experimental.pallas import tpu as pltpu
from jax.sharding import PartitionSpec as P

gll_nodes = np.array(
    [
        -1.0,
        -0.8717401485096066,
        -0.5917001814331423,
        -0.2092992179024789,
        0.2092992179024789,
        0.5917001814331423,
        0.8717401485096066,
        1.0,
    ]
)
viscosity = 0.005
F32, BF16 = jnp.float32, jnp.bfloat16
E = 128
HBM = pl.BlockSpec(memory_space=pltpu.HBM)
VM = pl.BlockSpec(memory_space=pltpu.VMEM)
LIMIT = 32 * 1024 * 1024
WHOLE = 64 * 1024 * 1024


def legendre_seven(points):
    prev = np.ones(points.shape)
    curr = np.array(points)
    for order in range(1, 7):
        nxt = ((2 * order + 1) * points * curr - order * prev) / (order + 1)
        prev, curr = (curr, nxt)
    return curr


def diff_matrix():
    values = legendre_seven(gll_nodes)
    result_mat = np.zeros((8, 8))
    for row in range(8):
        for col in range(8):
            if row != col:
                result_mat[row, col] = values[row] / (
                    values[col] * (gll_nodes[row] - gll_nodes[col])
                )
    result_mat[0, 0] = -14.0
    result_mat[7, 7] = 14.0
    return result_mat


def lagrange_at(points):
    basis = np.ones((8, 8))
    for row in range(8):
        for col in range(8):
            for other in range(8):
                if other != col:
                    basis[row, col] *= (points[row] - gll_nodes[other]) / (
                        gll_nodes[col] - gll_nodes[other]
                    )
    return basis


def face_tables():
    halves = [lagrange_at((gll_nodes - 1.0) / 2.0), lagrange_at((gll_nodes + 1.0) / 2.0)]
    perm_mat = np.zeros((64, 64))
    for col in range(64):
        perm_mat[col % 8 * 8 + col // 8, col] = 1.0
    tables = []
    for code in range(8):
        mat = np.kron(halves[code % 2], halves[code // 2 % 2])
        if code >= 4:
            mat = mat @ perm_mat
        tables.append(mat)
    return np.stack(tables)


def two_parts(mat):
    high = mat.astype(ml_dtypes.bfloat16)
    low = (mat - high.astype(np.float64)).astype(ml_dtypes.bfloat16)
    return high, low


def constants():
    dmat = diff_matrix()
    eye = np.eye(8)
    along_j = np.kron(np.eye(2), np.kron(dmat, eye))
    along_k = np.kron(np.eye(16), dmat)

    def forward(first, second):
        fh, fl = two_parts(viscosity * first.T)
        sh, sl = two_parts(viscosity * second.T)
        top = np.concatenate([fh, sh], 1)
        return np.concatenate([top, top], 0), np.concatenate([fl, sl], 1)

    def backward(first, second):
        fh, fl = two_parts(first)
        sh, sl = two_parts(second)
        return (
            np.concatenate([np.concatenate([fh, fl], 1), np.concatenate([sh, sl], 1)], 0),
            np.concatenate([fh, sh], 0),
        )

    def split_parity(mat):
        vectors = []
        for sign in (1.0, -1.0):
            small = (mat[:4, :4] + sign * mat[:4, ::-1][:, :4]) / 2
            for c in range(2):
                for other in range(2):
                    for swap in (0, 1):
                        vectors.append(
                            np.concatenate(
                                [
                                    np.full(64, small[2 * c + h, 2 * other + (h ^ swap)])
                                    for h in range(2)
                                ]
                            )
                        )
        return np.stack(vectors)

    coef = np.concatenate([split_parity(viscosity * dmat), split_parity(dmat.T)], 0)
    column = np.tile(np.repeat(viscosity * dmat[:, 0], 8), 2)[None]
    ends = [
        np.repeat(viscosity * dmat[2 * c : 2 * c + 2, end], 64)[None]
        for end in (0, 7)
        for c in range(4)
    ]
    coef = np.concatenate([coef, column, *ends, np.zeros((7, 128))], 0).astype(np.float32)

    tables = face_tables()
    fold = np.zeros((256, 512), ml_dtypes.bfloat16)
    for code in range(8):
        high, low = two_parts(tables[code])
        for i in range(8):
            for k in range(8):
                c, h = i // 2, i % 2
                spot = (56 + 64 * h + 16 * c + k) % 128
                cols = slice(64 * code, 64 * code + 64)
                fold[spot, cols] = high[8 * i + k]
                fold[(spot + 8) % 128, cols] = high[8 * i + k]
                fold[128 + spot, cols] = low[8 * i + k]

    spread = np.zeros((64, 512))
    place = np.zeros((64, 512))
    for i in range(8):
        for k in range(8):
            place[8 * i + k, 64 * i + k] = 1.0
            for j in range(8):
                spread[8 * i + k, 64 * i + 8 * j + k] = 1.0
    zero = np.zeros((64, 512))

    def pair(mat):
        one = np.concatenate(
            [np.concatenate([mat, zero], 1), np.concatenate([zero, mat], 1)], 0
        )
        return np.concatenate([one, one], 0).astype(ml_dtypes.bfloat16)

    return {
        "fold": fold,
        "forward": forward(along_j, along_k),
        "backward": backward(along_j, along_k),
        "spread": pair(spread),
        "place": pair(place),
        "coef": coef,
    }


def iota(dim, shape=(E, 128)):
    return lax.broadcasted_iota(jnp.int32, shape, dim)


def down(row):
    spots = jnp.where(iota(0) == iota(1), row, 0).astype(F32).astype(BF16)
    return jnp.dot(spots, jnp.ones((E, 128), BF16), preferred_element_type=F32)


def dot(a, b):
    return jnp.dot(a, b, preferred_element_type=F32)


def parts_of(x):
    high = x.astype(BF16)
    return high, (x - high.astype(F32)).astype(BF16)


def fetch(pairs, sems):
    copies = [
        pltpu.make_async_copy(src, dst, sems.at[n]) for n, (src, dst) in enumerate(pairs)
    ]
    for copy in copies:
        copy.start()
    return copies


def fold_kernel(
    route_hbm, target_hbm, code_hbm, hang_hbm, adj_hbm, fold_hbm, *refs
):
    outs, edges_out, ints, x, fold, wide, sems = refs[:5], *refs[5:]
    peers = lax.axis_size("dom")
    copies = fetch(
        [(ref, ints.at[n]) for n, ref in enumerate((route_hbm, target_hbm, code_hbm, hang_hbm))]
        + [(adj_hbm, x), (fold_hbm, fold)],
        sems,
    )
    for copy in copies:
        copy.wait()
    route, target, code, hang = (ints[n] for n in range(4))
    lane = iota(1)
    left = lane < 64
    slot = lax.rem(route - lax.axis_index("dom") + 2 + peers, peers)
    hit = (iota(0, (5 * E, E)) == slot * E + target).astype(F32).astype(BF16)
    marked = down(jnp.where(hang == 1, code, -2)) - (lane // 64).astype(F32)
    odd = lane % 16 >= 8
    group = (lane // 16 + 1) % 4
    for f in range(5):
        packed = jnp.zeros((E, 128), F32)
        for c in range(4):
            moved = x[f, :, 128 * c : 128 * c + 128]
            if c:
                moved = pltpu.roll(moved, 16 * c, 1)
            packed = jnp.where(odd & (group == c), moved, packed)
        high = packed.astype(BF16)
        high_f = high.astype(F32)
        both = jnp.where(odd, high_f, pltpu.roll(packed - high_f, 8, 1)).astype(BF16)
        wide[E * f : E * f + E, 0:128] = both
        wide[E * f : E * f + E, 128:256] = high
    mapped = dot(wide[...], fold[...])
    faces = []
    for f in range(5):
        total = jnp.zeros((E, 128), F32)
        for q in range(4):
            total = total + jnp.where(
                marked == 2.0 * q, mapped[E * f : E * f + E, 128 * q : 128 * q + 128], 0.0
            )
        faces.append(total + pltpu.roll(total, 64, 1))
    f01 = jnp.where(left, faces[0], faces[1]).astype(BF16)
    f23 = jnp.where(left, faces[2], faces[3]).astype(BF16)
    sums = dot(hit, jnp.concatenate([f01, f23, faces[4].astype(BF16)], 1))
    for o in range(5):
        ref = outs[o]
        mine = sums[o * E : o * E + E]
        last = jnp.where(left[:64], mine[:64, 256:384], mine[64:, 256:384])
        ref[0:128] = mine[:, 0:128].astype(ref.dtype)
        ref[128:256] = mine[:, 128:256].astype(ref.dtype)
        ref[256:320] = last.astype(ref.dtype)

    lane = iota(1, (1, 128))
    own = marked[0:1], marked[E - 1 : E]
    edges_out[...] = jnp.zeros((16, 128), F32)
    for n in range(3):
        first, second = 2 * n, min(2 * n + 1, 4)
        for end, (at, chunk) in enumerate(((0, 0), (E - 1, 3))):
            a = x[first, at : at + 1, 128 * chunk : 128 * chunk + 128]
            b = x[second, at : at + 1, 128 * chunk : 128 * chunk + 128]
            if end == 0:
                b = pltpu.roll(b, 64, 1)
            else:
                a = pltpu.roll(a, 64, 1)
            keep = jnp.where((lane % 64 >= 56) & (own[end] >= -1.5), 0.0, 1.0)
            spot = 8 * end + n
            edges_out[spot : spot + 1] = jnp.where(lane < 64, a, b) * keep


def folded_of(route, target, code, hang, adjoint, fold):
    return pl.pallas_call(
        fold_kernel,
        out_shape=[
            jax.ShapeDtypeStruct((320, 128), F32 if o == 2 else BF16) for o in range(5)
        ]
        + [jax.ShapeDtypeStruct((16, 128), F32)],
        in_specs=[HBM] * 6,
        out_specs=[VM] * 6,
        scratch_shapes=[
            pltpu.VMEM((4, 1, E), jnp.int32),
            pltpu.VMEM((5, E, 512), F32),
            pltpu.VMEM((256, 512), BF16),
            pltpu.VMEM((5 * E, 256), BF16),
            pltpu.SemaphoreType.DMA((6,)),
        ],
        compiler_params=pltpu.CompilerParams(vmem_limit_bytes=WHOLE),
        name="fold",
    )(route, target, code, hang, adjoint, fold)


def swap(x):
    return pltpu.roll(x, 64, 1)


def along_first(x, coef, base):
    r3, r2 = swap(x[3]), swap(x[2])
    parity = ((x[0] + r3, x[1] + r2), (x[0] - r3, x[1] - r2))
    sums = []
    for s in range(2):
        kept = (parity[s][0], swap(parity[s][0]), parity[s][1], swap(parity[s][1]))
        for c in range(2):
            at = base + 8 * s + 4 * c
            total = coef[at : at + 1] * kept[0]
            for n in range(1, 4):
                total = total + coef[at + n : at + n + 1] * kept[n]
            sums.append(total)
    p0, p1, q0, q1 = sums
    return [p0 + q0, p1 + q1, swap(q1 - p1), swap(q0 - p0)]


def main_kernel(
    adj_hbm, met_hbm, vel_hbm, hang, wf1, wf2, wb1, wb2, coef,
    out, q_out, plane_out, end_q, end_mv, x_ref, met, vel, sems,
):
    order = (1, 0, 2)
    pairs = [(adj_hbm.at[0], x_ref.at[0])]
    for d in order:
        pairs += [(met_hbm.at[d], met.at[d]), (vel_hbm.at[d], vel.at[d])]
    pairs += [(adj_hbm.at[f], x_ref.at[f]) for f in range(1, 5)]
    copies = fetch(pairs, sems)
    lane, row = iota(1), iota(0)
    keep = jnp.where(lane % 64 >= 56, 1.0 - down(hang[...]), 1.0)
    left = lane < 64
    for copy in copies[:3]:
        copy.wait()

    for c in range(4):
        at = slice(128 * c, 128 * c + 128)
        w = met[1, :, at] * coef[32:33] + jnp.where(lane % 64 < 8, vel[1, :, at], 0.0)
        high, low = parts_of(w)
        wide = dot(high, wb1[0:128])
        q_out[:, at] = wide[:, :128] + wide[:, 128:] + dot(low, wb2[0:128])

    for copy in copies[3:]:
        copy.wait()
    for n, (ref, d) in enumerate(((met, 0), (met, 2), (vel, 0), (vel, 2))):
        packed = jnp.zeros((E, 128), F32)
        for c in range(4):
            moved = ref[d, :, 128 * c : 128 * c + 128]
            if c:
                moved = pltpu.roll(moved, 16 * c, 1)
            packed = jnp.where((lane // 16) % 4 == c, moved, packed)
        even = jnp.where(left, packed, swap(packed))
        other = jnp.where(left, swap(packed), packed)
        plane_out[n] = jnp.where(lane % 16 < 8, even, pltpu.roll(other, 8, 1))

    small_left = iota(1, (8, 128)) < 64
    for end in range(2):
        rows = slice((E - 8) * end, (E - 8) * end + 8)
        w = []
        for c in range(4):
            at = slice(128 * c, 128 * c + 128)
            spot = 33 + 4 * end + c
            term = met[0, rows, at] * coef[spot : spot + 1]
            if c == 3 * end:
                term = term + jnp.where(small_left != (end == 1), vel[0, rows, at], 0.0)
            w.append(term)
        back = along_first(w, coef, 16)
        for c in range(4):
            end_q[end, c] = back[c]
        at = slice(384 * end, 384 * end + 128)
        for n, (ref, d) in enumerate(((met, 1), (met, 2), (vel, 1), (vel, 2))):
            end_mv[end, n] = ref[d, rows, at]

    def field(f, carry):
        x = [x_ref[f, :, 128 * c : 128 * c + 128] * keep for c in range(4)]
        low_faces = pltpu.roll(swap(x[0]), E - 1, 0)
        high_faces = pltpu.roll(swap(x[3]), 1, 0)
        x[0] = x[0] + jnp.where(left & (row > 0), high_faces, 0.0)
        x[3] = x[3] + jnp.where(left | (row == E - 1), 0.0, low_faces)
        g0 = along_first(x, coef, 0)
        inner0 = []
        totals = []
        for c in range(4):
            at = slice(128 * c, 128 * c + 128)
            high, low = parts_of(x[c])
            g = dot(jnp.concatenate([high, low], 1), wf1[...]) + dot(high, wf2[...])
            inner0.append(met[0, :, at] * g0[c] + vel[0, :, at] * x[c])
            in1 = met[1, :, at] * g[:, :128] + vel[1, :, at] * x[c]
            in2 = met[2, :, at] * g[:, 128:] + vel[2, :, at] * x[c]
            high1, low1 = parts_of(in1)
            high2, low2 = parts_of(in2)
            wide = dot(jnp.concatenate([high1, high2], 1), wb1[...])
            totals.append(
                wide[:, :128]
                + wide[:, 128:]
                + dot(jnp.concatenate([low1, low2], 1), wb2[...])
            )
        back = along_first(inner0, coef, 16)
        for c in range(4):
            out[f, :, 128 * c : 128 * c + 128] = totals[c] + back[c]
        return carry

    lax.fori_loop(0, 5, field, 0)


def main_of(adjoint, metric, velocity, hang, tables):
    return pl.pallas_call(
        main_kernel,
        out_shape=[
            jax.ShapeDtypeStruct((5, E, 512), F32),
            jax.ShapeDtypeStruct((E, 512), F32),
            jax.ShapeDtypeStruct((4, E, 128), F32),
            jax.ShapeDtypeStruct((2, 4, 8, 128), F32),
            jax.ShapeDtypeStruct((2, 4, 8, 128), F32),
        ],
        in_specs=[HBM] * 3 + [VM] * 6,
        out_specs=[VM] * 5,
        scratch_shapes=[
            pltpu.VMEM((5, E, 512), F32),
            pltpu.VMEM((3, E, 512), F32),
            pltpu.VMEM((3, E, 512), F32),
            pltpu.SemaphoreType.DMA((11,)),
        ],
        compiler_params=pltpu.CompilerParams(vmem_limit_bytes=LIMIT),
        cost_estimate=pl.CostEstimate(
            flops=4_000_000_000, bytes_accessed=6_000_000, transcendentals=0
        ),
        name="inner",
    )(
        adjoint, metric, velocity, hang,
        *tables["forward"], *tables["backward"], tables["coef"],
    )


def line_kernel(a, b, own, c, d, edges, low_out, high_out):
    def rows(start):
        return sum(ref[start : start + 16].astype(F32) for ref in (a, b, own, c, d))

    low_out[...] = edges[0:8]
    high_out[...] = edges[8:16]
    for n, (first, last) in enumerate(((0, 112), (128, 240), (256, 304))):
        low_out[3 + n : 4 + n] = pltpu.roll(rows(first)[0:1], 56, 1)
        line = rows(last)[15:16]
        high_out[3 + n : 4 + n] = pltpu.roll(swap(line) if n == 2 else line, 72, 1)


def lines_of(parts, edges):
    return pl.pallas_call(
        line_kernel,
        out_shape=[jax.ShapeDtypeStruct((8, 128), F32)] * 2,
        in_specs=[VM] * 6,
        out_specs=[VM] * 2,
        compiler_params=pltpu.CompilerParams(vmem_limit_bytes=LIMIT),
        name="lines",
    )(*parts, edges)


def post_kernel(
    a, b, own, c2, d, before, after, base, q_ref, plane, end_q, end_mv,
    wf1, wf2, wb1, wb2, spread, place, out_hbm, out, out_sems,
):
    out_copies = [
        pltpu.make_async_copy(out.at[f], out_hbm.at[f], out_sems.at[f]) for f in range(5)
    ]
    lane, row = iota(1), iota(0)
    left = lane < 64

    small_left = iota(1, (1, 128)) < 64
    halo = []
    for ref in (before, after):
        rows = []
        for n in range(3):
            pair = ref[n : n + 1]
            turned = pltpu.roll(pair, 64, 1)
            rows.append(jnp.where(small_left, pair, turned))
            rows.append(jnp.where(small_left, turned, pair))
        halo.append(jnp.concatenate(rows + [jnp.zeros((2, 128), F32)], 0))
    u = jnp.concatenate(halo, 0)
    mv = [
        jnp.concatenate(
            [
                jnp.broadcast_to(end_mv[0, n, 0:1], (8, 128)),
                jnp.broadcast_to(end_mv[1, n, 7:8], (8, 128)),
            ],
            0,
        )
        for n in range(4)
    ]

    def two_dims(y, m_first, m_second, v_first, v_second):
        high, low = parts_of(y)
        g = dot(jnp.concatenate([high, low], 1), wf1[...]) + dot(high, wf2[...])
        first = m_first * g[:, :128] + v_first * y
        second = m_second * g[:, 128:] + v_second * y
        high1, low1 = parts_of(first)
        high2, low2 = parts_of(second)
        wide = dot(jnp.concatenate([high1, high2], 1), wb1[...])
        return (
            wide[:, :128]
            + wide[:, 128:]
            + dot(jnp.concatenate([low1, low2], 1), wb2[...])
        )

    ends = two_dims(u, *mv)

    for n in range(3):
        rows = slice(128 * n, min(128 * n + 128, 320))
        m = sum(ref[rows].astype(F32) for ref in (a, b, own, c2, d))
        if n == 2:
            m = jnp.concatenate([m, swap(m)], 0)
        low_lines = pltpu.roll(pltpu.roll(m, 56, 1), E - 1, 0)
        high_lines = pltpu.roll(pltpu.roll(m, 72, 1), 1, 0)
        low_lines = jnp.where(row == E - 1, after[3 + n : 4 + n], low_lines)
        high_lines = jnp.where(row == 0, before[3 + n : 4 + n], high_lines)
        y = m + jnp.where(lane % 64 < 8, high_lines, 0.0)
        y = y + jnp.where(lane % 64 >= 56, low_lines, 0.0)
        y_parts = jnp.concatenate(parts_of(y), 1)
        r = two_dims(y, plane[0], plane[1], plane[2], plane[3])
        r_parts = jnp.concatenate(parts_of(r), 1)
        for f in range(2 * n, min(2 * n + 2, 5)):
            for c in range(4):
                at = slice(128 * c, 128 * c + 128)
                start = 512 * (f - 2 * n) + 128 * c
                cols = slice(start, start + 128)
                out[f, :, at] = (
                    base[f, :, at]
                    + q_ref[:, at] * dot(y_parts, spread[:, cols])
                    + dot(r_parts, place[:, cols])
                )
                first = end_q[0, c, 0:1] * halo[0][f : f + 1]
                final = end_q[1, c, 7:8] * halo[1][f : f + 1]
                if c == 0:
                    first = first + jnp.where(small_left, ends[f : f + 1], 0.0)
                if c == 3:
                    final = final + jnp.where(small_left, 0.0, ends[8 + f : 9 + f])
                out[f, 0:1, at] += first
                out[f, E - 1 : E, at] += final
            out_copies[f].start()
    for copy in out_copies:
        copy.wait()


def post_of(parts, before, after, local, tables):
    return pl.pallas_call(
        post_kernel,
        out_shape=jax.ShapeDtypeStruct((5, E, 512), F32),
        in_specs=[VM] * 18,
        out_specs=HBM,
        scratch_shapes=[pltpu.VMEM((5, E, 512), F32), pltpu.SemaphoreType.DMA((5,))],
        compiler_params=pltpu.CompilerParams(vmem_limit_bytes=LIMIT),
        name="outer",
    )(
        *parts, before, after, *local, *tables["forward"], *tables["backward"],
        tables["spread"], tables["place"],
    )


def shards(adjoint_field, metric, velocity, mortar_route, mortar_element, face_code, hanging):
    tables = constants()
    peers = lax.axis_size("dom")
    adjoint = jnp.transpose(adjoint_field, (1, 0, 2))
    met = jnp.transpose(metric, (1, 0, 2))
    vel = jnp.transpose(velocity, (1, 0, 2))
    route, target, code, hang = (
        x.reshape(1, E) for x in (mortar_route, mortar_element, face_code, hanging)
    )
    *parts, edges = folded_of(route, target, code, hang, adjoint, tables["fold"])
    for o in (0, 4, 1, 3):
        pairs = [(i, (i + o - 2) % peers) for i in range(peers)]
        parts[o] = lax.ppermute(parts[o], "dom", pairs)
    local = main_of(adjoint, met, vel, hang, tables)
    parts, local = lax.optimization_barrier((parts, local))
    low, high = lines_of(parts, edges)
    axes = ("dom", "sub")
    count = lax.axis_size(axes)
    before = lax.ppermute(high, axes, [(i, i + 1) for i in range(count - 1)])
    after = lax.ppermute(low, axes, [(i + 1, i) for i in range(count - 1)])
    result = post_of(parts, before, after, local, tables)
    return jnp.transpose(result, (1, 0, 2))


def solution(mesh):
    block = P(("dom", "sub"), None, None)
    flat = P(("dom", "sub"), None)
    return jax.shard_map(
        shards,
        mesh=mesh,
        in_specs=(block, block, block, flat, flat, flat, flat),
        out_specs=block,
        check_vma=False,
    )
```

```python
import jax
import jax.numpy as jnp
import ml_dtypes
import numpy as np
from jax import lax
from jax.experimental import pallas as pl
from jax.experimental.pallas import tpu as pltpu
from jax.sharding import PartitionSpec as P

gll_nodes = np.array(
    [
        -1.0,
        -0.8717401485096066,
        -0.5917001814331423,
        -0.2092992179024789,
        0.2092992179024789,
        0.5917001814331423,
        0.8717401485096066,
        1.0,
    ]
)
viscosity = 0.005
F32, BF16 = jnp.float32, jnp.bfloat16
E = 128
HBM = pl.BlockSpec(memory_space=pltpu.HBM)
VM = pl.BlockSpec(memory_space=pltpu.VMEM)
LIMIT = 32 * 1024 * 1024
WHOLE = 64 * 1024 * 1024


def legendre_seven(points):
    prev = np.ones(points.shape)
    curr = np.array(points)
    for order in range(1, 7):
        nxt = ((2 * order + 1) * points * curr - order * prev) / (order + 1)
        prev, curr = (curr, nxt)
    return curr


def diff_matrix():
    values = legendre_seven(gll_nodes)
    result_mat = np.zeros((8, 8))
    for row in range(8):
        for col in range(8):
            if row != col:
                result_mat[row, col] = values[row] / (
                    values[col] * (gll_nodes[row] - gll_nodes[col])
                )
    result_mat[0, 0] = -14.0
    result_mat[7, 7] = 14.0
    return result_mat


def lagrange_at(points):
    basis = np.ones((8, 8))
    for row in range(8):
        for col in range(8):
            for other in range(8):
                if other != col:
                    basis[row, col] *= (points[row] - gll_nodes[other]) / (
                        gll_nodes[col] - gll_nodes[other]
                    )
    return basis


def face_tables():
    halves = [lagrange_at((gll_nodes - 1.0) / 2.0), lagrange_at((gll_nodes + 1.0) / 2.0)]
    perm_mat = np.zeros((64, 64))
    for col in range(64):
        perm_mat[col % 8 * 8 + col // 8, col] = 1.0
    tables = []
    for code in range(8):
        mat = np.kron(halves[code % 2], halves[code // 2 % 2])
        if code >= 4:
            mat = mat @ perm_mat
        tables.append(mat)
    return np.stack(tables)


def two_parts(mat):
    high = mat.astype(ml_dtypes.bfloat16)
    low = (mat - high.astype(np.float64)).astype(ml_dtypes.bfloat16)
    return high, low


def constants():
    dmat = diff_matrix()
    eye = np.eye(8)
    along_j = np.kron(np.eye(2), np.kron(dmat, eye))
    along_k = np.kron(np.eye(16), dmat)

    def forward(first, second):
        fh, fl = two_parts(viscosity * first.T)
        sh, sl = two_parts(viscosity * second.T)
        top = np.concatenate([fh, sh], 1)
        return np.concatenate([top, top], 0), np.concatenate([fl, sl], 1)

    def backward(first, second):
        fh, fl = two_parts(first)
        sh, sl = two_parts(second)
        return (
            np.concatenate([np.concatenate([fh, fl], 1), np.concatenate([sh, sl], 1)], 0),
            np.concatenate([fh, sh], 0),
        )

    def split_parity(mat):
        vectors = []
        for sign in (1.0, -1.0):
            small = (mat[:4, :4] + sign * mat[:4, ::-1][:, :4]) / 2
            for c in range(2):
                for other in range(2):
                    for swap in (0, 1):
                        vectors.append(
                            np.concatenate(
                                [
                                    np.full(64, small[2 * c + h, 2 * other + (h ^ swap)])
                                    for h in range(2)
                                ]
                            )
                        )
        return np.stack(vectors)

    coef = np.concatenate([split_parity(viscosity * dmat), split_parity(dmat.T)], 0)
    column = np.tile(np.repeat(viscosity * dmat[:, 0], 8), 2)[None]
    ends = [
        np.repeat(viscosity * dmat[2 * c : 2 * c + 2, end], 64)[None]
        for end in (0, 7)
        for c in range(4)
    ]
    coef = np.concatenate([coef, column, *ends, np.zeros((7, 128))], 0).astype(np.float32)

    tables = face_tables()
    fold = np.zeros((256, 512), ml_dtypes.bfloat16)
    for code in range(8):
        high, low = two_parts(tables[code])
        for i in range(8):
            for k in range(8):
                c, h = i // 2, i % 2
                spot = (56 + 64 * h + 16 * c + k) % 128
                cols = slice(64 * code, 64 * code + 64)
                fold[spot, cols] = high[8 * i + k]
                fold[(spot + 8) % 128, cols] = high[8 * i + k]
                fold[128 + spot, cols] = low[8 * i + k]

    spread = np.zeros((64, 512))
    place = np.zeros((64, 512))
    for i in range(8):
        for k in range(8):
            place[8 * i + k, 64 * i + k] = 1.0
            for j in range(8):
                spread[8 * i + k, 64 * i + 8 * j + k] = 1.0
    zero = np.zeros((64, 512))

    def pair(mat):
        one = np.concatenate(
            [np.concatenate([mat, zero], 1), np.concatenate([zero, mat], 1)], 0
        )
        return np.concatenate([one, one], 0).astype(ml_dtypes.bfloat16)

    return {
        "fold": fold,
        "forward": forward(along_j, along_k),
        "backward": backward(along_j, along_k),
        "spread": pair(spread),
        "place": pair(place),
        "coef": coef,
    }


def iota(dim, shape=(E, 128)):
    return lax.broadcasted_iota(jnp.int32, shape, dim)


def down(row):
    spots = jnp.where(iota(0) == iota(1), row, 0).astype(F32).astype(BF16)
    return jnp.dot(spots, jnp.ones((E, 128), BF16), preferred_element_type=F32)


def dot(a, b):
    return jnp.dot(a, b, preferred_element_type=F32)


def parts_of(x):
    high = x.astype(BF16)
    return high, (x - high.astype(F32)).astype(BF16)


def fetch(pairs, sems):
    copies = [
        pltpu.make_async_copy(src, dst, sems.at[n]) for n, (src, dst) in enumerate(pairs)
    ]
    for copy in copies:
        copy.start()
    return copies


def fold_kernel(
    route_hbm, target_hbm, code_hbm, hang_hbm, adj_hbm, fold_hbm, *refs
):
    outs, edges_out, marks_out, ints, x, fold, wide, sems = refs[:5], *refs[5:]
    peers = lax.axis_size("dom")
    copies = fetch(
        [(ref, ints.at[n]) for n, ref in enumerate((route_hbm, target_hbm, code_hbm, hang_hbm))]
        + [(adj_hbm, x), (fold_hbm, fold)],
        sems,
    )
    for copy in copies:
        copy.wait()
    route, target, code, hang = (ints[n] for n in range(4))
    lane = iota(1)
    left = lane < 64
    slot = lax.rem(route - lax.axis_index("dom") + 2 + peers, peers)
    hit = (iota(0, (5 * E, E)) == slot * E + target).astype(F32).astype(BF16)
    marked = down(jnp.where(hang == 1, code, -2)) - (lane // 64).astype(F32)
    odd = lane % 16 >= 8
    group = (lane // 16 + 1) % 4
    for f in range(5):
        packed = jnp.zeros((E, 128), F32)
        for c in range(4):
            moved = x[f, :, 128 * c : 128 * c + 128]
            if c:
                moved = pltpu.roll(moved, 16 * c, 1)
            packed = jnp.where(odd & (group == c), moved, packed)
        high = packed.astype(BF16)
        high_f = high.astype(F32)
        both = jnp.where(odd, high_f, pltpu.roll(packed - high_f, 8, 1)).astype(BF16)
        wide[E * f : E * f + E, 0:128] = both
        wide[E * f : E * f + E, 128:256] = high
    mapped = dot(wide[...], fold[...])
    faces = []
    for f in range(5):
        total = jnp.zeros((E, 128), F32)
        for q in range(4):
            total = total + jnp.where(
                marked == 2.0 * q, mapped[E * f : E * f + E, 128 * q : 128 * q + 128], 0.0
            )
        faces.append(total + pltpu.roll(total, 64, 1))
    f01 = jnp.where(left, faces[0], faces[1]).astype(BF16)
    f23 = jnp.where(left, faces[2], faces[3]).astype(BF16)
    sums = dot(hit, jnp.concatenate([f01, f23, faces[4].astype(BF16)], 1))
    for o in range(5):
        ref = outs[o]
        mine = sums[o * E : o * E + E]
        last = jnp.where(left[:64], mine[:64, 256:384], mine[64:, 256:384])
        ref[0:128] = mine[:, 0:128].astype(ref.dtype)
        ref[128:256] = mine[:, 128:256].astype(ref.dtype)
        ref[256:320] = last.astype(ref.dtype)

    marks_out[...] = jnp.broadcast_to(1.0 - hang.astype(F32), (8, E))
    lane = iota(1, (1, 128))
    own = marked[0:1], marked[E - 1 : E]
    edges_out[...] = jnp.zeros((16, 128), F32)
    for n in range(3):
        first, second = 2 * n, min(2 * n + 1, 4)
        for end, (at, chunk) in enumerate(((0, 0), (E - 1, 3))):
            a = x[first, at : at + 1, 128 * chunk : 128 * chunk + 128]
            b = x[second, at : at + 1, 128 * chunk : 128 * chunk + 128]
            if end == 0:
                b = pltpu.roll(b, 64, 1)
            else:
                a = pltpu.roll(a, 64, 1)
            keep = jnp.where((lane % 64 >= 56) & (own[end] >= -1.5), 0.0, 1.0)
            spot = 8 * end + n
            edges_out[spot : spot + 1] = jnp.where(lane < 64, a, b) * keep


def folded_of(route, target, code, hang, adjoint, fold):
    return pl.pallas_call(
        fold_kernel,
        out_shape=[
            jax.ShapeDtypeStruct((320, 128), F32 if o == 2 else BF16) for o in range(5)
        ]
        + [jax.ShapeDtypeStruct((16, 128), F32), jax.ShapeDtypeStruct((8, 128), F32)],
        in_specs=[HBM] * 6,
        out_specs=[VM] * 7,
        scratch_shapes=[
            pltpu.VMEM((4, 1, E), jnp.int32),
            pltpu.VMEM((5, E, 512), F32),
            pltpu.VMEM((256, 512), BF16),
            pltpu.VMEM((5 * E, 256), BF16),
            pltpu.SemaphoreType.DMA((6,)),
        ],
        compiler_params=pltpu.CompilerParams(vmem_limit_bytes=WHOLE),
        name="fold",
    )(route, target, code, hang, adjoint, fold)


def swap(x):
    return pltpu.roll(x, 64, 1)


def along_first(x, coef, base):
    r3, r2 = swap(x[3]), swap(x[2])
    parity = ((x[0] + r3, x[1] + r2), (x[0] - r3, x[1] - r2))
    sums = []
    for s in range(2):
        kept = (parity[s][0], swap(parity[s][0]), parity[s][1], swap(parity[s][1]))
        for c in range(2):
            at = base + 8 * s + 4 * c
            total = coef[at : at + 1] * kept[0]
            for n in range(1, 4):
                total = total + coef[at + n : at + n + 1] * kept[n]
            sums.append(total)
    p0, p1, q0, q1 = sums
    return [p0 + q0, p1 + q1, swap(q1 - p1), swap(q0 - p0)]


def main_kernel(
    adj_hbm, met_hbm, vel_hbm, keep_ref, wf1, wf2, wb1, wb2, coef,
    out, q_out, plane_out, end_q, end_mv, x_ref, met, vel, sems,
):
    order = (1, 0, 2)
    pairs = [(adj_hbm.at[0], x_ref.at[0])]
    for d in order:
        pairs += [(met_hbm.at[d], met.at[d]), (vel_hbm.at[d], vel.at[d])]
    pairs += [(adj_hbm.at[f], x_ref.at[f]) for f in range(1, 5)]
    copies = fetch(pairs, sems)
    lane, row = iota(1), iota(0)
    keep = keep_ref[...]
    left = lane < 64
    for copy in copies[:3]:
        copy.wait()

    for c in range(4):
        at = slice(128 * c, 128 * c + 128)
        w = met[1, :, at] * coef[32:33] + jnp.where(lane % 64 < 8, vel[1, :, at], 0.0)
        high, low = parts_of(w)
        wide = dot(high, wb1[0:128])
        q_out[:, at] = wide[:, :128] + wide[:, 128:] + dot(low, wb2[0:128])

    for copy in copies[3:]:
        copy.wait()
    for n, (ref, d) in enumerate(((met, 0), (met, 2), (vel, 0), (vel, 2))):
        packed = jnp.zeros((E, 128), F32)
        for c in range(4):
            moved = ref[d, :, 128 * c : 128 * c + 128]
            if c:
                moved = pltpu.roll(moved, 16 * c, 1)
            packed = jnp.where((lane // 16) % 4 == c, moved, packed)
        even = jnp.where(left, packed, swap(packed))
        other = jnp.where(left, swap(packed), packed)
        plane_out[n] = jnp.where(lane % 16 < 8, even, pltpu.roll(other, 8, 1))

    small_left = iota(1, (8, 128)) < 64
    for end in range(2):
        rows = slice((E - 8) * end, (E - 8) * end + 8)
        w = []
        for c in range(4):
            at = slice(128 * c, 128 * c + 128)
            spot = 33 + 4 * end + c
            term = met[0, rows, at] * coef[spot : spot + 1]
            if c == 3 * end:
                term = term + jnp.where(small_left != (end == 1), vel[0, rows, at], 0.0)
            w.append(term)
        back = along_first(w, coef, 16)
        for c in range(4):
            end_q[end, c] = back[c]
        at = slice(384 * end, 384 * end + 128)
        for n, (ref, d) in enumerate(((met, 1), (met, 2), (vel, 1), (vel, 2))):
            end_mv[end, n] = ref[d, rows, at]

    def field(f, carry):
        x = [x_ref[f, :, 128 * c : 128 * c + 128] * keep for c in range(4)]
        low_faces = pltpu.roll(swap(x[0]), E - 1, 0)
        high_faces = pltpu.roll(swap(x[3]), 1, 0)
        x[0] = x[0] + jnp.where(left & (row > 0), high_faces, 0.0)
        x[3] = x[3] + jnp.where(left | (row == E - 1), 0.0, low_faces)
        g0 = along_first(x, coef, 0)
        inner0 = []
        totals = []
        for c in range(4):
            at = slice(128 * c, 128 * c + 128)
            high, low = parts_of(x[c])
            g = dot(jnp.concatenate([high, low], 1), wf1[...]) + dot(high, wf2[...])
            inner0.append(met[0, :, at] * g0[c] + vel[0, :, at] * x[c])
            in1 = met[1, :, at] * g[:, :128] + vel[1, :, at] * x[c]
            in2 = met[2, :, at] * g[:, 128:] + vel[2, :, at] * x[c]
            high1, low1 = parts_of(in1)
            high2, low2 = parts_of(in2)
            wide = dot(jnp.concatenate([high1, high2], 1), wb1[...])
            totals.append(
                wide[:, :128]
                + wide[:, 128:]
                + dot(jnp.concatenate([low1, low2], 1), wb2[...])
            )
        back = along_first(inner0, coef, 16)
        for c in range(4):
            out[f, :, 128 * c : 128 * c + 128] = totals[c] + back[c]
        return carry

    lax.fori_loop(0, 5, field, 0)


def keep_kernel(marks, out):
    kept = jnp.where(iota(0) == iota(1), marks[0:1], 0.0).astype(BF16)
    column = dot(kept, jnp.ones((E, 128), BF16))
    out[...] = jnp.where(iota(1) % 64 >= 56, column, 1.0)


def kept_of(marks):
    return pl.pallas_call(
        keep_kernel,
        out_shape=jax.ShapeDtypeStruct((E, 128), F32),
        in_specs=[VM],
        out_specs=VM,
        compiler_params=pltpu.CompilerParams(vmem_limit_bytes=16 * 1024 * 1024),
        cost_estimate=pl.CostEstimate(
            flops=8_000_000_000, bytes_accessed=30_000_000, transcendentals=0
        ),
        name="keep",
    )(marks)


def main_of(adjoint, metric, velocity, keep, tables):
    return pl.pallas_call(
        main_kernel,
        out_shape=[
            jax.ShapeDtypeStruct((5, E, 512), F32),
            jax.ShapeDtypeStruct((E, 512), F32),
            jax.ShapeDtypeStruct((4, E, 128), F32),
            jax.ShapeDtypeStruct((2, 4, 8, 128), F32),
            jax.ShapeDtypeStruct((2, 4, 8, 128), F32),
        ],
        in_specs=[HBM] * 3 + [VM] * 6,
        out_specs=[VM] * 5,
        scratch_shapes=[
            pltpu.VMEM((5, E, 512), F32),
            pltpu.VMEM((3, E, 512), F32),
            pltpu.VMEM((3, E, 512), F32),
            pltpu.SemaphoreType.DMA((11,)),
        ],
        compiler_params=pltpu.CompilerParams(vmem_limit_bytes=LIMIT),
        cost_estimate=pl.CostEstimate(
            flops=4_000_000_000, bytes_accessed=6_000_000, transcendentals=0
        ),
        name="inner",
    )(
        adjoint, metric, velocity, keep,
        *tables["forward"], *tables["backward"], tables["coef"],
    )


def odd_device():
    index = lax.axis_index("dom") * lax.axis_size("sub") + lax.axis_index("sub")
    return lax.rem(index, 2) == 1


def line_kernel(a, b, own, c, d, edges, across, inside):
    def rows(start):
        return sum(ref[start : start + 16].astype(F32) for ref in (a, b, own, c, d))

    low = [edges[0:3]]
    high = [edges[8:11]]
    for n, (first, last) in enumerate(((0, 112), (128, 240), (256, 304))):
        low.append(pltpu.roll(rows(first)[0:1], 56, 1))
        line = rows(last)[15:16]
        high.append(pltpu.roll(swap(line) if n == 2 else line, 72, 1))
    zero = jnp.zeros((2, 128), F32)
    low = jnp.concatenate(low + [zero], 0)
    high = jnp.concatenate(high + [zero], 0)
    odd = odd_device()
    across[...] = jnp.where(odd, high, low)
    inside[...] = jnp.where(odd, low, high)


def lines_of(parts, edges):
    return pl.pallas_call(
        line_kernel,
        out_shape=[jax.ShapeDtypeStruct((8, 128), F32)] * 2,
        in_specs=[VM] * 6,
        out_specs=[VM] * 2,
        compiler_params=pltpu.CompilerParams(vmem_limit_bytes=LIMIT),
        name="lines",
    )(*parts, edges)


def post_kernel(
    a, b, own, c2, d, across, inside, base, q_ref, plane, end_q, end_mv,
    wf1, wf2, wb1, wb2, spread, place, out_hbm, out, out_sems,
):
    out_copies = [
        pltpu.make_async_copy(out.at[f], out_hbm.at[f], out_sems.at[f]) for f in range(5)
    ]
    lane, row = iota(1), iota(0)
    left = lane < 64

    small_left = iota(1, (1, 128)) < 64
    halo = []
    odd = odd_device()
    before = jnp.where(odd, inside[...], across[...])
    after = jnp.where(odd, across[...], inside[...])
    for got in (before, after):
        rows = []
        for n in range(3):
            pair = got[n : n + 1]
            turned = pltpu.roll(pair, 64, 1)
            rows.append(jnp.where(small_left, pair, turned))
            rows.append(jnp.where(small_left, turned, pair))
        halo.append(jnp.concatenate(rows + [jnp.zeros((2, 128), F32)], 0))
    u = jnp.concatenate(halo, 0)
    mv = [
        jnp.concatenate(
            [
                jnp.broadcast_to(end_mv[0, n, 0:1], (8, 128)),
                jnp.broadcast_to(end_mv[1, n, 7:8], (8, 128)),
            ],
            0,
        )
        for n in range(4)
    ]

    def two_dims(y, m_first, m_second, v_first, v_second):
        high, low = parts_of(y)
        g = dot(jnp.concatenate([high, low], 1), wf1[...]) + dot(high, wf2[...])
        first = m_first * g[:, :128] + v_first * y
        second = m_second * g[:, 128:] + v_second * y
        high1, low1 = parts_of(first)
        high2, low2 = parts_of(second)
        wide = dot(jnp.concatenate([high1, high2], 1), wb1[...])
        return (
            wide[:, :128]
            + wide[:, 128:]
            + dot(jnp.concatenate([low1, low2], 1), wb2[...])
        )

    ends = two_dims(u, *mv)

    for n in range(3):
        rows = slice(128 * n, min(128 * n + 128, 320))
        m = sum(ref[rows].astype(F32) for ref in (a, b, own, c2, d))
        if n == 2:
            m = jnp.concatenate([m, swap(m)], 0)
        low_lines = pltpu.roll(pltpu.roll(m, 56, 1), E - 1, 0)
        high_lines = pltpu.roll(pltpu.roll(m, 72, 1), 1, 0)
        low_lines = jnp.where(row == E - 1, after[3 + n : 4 + n], low_lines)
        high_lines = jnp.where(row == 0, before[3 + n : 4 + n], high_lines)
        y = m + jnp.where(lane % 64 < 8, high_lines, 0.0)
        y = y + jnp.where(lane % 64 >= 56, low_lines, 0.0)
        y_parts = jnp.concatenate(parts_of(y), 1)
        r = two_dims(y, plane[0], plane[1], plane[2], plane[3])
        r_parts = jnp.concatenate(parts_of(r), 1)
        for f in range(2 * n, min(2 * n + 2, 5)):
            for c in range(4):
                at = slice(128 * c, 128 * c + 128)
                start = 512 * (f - 2 * n) + 128 * c
                cols = slice(start, start + 128)
                out[f, :, at] = (
                    base[f, :, at]
                    + q_ref[:, at] * dot(y_parts, spread[:, cols])
                    + dot(r_parts, place[:, cols])
                )
                first = end_q[0, c, 0:1] * halo[0][f : f + 1]
                final = end_q[1, c, 7:8] * halo[1][f : f + 1]
                if c == 0:
                    first = first + jnp.where(small_left, ends[f : f + 1], 0.0)
                if c == 3:
                    final = final + jnp.where(small_left, 0.0, ends[8 + f : 9 + f])
                out[f, 0:1, at] += first
                out[f, E - 1 : E, at] += final
            out_copies[f].start()
    for copy in out_copies:
        copy.wait()


def post_of(parts, across, inside, local, tables):
    return pl.pallas_call(
        post_kernel,
        out_shape=jax.ShapeDtypeStruct((5, E, 512), F32),
        in_specs=[VM] * 18,
        out_specs=HBM,
        scratch_shapes=[pltpu.VMEM((5, E, 512), F32), pltpu.SemaphoreType.DMA((5,))],
        compiler_params=pltpu.CompilerParams(vmem_limit_bytes=LIMIT),
        name="outer",
    )(
        *parts, across, inside, *local, *tables["forward"], *tables["backward"],
        tables["spread"], tables["place"],
    )


def shards(adjoint_field, metric, velocity, mortar_route, mortar_element, face_code, hanging):
    tables = constants()
    peers = lax.axis_size("dom")
    adjoint = jnp.transpose(adjoint_field, (1, 0, 2))
    met = jnp.transpose(metric, (1, 0, 2))
    vel = jnp.transpose(velocity, (1, 0, 2))
    route, target, code, hang = (
        x.reshape(1, E) for x in (mortar_route, mortar_element, face_code, hanging)
    )
    *parts, edges, marks = folded_of(route, target, code, hang, adjoint, tables["fold"])
    for o in (0, 4, 1, 3):
        pairs = [(i, (i + o - 2) % peers) for i in range(peers)]
        parts[o] = lax.ppermute(parts[o], "dom", pairs)
    local = main_of(adjoint, met, vel, kept_of(marks), tables)
    parts, local = lax.optimization_barrier((parts, local))
    out_a, out_b = lines_of(parts, edges)
    axes = ("dom", "sub")
    count = lax.axis_size(axes)
    inside = [(i, i ^ 1) for i in range(count)]
    across = [(i, i + 1 if i % 2 else i - 1) for i in range(1, count - 1)]
    outward = lax.ppermute(out_a, axes, across)
    inward = lax.ppermute(out_b, axes, inside)
    result = post_of(parts, outward, inward, local, tables)
    return jnp.transpose(result, (1, 0, 2))


def solution(mesh):
    block = P(("dom", "sub"), None, None)
    flat = P(("dom", "sub"), None)
    return jax.shard_map(
        shards,
        mesh=mesh,
        in_specs=(block, block, block, flat, flat, flat, flat),
        out_specs=block,
        check_vma=False,
    )
```

```python
import jax
import jax.numpy as jnp
import ml_dtypes
import numpy as np
from jax import lax
from jax.experimental import pallas as pl
from jax.experimental.pallas import tpu as pltpu
from jax.sharding import PartitionSpec as P

gll_nodes = np.array(
    [
        -1.0,
        -0.8717401485096066,
        -0.5917001814331423,
        -0.2092992179024789,
        0.2092992179024789,
        0.5917001814331423,
        0.8717401485096066,
        1.0,
    ]
)
viscosity = 0.005
F32, BF16 = jnp.float32, jnp.bfloat16
E = 128
HBM = pl.BlockSpec(memory_space=pltpu.HBM)
VM = pl.BlockSpec(memory_space=pltpu.VMEM)
LIMIT = 32 * 1024 * 1024
WHOLE = 64 * 1024 * 1024


def legendre_seven(points):
    prev = np.ones(points.shape)
    curr = np.array(points)
    for order in range(1, 7):
        nxt = ((2 * order + 1) * points * curr - order * prev) / (order + 1)
        prev, curr = (curr, nxt)
    return curr


def diff_matrix():
    values = legendre_seven(gll_nodes)
    result_mat = np.zeros((8, 8))
    for row in range(8):
        for col in range(8):
            if row != col:
                result_mat[row, col] = values[row] / (
                    values[col] * (gll_nodes[row] - gll_nodes[col])
                )
    result_mat[0, 0] = -14.0
    result_mat[7, 7] = 14.0
    return result_mat


def lagrange_at(points):
    basis = np.ones((8, 8))
    for row in range(8):
        for col in range(8):
            for other in range(8):
                if other != col:
                    basis[row, col] *= (points[row] - gll_nodes[other]) / (
                        gll_nodes[col] - gll_nodes[other]
                    )
    return basis


def face_tables():
    halves = [lagrange_at((gll_nodes - 1.0) / 2.0), lagrange_at((gll_nodes + 1.0) / 2.0)]
    perm_mat = np.zeros((64, 64))
    for col in range(64):
        perm_mat[col % 8 * 8 + col // 8, col] = 1.0
    tables = []
    for code in range(8):
        mat = np.kron(halves[code % 2], halves[code // 2 % 2])
        if code >= 4:
            mat = mat @ perm_mat
        tables.append(mat)
    return np.stack(tables)


def two_parts(mat):
    high = mat.astype(ml_dtypes.bfloat16)
    low = (mat - high.astype(np.float64)).astype(ml_dtypes.bfloat16)
    return high, low


def constants():
    dmat = diff_matrix()
    eye = np.eye(8)
    along_j = np.kron(np.eye(2), np.kron(dmat, eye))
    along_k = np.kron(np.eye(16), dmat)

    def forward(first, second):
        fh, fl = two_parts(viscosity * first.T)
        sh, sl = two_parts(viscosity * second.T)
        top = np.concatenate([fh, sh], 1)
        return np.concatenate([top, top], 0), np.concatenate([fl, sl], 1)

    def backward(first, second):
        fh, fl = two_parts(first)
        sh, sl = two_parts(second)
        return (
            np.concatenate([np.concatenate([fh, fl], 1), np.concatenate([sh, sl], 1)], 0),
            np.concatenate([fh, sh], 0),
        )

    def split_parity(mat):
        vectors = []
        for sign in (1.0, -1.0):
            small = (mat[:4, :4] + sign * mat[:4, ::-1][:, :4]) / 2
            for c in range(2):
                for other in range(2):
                    for swap in (0, 1):
                        vectors.append(
                            np.concatenate(
                                [
                                    np.full(64, small[2 * c + h, 2 * other + (h ^ swap)])
                                    for h in range(2)
                                ]
                            )
                        )
        return np.stack(vectors)

    coef = np.concatenate([split_parity(viscosity * dmat), split_parity(dmat.T)], 0)
    column = np.tile(np.repeat(viscosity * dmat[:, 0], 8), 2)[None]
    ends = [
        np.repeat(viscosity * dmat[2 * c : 2 * c + 2, end], 64)[None]
        for end in (0, 7)
        for c in range(4)
    ]
    coef = np.concatenate([coef, column, *ends, np.zeros((7, 128))], 0).astype(np.float32)

    tables = face_tables()
    fold = np.zeros((256, 512), ml_dtypes.bfloat16)
    for code in range(8):
        high, low = two_parts(tables[code])
        for i in range(8):
            for k in range(8):
                c, h = i // 2, i % 2
                spot = (56 + 64 * h + 16 * c + k) % 128
                cols = slice(64 * code, 64 * code + 64)
                fold[spot, cols] = high[8 * i + k]
                fold[(spot + 8) % 128, cols] = high[8 * i + k]
                fold[128 + spot, cols] = low[8 * i + k]

    spread = np.zeros((64, 512))
    place = np.zeros((64, 512))
    for i in range(8):
        for k in range(8):
            place[8 * i + k, 64 * i + k] = 1.0
            for j in range(8):
                spread[8 * i + k, 64 * i + 8 * j + k] = 1.0
    zero = np.zeros((64, 512))

    def pair(mat):
        one = np.concatenate(
            [np.concatenate([mat, zero], 1), np.concatenate([zero, mat], 1)], 0
        )
        return np.concatenate([one, one], 0).astype(ml_dtypes.bfloat16)

    return {
        "fold": fold,
        "forward": forward(along_j, along_k),
        "backward": backward(along_j, along_k),
        "spread": pair(spread),
        "place": pair(place),
        "coef": coef,
    }


def iota(dim, shape=(E, 128)):
    return lax.broadcasted_iota(jnp.int32, shape, dim)


def down(row):
    spots = jnp.where(iota(0) == iota(1), row, 0).astype(F32).astype(BF16)
    return jnp.dot(spots, jnp.ones((E, 128), BF16), preferred_element_type=F32)


def dot(a, b):
    return jnp.dot(a, b, preferred_element_type=F32)


def parts_of(x):
    high = x.astype(BF16)
    return high, (x - high.astype(F32)).astype(BF16)


def fetch(pairs, sems):
    copies = [
        pltpu.make_async_copy(src, dst, sems.at[n]) for n, (src, dst) in enumerate(pairs)
    ]
    for copy in copies:
        copy.start()
    return copies


def fold_kernel(
    route_hbm, target_hbm, code_hbm, hang_hbm, adj_hbm, fold_hbm, *refs
):
    outs, edges_out, marks_out, ints, x, fold, wide, sems = refs[:5], *refs[5:]
    peers = lax.axis_size("dom")
    copies = fetch(
        [(ref, ints.at[n]) for n, ref in enumerate((route_hbm, target_hbm, code_hbm, hang_hbm))]
        + [(adj_hbm.at[f], x.at[f]) for f in range(5)]
        + [(fold_hbm, fold)],
        sems,
    )
    for copy in copies[:4]:
        copy.wait()
    route, target, code, hang = (ints[n] for n in range(4))
    lane = iota(1)
    left = lane < 64
    slot = lax.rem(route - lax.axis_index("dom") + 2 + peers, peers)
    hit = (iota(0, (5 * E, E)) == slot * E + target).astype(F32).astype(BF16)
    marked = down(jnp.where(hang == 1, code, -2)) - (lane // 64).astype(F32)
    odd = lane % 16 >= 8
    group = (lane // 16 + 1) % 4
    for f in range(5):
        copies[4 + f].wait()
        packed = jnp.zeros((E, 128), F32)
        for c in range(4):
            moved = x[f, :, 128 * c : 128 * c + 128]
            if c:
                moved = pltpu.roll(moved, 16 * c, 1)
            packed = jnp.where(odd & (group == c), moved, packed)
        high = packed.astype(BF16)
        high_f = high.astype(F32)
        both = jnp.where(odd, high_f, pltpu.roll(packed - high_f, 8, 1)).astype(BF16)
        wide[E * f : E * f + E, 0:128] = both
        wide[E * f : E * f + E, 128:256] = high
    copies[9].wait()
    mapped = dot(wide[...], fold[...])
    faces = []
    for f in range(5):
        total = jnp.zeros((E, 128), F32)
        for q in range(4):
            total = total + jnp.where(
                marked == 2.0 * q, mapped[E * f : E * f + E, 128 * q : 128 * q + 128], 0.0
            )
        faces.append(total + pltpu.roll(total, 64, 1))
    f01 = jnp.where(left, faces[0], faces[1]).astype(BF16)
    f23 = jnp.where(left, faces[2], faces[3]).astype(BF16)
    sums = dot(hit, jnp.concatenate([f01, f23, faces[4].astype(BF16)], 1))
    for o in range(5):
        ref = outs[o]
        mine = sums[o * E : o * E + E]
        last = jnp.where(left[:64], mine[:64, 256:384], mine[64:, 256:384])
        ref[0:128] = mine[:, 0:128].astype(ref.dtype)
        ref[128:256] = mine[:, 128:256].astype(ref.dtype)
        ref[256:320] = last.astype(ref.dtype)

    marks_out[...] = jnp.broadcast_to(1.0 - hang.astype(F32), (8, E))
    lane = iota(1, (1, 128))
    own = marked[0:1], marked[E - 1 : E]
    edges_out[...] = jnp.zeros((16, 128), F32)
    for n in range(3):
        first, second = 2 * n, min(2 * n + 1, 4)
        for end, (at, chunk) in enumerate(((0, 0), (E - 1, 3))):
            a = x[first, at : at + 1, 128 * chunk : 128 * chunk + 128]
            b = x[second, at : at + 1, 128 * chunk : 128 * chunk + 128]
            if end == 0:
                b = pltpu.roll(b, 64, 1)
            else:
                a = pltpu.roll(a, 64, 1)
            keep = jnp.where((lane % 64 >= 56) & (own[end] >= -1.5), 0.0, 1.0)
            spot = 8 * end + n
            edges_out[spot : spot + 1] = jnp.where(lane < 64, a, b) * keep


def folded_of(route, target, code, hang, adjoint, fold):
    return pl.pallas_call(
        fold_kernel,
        out_shape=[
            jax.ShapeDtypeStruct((320, 128), F32 if o == 2 else BF16) for o in range(5)
        ]
        + [jax.ShapeDtypeStruct((16, 128), F32), jax.ShapeDtypeStruct((8, 128), F32)],
        in_specs=[HBM] * 6,
        out_specs=[VM] * 7,
        scratch_shapes=[
            pltpu.VMEM((4, 1, E), jnp.int32),
            pltpu.VMEM((5, E, 512), F32),
            pltpu.VMEM((256, 512), BF16),
            pltpu.VMEM((5 * E, 256), BF16),
            pltpu.SemaphoreType.DMA((10,)),
        ],
        compiler_params=pltpu.CompilerParams(vmem_limit_bytes=WHOLE),
        name="fold",
    )(route, target, code, hang, adjoint, fold)


def swap(x):
    return pltpu.roll(x, 64, 1)


def along_first(x, coef, base):
    r3, r2 = swap(x[3]), swap(x[2])
    parity = ((x[0] + r3, x[1] + r2), (x[0] - r3, x[1] - r2))
    sums = []
    for s in range(2):
        kept = (parity[s][0], swap(parity[s][0]), parity[s][1], swap(parity[s][1]))
        for c in range(2):
            at = base + 8 * s + 4 * c
            total = coef[at : at + 1] * kept[0]
            for n in range(1, 4):
                total = total + coef[at + n : at + n + 1] * kept[n]
            sums.append(total)
    p0, p1, q0, q1 = sums
    return [p0 + q0, p1 + q1, swap(q1 - p1), swap(q0 - p0)]


def chunks_of(ref, d):
    return jnp.concatenate([ref[d, :, 128 * c : 128 * c + 128] for c in range(4)], 0)


def two_dims(y, m_first, m_second, v_first, v_second, wf1, wf2, wb1, wb2):
    high, low = parts_of(y)
    g = dot(jnp.concatenate([high, low], 1), wf1[...]) + dot(high, wf2[...])
    high1, low1 = parts_of(m_first * g[:, :128] + v_first * y)
    high2, low2 = parts_of(m_second * g[:, 128:] + v_second * y)
    wide = dot(jnp.concatenate([high1, high2], 1), wb1[...])
    low = dot(jnp.concatenate([low1, low2], 1), wb2[...])
    return wide[:, :128] + wide[:, 128:] + low


def main_kernel(
    x_ref, met, vel, keep_ref, wf1, wf2, wb1, wb2, coef, out, q_out, plane_out, end_q, end_mv,
):
    lane, row = iota(1), iota(0)
    keep = keep_ref[...]
    left = lane < 64

    for c in range(4):
        at = slice(128 * c, 128 * c + 128)
        w = met[1, :, at] * coef[32:33] + jnp.where(lane % 64 < 8, vel[1, :, at], 0.0)
        high, low = parts_of(w)
        wide = dot(high, wb1[0:128])
        q_out[:, at] = wide[:, :128] + wide[:, 128:] + dot(low, wb2[0:128])

    for n, (ref, d) in enumerate(((met, 0), (met, 2), (vel, 0), (vel, 2))):
        packed = jnp.zeros((E, 128), F32)
        for c in range(4):
            moved = ref[d, :, 128 * c : 128 * c + 128]
            if c:
                moved = pltpu.roll(moved, 16 * c, 1)
            packed = jnp.where((lane // 16) % 4 == c, moved, packed)
        even = jnp.where(left, packed, swap(packed))
        other = jnp.where(left, swap(packed), packed)
        plane_out[n] = jnp.where(lane % 16 < 8, even, pltpu.roll(other, 8, 1))

    small_left = iota(1, (8, 128)) < 64
    for end in range(2):
        rows = slice((E - 8) * end, (E - 8) * end + 8)
        w = []
        for c in range(4):
            at = slice(128 * c, 128 * c + 128)
            spot = 33 + 4 * end + c
            term = met[0, rows, at] * coef[spot : spot + 1]
            if c == 3 * end:
                term = term + jnp.where(small_left != (end == 1), vel[0, rows, at], 0.0)
            w.append(term)
        back = along_first(w, coef, 16)
        for c in range(4):
            end_q[end, c] = back[c]
        at = slice(384 * end, 384 * end + 128)
        for n, (ref, d) in enumerate(((met, 1), (met, 2), (vel, 1), (vel, 2))):
            end_mv[end, n] = ref[d, rows, at]

    def field(f, carry):
        x = [x_ref[f, :, 128 * c : 128 * c + 128] * keep for c in range(4)]
        low_faces = pltpu.roll(swap(x[0]), E - 1, 0)
        high_faces = pltpu.roll(swap(x[3]), 1, 0)
        x[0] = x[0] + jnp.where(left & (row > 0), high_faces, 0.0)
        x[3] = x[3] + jnp.where(left | (row == E - 1), 0.0, low_faces)
        stacked = jnp.concatenate(x, 0)
        rest = two_dims(
            stacked, chunks_of(met, 1), chunks_of(met, 2), chunks_of(vel, 1), chunks_of(vel, 2),
            wf1, wf2, wb1, wb2,
        )
        g0 = along_first(x, coef, 0)
        inner0 = []
        for c in range(4):
            at = slice(128 * c, 128 * c + 128)
            inner0.append(met[0, :, at] * g0[c] + vel[0, :, at] * x[c])
        back = along_first(inner0, coef, 16)
        for c in range(4):
            out[f, :, 128 * c : 128 * c + 128] = rest[E * c : E * c + E] + back[c]
        return carry

    lax.fori_loop(0, 5, field, 0)


def keep_kernel(marks, out):
    kept = jnp.where(iota(0) == iota(1), marks[0:1], 0.0).astype(BF16)
    column = dot(kept, jnp.ones((E, 128), BF16))
    out[...] = jnp.where(iota(1) % 64 >= 56, column, 1.0)


def kept_of(marks):
    return pl.pallas_call(
        keep_kernel,
        out_shape=jax.ShapeDtypeStruct((E, 128), F32),
        in_specs=[VM],
        out_specs=VM,
        compiler_params=pltpu.CompilerParams(vmem_limit_bytes=16 * 1024 * 1024),
        cost_estimate=pl.CostEstimate(
            flops=1_200_000_000, bytes_accessed=1_000_000, transcendentals=0
        ),
        name="keep",
    )(marks)


def main_of(adjoint, metric, velocity, keep, tables):
    return pl.pallas_call(
        main_kernel,
        out_shape=[
            jax.ShapeDtypeStruct((5, E, 512), F32),
            jax.ShapeDtypeStruct((E, 512), F32),
            jax.ShapeDtypeStruct((4, E, 128), F32),
            jax.ShapeDtypeStruct((2, 4, 8, 128), F32),
            jax.ShapeDtypeStruct((2, 4, 8, 128), F32),
        ],
        in_specs=[VM] * 9,
        out_specs=[VM] * 5,
        compiler_params=pltpu.CompilerParams(vmem_limit_bytes=LIMIT),
        cost_estimate=pl.CostEstimate(
            flops=4_000_000_000, bytes_accessed=6_000_000, transcendentals=0
        ),
        name="inner",
    )(
        adjoint, metric, velocity, keep,
        *tables["forward"], *tables["backward"], tables["coef"],
    )


def odd_device():
    index = lax.axis_index("dom") * lax.axis_size("sub") + lax.axis_index("sub")
    return lax.rem(index, 2) == 1


def line_kernel(a, b, own, c, d, edges, across, inside):
    def rows(start):
        return sum(ref[start : start + 16].astype(F32) for ref in (a, b, own, c, d))

    low = [edges[0:3]]
    high = [edges[8:11]]
    for n, (first, last) in enumerate(((0, 112), (128, 240), (256, 304))):
        low.append(pltpu.roll(rows(first)[0:1], 56, 1))
        line = rows(last)[15:16]
        high.append(pltpu.roll(swap(line) if n == 2 else line, 72, 1))
    zero = jnp.zeros((2, 128), F32)
    low = jnp.concatenate(low + [zero], 0)
    high = jnp.concatenate(high + [zero], 0)
    odd = odd_device()
    across[...] = jnp.where(odd, high, low)
    inside[...] = jnp.where(odd, low, high)


def lines_of(parts, edges):
    return pl.pallas_call(
        line_kernel,
        out_shape=[jax.ShapeDtypeStruct((8, 128), F32)] * 2,
        in_specs=[VM] * 6,
        out_specs=[VM] * 2,
        compiler_params=pltpu.CompilerParams(vmem_limit_bytes=LIMIT),
        name="lines",
    )(*parts, edges)


def post_kernel(
    a, b, own, c2, d, across, inside, base, q_ref, plane, end_q, end_mv,
    wf1, wf2, wb1, wb2, spread, place, out_hbm, out, out_sems,
):
    out_copies = [
        pltpu.make_async_copy(out.at[f], out_hbm.at[f], out_sems.at[f]) for f in range(5)
    ]
    lane, row = iota(1), iota(0)
    left = lane < 64

    small_left = iota(1, (1, 128)) < 64
    halo = []
    odd = odd_device()
    before = jnp.where(odd, inside[...], across[...])
    after = jnp.where(odd, across[...], inside[...])
    for got in (before, after):
        rows = []
        for n in range(3):
            pair = got[n : n + 1]
            turned = pltpu.roll(pair, 64, 1)
            rows.append(jnp.where(small_left, pair, turned))
            rows.append(jnp.where(small_left, turned, pair))
        halo.append(jnp.concatenate(rows + [jnp.zeros((2, 128), F32)], 0))
    u = jnp.concatenate(halo, 0)
    faces = []
    for n in range(3):
        rows = slice(128 * n, min(128 * n + 128, 320))
        m = sum(ref[rows].astype(F32) for ref in (a, b, own, c2, d))
        if n == 2:
            m = jnp.concatenate([m, swap(m)], 0)
        low_lines = pltpu.roll(pltpu.roll(m, 56, 1), E - 1, 0)
        high_lines = pltpu.roll(pltpu.roll(m, 72, 1), 1, 0)
        low_lines = jnp.where(row == E - 1, after[3 + n : 4 + n], low_lines)
        high_lines = jnp.where(row == 0, before[3 + n : 4 + n], high_lines)
        y = m + jnp.where(lane % 64 < 8, high_lines, 0.0)
        y = y + jnp.where(lane % 64 >= 56, low_lines, 0.0)
        faces.append(y)
    stacked = jnp.concatenate(faces + [u], 0)
    factors = [
        jnp.concatenate(
            [plane[at]] * 3
            + [
                jnp.broadcast_to(end_mv[0, n, 0:1], (8, 128)),
                jnp.broadcast_to(end_mv[1, n, 7:8], (8, 128)),
            ],
            0,
        )
        for n, at in enumerate((0, 1, 2, 3))
    ]
    r = two_dims(stacked, *factors, wf1, wf2, wb1, wb2)
    ends = r[3 * E :]
    y_parts = jnp.concatenate(parts_of(stacked[: 3 * E]), 1)
    r_parts = jnp.concatenate(parts_of(r[: 3 * E]), 1)
    for n in range(3):
        rows = slice(E * n, E * n + E)
        for f in range(2 * n, min(2 * n + 2, 5)):
            cols = slice(512 * (f - 2 * n), 512 * (f - 2 * n) + 512)
            out[f] = (
                base[f]
                + q_ref[...] * dot(y_parts[rows], spread[:, cols])
                + dot(r_parts[rows], place[:, cols])
            )
            for c in range(4):
                at = slice(128 * c, 128 * c + 128)
                first = end_q[0, c, 0:1] * halo[0][f : f + 1]
                final = end_q[1, c, 7:8] * halo[1][f : f + 1]
                if c == 0:
                    first = first + jnp.where(small_left, ends[f : f + 1], 0.0)
                if c == 3:
                    final = final + jnp.where(small_left, 0.0, ends[8 + f : 9 + f])
                out[f, 0:1, at] += first
                out[f, E - 1 : E, at] += final
            out_copies[f].start()
    for copy in out_copies:
        copy.wait()


def post_of(parts, across, inside, local, tables):
    return pl.pallas_call(
        post_kernel,
        out_shape=jax.ShapeDtypeStruct((5, E, 512), F32),
        in_specs=[VM] * 18,
        out_specs=HBM,
        scratch_shapes=[pltpu.VMEM((5, E, 512), F32), pltpu.SemaphoreType.DMA((5,))],
        compiler_params=pltpu.CompilerParams(vmem_limit_bytes=LIMIT),
        name="outer",
    )(
        *parts, across, inside, *local, *tables["forward"], *tables["backward"],
        tables["spread"], tables["place"],
    )


def shards(adjoint_field, metric, velocity, mortar_route, mortar_element, face_code, hanging):
    tables = constants()
    peers = lax.axis_size("dom")
    adjoint = jnp.transpose(adjoint_field, (1, 0, 2))
    met = jnp.transpose(metric, (1, 0, 2))
    vel = jnp.transpose(velocity, (1, 0, 2))
    route, target, code, hang = (
        x.reshape(1, E) for x in (mortar_route, mortar_element, face_code, hanging)
    )
    *parts, edges, marks = folded_of(route, target, code, hang, adjoint, tables["fold"])
    for o in (0, 4, 1, 3):
        pairs = [(i, (i + o - 2) % peers) for i in range(peers)]
        parts[o] = lax.ppermute(parts[o], "dom", pairs)
    local = main_of(adjoint, met, vel, kept_of(marks), tables)
    parts, local = lax.optimization_barrier((parts, local))
    out_a, out_b = lines_of(parts, edges)
    axes = ("dom", "sub")
    count = lax.axis_size(axes)
    inside = [(i, i ^ 1) for i in range(count)]
    across = [(i, i + 1 if i % 2 else i - 1) for i in range(1, count - 1)]
    outward = lax.ppermute(out_a, axes, across)
    inward = lax.ppermute(out_b, axes, inside)
    result = post_of(parts, outward, inward, local, tables)
    return jnp.transpose(result, (1, 0, 2))


def solution(mesh):
    block = P(("dom", "sub"), None, None)
    flat = P(("dom", "sub"), None)
    return jax.shard_map(
        shards,
        mesh=mesh,
        in_specs=(block, block, block, flat, flat, flat, flat),
        out_specs=block,
        check_vma=False,
    )
```

```python
import jax
import jax.numpy as jnp
import ml_dtypes
import numpy as np
from jax import lax
from jax.experimental import pallas as pl
from jax.experimental.pallas import tpu as pltpu
from jax.sharding import PartitionSpec as P

gll_nodes = np.array(
    [
        -1.0,
        -0.8717401485096066,
        -0.5917001814331423,
        -0.2092992179024789,
        0.2092992179024789,
        0.5917001814331423,
        0.8717401485096066,
        1.0,
    ]
)
viscosity = 0.005
F32, BF16 = jnp.float32, jnp.bfloat16
E = 128
HBM = pl.BlockSpec(memory_space=pltpu.HBM)
VM = pl.BlockSpec(memory_space=pltpu.VMEM)
LIMIT = 32 * 1024 * 1024
WHOLE = 64 * 1024 * 1024


def legendre_seven(points):
    prev = np.ones(points.shape)
    curr = np.array(points)
    for order in range(1, 7):
        nxt = ((2 * order + 1) * points * curr - order * prev) / (order + 1)
        prev, curr = (curr, nxt)
    return curr


def diff_matrix():
    values = legendre_seven(gll_nodes)
    result_mat = np.zeros((8, 8))
    for row in range(8):
        for col in range(8):
            if row != col:
                result_mat[row, col] = values[row] / (
                    values[col] * (gll_nodes[row] - gll_nodes[col])
                )
    result_mat[0, 0] = -14.0
    result_mat[7, 7] = 14.0
    return result_mat


def lagrange_at(points):
    basis = np.ones((8, 8))
    for row in range(8):
        for col in range(8):
            for other in range(8):
                if other != col:
                    basis[row, col] *= (points[row] - gll_nodes[other]) / (
                        gll_nodes[col] - gll_nodes[other]
                    )
    return basis


def face_tables():
    halves = [lagrange_at((gll_nodes - 1.0) / 2.0), lagrange_at((gll_nodes + 1.0) / 2.0)]
    perm_mat = np.zeros((64, 64))
    for col in range(64):
        perm_mat[col % 8 * 8 + col // 8, col] = 1.0
    tables = []
    for code in range(8):
        mat = np.kron(halves[code % 2], halves[code // 2 % 2])
        if code >= 4:
            mat = mat @ perm_mat
        tables.append(mat)
    return np.stack(tables)


def two_parts(mat):
    high = mat.astype(ml_dtypes.bfloat16)
    low = (mat - high.astype(np.float64)).astype(ml_dtypes.bfloat16)
    return high, low


def constants():
    dmat = diff_matrix()
    eye = np.eye(8)
    along_j = np.kron(np.eye(2), np.kron(dmat, eye))
    along_k = np.kron(np.eye(16), dmat)

    def forward(first, second):
        fh, fl = two_parts(viscosity * first.T)
        sh, sl = two_parts(viscosity * second.T)
        top = np.concatenate([fh, sh], 1)
        return np.concatenate([top, top], 0), np.concatenate([fl, sl], 1)

    def backward(first, second):
        fh, fl = two_parts(first)
        sh, sl = two_parts(second)
        return (
            np.concatenate([np.concatenate([fh, fl], 1), np.concatenate([sh, sl], 1)], 0),
            np.concatenate([fh, sh], 0),
        )

    def split_parity(mat):
        vectors = []
        for sign in (1.0, -1.0):
            small = (mat[:4, :4] + sign * mat[:4, ::-1][:, :4]) / 2
            for c in range(2):
                for other in range(2):
                    for swap in (0, 1):
                        vectors.append(
                            np.concatenate(
                                [
                                    np.full(64, small[2 * c + h, 2 * other + (h ^ swap)])
                                    for h in range(2)
                                ]
                            )
                        )
        return np.stack(vectors)

    coef = np.concatenate([split_parity(viscosity * dmat), split_parity(dmat.T)], 0)
    column = np.tile(np.repeat(viscosity * dmat[:, 0], 8), 2)[None]
    ends = [
        np.repeat(viscosity * dmat[2 * c : 2 * c + 2, end], 64)[None]
        for end in (0, 7)
        for c in range(4)
    ]
    coef = np.concatenate([coef, column, *ends, np.zeros((7, 128))], 0).astype(np.float32)

    tables = face_tables()
    fold = np.zeros((256, 512), ml_dtypes.bfloat16)
    for code in range(8):
        high, low = two_parts(tables[code])
        for i in range(8):
            for k in range(8):
                c, h = i // 2, i % 2
                spot = (56 + 64 * h + 16 * c + k) % 128
                cols = slice(64 * code, 64 * code + 64)
                fold[spot, cols] = high[8 * i + k]
                fold[(spot + 8) % 128, cols] = high[8 * i + k]
                fold[128 + spot, cols] = low[8 * i + k]

    spread = np.zeros((64, 512))
    place = np.zeros((64, 512))
    for i in range(8):
        for k in range(8):
            place[8 * i + k, 64 * i + k] = 1.0
            for j in range(8):
                spread[8 * i + k, 64 * i + 8 * j + k] = 1.0
    zero = np.zeros((64, 512))

    def pair(mat):
        one = np.concatenate(
            [np.concatenate([mat, zero], 1), np.concatenate([zero, mat], 1)], 0
        )
        return np.concatenate([one, one], 0).astype(ml_dtypes.bfloat16)

    return {
        "fold": fold,
        "forward": forward(along_j, along_k),
        "backward": backward(along_j, along_k),
        "spread": pair(spread),
        "place": pair(place),
        "coef": coef,
    }


def iota(dim, shape=(E, 128)):
    return lax.broadcasted_iota(jnp.int32, shape, dim)


def down(row):
    spots = jnp.where(iota(0) == iota(1), row, 0).astype(F32).astype(BF16)
    return jnp.dot(spots, jnp.ones((E, 128), BF16), preferred_element_type=F32)


def dot(a, b):
    return jnp.dot(a, b, preferred_element_type=F32)


def parts_of(x):
    high = x.astype(BF16)
    return high, (x - high.astype(F32)).astype(BF16)


def fetch(pairs, sems):
    copies = [
        pltpu.make_async_copy(src, dst, sems.at[n]) for n, (src, dst) in enumerate(pairs)
    ]
    for copy in copies:
        copy.start()
    return copies


def fold_kernel(
    route_hbm, target_hbm, code_hbm, hang_hbm, adj_hbm, fold_hbm, *refs
):
    outs, edges_out, marks_out, ints, x, fold, wide, sems = refs[:5], *refs[5:]
    peers = lax.axis_size("dom")
    copies = fetch(
        [(ref, ints.at[n]) for n, ref in enumerate((route_hbm, target_hbm, code_hbm, hang_hbm))]
        + [(adj_hbm.at[f], x.at[f]) for f in range(5)]
        + [(fold_hbm, fold)],
        sems,
    )
    for copy in copies[:4]:
        copy.wait()
    route, target, code, hang = (ints[n] for n in range(4))
    lane = iota(1)
    left = lane < 64
    slot = lax.rem(route - lax.axis_index("dom") + 2 + peers, peers)
    hit = (iota(0, (5 * E, E)) == slot * E + target).astype(F32).astype(BF16)
    marked = down(jnp.where(hang == 1, code, -2)) - (lane // 64).astype(F32)
    odd = lane % 16 >= 8
    group = (lane // 16 + 1) % 4
    for f in range(5):
        copies[4 + f].wait()
        packed = jnp.zeros((E, 128), F32)
        for c in range(4):
            moved = x[f, :, 128 * c : 128 * c + 128]
            if c:
                moved = pltpu.roll(moved, 16 * c, 1)
            packed = jnp.where(odd & (group == c), moved, packed)
        high = packed.astype(BF16)
        high_f = high.astype(F32)
        both = jnp.where(odd, high_f, pltpu.roll(packed - high_f, 8, 1)).astype(BF16)
        wide[E * f : E * f + E, 0:128] = both
        wide[E * f : E * f + E, 128:256] = high
    copies[9].wait()
    mapped = dot(wide[...], fold[...])
    faces = []
    for f in range(5):
        total = jnp.zeros((E, 128), F32)
        for q in range(4):
            total = total + jnp.where(
                marked == 2.0 * q, mapped[E * f : E * f + E, 128 * q : 128 * q + 128], 0.0
            )
        faces.append(total + pltpu.roll(total, 64, 1))
    f01 = jnp.where(left, faces[0], faces[1]).astype(BF16)
    f23 = jnp.where(left, faces[2], faces[3]).astype(BF16)
    sums = dot(hit, jnp.concatenate([f01, f23, faces[4].astype(BF16)], 1))
    for o in range(5):
        ref = outs[o]
        mine = sums[o * E : o * E + E]
        last = jnp.where(left[:64], mine[:64, 256:384], mine[64:, 256:384])
        ref[0:128] = mine[:, 0:128].astype(ref.dtype)
        ref[128:256] = mine[:, 128:256].astype(ref.dtype)
        ref[256:320] = last.astype(ref.dtype)

    marks_out[...] = jnp.broadcast_to(1.0 - hang.astype(F32), (8, E))
    lane = iota(1, (1, 128))
    own = marked[0:1], marked[E - 1 : E]
    edges_out[...] = jnp.zeros((16, 128), F32)
    for n in range(3):
        first, second = 2 * n, min(2 * n + 1, 4)
        for end, (at, chunk) in enumerate(((0, 0), (E - 1, 3))):
            a = x[first, at : at + 1, 128 * chunk : 128 * chunk + 128]
            b = x[second, at : at + 1, 128 * chunk : 128 * chunk + 128]
            if end == 0:
                b = pltpu.roll(b, 64, 1)
            else:
                a = pltpu.roll(a, 64, 1)
            keep = jnp.where((lane % 64 >= 56) & (own[end] >= -1.5), 0.0, 1.0)
            spot = 8 * end + n
            edges_out[spot : spot + 1] = jnp.where(lane < 64, a, b) * keep


def folded_of(route, target, code, hang, adjoint, fold):
    return pl.pallas_call(
        fold_kernel,
        out_shape=[
            jax.ShapeDtypeStruct((320, 128), F32 if o == 2 else BF16) for o in range(5)
        ]
        + [jax.ShapeDtypeStruct((16, 128), F32), jax.ShapeDtypeStruct((8, 128), F32)],
        in_specs=[HBM] * 6,
        out_specs=[VM] * 7,
        scratch_shapes=[
            pltpu.VMEM((4, 1, E), jnp.int32),
            pltpu.VMEM((5, E, 512), F32),
            pltpu.VMEM((256, 512), BF16),
            pltpu.VMEM((5 * E, 256), BF16),
            pltpu.SemaphoreType.DMA((10,)),
        ],
        compiler_params=pltpu.CompilerParams(vmem_limit_bytes=WHOLE),
        name="fold",
    )(route, target, code, hang, adjoint, fold)


def swap(x):
    return pltpu.roll(x, 64, 1)


def along_first(x, coef, base):
    r3, r2 = swap(x[3]), swap(x[2])
    parity = ((x[0] + r3, x[1] + r2), (x[0] - r3, x[1] - r2))
    sums = []
    for s in range(2):
        kept = (parity[s][0], swap(parity[s][0]), parity[s][1], swap(parity[s][1]))
        for c in range(2):
            at = base + 8 * s + 4 * c
            total = coef[at : at + 1] * kept[0]
            for n in range(1, 4):
                total = total + coef[at + n : at + n + 1] * kept[n]
            sums.append(total)
    p0, p1, q0, q1 = sums
    return [p0 + q0, p1 + q1, swap(q1 - p1), swap(q0 - p0)]


def chunks_of(ref, d):
    return jnp.concatenate([ref[d, :, 128 * c : 128 * c + 128] for c in range(4)], 0)


def two_dims(y, m_first, m_second, v_first, v_second, wf1, wf2, wb1, wb2):
    high, low = parts_of(y)
    g = dot(jnp.concatenate([high, low], 1), wf1[...]) + dot(high, wf2[...])
    high1, low1 = parts_of(m_first * g[:, :128] + v_first * y)
    high2, low2 = parts_of(m_second * g[:, 128:] + v_second * y)
    wide = dot(jnp.concatenate([high1, high2], 1), wb1[...])
    low = dot(jnp.concatenate([low1, low2], 1), wb2[...])
    return wide[:, :128] + wide[:, 128:] + low


def factors_of(met, vel, wb1, wb2, coef, q_out, plane_out, end_q, end_mv):
    lane = iota(1)
    left = lane < 64
    for c in range(4):
        at = slice(128 * c, 128 * c + 128)
        w = met[1, :, at] * coef[32:33] + jnp.where(lane % 64 < 8, vel[1, :, at], 0.0)
        high, low = parts_of(w)
        wide = dot(high, wb1[0:128])
        q_out[:, at] = wide[:, :128] + wide[:, 128:] + dot(low, wb2[0:128])

    for n, (ref, d) in enumerate(((met, 0), (met, 2), (vel, 0), (vel, 2))):
        packed = jnp.zeros((E, 128), F32)
        for c in range(4):
            moved = ref[d, :, 128 * c : 128 * c + 128]
            if c:
                moved = pltpu.roll(moved, 16 * c, 1)
            packed = jnp.where((lane // 16) % 4 == c, moved, packed)
        even = jnp.where(left, packed, swap(packed))
        other = jnp.where(left, swap(packed), packed)
        plane_out[n] = jnp.where(lane % 16 < 8, even, pltpu.roll(other, 8, 1))

    small_left = iota(1, (8, 128)) < 64
    for end in range(2):
        rows = slice((E - 8) * end, (E - 8) * end + 8)
        w = []
        for c in range(4):
            at = slice(128 * c, 128 * c + 128)
            spot = 33 + 4 * end + c
            term = met[0, rows, at] * coef[spot : spot + 1]
            if c == 3 * end:
                term = term + jnp.where(small_left != (end == 1), vel[0, rows, at], 0.0)
            w.append(term)
        back = along_first(w, coef, 16)
        for c in range(4):
            end_q[end, c] = back[c]
        at = slice(384 * end, 384 * end + 128)
        for n, (ref, d) in enumerate(((met, 1), (met, 2), (vel, 1), (vel, 2))):
            end_mv[end, n] = ref[d, rows, at]


def main_kernel(fields, x_ref, met, vel, keep_ref, wf1, wf2, wb1, wb2, coef, out, *factors):
    lane, row = iota(1), iota(0)
    keep = keep_ref[...]
    left = lane < 64
    if factors:
        factors_of(met, vel, wb1, wb2, coef, *factors)

    def field(n, carry):
        f = n + fields[0]
        x = [x_ref[f, :, 128 * c : 128 * c + 128] * keep for c in range(4)]
        low_faces = pltpu.roll(swap(x[0]), E - 1, 0)
        high_faces = pltpu.roll(swap(x[3]), 1, 0)
        x[0] = x[0] + jnp.where(left & (row > 0), high_faces, 0.0)
        x[3] = x[3] + jnp.where(left | (row == E - 1), 0.0, low_faces)
        stacked = jnp.concatenate(x, 0)
        rest = two_dims(
            stacked, chunks_of(met, 1), chunks_of(met, 2), chunks_of(vel, 1), chunks_of(vel, 2),
            wf1, wf2, wb1, wb2,
        )
        g0 = along_first(x, coef, 0)
        inner0 = []
        for c in range(4):
            at = slice(128 * c, 128 * c + 128)
            inner0.append(met[0, :, at] * g0[c] + vel[0, :, at] * x[c])
        back = along_first(inner0, coef, 16)
        for c in range(4):
            out[n, :, 128 * c : 128 * c + 128] = rest[E * c : E * c + E] + back[c]
        return carry

    lax.fori_loop(0, len(fields), field, 0)


def keep_kernel(marks, out):
    kept = jnp.where(iota(0) == iota(1), marks[0:1], 0.0).astype(BF16)
    column = dot(kept, jnp.ones((E, 128), BF16))
    out[...] = jnp.where(iota(1) % 64 >= 56, column, 1.0)


def kept_of(marks):
    return pl.pallas_call(
        keep_kernel,
        out_shape=jax.ShapeDtypeStruct((E, 128), F32),
        in_specs=[VM],
        out_specs=VM,
        compiler_params=pltpu.CompilerParams(vmem_limit_bytes=16 * 1024 * 1024),
        cost_estimate=pl.CostEstimate(
            flops=1_200_000_000, bytes_accessed=1_000_000, transcendentals=0
        ),
        name="keep",
    )(marks)


def main_of(adjoint, metric, velocity, keep, tables, fields, factors):
    def body(*refs):
        main_kernel(fields, *refs)

    return pl.pallas_call(
        body,
        out_shape=[
            jax.ShapeDtypeStruct(shape, F32)
            for shape in [(len(fields), E, 512)]
            + [(E, 512), (4, E, 128), (2, 4, 8, 128), (2, 4, 8, 128)] * factors
        ],
        in_specs=[VM] * 9,
        out_specs=[VM] * (5 if factors else 1),
        compiler_params=pltpu.CompilerParams(vmem_limit_bytes=LIMIT),
        cost_estimate=pl.CostEstimate(
            flops=800_000_000 * len(fields), bytes_accessed=5_000_000, transcendentals=0
        ),
        name="inner",
    )(
        adjoint, metric, velocity, keep,
        *tables["forward"], *tables["backward"], tables["coef"],
    )


def odd_device():
    index = lax.axis_index("dom") * lax.axis_size("sub") + lax.axis_index("sub")
    return lax.rem(index, 2) == 1


def line_kernel(a, b, own, c, d, edges, across, inside):
    def rows(start):
        return sum(ref[start : start + 16].astype(F32) for ref in (a, b, own, c, d))

    low = [edges[0:3]]
    high = [edges[8:11]]
    for n, (first, last) in enumerate(((0, 112), (128, 240), (256, 304))):
        low.append(pltpu.roll(rows(first)[0:1], 56, 1))
        line = rows(last)[15:16]
        high.append(pltpu.roll(swap(line) if n == 2 else line, 72, 1))
    zero = jnp.zeros((2, 128), F32)
    low = jnp.concatenate(low + [zero], 0)
    high = jnp.concatenate(high + [zero], 0)
    odd = odd_device()
    across[...] = jnp.where(odd, high, low)
    inside[...] = jnp.where(odd, low, high)


def lines_of(parts, edges):
    return pl.pallas_call(
        line_kernel,
        out_shape=[jax.ShapeDtypeStruct((8, 128), F32)] * 2,
        in_specs=[VM] * 6,
        out_specs=[VM] * 2,
        compiler_params=pltpu.CompilerParams(vmem_limit_bytes=LIMIT),
        name="lines",
    )(*parts, edges)


def post_kernel(
    a, b, own, c2, d, across, inside, base_a, base_b, q_ref, plane, end_q, end_mv,
    wf1, wf2, wb1, wb2, spread, place, out_hbm, out, out_sems,
):
    out_copies = [
        pltpu.make_async_copy(out.at[f], out_hbm.at[f], out_sems.at[f]) for f in range(5)
    ]
    lane, row = iota(1), iota(0)
    left = lane < 64

    small_left = iota(1, (1, 128)) < 64
    halo = []
    odd = odd_device()
    before = jnp.where(odd, inside[...], across[...])
    after = jnp.where(odd, across[...], inside[...])
    for got in (before, after):
        rows = []
        for n in range(3):
            pair = got[n : n + 1]
            turned = pltpu.roll(pair, 64, 1)
            rows.append(jnp.where(small_left, pair, turned))
            rows.append(jnp.where(small_left, turned, pair))
        halo.append(jnp.concatenate(rows + [jnp.zeros((2, 128), F32)], 0))
    u = jnp.concatenate(halo, 0)
    faces = []
    for n in range(3):
        rows = slice(128 * n, min(128 * n + 128, 320))
        m = sum(ref[rows].astype(F32) for ref in (a, b, own, c2, d))
        if n == 2:
            m = jnp.concatenate([m, swap(m)], 0)
        low_lines = pltpu.roll(pltpu.roll(m, 56, 1), E - 1, 0)
        high_lines = pltpu.roll(pltpu.roll(m, 72, 1), 1, 0)
        low_lines = jnp.where(row == E - 1, after[3 + n : 4 + n], low_lines)
        high_lines = jnp.where(row == 0, before[3 + n : 4 + n], high_lines)
        y = m + jnp.where(lane % 64 < 8, high_lines, 0.0)
        y = y + jnp.where(lane % 64 >= 56, low_lines, 0.0)
        faces.append(y)
    stacked = jnp.concatenate(faces + [u], 0)
    factors = [
        jnp.concatenate(
            [plane[at]] * 3
            + [
                jnp.broadcast_to(end_mv[0, n, 0:1], (8, 128)),
                jnp.broadcast_to(end_mv[1, n, 7:8], (8, 128)),
            ],
            0,
        )
        for n, at in enumerate((0, 1, 2, 3))
    ]
    r = two_dims(stacked, *factors, wf1, wf2, wb1, wb2)
    ends = r[3 * E :]
    y_parts = jnp.concatenate(parts_of(stacked[: 3 * E]), 1)
    r_parts = jnp.concatenate(parts_of(r[: 3 * E]), 1)
    for n in range(3):
        rows = slice(E * n, E * n + E)
        for f in range(2 * n, min(2 * n + 2, 5)):
            cols = slice(512 * (f - 2 * n), 512 * (f - 2 * n) + 512)
            out[f] = (
                (base_a[f] if f < 2 else base_b[f - 2])
                + q_ref[...] * dot(y_parts[rows], spread[:, cols])
                + dot(r_parts[rows], place[:, cols])
            )
            for c in range(4):
                at = slice(128 * c, 128 * c + 128)
                first = end_q[0, c, 0:1] * halo[0][f : f + 1]
                final = end_q[1, c, 7:8] * halo[1][f : f + 1]
                if c == 0:
                    first = first + jnp.where(small_left, ends[f : f + 1], 0.0)
                if c == 3:
                    final = final + jnp.where(small_left, 0.0, ends[8 + f : 9 + f])
                out[f, 0:1, at] += first
                out[f, E - 1 : E, at] += final
            out_copies[f].start()
    for copy in out_copies:
        copy.wait()


def post_of(parts, across, inside, local, tables):
    return pl.pallas_call(
        post_kernel,
        out_shape=jax.ShapeDtypeStruct((5, E, 512), F32),
        in_specs=[VM] * 19,
        out_specs=HBM,
        scratch_shapes=[pltpu.VMEM((5, E, 512), F32), pltpu.SemaphoreType.DMA((5,))],
        compiler_params=pltpu.CompilerParams(vmem_limit_bytes=LIMIT),
        name="outer",
    )(
        *parts, across, inside, *local, *tables["forward"], *tables["backward"],
        tables["spread"], tables["place"],
    )


def shards(adjoint_field, metric, velocity, mortar_route, mortar_element, face_code, hanging):
    tables = constants()
    peers = lax.axis_size("dom")
    adjoint = jnp.transpose(adjoint_field, (1, 0, 2))
    met = jnp.transpose(metric, (1, 0, 2))
    vel = jnp.transpose(velocity, (1, 0, 2))
    route, target, code, hang = (
        x.reshape(1, E) for x in (mortar_route, mortar_element, face_code, hanging)
    )
    *parts, edges, marks = folded_of(route, target, code, hang, adjoint, tables["fold"])
    for o in (0, 4, 1, 3):
        pairs = [(i, (i + o - 2) % peers) for i in range(peers)]
        parts[o] = lax.ppermute(parts[o], "dom", pairs)
    kept = kept_of(marks)
    early, *factors = main_of(adjoint, met, vel, kept, tables, (0, 1), True)
    parts, early = lax.optimization_barrier((parts, early))
    lines = lines_of(parts, edges)
    (out_a, out_b), kept = lax.optimization_barrier((lines, kept))
    axes = ("dom", "sub")
    count = lax.axis_size(axes)
    inside = [(i, i ^ 1) for i in range(count)]
    across = [(i, i + 1 if i % 2 else i - 1) for i in range(1, count - 1)]
    outward = lax.ppermute(out_a, axes, across)
    inward = lax.ppermute(out_b, axes, inside)
    (late,) = main_of(adjoint, met, vel, kept, tables, (2, 3, 4), False)
    result = post_of(parts, outward, inward, (early, late, *factors), tables)
    return jnp.transpose(result, (1, 0, 2))


def solution(mesh):
    block = P(("dom", "sub"), None, None)
    flat = P(("dom", "sub"), None)
    return jax.shard_map(
        shards,
        mesh=mesh,
        in_specs=(block, block, block, flat, flat, flat, flat),
        out_specs=block,
        check_vma=False,
    )
```

```python
import jax
import jax.numpy as jnp
import ml_dtypes
import numpy as np
from jax import lax
from jax.experimental import pallas as pl
from jax.experimental.pallas import tpu as pltpu
from jax.sharding import PartitionSpec as P

gll_nodes = np.array(
    [
        -1.0,
        -0.8717401485096066,
        -0.5917001814331423,
        -0.2092992179024789,
        0.2092992179024789,
        0.5917001814331423,
        0.8717401485096066,
        1.0,
    ]
)
viscosity = 0.005
F32, BF16 = jnp.float32, jnp.bfloat16
E = 128
HBM = pl.BlockSpec(memory_space=pltpu.HBM)
VM = pl.BlockSpec(memory_space=pltpu.VMEM)
LIMIT = 32 * 1024 * 1024
WHOLE = 64 * 1024 * 1024


def legendre_seven(points):
    prev = np.ones(points.shape)
    curr = np.array(points)
    for order in range(1, 7):
        nxt = ((2 * order + 1) * points * curr - order * prev) / (order + 1)
        prev, curr = (curr, nxt)
    return curr


def diff_matrix():
    values = legendre_seven(gll_nodes)
    result_mat = np.zeros((8, 8))
    for row in range(8):
        for col in range(8):
            if row != col:
                result_mat[row, col] = values[row] / (
                    values[col] * (gll_nodes[row] - gll_nodes[col])
                )
    result_mat[0, 0] = -14.0
    result_mat[7, 7] = 14.0
    return result_mat


def lagrange_at(points):
    basis = np.ones((8, 8))
    for row in range(8):
        for col in range(8):
            for other in range(8):
                if other != col:
                    basis[row, col] *= (points[row] - gll_nodes[other]) / (
                        gll_nodes[col] - gll_nodes[other]
                    )
    return basis


def face_tables():
    halves = [lagrange_at((gll_nodes - 1.0) / 2.0), lagrange_at((gll_nodes + 1.0) / 2.0)]
    perm_mat = np.zeros((64, 64))
    for col in range(64):
        perm_mat[col % 8 * 8 + col // 8, col] = 1.0
    tables = []
    for code in range(8):
        mat = np.kron(halves[code % 2], halves[code // 2 % 2])
        if code >= 4:
            mat = mat @ perm_mat
        tables.append(mat)
    return np.stack(tables)


def two_parts(mat):
    high = mat.astype(ml_dtypes.bfloat16)
    low = (mat - high.astype(np.float64)).astype(ml_dtypes.bfloat16)
    return high, low


def constants():
    dmat = diff_matrix()
    eye = np.eye(8)
    along_j = np.kron(np.eye(2), np.kron(dmat, eye))
    along_k = np.kron(np.eye(16), dmat)

    def forward(first, second):
        fh, fl = two_parts(viscosity * first.T)
        sh, sl = two_parts(viscosity * second.T)
        top = np.concatenate([fh, sh], 1)
        return np.concatenate([top, top], 0), np.concatenate([fl, sl], 1)

    def backward(first, second):
        fh, fl = two_parts(first)
        sh, sl = two_parts(second)
        return (
            np.concatenate([np.concatenate([fh, fl], 1), np.concatenate([sh, sl], 1)], 0),
            np.concatenate([fh, sh], 0),
        )

    def split_parity(mat):
        vectors = []
        for sign in (1.0, -1.0):
            small = (mat[:4, :4] + sign * mat[:4, ::-1][:, :4]) / 2
            for c in range(2):
                for other in range(2):
                    for swap in (0, 1):
                        vectors.append(
                            np.concatenate(
                                [
                                    np.full(64, small[2 * c + h, 2 * other + (h ^ swap)])
                                    for h in range(2)
                                ]
                            )
                        )
        return np.stack(vectors)

    coef = np.concatenate([split_parity(viscosity * dmat), split_parity(dmat.T)], 0)
    column = np.tile(np.repeat(viscosity * dmat[:, 0], 8), 2)[None]
    ends = [
        np.repeat(viscosity * dmat[2 * c : 2 * c + 2, end], 64)[None]
        for end in (0, 7)
        for c in range(4)
    ]
    coef = np.concatenate([coef, column, *ends, np.zeros((7, 128))], 0).astype(np.float32)

    tables = face_tables()
    fold = np.zeros((256, 512), ml_dtypes.bfloat16)
    for code in range(8):
        high, low = two_parts(tables[code])
        for i in range(8):
            for k in range(8):
                c, h = i // 2, i % 2
                spot = (56 + 64 * h + 16 * c + k) % 128
                cols = slice(64 * code, 64 * code + 64)
                fold[spot, cols] = high[8 * i + k]
                fold[(spot + 8) % 128, cols] = high[8 * i + k]
                fold[128 + spot, cols] = low[8 * i + k]

    spread = np.zeros((64, 512))
    place = np.zeros((64, 512))
    for i in range(8):
        for k in range(8):
            place[8 * i + k, 64 * i + k] = 1.0
            for j in range(8):
                spread[8 * i + k, 64 * i + 8 * j + k] = 1.0
    zero = np.zeros((64, 512))

    def pair(mat):
        one = np.concatenate(
            [np.concatenate([mat, zero], 1), np.concatenate([zero, mat], 1)], 0
        )
        return np.concatenate([one, one], 0).astype(ml_dtypes.bfloat16)

    return {
        "fold": fold,
        "forward": forward(along_j, along_k),
        "backward": backward(along_j, along_k),
        "spread": pair(spread),
        "place": pair(place),
        "coef": coef,
    }


def iota(dim, shape=(E, 128)):
    return lax.broadcasted_iota(jnp.int32, shape, dim)


def down(row):
    spots = jnp.where(iota(0) == iota(1), row, 0).astype(F32).astype(BF16)
    return jnp.dot(spots, jnp.ones((E, 128), BF16), preferred_element_type=F32)


def dot(a, b):
    return jnp.dot(a, b, preferred_element_type=F32)


def parts_of(x):
    high = x.astype(BF16)
    return high, (x - high.astype(F32)).astype(BF16)


def fetch(pairs, sems):
    copies = [
        pltpu.make_async_copy(src, dst, sems.at[n]) for n, (src, dst) in enumerate(pairs)
    ]
    for copy in copies:
        copy.start()
    return copies


def fold_kernel(
    route_hbm, target_hbm, code_hbm, hang_hbm, adj_hbm, fold_hbm, *refs
):
    out, ints, x, fold, wide, sems = refs
    faces_out, edges_out = out.at[0:E], out.at[E : E + 32, 0:128]
    peers = lax.axis_size("dom")
    copies = fetch(
        [(ref, ints.at[n]) for n, ref in enumerate((route_hbm, target_hbm, code_hbm, hang_hbm))]
        + [(adj_hbm.at[f], x.at[f]) for f in range(5)]
        + [(fold_hbm, fold)],
        sems,
    )
    for copy in copies[:4]:
        copy.wait()
    route, target, code, hang = (ints[n] for n in range(4))
    lane = iota(1)
    left = lane < 64
    slot = lax.rem(route - lax.axis_index("dom") + 2 + peers, peers)
    marked = down(jnp.where(hang == 1, code, -2)) - (lane // 64).astype(F32)
    odd = lane % 16 >= 8
    group = (lane // 16 + 1) % 4
    for f in range(5):
        copies[4 + f].wait()
        packed = jnp.zeros((E, 128), F32)
        for c in range(4):
            moved = x[f, :, 128 * c : 128 * c + 128]
            if c:
                moved = pltpu.roll(moved, 16 * c, 1)
            packed = jnp.where(odd & (group == c), moved, packed)
        high = packed.astype(BF16)
        high_f = high.astype(F32)
        both = jnp.where(odd, high_f, pltpu.roll(packed - high_f, 8, 1)).astype(BF16)
        wide[E * f : E * f + E, 0:128] = both
        wide[E * f : E * f + E, 128:256] = high
    copies[9].wait()
    mapped = dot(wide[...], fold[...])
    faces = []
    for f in range(5):
        total = jnp.zeros((E, 128), F32)
        for q in range(4):
            total = total + jnp.where(
                marked == 2.0 * q, mapped[E * f : E * f + E, 128 * q : 128 * q + 128], 0.0
            )
        faces.append(total + pltpu.roll(total, 64, 1))
    faces_out[:, 0:128] = jnp.where(left, faces[0], faces[1])
    faces_out[:, 128:256] = jnp.where(left, faces[2], faces[3])
    faces_out[:, 256:384] = faces[4]

    edges_out[...] = jnp.zeros((32, 128), F32)
    edges_out[16:17] = (slot * E + target).astype(F32)
    edges_out[17:18] = 1.0 - hang.astype(F32)
    lane = iota(1, (1, 128))
    own = marked[0:1], marked[E - 1 : E]
    for n in range(3):
        first, second = 2 * n, min(2 * n + 1, 4)
        for end, (at, chunk) in enumerate(((0, 0), (E - 1, 3))):
            a = x[first, at : at + 1, 128 * chunk : 128 * chunk + 128]
            b = x[second, at : at + 1, 128 * chunk : 128 * chunk + 128]
            if end == 0:
                b = pltpu.roll(b, 64, 1)
            else:
                a = pltpu.roll(a, 64, 1)
            keep = jnp.where((lane % 64 >= 56) & (own[end] >= -1.5), 0.0, 1.0)
            spot = 8 * end + n
            edges_out[spot : spot + 1] = jnp.where(lane < 64, a, b) * keep


def folded_of(route, target, code, hang, adjoint, fold):
    return pl.pallas_call(
        fold_kernel,
        out_shape=jax.ShapeDtypeStruct((E + 32, 384), F32),
        in_specs=[HBM] * 6,
        out_specs=VM,
        scratch_shapes=[
            pltpu.VMEM((4, 1, E), jnp.int32),
            pltpu.VMEM((5, E, 512), F32),
            pltpu.VMEM((256, 512), BF16),
            pltpu.VMEM((5 * E, 256), BF16),
            pltpu.SemaphoreType.DMA((10,)),
        ],
        compiler_params=pltpu.CompilerParams(vmem_limit_bytes=WHOLE),
        name="fold",
    )(route, target, code, hang, adjoint, fold)


def swap(x):
    return pltpu.roll(x, 64, 1)


def along_first(x, coef, base):
    r3, r2 = swap(x[3]), swap(x[2])
    parity = ((x[0] + r3, x[1] + r2), (x[0] - r3, x[1] - r2))
    sums = []
    for s in range(2):
        kept = (parity[s][0], swap(parity[s][0]), parity[s][1], swap(parity[s][1]))
        for c in range(2):
            at = base + 8 * s + 4 * c
            total = coef[at : at + 1] * kept[0]
            for n in range(1, 4):
                total = total + coef[at + n : at + n + 1] * kept[n]
            sums.append(total)
    p0, p1, q0, q1 = sums
    return [p0 + q0, p1 + q1, swap(q1 - p1), swap(q0 - p0)]


def chunks_of(ref, d):
    return jnp.concatenate([ref[d, :, 128 * c : 128 * c + 128] for c in range(4)], 0)


def two_dims(y, m_first, m_second, v_first, v_second, wf1, wf2, wb1, wb2):
    high, low = parts_of(y)
    g = dot(jnp.concatenate([high, low], 1), wf1[...]) + dot(high, wf2[...])
    high1, low1 = parts_of(m_first * g[:, :128] + v_first * y)
    high2, low2 = parts_of(m_second * g[:, 128:] + v_second * y)
    wide = dot(jnp.concatenate([high1, high2], 1), wb1[...])
    low = dot(jnp.concatenate([low1, low2], 1), wb2[...])
    return wide[:, :128] + wide[:, 128:] + low


def factors_of(met, vel, wb1, wb2, coef, q_out, plane_out, end_q, end_mv):
    lane = iota(1)
    left = lane < 64
    for c in range(4):
        at = slice(128 * c, 128 * c + 128)
        w = met[1, :, at] * coef[32:33] + jnp.where(lane % 64 < 8, vel[1, :, at], 0.0)
        high, low = parts_of(w)
        wide = dot(high, wb1[0:128])
        q_out[:, at] = wide[:, :128] + wide[:, 128:] + dot(low, wb2[0:128])

    for n, (ref, d) in enumerate(((met, 0), (met, 2), (vel, 0), (vel, 2))):
        packed = jnp.zeros((E, 128), F32)
        for c in range(4):
            moved = ref[d, :, 128 * c : 128 * c + 128]
            if c:
                moved = pltpu.roll(moved, 16 * c, 1)
            packed = jnp.where((lane // 16) % 4 == c, moved, packed)
        even = jnp.where(left, packed, swap(packed))
        other = jnp.where(left, swap(packed), packed)
        plane_out[n] = jnp.where(lane % 16 < 8, even, pltpu.roll(other, 8, 1))

    small_left = iota(1, (8, 128)) < 64
    for end in range(2):
        rows = slice((E - 8) * end, (E - 8) * end + 8)
        w = []
        for c in range(4):
            at = slice(128 * c, 128 * c + 128)
            spot = 33 + 4 * end + c
            term = met[0, rows, at] * coef[spot : spot + 1]
            if c == 3 * end:
                term = term + jnp.where(small_left != (end == 1), vel[0, rows, at], 0.0)
            w.append(term)
        back = along_first(w, coef, 16)
        for c in range(4):
            end_q[end, c] = back[c]
        at = slice(384 * end, 384 * end + 128)
        for n, (ref, d) in enumerate(((met, 1), (met, 2), (vel, 1), (vel, 2))):
            end_mv[end, n] = ref[d, rows, at]


def main_kernel(fields, x_ref, met, vel, keep_ref, wf1, wf2, wb1, wb2, coef, out, *factors):
    lane, row = iota(1), iota(0)
    keep = keep_ref[...]
    left = lane < 64
    if factors:
        factors_of(met, vel, wb1, wb2, coef, *factors)

    def field(n, carry):
        f = n + fields[0]
        x = [x_ref[f, :, 128 * c : 128 * c + 128] * keep for c in range(4)]
        low_faces = pltpu.roll(swap(x[0]), E - 1, 0)
        high_faces = pltpu.roll(swap(x[3]), 1, 0)
        x[0] = x[0] + jnp.where(left & (row > 0), high_faces, 0.0)
        x[3] = x[3] + jnp.where(left | (row == E - 1), 0.0, low_faces)
        stacked = jnp.concatenate(x, 0)
        rest = two_dims(
            stacked, chunks_of(met, 1), chunks_of(met, 2), chunks_of(vel, 1), chunks_of(vel, 2),
            wf1, wf2, wb1, wb2,
        )
        g0 = along_first(x, coef, 0)
        inner0 = []
        for c in range(4):
            at = slice(128 * c, 128 * c + 128)
            inner0.append(met[0, :, at] * g0[c] + vel[0, :, at] * x[c])
        back = along_first(inner0, coef, 16)
        for c in range(4):
            out[n, :, 128 * c : 128 * c + 128] = rest[E * c : E * c + E] + back[c]
        return carry

    lax.fori_loop(0, len(fields), field, 0)


def sum_kernel(both, *outs):
    faces, edges = both.at[0:E], both.at[E : E + 32, 0:128]
    column = jnp.where(iota(0) == iota(1), edges[17:18], 0.0).astype(BF16)
    column = dot(column, jnp.ones((E, 128), BF16))
    outs[5][...] = jnp.where(iota(1) % 64 >= 56, column, 1.0)
    spot = edges[16:17].astype(jnp.int32)
    hit = (iota(0, (5 * E, E)) == spot).astype(F32).astype(BF16)
    sums = dot(hit, faces[...].astype(BF16))
    left = iota(1, (64, 128)) < 64
    for o in range(5):
        ref = outs[o]
        mine = sums[o * E : o * E + E]
        ref[0:128] = mine[:, 0:128].astype(ref.dtype)
        ref[128:256] = mine[:, 128:256].astype(ref.dtype)
        ref[256:320] = jnp.where(left, mine[:64, 256:384], mine[64:, 256:384]).astype(ref.dtype)


def sums_of(both):
    return pl.pallas_call(
        sum_kernel,
        out_shape=[
            jax.ShapeDtypeStruct((320, 128), F32 if o == 2 else BF16) for o in range(5)
        ]
        + [jax.ShapeDtypeStruct((E, 128), F32)],
        in_specs=[VM],
        out_specs=[VM] * 6,
        compiler_params=pltpu.CompilerParams(vmem_limit_bytes=16 * 1024 * 1024),
        cost_estimate=pl.CostEstimate(
            flops=8_000_000_000, bytes_accessed=30_000_000, transcendentals=0
        ),
        name="sums",
    )(both)


def main_of(adjoint, metric, velocity, keep, tables, fields, factors):
    def body(*refs):
        main_kernel(fields, *refs)

    return pl.pallas_call(
        body,
        out_shape=[
            jax.ShapeDtypeStruct(shape, F32)
            for shape in [(len(fields), E, 512)]
            + [(E, 512), (4, E, 128), (2, 4, 8, 128), (2, 4, 8, 128)] * factors
        ],
        in_specs=[VM] * 9,
        out_specs=[VM] * (5 if factors else 1),
        compiler_params=pltpu.CompilerParams(vmem_limit_bytes=LIMIT),
        cost_estimate=pl.CostEstimate(
            flops=800_000_000 * len(fields), bytes_accessed=5_000_000, transcendentals=0
        ),
        name="inner",
    )(
        adjoint, metric, velocity, keep,
        *tables["forward"], *tables["backward"], tables["coef"],
    )


def odd_device():
    index = lax.axis_index("dom") * lax.axis_size("sub") + lax.axis_index("sub")
    return lax.rem(index, 2) == 1


def line_kernel(a, b, own, c, d, both, across, inside):
    edges = both.at[E : E + 32, 0:128]
    def rows(start):
        return sum(ref[start : start + 16].astype(F32) for ref in (a, b, own, c, d))

    low = [edges[0:3]]
    high = [edges[8:11]]
    for n, (first, last) in enumerate(((0, 112), (128, 240), (256, 304))):
        low.append(pltpu.roll(rows(first)[0:1], 56, 1))
        line = rows(last)[15:16]
        high.append(pltpu.roll(swap(line) if n == 2 else line, 72, 1))
    zero = jnp.zeros((2, 128), F32)
    low = jnp.concatenate(low + [zero], 0)
    high = jnp.concatenate(high + [zero], 0)
    odd = odd_device()
    across[...] = jnp.where(odd, high, low)
    inside[...] = jnp.where(odd, low, high)


def lines_of(parts, both):
    return pl.pallas_call(
        line_kernel,
        out_shape=[jax.ShapeDtypeStruct((8, 128), F32)] * 2,
        in_specs=[VM] * 6,
        out_specs=[VM] * 2,
        compiler_params=pltpu.CompilerParams(vmem_limit_bytes=LIMIT),
        name="lines",
    )(*parts, both)


def post_kernel(
    a, b, own, c2, d, across, inside, base_a, base_b, q_ref, plane, end_q, end_mv,
    wf1, wf2, wb1, wb2, spread, place, out_hbm, out, out_sems,
):
    out_copies = [
        pltpu.make_async_copy(out.at[f], out_hbm.at[f], out_sems.at[f]) for f in range(5)
    ]
    lane, row = iota(1), iota(0)
    left = lane < 64

    small_left = iota(1, (1, 128)) < 64
    halo = []
    odd = odd_device()
    before = jnp.where(odd, inside[...], across[...])
    after = jnp.where(odd, across[...], inside[...])
    for got in (before, after):
        rows = []
        for n in range(3):
            pair = got[n : n + 1]
            turned = pltpu.roll(pair, 64, 1)
            rows.append(jnp.where(small_left, pair, turned))
            rows.append(jnp.where(small_left, turned, pair))
        halo.append(jnp.concatenate(rows + [jnp.zeros((2, 128), F32)], 0))
    u = jnp.concatenate(halo, 0)
    faces = []
    for n in range(3):
        rows = slice(128 * n, min(128 * n + 128, 320))
        m = sum(ref[rows].astype(F32) for ref in (a, b, own, c2, d))
        if n == 2:
            m = jnp.concatenate([m, swap(m)], 0)
        low_lines = pltpu.roll(pltpu.roll(m, 56, 1), E - 1, 0)
        high_lines = pltpu.roll(pltpu.roll(m, 72, 1), 1, 0)
        low_lines = jnp.where(row == E - 1, after[3 + n : 4 + n], low_lines)
        high_lines = jnp.where(row == 0, before[3 + n : 4 + n], high_lines)
        y = m + jnp.where(lane % 64 < 8, high_lines, 0.0)
        y = y + jnp.where(lane % 64 >= 56, low_lines, 0.0)
        faces.append(y)
    stacked = jnp.concatenate(faces + [u], 0)
    factors = [
        jnp.concatenate(
            [plane[at]] * 3
            + [
                jnp.broadcast_to(end_mv[0, n, 0:1], (8, 128)),
                jnp.broadcast_to(end_mv[1, n, 7:8], (8, 128)),
            ],
            0,
        )
        for n, at in enumerate((0, 1, 2, 3))
    ]
    r = two_dims(stacked, *factors, wf1, wf2, wb1, wb2)
    ends = r[3 * E :]
    y_parts = jnp.concatenate(parts_of(stacked[: 3 * E]), 1)
    r_parts = jnp.concatenate(parts_of(r[: 3 * E]), 1)
    for n in range(3):
        rows = slice(E * n, E * n + E)
        for f in range(2 * n, min(2 * n + 2, 5)):
            cols = slice(512 * (f - 2 * n), 512 * (f - 2 * n) + 512)
            out[f] = (
                (base_a[f] if f < 2 else base_b[f - 2])
                + q_ref[...] * dot(y_parts[rows], spread[:, cols])
                + dot(r_parts[rows], place[:, cols])
            )
            for c in range(4):
                at = slice(128 * c, 128 * c + 128)
                first = end_q[0, c, 0:1] * halo[0][f : f + 1]
                final = end_q[1, c, 7:8] * halo[1][f : f + 1]
                if c == 0:
                    first = first + jnp.where(small_left, ends[f : f + 1], 0.0)
                if c == 3:
                    final = final + jnp.where(small_left, 0.0, ends[8 + f : 9 + f])
                out[f, 0:1, at] += first
                out[f, E - 1 : E, at] += final
            out_copies[f].start()
    for copy in out_copies:
        copy.wait()


def post_of(parts, across, inside, local, tables):
    return pl.pallas_call(
        post_kernel,
        out_shape=jax.ShapeDtypeStruct((5, E, 512), F32),
        in_specs=[VM] * 19,
        out_specs=HBM,
        scratch_shapes=[pltpu.VMEM((5, E, 512), F32), pltpu.SemaphoreType.DMA((5,))],
        compiler_params=pltpu.CompilerParams(vmem_limit_bytes=LIMIT),
        name="outer",
    )(
        *parts, across, inside, *local, *tables["forward"], *tables["backward"],
        tables["spread"], tables["place"],
    )


def shards(adjoint_field, metric, velocity, mortar_route, mortar_element, face_code, hanging):
    tables = constants()
    peers = lax.axis_size("dom")
    adjoint = jnp.transpose(adjoint_field, (1, 0, 2))
    met = jnp.transpose(metric, (1, 0, 2))
    vel = jnp.transpose(velocity, (1, 0, 2))
    route, target, code, hang = (
        x.reshape(1, E) for x in (mortar_route, mortar_element, face_code, hanging)
    )
    both = folded_of(route, target, code, hang, adjoint, tables["fold"])
    *parts, kept = sums_of(both)
    for o in (0, 4, 3, 1):
        pairs = [(i, (i + o - 2) % peers) for i in range(peers)]
        parts[o] = lax.ppermute(parts[o], "dom", pairs)
    early, *factors = main_of(adjoint, met, vel, kept, tables, (0, 1), True)
    parts, early = lax.optimization_barrier((parts, early))
    lines = lines_of(parts, both)
    (out_a, out_b), kept = lax.optimization_barrier((lines, kept))
    axes = ("dom", "sub")
    count = lax.axis_size(axes)
    inside = [(i, i ^ 1) for i in range(count)]
    across = [(i, i + 1 if i % 2 else i - 1) for i in range(1, count - 1)]
    outward = lax.ppermute(out_a, axes, across)
    inward = lax.ppermute(out_b, axes, inside)
    (late,) = main_of(adjoint, met, vel, kept, tables, (2, 3, 4), False)
    result = post_of(parts, outward, inward, (early, late, *factors), tables)
    return jnp.transpose(result, (1, 0, 2))


def solution(mesh):
    block = P(("dom", "sub"), None, None)
    flat = P(("dom", "sub"), None)
    return jax.shard_map(
        shards,
        mesh=mesh,
        in_specs=(block, block, block, flat, flat, flat, flat),
        out_specs=block,
        check_vma=False,
    )
```

```python
import jax
import jax.numpy as jnp
import ml_dtypes
import numpy as np
from jax import lax
from jax.experimental import pallas as pl
from jax.experimental.pallas import tpu as pltpu
from jax.sharding import PartitionSpec as P

gll_nodes = np.array(
    [
        -1.0,
        -0.8717401485096066,
        -0.5917001814331423,
        -0.2092992179024789,
        0.2092992179024789,
        0.5917001814331423,
        0.8717401485096066,
        1.0,
    ]
)
viscosity = 0.005
F32, BF16 = jnp.float32, jnp.bfloat16
E = 128
HBM = pl.BlockSpec(memory_space=pltpu.HBM)
VM = pl.BlockSpec(memory_space=pltpu.VMEM)
LIMIT = 32 * 1024 * 1024
ORDER = (3, 4, 2, 1, 0)
WHOLE = 64 * 1024 * 1024


def legendre_seven(points):
    prev = np.ones(points.shape)
    curr = np.array(points)
    for order in range(1, 7):
        nxt = ((2 * order + 1) * points * curr - order * prev) / (order + 1)
        prev, curr = (curr, nxt)
    return curr


def diff_matrix():
    values = legendre_seven(gll_nodes)
    result_mat = np.zeros((8, 8))
    for row in range(8):
        for col in range(8):
            if row != col:
                result_mat[row, col] = values[row] / (
                    values[col] * (gll_nodes[row] - gll_nodes[col])
                )
    result_mat[0, 0] = -14.0
    result_mat[7, 7] = 14.0
    return result_mat


def lagrange_at(points):
    basis = np.ones((8, 8))
    for row in range(8):
        for col in range(8):
            for other in range(8):
                if other != col:
                    basis[row, col] *= (points[row] - gll_nodes[other]) / (
                        gll_nodes[col] - gll_nodes[other]
                    )
    return basis


def face_tables():
    halves = [lagrange_at((gll_nodes - 1.0) / 2.0), lagrange_at((gll_nodes + 1.0) / 2.0)]
    perm_mat = np.zeros((64, 64))
    for col in range(64):
        perm_mat[col % 8 * 8 + col // 8, col] = 1.0
    tables = []
    for code in range(8):
        mat = np.kron(halves[code % 2], halves[code // 2 % 2])
        if code >= 4:
            mat = mat @ perm_mat
        tables.append(mat)
    return np.stack(tables)


def two_parts(mat):
    high = mat.astype(ml_dtypes.bfloat16)
    low = (mat - high.astype(np.float64)).astype(ml_dtypes.bfloat16)
    return high, low


def constants():
    dmat = diff_matrix()
    eye = np.eye(8)
    along_j = np.kron(np.eye(2), np.kron(dmat, eye))
    along_k = np.kron(np.eye(16), dmat)

    def forward(first, second):
        fh, fl = two_parts(viscosity * first.T)
        sh, sl = two_parts(viscosity * second.T)
        top = np.concatenate([fh, sh], 1)
        return np.concatenate([top, top], 0), np.concatenate([fl, sl], 1)

    def backward(first, second):
        fh, fl = two_parts(first)
        sh, sl = two_parts(second)
        return (
            np.concatenate([np.concatenate([fh, fl], 1), np.concatenate([sh, sl], 1)], 0),
            np.concatenate([fh, sh], 0),
        )

    def split_parity(mat):
        vectors = []
        for sign in (1.0, -1.0):
            small = (mat[:4, :4] + sign * mat[:4, ::-1][:, :4]) / 2
            for c in range(2):
                for other in range(2):
                    for swap in (0, 1):
                        vectors.append(
                            np.concatenate(
                                [
                                    np.full(64, small[2 * c + h, 2 * other + (h ^ swap)])
                                    for h in range(2)
                                ]
                            )
                        )
        return np.stack(vectors)

    coef = np.concatenate([split_parity(viscosity * dmat), split_parity(dmat.T)], 0)
    column = np.tile(np.repeat(viscosity * dmat[:, 0], 8), 2)[None]
    ends = [
        np.repeat(viscosity * dmat[2 * c : 2 * c + 2, end], 64)[None]
        for end in (0, 7)
        for c in range(4)
    ]
    coef = np.concatenate([coef, column, *ends, np.zeros((7, 128))], 0).astype(np.float32)

    tables = face_tables()
    fold = np.zeros((256, 512), ml_dtypes.bfloat16)
    for code in range(8):
        high, low = two_parts(tables[code])
        for i in range(8):
            for k in range(8):
                c, h = i // 2, i % 2
                spot = (56 + 64 * h + 16 * c + k) % 128
                cols = slice(64 * code, 64 * code + 64)
                fold[spot, cols] = high[8 * i + k]
                fold[(spot + 8) % 128, cols] = high[8 * i + k]
                fold[128 + spot, cols] = low[8 * i + k]

    spread = np.zeros((64, 512))
    place = np.zeros((64, 512))
    for i in range(8):
        for k in range(8):
            place[8 * i + k, 64 * i + k] = 1.0
            for j in range(8):
                spread[8 * i + k, 64 * i + 8 * j + k] = 1.0
    zero = np.zeros((64, 512))

    def pair(mat):
        one = np.concatenate(
            [np.concatenate([mat, zero], 1), np.concatenate([zero, mat], 1)], 0
        )
        return np.concatenate([one, one], 0).astype(ml_dtypes.bfloat16)

    return {
        "fold": fold,
        "forward": forward(along_j, along_k),
        "backward": backward(along_j, along_k),
        "spread": pair(spread),
        "place": pair(place),
        "coef": coef,
    }


def iota(dim, shape=(E, 128)):
    return lax.broadcasted_iota(jnp.int32, shape, dim)


def down(row):
    spots = jnp.where(iota(0) == iota(1), row, 0).astype(F32).astype(BF16)
    return jnp.dot(spots, jnp.ones((E, 128), BF16), preferred_element_type=F32)


def dot(a, b):
    return jnp.dot(a, b, preferred_element_type=F32)


def parts_of(x):
    high = x.astype(BF16)
    return high, (x - high.astype(F32)).astype(BF16)


def fetch(pairs, sems):
    copies = [
        pltpu.make_async_copy(src, dst, sems.at[n]) for n, (src, dst) in enumerate(pairs)
    ]
    for copy in copies:
        copy.start()
    return copies


def fold_kernel(
    route_hbm, target_hbm, code_hbm, hang_hbm, adj_hbm, fold_hbm, *refs
):
    out, ints, x, fold, wide, sems = refs
    faces_out, edges_out = out.at[0:E], out.at[E : E + 32, 0:128]
    peers = lax.axis_size("dom")
    copies = fetch(
        [(ref, ints.at[n]) for n, ref in enumerate((route_hbm, target_hbm, code_hbm, hang_hbm))]
        + [(adj_hbm.at[f], x.at[f]) for f in range(5)]
        + [(fold_hbm, fold)],
        sems,
    )
    for copy in copies[:4]:
        copy.wait()
    route, target, code, hang = (ints[n] for n in range(4))
    lane = iota(1)
    left = lane < 64
    slot = lax.rem(route - lax.axis_index("dom") + 2 + peers, peers)
    marked = down(jnp.where(hang == 1, code, -2)) - (lane // 64).astype(F32)
    odd = lane % 16 >= 8
    group = (lane // 16 + 1) % 4
    for f in range(5):
        copies[4 + f].wait()
        packed = jnp.zeros((E, 128), F32)
        for c in range(4):
            moved = x[f, :, 128 * c : 128 * c + 128]
            if c:
                moved = pltpu.roll(moved, 16 * c, 1)
            packed = jnp.where(odd & (group == c), moved, packed)
        high = packed.astype(BF16)
        high_f = high.astype(F32)
        both = jnp.where(odd, high_f, pltpu.roll(packed - high_f, 8, 1)).astype(BF16)
        wide[E * f : E * f + E, 0:128] = both
        wide[E * f : E * f + E, 128:256] = high
    copies[9].wait()
    mapped = dot(wide[...], fold[...])
    faces = []
    for f in range(5):
        total = jnp.zeros((E, 128), F32)
        for q in range(4):
            total = total + jnp.where(
                marked == 2.0 * q, mapped[E * f : E * f + E, 128 * q : 128 * q + 128], 0.0
            )
        faces.append(total + pltpu.roll(total, 64, 1))
    faces_out[:, 0:128] = jnp.where(left, faces[0], faces[1])
    faces_out[:, 128:256] = jnp.where(left, faces[2], faces[3])
    faces_out[:, 256:384] = faces[4]

    edges_out[...] = jnp.zeros((32, 128), F32)
    edges_out[16:17] = (slot * E + target).astype(F32)
    edges_out[17:18] = 1.0 - hang.astype(F32)
    lane = iota(1, (1, 128))
    own = marked[0:1], marked[E - 1 : E]
    for n in range(3):
        first, second = 2 * n, min(2 * n + 1, 4)
        for end, (at, chunk) in enumerate(((0, 0), (E - 1, 3))):
            a = x[first, at : at + 1, 128 * chunk : 128 * chunk + 128]
            b = x[second, at : at + 1, 128 * chunk : 128 * chunk + 128]
            if end == 0:
                b = pltpu.roll(b, 64, 1)
            else:
                a = pltpu.roll(a, 64, 1)
            keep = jnp.where((lane % 64 >= 56) & (own[end] >= -1.5), 0.0, 1.0)
            spot = 8 * end + n
            edges_out[spot : spot + 1] = jnp.where(lane < 64, a, b) * keep


def folded_of(route, target, code, hang, adjoint, fold):
    return pl.pallas_call(
        fold_kernel,
        out_shape=jax.ShapeDtypeStruct((E + 32, 384), F32),
        in_specs=[HBM] * 6,
        out_specs=VM,
        scratch_shapes=[
            pltpu.VMEM((4, 1, E), jnp.int32),
            pltpu.VMEM((5, E, 512), F32),
            pltpu.VMEM((256, 512), BF16),
            pltpu.VMEM((5 * E, 256), BF16),
            pltpu.SemaphoreType.DMA((10,)),
        ],
        compiler_params=pltpu.CompilerParams(vmem_limit_bytes=WHOLE),
        name="fold",
    )(route, target, code, hang, adjoint, fold)


def swap(x):
    return pltpu.roll(x, 64, 1)


def along_first(x, coef, base):
    r3, r2 = swap(x[3]), swap(x[2])
    parity = ((x[0] + r3, x[1] + r2), (x[0] - r3, x[1] - r2))
    sums = []
    for s in range(2):
        kept = (parity[s][0], swap(parity[s][0]), parity[s][1], swap(parity[s][1]))
        for c in range(2):
            at = base + 8 * s + 4 * c
            total = coef[at : at + 1] * kept[0]
            for n in range(1, 4):
                total = total + coef[at + n : at + n + 1] * kept[n]
            sums.append(total)
    p0, p1, q0, q1 = sums
    return [p0 + q0, p1 + q1, swap(q1 - p1), swap(q0 - p0)]


def chunks_of(ref, d):
    return jnp.concatenate([ref[d, :, 128 * c : 128 * c + 128] for c in range(4)], 0)


def two_dims(y, m_first, m_second, v_first, v_second, wf1, wf2, wb1, wb2):
    high, low = parts_of(y)
    g = dot(jnp.concatenate([high, low], 1), wf1[...]) + dot(high, wf2[...])
    high1, low1 = parts_of(m_first * g[:, :128] + v_first * y)
    high2, low2 = parts_of(m_second * g[:, 128:] + v_second * y)
    wide = dot(jnp.concatenate([high1, high2], 1), wb1[...])
    low = dot(jnp.concatenate([low1, low2], 1), wb2[...])
    return wide[:, :128] + wide[:, 128:] + low


def factors_of(met, vel, wb1, wb2, coef, q_out, plane_out, end_q, end_mv):
    lane = iota(1)
    left = lane < 64
    for c in range(4):
        at = slice(128 * c, 128 * c + 128)
        w = met[1, :, at] * coef[32:33] + jnp.where(lane % 64 < 8, vel[1, :, at], 0.0)
        high, low = parts_of(w)
        wide = dot(high, wb1[0:128])
        q_out[:, at] = wide[:, :128] + wide[:, 128:] + dot(low, wb2[0:128])

    for n, (ref, d) in enumerate(((met, 0), (met, 2), (vel, 0), (vel, 2))):
        packed = jnp.zeros((E, 128), F32)
        for c in range(4):
            moved = ref[d, :, 128 * c : 128 * c + 128]
            if c:
                moved = pltpu.roll(moved, 16 * c, 1)
            packed = jnp.where((lane // 16) % 4 == c, moved, packed)
        even = jnp.where(left, packed, swap(packed))
        other = jnp.where(left, swap(packed), packed)
        plane_out[n] = jnp.where(lane % 16 < 8, even, pltpu.roll(other, 8, 1))

    small_left = iota(1, (8, 128)) < 64
    for end in range(2):
        rows = slice((E - 8) * end, (E - 8) * end + 8)
        w = []
        for c in range(4):
            at = slice(128 * c, 128 * c + 128)
            spot = 33 + 4 * end + c
            term = met[0, rows, at] * coef[spot : spot + 1]
            if c == 3 * end:
                term = term + jnp.where(small_left != (end == 1), vel[0, rows, at], 0.0)
            w.append(term)
        back = along_first(w, coef, 16)
        for c in range(4):
            end_q[end, c] = back[c]
        at = slice(384 * end, 384 * end + 128)
        for n, (ref, d) in enumerate(((met, 1), (met, 2), (vel, 1), (vel, 2))):
            end_mv[end, n] = ref[d, rows, at]


def main_kernel(fields, x_ref, met, vel, keep_ref, wf1, wf2, wb1, wb2, coef, out, *factors):
    lane, row = iota(1), iota(0)
    keep = keep_ref[...]
    left = lane < 64
    if factors:
        factors_of(met, vel, wb1, wb2, coef, *factors)

    def field(n, carry):
        f = n + fields[0]
        x = [x_ref[f, :, 128 * c : 128 * c + 128] * keep for c in range(4)]
        low_faces = pltpu.roll(swap(x[0]), E - 1, 0)
        high_faces = pltpu.roll(swap(x[3]), 1, 0)
        x[0] = x[0] + jnp.where(left & (row > 0), high_faces, 0.0)
        x[3] = x[3] + jnp.where(left | (row == E - 1), 0.0, low_faces)
        stacked = jnp.concatenate(x, 0)
        rest = two_dims(
            stacked, chunks_of(met, 1), chunks_of(met, 2), chunks_of(vel, 1), chunks_of(vel, 2),
            wf1, wf2, wb1, wb2,
        )
        g0 = along_first(x, coef, 0)
        inner0 = []
        for c in range(4):
            at = slice(128 * c, 128 * c + 128)
            inner0.append(met[0, :, at] * g0[c] + vel[0, :, at] * x[c])
        back = along_first(inner0, coef, 16)
        for c in range(4):
            out[n, :, 128 * c : 128 * c + 128] = rest[E * c : E * c + E] + back[c]
        return carry

    lax.fori_loop(0, len(fields), field, 0)


def sum_kernel(both, *outs):
    faces, edges = both.at[0:E], both.at[E : E + 32, 0:128]
    column = jnp.where(iota(0) == iota(1), edges[17:18], 0.0).astype(BF16)
    column = dot(column, jnp.ones((E, 128), BF16))
    outs[5][...] = jnp.where(iota(1) % 64 >= 56, column, 1.0)
    spot = edges[16:17].astype(jnp.int32)
    hit = (iota(0, (5 * E, E)) == spot).astype(F32).astype(BF16)
    sums = dot(hit, faces[...].astype(BF16))
    left = iota(1, (64, 128)) < 64
    for ref, o in zip(outs, ORDER):
        mine = sums[o * E : o * E + E]
        ref[0:128] = mine[:, 0:128].astype(ref.dtype)
        ref[128:256] = mine[:, 128:256].astype(ref.dtype)
        ref[256:320] = jnp.where(left, mine[:64, 256:384], mine[64:, 256:384]).astype(ref.dtype)


def sums_of(both):
    return pl.pallas_call(
        sum_kernel,
        out_shape=[
            jax.ShapeDtypeStruct((320, 128), F32 if o == 2 else BF16) for o in range(5)
        ]
        + [jax.ShapeDtypeStruct((E, 128), F32)],
        in_specs=[VM],
        out_specs=[VM] * 6,
        compiler_params=pltpu.CompilerParams(vmem_limit_bytes=16 * 1024 * 1024),
        cost_estimate=pl.CostEstimate(
            flops=8_000_000_000, bytes_accessed=30_000_000, transcendentals=0
        ),
        name="sums",
    )(both)


def main_of(adjoint, metric, velocity, keep, tables, fields, factors):
    def body(*refs):
        main_kernel(fields, *refs)

    return pl.pallas_call(
        body,
        out_shape=[
            jax.ShapeDtypeStruct(shape, F32)
            for shape in [(len(fields), E, 512)]
            + [(E, 512), (4, E, 128), (2, 4, 8, 128), (2, 4, 8, 128)] * factors
        ],
        in_specs=[VM] * 9,
        out_specs=[VM] * (5 if factors else 1),
        compiler_params=pltpu.CompilerParams(vmem_limit_bytes=LIMIT),
        cost_estimate=pl.CostEstimate(
            flops=800_000_000 * len(fields), bytes_accessed=5_000_000, transcendentals=0
        ),
        name="inner",
    )(
        adjoint, metric, velocity, keep,
        *tables["forward"], *tables["backward"], tables["coef"],
    )


def odd_device():
    index = lax.axis_index("dom") * lax.axis_size("sub") + lax.axis_index("sub")
    return lax.rem(index, 2) == 1


def line_kernel(a, b, own, c, d, both, across, inside):
    edges = both.at[E : E + 32, 0:128]
    def rows(start):
        return sum(ref[start : start + 16].astype(F32) for ref in (a, b, own, c, d))

    low = [edges[0:3]]
    high = [edges[8:11]]
    for n, (first, last) in enumerate(((0, 112), (128, 240), (256, 304))):
        low.append(pltpu.roll(rows(first)[0:1], 56, 1))
        line = rows(last)[15:16]
        high.append(pltpu.roll(swap(line) if n == 2 else line, 72, 1))
    zero = jnp.zeros((2, 128), F32)
    low = jnp.concatenate(low + [zero], 0)
    high = jnp.concatenate(high + [zero], 0)
    odd = odd_device()
    across[...] = jnp.where(odd, high, low)
    inside[...] = jnp.where(odd, low, high)


def lines_of(parts, both):
    return pl.pallas_call(
        line_kernel,
        out_shape=[jax.ShapeDtypeStruct((8, 128), F32)] * 2,
        in_specs=[VM] * 6,
        out_specs=[VM] * 2,
        compiler_params=pltpu.CompilerParams(vmem_limit_bytes=LIMIT),
        name="lines",
    )(*parts, both)


def post_kernel(
    a, b, own, c2, d, across, inside, base_a, base_b, q_ref, plane, end_q, end_mv,
    wf1, wf2, wb1, wb2, spread, place, out_hbm, out, out_sems,
):
    out_copies = [
        pltpu.make_async_copy(out.at[f], out_hbm.at[f], out_sems.at[f]) for f in range(5)
    ]
    lane, row = iota(1), iota(0)
    left = lane < 64

    small_left = iota(1, (1, 128)) < 64
    halo = []
    odd = odd_device()
    before = jnp.where(odd, inside[...], across[...])
    after = jnp.where(odd, across[...], inside[...])
    for got in (before, after):
        rows = []
        for n in range(3):
            pair = got[n : n + 1]
            turned = pltpu.roll(pair, 64, 1)
            rows.append(jnp.where(small_left, pair, turned))
            rows.append(jnp.where(small_left, turned, pair))
        halo.append(jnp.concatenate(rows + [jnp.zeros((2, 128), F32)], 0))
    u = jnp.concatenate(halo, 0)
    faces = []
    for n in range(3):
        rows = slice(128 * n, min(128 * n + 128, 320))
        m = sum(ref[rows].astype(F32) for ref in (a, b, own, c2, d))
        if n == 2:
            m = jnp.concatenate([m, swap(m)], 0)
        low_lines = pltpu.roll(pltpu.roll(m, 56, 1), E - 1, 0)
        high_lines = pltpu.roll(pltpu.roll(m, 72, 1), 1, 0)
        low_lines = jnp.where(row == E - 1, after[3 + n : 4 + n], low_lines)
        high_lines = jnp.where(row == 0, before[3 + n : 4 + n], high_lines)
        y = m + jnp.where(lane % 64 < 8, high_lines, 0.0)
        y = y + jnp.where(lane % 64 >= 56, low_lines, 0.0)
        faces.append(y)
    stacked = jnp.concatenate(faces + [u], 0)
    factors = [
        jnp.concatenate(
            [plane[at]] * 3
            + [
                jnp.broadcast_to(end_mv[0, n, 0:1], (8, 128)),
                jnp.broadcast_to(end_mv[1, n, 7:8], (8, 128)),
            ],
            0,
        )
        for n, at in enumerate((0, 1, 2, 3))
    ]
    r = two_dims(stacked, *factors, wf1, wf2, wb1, wb2)
    ends = r[3 * E :]
    y_parts = jnp.concatenate(parts_of(stacked[: 3 * E]), 1)
    r_parts = jnp.concatenate(parts_of(r[: 3 * E]), 1)
    for n in range(3):
        rows = slice(E * n, E * n + E)
        for f in range(2 * n, min(2 * n + 2, 5)):
            cols = slice(512 * (f - 2 * n), 512 * (f - 2 * n) + 512)
            out[f] = (
                (base_a[f] if f < 2 else base_b[f - 2])
                + q_ref[...] * dot(y_parts[rows], spread[:, cols])
                + dot(r_parts[rows], place[:, cols])
            )
            for c in range(4):
                at = slice(128 * c, 128 * c + 128)
                first = end_q[0, c, 0:1] * halo[0][f : f + 1]
                final = end_q[1, c, 7:8] * halo[1][f : f + 1]
                if c == 0:
                    first = first + jnp.where(small_left, ends[f : f + 1], 0.0)
                if c == 3:
                    final = final + jnp.where(small_left, 0.0, ends[8 + f : 9 + f])
                out[f, 0:1, at] += first
                out[f, E - 1 : E, at] += final
            out_copies[f].start()
    for copy in out_copies:
        copy.wait()


def post_of(parts, across, inside, local, tables):
    return pl.pallas_call(
        post_kernel,
        out_shape=jax.ShapeDtypeStruct((5, E, 512), F32),
        in_specs=[VM] * 19,
        out_specs=HBM,
        scratch_shapes=[pltpu.VMEM((5, E, 512), F32), pltpu.SemaphoreType.DMA((5,))],
        compiler_params=pltpu.CompilerParams(vmem_limit_bytes=LIMIT),
        name="outer",
    )(
        *parts, across, inside, *local, *tables["forward"], *tables["backward"],
        tables["spread"], tables["place"],
    )


def shards(adjoint_field, metric, velocity, mortar_route, mortar_element, face_code, hanging):
    tables = constants()
    peers = lax.axis_size("dom")
    adjoint = jnp.transpose(adjoint_field, (1, 0, 2))
    met = jnp.transpose(metric, (1, 0, 2))
    vel = jnp.transpose(velocity, (1, 0, 2))
    route, target, code, hang = (
        x.reshape(1, E) for x in (mortar_route, mortar_element, face_code, hanging)
    )
    both = folded_of(route, target, code, hang, adjoint, tables["fold"])
    *parts, kept = sums_of(both)
    for n in (0, 1, 3, 4):
        pairs = [(i, (i + ORDER[n] - 2) % peers) for i in range(peers)]
        parts[n] = lax.ppermute(parts[n], "dom", pairs)
    early, *factors = main_of(adjoint, met, vel, kept, tables, (0, 1), True)
    parts, early = lax.optimization_barrier((parts, early))
    lines = lines_of(parts, both)
    (out_a, out_b), kept = lax.optimization_barrier((lines, kept))
    axes = ("dom", "sub")
    count = lax.axis_size(axes)
    inside = [(i, i ^ 1) for i in range(count)]
    across = [(i, i + 1 if i % 2 else i - 1) for i in range(1, count - 1)]
    outward = lax.ppermute(out_a, axes, across)
    inward = lax.ppermute(out_b, axes, inside)
    (late,) = main_of(adjoint, met, vel, kept, tables, (2, 3, 4), False)
    result = post_of(parts, outward, inward, (early, late, *factors), tables)
    return jnp.transpose(result, (1, 0, 2))


def solution(mesh):
    block = P(("dom", "sub"), None, None)
    flat = P(("dom", "sub"), None)
    return jax.shard_map(
        shards,
        mesh=mesh,
        in_specs=(block, block, block, flat, flat, flat, flat),
        out_specs=block,
        check_vma=False,
    )
```

```python
import jax
import jax.numpy as jnp
import ml_dtypes
import numpy as np
from jax import lax
from jax.experimental import pallas as pl
from jax.experimental.pallas import tpu as pltpu
from jax.sharding import PartitionSpec as P

gll_nodes = np.array(
    [
        -1.0,
        -0.8717401485096066,
        -0.5917001814331423,
        -0.2092992179024789,
        0.2092992179024789,
        0.5917001814331423,
        0.8717401485096066,
        1.0,
    ]
)
viscosity = 0.005
F32, BF16 = jnp.float32, jnp.bfloat16
E = 128
HBM = pl.BlockSpec(memory_space=pltpu.HBM)
VM = pl.BlockSpec(memory_space=pltpu.VMEM)
LIMIT = 32 * 1024 * 1024
ORDER = (3, 4, 2, 1, 0)
WHOLE = 64 * 1024 * 1024


def legendre_seven(points):
    prev = np.ones(points.shape)
    curr = np.array(points)
    for order in range(1, 7):
        nxt = ((2 * order + 1) * points * curr - order * prev) / (order + 1)
        prev, curr = (curr, nxt)
    return curr


def diff_matrix():
    values = legendre_seven(gll_nodes)
    result_mat = np.zeros((8, 8))
    for row in range(8):
        for col in range(8):
            if row != col:
                result_mat[row, col] = values[row] / (
                    values[col] * (gll_nodes[row] - gll_nodes[col])
                )
    result_mat[0, 0] = -14.0
    result_mat[7, 7] = 14.0
    return result_mat


def lagrange_at(points):
    basis = np.ones((8, 8))
    for row in range(8):
        for col in range(8):
            for other in range(8):
                if other != col:
                    basis[row, col] *= (points[row] - gll_nodes[other]) / (
                        gll_nodes[col] - gll_nodes[other]
                    )
    return basis


def face_tables():
    halves = [lagrange_at((gll_nodes - 1.0) / 2.0), lagrange_at((gll_nodes + 1.0) / 2.0)]
    perm_mat = np.zeros((64, 64))
    for col in range(64):
        perm_mat[col % 8 * 8 + col // 8, col] = 1.0
    tables = []
    for code in range(8):
        mat = np.kron(halves[code % 2], halves[code // 2 % 2])
        if code >= 4:
            mat = mat @ perm_mat
        tables.append(mat)
    return np.stack(tables)


def two_parts(mat):
    high = mat.astype(ml_dtypes.bfloat16)
    low = (mat - high.astype(np.float64)).astype(ml_dtypes.bfloat16)
    return high, low


def constants():
    dmat = diff_matrix()
    eye = np.eye(8)
    along_j = np.kron(np.eye(2), np.kron(dmat, eye))
    along_k = np.kron(np.eye(16), dmat)

    def forward(first, second):
        fh, fl = two_parts(viscosity * first.T)
        sh, sl = two_parts(viscosity * second.T)
        top = np.concatenate([fh, sh], 1)
        return np.concatenate([top, top], 0), np.concatenate([fl, sl], 1)

    def backward(first, second):
        fh, fl = two_parts(first)
        sh, sl = two_parts(second)
        return (
            np.concatenate([np.concatenate([fh, fl], 1), np.concatenate([sh, sl], 1)], 0),
            np.concatenate([fh, sh], 0),
        )

    def split_parity(mat):
        vectors = []
        for sign in (1.0, -1.0):
            small = (mat[:4, :4] + sign * mat[:4, ::-1][:, :4]) / 2
            for c in range(2):
                for other in range(2):
                    for swap in (0, 1):
                        vectors.append(
                            np.concatenate(
                                [
                                    np.full(64, small[2 * c + h, 2 * other + (h ^ swap)])
                                    for h in range(2)
                                ]
                            )
                        )
        return np.stack(vectors)

    coef = np.concatenate([split_parity(viscosity * dmat), split_parity(dmat.T)], 0)
    column = np.tile(np.repeat(viscosity * dmat[:, 0], 8), 2)[None]
    ends = [
        np.repeat(viscosity * dmat[2 * c : 2 * c + 2, end], 64)[None]
        for end in (0, 7)
        for c in range(4)
    ]
    coef = np.concatenate([coef, column, *ends, np.zeros((7, 128))], 0).astype(np.float32)

    tables = face_tables()
    fold = np.zeros((256, 512), ml_dtypes.bfloat16)
    for code in range(8):
        high, low = two_parts(tables[code])
        for i in range(8):
            for k in range(8):
                c, h = i // 2, i % 2
                spot = (56 + 64 * h + 16 * c + k) % 128
                cols = slice(64 * code, 64 * code + 64)
                fold[spot, cols] = high[8 * i + k]
                fold[(spot + 8) % 128, cols] = high[8 * i + k]
                fold[128 + spot, cols] = low[8 * i + k]

    spread = np.zeros((64, 512))
    place = np.zeros((64, 512))
    for i in range(8):
        for k in range(8):
            place[8 * i + k, 64 * i + k] = 1.0
            for j in range(8):
                spread[8 * i + k, 64 * i + 8 * j + k] = 1.0
    zero = np.zeros((64, 512))

    def pair(mat):
        one = np.concatenate(
            [np.concatenate([mat, zero], 1), np.concatenate([zero, mat], 1)], 0
        )
        return np.concatenate([one, one], 0).astype(ml_dtypes.bfloat16)

    return {
        "fold": fold,
        "forward": forward(along_j, along_k),
        "backward": backward(along_j, along_k),
        "spread": pair(spread),
        "place": pair(place),
        "coef": coef,
    }


def iota(dim, shape=(E, 128)):
    return lax.broadcasted_iota(jnp.int32, shape, dim)


def down(row):
    spots = jnp.where(iota(0) == iota(1), row, 0).astype(F32).astype(BF16)
    return jnp.dot(spots, jnp.ones((E, 128), BF16), preferred_element_type=F32)


def dot(a, b):
    return jnp.dot(a, b, preferred_element_type=F32)


def parts_of(x):
    high = x.astype(BF16)
    return high, (x - high.astype(F32)).astype(BF16)


def fetch(pairs, sems):
    copies = [
        pltpu.make_async_copy(src, dst, sems.at[n]) for n, (src, dst) in enumerate(pairs)
    ]
    for copy in copies:
        copy.start()
    return copies


def fold_kernel(
    route_hbm, target_hbm, code_hbm, hang_hbm, adj_hbm, fold_hbm, *refs
):
    outs, edges_out, marks_out, ints, x, fold, wide, sems = refs[:5], *refs[5:]
    peers = lax.axis_size("dom")
    copies = fetch(
        [(ref, ints.at[n]) for n, ref in enumerate((route_hbm, target_hbm, code_hbm, hang_hbm))]
        + [(adj_hbm.at[f], x.at[f]) for f in range(5)]
        + [(fold_hbm, fold)],
        sems,
    )
    for copy in copies:
        copy.wait()
    route, target, code, hang = (ints[n] for n in range(4))
    lane = iota(1)
    left = lane < 64
    slot = lax.rem(route - lax.axis_index("dom") + 2 + peers, peers)
    hit = (iota(0, (5 * E, E)) == slot * E + target).astype(F32).astype(BF16)
    marked = down(jnp.where(hang == 1, code, -2)) - (lane // 64).astype(F32)
    odd = lane % 16 >= 8
    group = (lane // 16 + 1) % 4
    for f in range(5):
        packed = jnp.zeros((E, 128), F32)
        for c in range(4):
            moved = x[f, :, 128 * c : 128 * c + 128]
            if c:
                moved = pltpu.roll(moved, 16 * c, 1)
            packed = jnp.where(odd & (group == c), moved, packed)
        high = packed.astype(BF16)
        high_f = high.astype(F32)
        both = jnp.where(odd, high_f, pltpu.roll(packed - high_f, 8, 1)).astype(BF16)
        wide[E * f : E * f + E, 0:128] = both
        wide[E * f : E * f + E, 128:256] = high
    mapped = dot(wide[...], fold[...])
    faces = []
    for f in range(5):
        total = jnp.zeros((E, 128), F32)
        for q in range(4):
            total = total + jnp.where(
                marked == 2.0 * q, mapped[E * f : E * f + E, 128 * q : 128 * q + 128], 0.0
            )
        faces.append(total + pltpu.roll(total, 64, 1))
    f01 = jnp.where(left, faces[0], faces[1]).astype(BF16)
    f23 = jnp.where(left, faces[2], faces[3]).astype(BF16)
    sums = dot(hit, jnp.concatenate([f01, f23, faces[4].astype(BF16)], 1))
    for ref, o in zip(outs, ORDER):
        mine = sums[o * E : o * E + E]
        last = jnp.where(left[:64], mine[:64, 256:384], mine[64:, 256:384])
        ref[0:128] = mine[:, 0:128].astype(ref.dtype)
        ref[128:256] = mine[:, 128:256].astype(ref.dtype)
        ref[256:320] = last.astype(ref.dtype)

    marks_out[...] = jnp.broadcast_to(1.0 - hang.astype(F32), (8, E))
    lane = iota(1, (1, 128))
    own = marked[0:1], marked[E - 1 : E]
    edges_out[...] = jnp.zeros((16, 128), F32)
    for n in range(3):
        first, second = 2 * n, min(2 * n + 1, 4)
        for end, (at, chunk) in enumerate(((0, 0), (E - 1, 3))):
            a = x[first, at : at + 1, 128 * chunk : 128 * chunk + 128]
            b = x[second, at : at + 1, 128 * chunk : 128 * chunk + 128]
            if end == 0:
                b = pltpu.roll(b, 64, 1)
            else:
                a = pltpu.roll(a, 64, 1)
            keep = jnp.where((lane % 64 >= 56) & (own[end] >= -1.5), 0.0, 1.0)
            spot = 8 * end + n
            edges_out[spot : spot + 1] = jnp.where(lane < 64, a, b) * keep


def folded_of(route, target, code, hang, adjoint, fold):
    return pl.pallas_call(
        fold_kernel,
        out_shape=[
            jax.ShapeDtypeStruct((320, 128), F32 if o == 2 else BF16) for o in range(5)
        ]
        + [jax.ShapeDtypeStruct((16, 128), F32), jax.ShapeDtypeStruct((8, 128), F32)],
        in_specs=[HBM] * 6,
        out_specs=[VM] * 7,
        scratch_shapes=[
            pltpu.VMEM((4, 1, E), jnp.int32),
            pltpu.VMEM((5, E, 512), F32),
            pltpu.VMEM((256, 512), BF16),
            pltpu.VMEM((5 * E, 256), BF16),
            pltpu.SemaphoreType.DMA((10,)),
        ],
        compiler_params=pltpu.CompilerParams(vmem_limit_bytes=WHOLE),
        name="fold",
    )(route, target, code, hang, adjoint, fold)


def swap(x):
    return pltpu.roll(x, 64, 1)


def along_first(x, coef, base):
    r3, r2 = swap(x[3]), swap(x[2])
    parity = ((x[0] + r3, x[1] + r2), (x[0] - r3, x[1] - r2))
    sums = []
    for s in range(2):
        kept = (parity[s][0], swap(parity[s][0]), parity[s][1], swap(parity[s][1]))
        for c in range(2):
            at = base + 8 * s + 4 * c
            total = coef[at : at + 1] * kept[0]
            for n in range(1, 4):
                total = total + coef[at + n : at + n + 1] * kept[n]
            sums.append(total)
    p0, p1, q0, q1 = sums
    return [p0 + q0, p1 + q1, swap(q1 - p1), swap(q0 - p0)]


def chunks_of(ref, d):
    return jnp.concatenate([ref[d, :, 128 * c : 128 * c + 128] for c in range(4)], 0)


def two_dims(y, m_first, m_second, v_first, v_second, wf1, wf2, wb1, wb2):
    high, low = parts_of(y)
    g = dot(jnp.concatenate([high, low], 1), wf1[...]) + dot(high, wf2[...])
    high1, low1 = parts_of(m_first * g[:, :128] + v_first * y)
    high2, low2 = parts_of(m_second * g[:, 128:] + v_second * y)
    wide = dot(jnp.concatenate([high1, high2], 1), wb1[...])
    low = dot(jnp.concatenate([low1, low2], 1), wb2[...])
    return wide[:, :128] + wide[:, 128:] + low


def factors_of(met, vel, wb1, wb2, coef, q_out, plane_out, end_q, end_mv):
    lane = iota(1)
    left = lane < 64
    for c in range(4):
        at = slice(128 * c, 128 * c + 128)
        w = met[1, :, at] * coef[32:33] + jnp.where(lane % 64 < 8, vel[1, :, at], 0.0)
        high, low = parts_of(w)
        wide = dot(high, wb1[0:128])
        q_out[:, at] = wide[:, :128] + wide[:, 128:] + dot(low, wb2[0:128])

    for n, (ref, d) in enumerate(((met, 0), (met, 2), (vel, 0), (vel, 2))):
        packed = jnp.zeros((E, 128), F32)
        for c in range(4):
            moved = ref[d, :, 128 * c : 128 * c + 128]
            if c:
                moved = pltpu.roll(moved, 16 * c, 1)
            packed = jnp.where((lane // 16) % 4 == c, moved, packed)
        even = jnp.where(left, packed, swap(packed))
        other = jnp.where(left, swap(packed), packed)
        plane_out[n] = jnp.where(lane % 16 < 8, even, pltpu.roll(other, 8, 1))

    small_left = iota(1, (8, 128)) < 64
    for end in range(2):
        rows = slice((E - 8) * end, (E - 8) * end + 8)
        w = []
        for c in range(4):
            at = slice(128 * c, 128 * c + 128)
            spot = 33 + 4 * end + c
            term = met[0, rows, at] * coef[spot : spot + 1]
            if c == 3 * end:
                term = term + jnp.where(small_left != (end == 1), vel[0, rows, at], 0.0)
            w.append(term)
        back = along_first(w, coef, 16)
        for c in range(4):
            end_q[end, c] = back[c]
        at = slice(384 * end, 384 * end + 128)
        for n, (ref, d) in enumerate(((met, 1), (met, 2), (vel, 1), (vel, 2))):
            end_mv[end, n] = ref[d, rows, at]


def main_kernel(fields, x_ref, met, vel, keep_ref, wf1, wf2, wb1, wb2, coef, out, *factors):
    lane, row = iota(1), iota(0)
    keep = keep_ref[...]
    left = lane < 64
    if factors:
        factors_of(met, vel, wb1, wb2, coef, *factors)

    def field(n, carry):
        f = n + fields[0]
        x = [x_ref[f, :, 128 * c : 128 * c + 128] * keep for c in range(4)]
        low_faces = pltpu.roll(swap(x[0]), E - 1, 0)
        high_faces = pltpu.roll(swap(x[3]), 1, 0)
        x[0] = x[0] + jnp.where(left & (row > 0), high_faces, 0.0)
        x[3] = x[3] + jnp.where(left | (row == E - 1), 0.0, low_faces)
        stacked = jnp.concatenate(x, 0)
        rest = two_dims(
            stacked, chunks_of(met, 1), chunks_of(met, 2), chunks_of(vel, 1), chunks_of(vel, 2),
            wf1, wf2, wb1, wb2,
        )
        g0 = along_first(x, coef, 0)
        inner0 = []
        for c in range(4):
            at = slice(128 * c, 128 * c + 128)
            inner0.append(met[0, :, at] * g0[c] + vel[0, :, at] * x[c])
        back = along_first(inner0, coef, 16)
        for c in range(4):
            out[n, :, 128 * c : 128 * c + 128] = rest[E * c : E * c + E] + back[c]
        return carry

    lax.fori_loop(0, len(fields), field, 0)


def keep_kernel(marks, out):
    kept = jnp.where(iota(0) == iota(1), marks[0:1], 0.0).astype(BF16)
    column = dot(kept, jnp.ones((E, 128), BF16))
    out[...] = jnp.where(iota(1) % 64 >= 56, column, 1.0)


def kept_of(marks):
    return pl.pallas_call(
        keep_kernel,
        out_shape=jax.ShapeDtypeStruct((E, 128), F32),
        in_specs=[VM],
        out_specs=VM,
        compiler_params=pltpu.CompilerParams(vmem_limit_bytes=16 * 1024 * 1024),
        cost_estimate=pl.CostEstimate(
            flops=8_000_000_000, bytes_accessed=30_000_000, transcendentals=0
        ),
        name="keep",
    )(marks)


def main_of(adjoint, metric, velocity, keep, tables, fields, factors):
    def body(*refs):
        main_kernel(fields, *refs)

    return pl.pallas_call(
        body,
        out_shape=[
            jax.ShapeDtypeStruct(shape, F32)
            for shape in [(len(fields), E, 512)]
            + [(E, 512), (4, E, 128), (2, 4, 8, 128), (2, 4, 8, 128)] * factors
        ],
        in_specs=[VM] * 9,
        out_specs=[VM] * (5 if factors else 1),
        compiler_params=pltpu.CompilerParams(vmem_limit_bytes=LIMIT),
        cost_estimate=pl.CostEstimate(
            flops=800_000_000 * len(fields), bytes_accessed=5_000_000, transcendentals=0
        ),
        name="inner",
    )(
        adjoint, metric, velocity, keep,
        *tables["forward"], *tables["backward"], tables["coef"],
    )


def odd_device():
    index = lax.axis_index("dom") * lax.axis_size("sub") + lax.axis_index("sub")
    return lax.rem(index, 2) == 1


def line_kernel(a, b, own, c, d, edges, inside, across):
    def rows(start):
        return sum(ref[start : start + 16].astype(F32) for ref in (a, b, own, c, d))

    low = [edges[0:3]]
    high = [edges[8:11]]
    for n, (first, last) in enumerate(((0, 112), (128, 240), (256, 304))):
        low.append(pltpu.roll(rows(first)[0:1], 56, 1))
        line = rows(last)[15:16]
        high.append(pltpu.roll(swap(line) if n == 2 else line, 72, 1))
    zero = jnp.zeros((2, 128), F32)
    low = jnp.concatenate(low + [zero], 0)
    high = jnp.concatenate(high + [zero], 0)
    odd = odd_device()
    across[...] = jnp.where(odd, high, low)
    inside[...] = jnp.where(odd, low, high)


def lines_of(parts, edges):
    return pl.pallas_call(
        line_kernel,
        out_shape=[jax.ShapeDtypeStruct((8, 128), F32)] * 2,
        in_specs=[VM] * 6,
        out_specs=[VM] * 2,
        compiler_params=pltpu.CompilerParams(vmem_limit_bytes=LIMIT),
        name="lines",
    )(*parts, edges)


def post_kernel(
    a, b, own, c2, d, across, inside, base_a, base_b, q_ref, plane, end_q, end_mv,
    wf1, wf2, wb1, wb2, spread, place, out_hbm, out, out_sems,
):
    out_copies = [
        pltpu.make_async_copy(out.at[f], out_hbm.at[f], out_sems.at[f]) for f in range(5)
    ]
    lane, row = iota(1), iota(0)
    left = lane < 64

    small_left = iota(1, (1, 128)) < 64
    halo = []
    odd = odd_device()
    before = jnp.where(odd, inside[...], across[...])
    after = jnp.where(odd, across[...], inside[...])
    for got in (before, after):
        rows = []
        for n in range(3):
            pair = got[n : n + 1]
            turned = pltpu.roll(pair, 64, 1)
            rows.append(jnp.where(small_left, pair, turned))
            rows.append(jnp.where(small_left, turned, pair))
        halo.append(jnp.concatenate(rows + [jnp.zeros((2, 128), F32)], 0))
    u = jnp.concatenate(halo, 0)
    faces = []
    for n in range(3):
        rows = slice(128 * n, min(128 * n + 128, 320))
        m = sum(ref[rows].astype(F32) for ref in (a, b, own, c2, d))
        if n == 2:
            m = jnp.concatenate([m, swap(m)], 0)
        low_lines = pltpu.roll(pltpu.roll(m, 56, 1), E - 1, 0)
        high_lines = pltpu.roll(pltpu.roll(m, 72, 1), 1, 0)
        low_lines = jnp.where(row == E - 1, after[3 + n : 4 + n], low_lines)
        high_lines = jnp.where(row == 0, before[3 + n : 4 + n], high_lines)
        y = m + jnp.where(lane % 64 < 8, high_lines, 0.0)
        y = y + jnp.where(lane % 64 >= 56, low_lines, 0.0)
        faces.append(y)
    stacked = jnp.concatenate(faces + [u], 0)
    factors = [
        jnp.concatenate(
            [plane[at]] * 3
            + [
                jnp.broadcast_to(end_mv[0, n, 0:1], (8, 128)),
                jnp.broadcast_to(end_mv[1, n, 7:8], (8, 128)),
            ],
            0,
        )
        for n, at in enumerate((0, 1, 2, 3))
    ]
    r = two_dims(stacked, *factors, wf1, wf2, wb1, wb2)
    ends = r[3 * E :]
    y_parts = jnp.concatenate(parts_of(stacked[: 3 * E]), 1)
    r_parts = jnp.concatenate(parts_of(r[: 3 * E]), 1)
    for n in range(3):
        rows = slice(E * n, E * n + E)
        for f in range(2 * n, min(2 * n + 2, 5)):
            cols = slice(512 * (f - 2 * n), 512 * (f - 2 * n) + 512)
            out[f] = (
                (base_a[f] if f < 2 else base_b[f - 2])
                + q_ref[...] * dot(y_parts[rows], spread[:, cols])
                + dot(r_parts[rows], place[:, cols])
            )
            for c in range(4):
                at = slice(128 * c, 128 * c + 128)
                first = end_q[0, c, 0:1] * halo[0][f : f + 1]
                final = end_q[1, c, 7:8] * halo[1][f : f + 1]
                if c == 0:
                    first = first + jnp.where(small_left, ends[f : f + 1], 0.0)
                if c == 3:
                    final = final + jnp.where(small_left, 0.0, ends[8 + f : 9 + f])
                out[f, 0:1, at] += first
                out[f, E - 1 : E, at] += final
            out_copies[f].start()
    for copy in out_copies:
        copy.wait()


def post_of(parts, across, inside, local, tables):
    return pl.pallas_call(
        post_kernel,
        out_shape=jax.ShapeDtypeStruct((5, E, 512), F32),
        in_specs=[VM] * 19,
        out_specs=HBM,
        scratch_shapes=[pltpu.VMEM((5, E, 512), F32), pltpu.SemaphoreType.DMA((5,))],
        compiler_params=pltpu.CompilerParams(vmem_limit_bytes=LIMIT),
        name="outer",
    )(
        *parts, across, inside, *local, *tables["forward"], *tables["backward"],
        tables["spread"], tables["place"],
    )


def shards(adjoint_field, metric, velocity, mortar_route, mortar_element, face_code, hanging):
    tables = constants()
    peers = lax.axis_size("dom")
    adjoint = jnp.transpose(adjoint_field, (1, 0, 2))
    met = jnp.transpose(metric, (1, 0, 2))
    vel = jnp.transpose(velocity, (1, 0, 2))
    route, target, code, hang = (
        x.reshape(1, E) for x in (mortar_route, mortar_element, face_code, hanging)
    )
    *parts, edges, marks = folded_of(route, target, code, hang, adjoint, tables["fold"])
    for n in (0, 1, 3, 4):
        pairs = [(i, (i + ORDER[n] - 2) % peers) for i in range(peers)]
        parts[n] = lax.ppermute(parts[n], "dom", pairs)
    kept = kept_of(marks)
    early, *factors = main_of(adjoint, met, vel, kept, tables, (0, 1), True)
    parts, early = lax.optimization_barrier((parts, early))
    lines = lines_of(parts, edges)
    (out_b, out_a), kept = lax.optimization_barrier((lines, kept))
    axes = ("dom", "sub")
    count = lax.axis_size(axes)
    inside = [(i, i ^ 1) for i in range(count)]
    across = [(i, i + 1 if i % 2 else i - 1) for i in range(1, count - 1)]
    inward = lax.ppermute(out_b, axes, inside)
    outward = lax.ppermute(out_a, axes, across)
    (late,) = main_of(adjoint, met, vel, kept, tables, (2, 3, 4), False)
    result = post_of(parts, outward, inward, (early, late, *factors), tables)
    return jnp.transpose(result, (1, 0, 2))


def solution(mesh):
    block = P(("dom", "sub"), None, None)
    flat = P(("dom", "sub"), None)
    return jax.shard_map(
        shards,
        mesh=mesh,
        in_specs=(block, block, block, flat, flat, flat, flat),
        out_specs=block,
        check_vma=False,
    )
```

```python
import jax
import jax.numpy as jnp
import ml_dtypes
import numpy as np
from jax import lax
from jax.experimental import pallas as pl
from jax.experimental.pallas import tpu as pltpu
from jax.sharding import PartitionSpec as P

gll_nodes = np.array(
    [
        -1.0,
        -0.8717401485096066,
        -0.5917001814331423,
        -0.2092992179024789,
        0.2092992179024789,
        0.5917001814331423,
        0.8717401485096066,
        1.0,
    ]
)
viscosity = 0.005
F32, BF16 = jnp.float32, jnp.bfloat16
E = 128
HBM = pl.BlockSpec(memory_space=pltpu.HBM)
VM = pl.BlockSpec(memory_space=pltpu.VMEM)
LIMIT = 32 * 1024 * 1024
ORDER = (3, 4, 2, 1, 0)
WHOLE = 64 * 1024 * 1024


def legendre_seven(points):
    prev = np.ones(points.shape)
    curr = np.array(points)
    for order in range(1, 7):
        nxt = ((2 * order + 1) * points * curr - order * prev) / (order + 1)
        prev, curr = (curr, nxt)
    return curr


def diff_matrix():
    values = legendre_seven(gll_nodes)
    result_mat = np.zeros((8, 8))
    for row in range(8):
        for col in range(8):
            if row != col:
                result_mat[row, col] = values[row] / (
                    values[col] * (gll_nodes[row] - gll_nodes[col])
                )
    result_mat[0, 0] = -14.0
    result_mat[7, 7] = 14.0
    return result_mat


def lagrange_at(points):
    basis = np.ones((8, 8))
    for row in range(8):
        for col in range(8):
            for other in range(8):
                if other != col:
                    basis[row, col] *= (points[row] - gll_nodes[other]) / (
                        gll_nodes[col] - gll_nodes[other]
                    )
    return basis


def face_tables():
    halves = [lagrange_at((gll_nodes - 1.0) / 2.0), lagrange_at((gll_nodes + 1.0) / 2.0)]
    perm_mat = np.zeros((64, 64))
    for col in range(64):
        perm_mat[col % 8 * 8 + col // 8, col] = 1.0
    tables = []
    for code in range(8):
        mat = np.kron(halves[code % 2], halves[code // 2 % 2])
        if code >= 4:
            mat = mat @ perm_mat
        tables.append(mat)
    return np.stack(tables)


def two_parts(mat):
    high = mat.astype(ml_dtypes.bfloat16)
    low = (mat - high.astype(np.float64)).astype(ml_dtypes.bfloat16)
    return high, low


def constants():
    dmat = diff_matrix()
    eye = np.eye(8)
    along_j = np.kron(np.eye(2), np.kron(dmat, eye))
    along_k = np.kron(np.eye(16), dmat)

    def forward(first, second):
        fh, fl = two_parts(viscosity * first.T)
        sh, sl = two_parts(viscosity * second.T)
        top = np.concatenate([fh, sh], 1)
        return np.concatenate([top, top], 0), np.concatenate([fl, sl], 1)

    def backward(first, second):
        fh, fl = two_parts(first)
        sh, sl = two_parts(second)
        return (
            np.concatenate([np.concatenate([fh, fl], 1), np.concatenate([sh, sl], 1)], 0),
            np.concatenate([fh, sh], 0),
        )

    def split_parity(mat):
        vectors = []
        for sign in (1.0, -1.0):
            small = (mat[:4, :4] + sign * mat[:4, ::-1][:, :4]) / 2
            for c in range(2):
                for other in range(2):
                    for swap in (0, 1):
                        vectors.append(
                            np.concatenate(
                                [
                                    np.full(64, small[2 * c + h, 2 * other + (h ^ swap)])
                                    for h in range(2)
                                ]
                            )
                        )
        return np.stack(vectors)

    coef = np.concatenate([split_parity(viscosity * dmat), split_parity(dmat.T)], 0)
    column = np.tile(np.repeat(viscosity * dmat[:, 0], 8), 2)[None]
    ends = [
        np.repeat(viscosity * dmat[2 * c : 2 * c + 2, end], 64)[None]
        for end in (0, 7)
        for c in range(4)
    ]
    coef = np.concatenate([coef, column, *ends, np.zeros((7, 128))], 0).astype(np.float32)

    tables = face_tables()
    fold = np.zeros((256, 512), ml_dtypes.bfloat16)
    for code in range(8):
        high, low = two_parts(tables[code])
        for i in range(8):
            for k in range(8):
                c, h = i // 2, i % 2
                spot = (56 + 64 * h + 16 * c + k) % 128
                cols = slice(64 * code, 64 * code + 64)
                fold[spot, cols] = high[8 * i + k]
                fold[(spot + 8) % 128, cols] = high[8 * i + k]
                fold[128 + spot, cols] = low[8 * i + k]

    spread = np.zeros((64, 512))
    place = np.zeros((64, 512))
    for i in range(8):
        for k in range(8):
            place[8 * i + k, 64 * i + k] = 1.0
            for j in range(8):
                spread[8 * i + k, 64 * i + 8 * j + k] = 1.0
    zero = np.zeros((64, 512))

    def pair(mat):
        one = np.concatenate(
            [np.concatenate([mat, zero], 1), np.concatenate([zero, mat], 1)], 0
        )
        return np.concatenate([one, one], 0).astype(ml_dtypes.bfloat16)

    return {
        "fold": fold,
        "forward": forward(along_j, along_k),
        "backward": backward(along_j, along_k),
        "spread": pair(spread),
        "place": pair(place),
        "coef": coef,
    }


def iota(dim, shape=(E, 128)):
    return lax.broadcasted_iota(jnp.int32, shape, dim)


def down(row):
    spots = jnp.where(iota(0) == iota(1), row, 0).astype(F32).astype(BF16)
    return jnp.dot(spots, jnp.ones((E, 128), BF16), preferred_element_type=F32)


def dot(a, b):
    return jnp.dot(a, b, preferred_element_type=F32)


def parts_of(x):
    high = x.astype(BF16)
    return high, (x - high.astype(F32)).astype(BF16)


def fetch(pairs, sems):
    copies = [
        pltpu.make_async_copy(src, dst, sems.at[n]) for n, (src, dst) in enumerate(pairs)
    ]
    for copy in copies:
        copy.start()
    return copies


def fold_kernel(
    route_hbm, target_hbm, code_hbm, hang_hbm, adj_hbm, fold_hbm, *refs
):
    outs, edges_out, marks_out, ints, x, fold, wide, sems = refs[:5], *refs[5:]
    peers = lax.axis_size("dom")
    copies = fetch(
        [(ref, ints.at[n]) for n, ref in enumerate((route_hbm, target_hbm, code_hbm, hang_hbm))]
        + [(adj_hbm.at[f], x.at[f]) for f in range(5)]
        + [(fold_hbm, fold)],
        sems,
    )
    for copy in copies:
        copy.wait()
    route, target, code, hang = (ints[n] for n in range(4))
    lane = iota(1)
    left = lane < 64
    slot = lax.rem(route - lax.axis_index("dom") + 2 + peers, peers)
    hit = (iota(0, (5 * E, E)) == slot * E + target).astype(F32).astype(BF16)
    marked = down(jnp.where(hang == 1, code, -2)) - (lane // 64).astype(F32)
    odd = lane % 16 >= 8
    group = (lane // 16 + 1) % 4
    for f in range(5):
        packed = jnp.zeros((E, 128), F32)
        for c in range(4):
            moved = x[f, :, 128 * c : 128 * c + 128]
            if c:
                moved = pltpu.roll(moved, 16 * c, 1)
            packed = jnp.where(odd & (group == c), moved, packed)
        high = packed.astype(BF16)
        high_f = high.astype(F32)
        both = jnp.where(odd, high_f, pltpu.roll(packed - high_f, 8, 1)).astype(BF16)
        wide[E * f : E * f + E, 0:128] = both
        wide[E * f : E * f + E, 128:256] = high
    mapped = dot(wide[...], fold[...])
    faces = []
    for f in range(5):
        total = jnp.zeros((E, 128), F32)
        for q in range(4):
            total = total + jnp.where(
                marked == 2.0 * q, mapped[E * f : E * f + E, 128 * q : 128 * q + 128], 0.0
            )
        faces.append(total + pltpu.roll(total, 64, 1))
    f01 = jnp.where(left, faces[0], faces[1]).astype(BF16)
    f23 = jnp.where(left, faces[2], faces[3]).astype(BF16)
    sums = dot(hit, jnp.concatenate([f01, f23, faces[4].astype(BF16)], 1))
    for ref, o in zip(outs, ORDER):
        mine = sums[o * E : o * E + E]
        last = jnp.where(left[:64], mine[:64, 256:384], mine[64:, 256:384])
        ref[0:128] = mine[:, 0:128].astype(ref.dtype)
        ref[128:256] = mine[:, 128:256].astype(ref.dtype)
        ref[256:320] = last.astype(ref.dtype)

    marks_out[...] = jnp.broadcast_to(1.0 - hang.astype(F32), (8, E))
    lane = iota(1, (1, 128))
    own = marked[0:1], marked[E - 1 : E]
    edges_out[...] = jnp.zeros((16, 128), F32)
    for n in range(3):
        first, second = 2 * n, min(2 * n + 1, 4)
        for end, (at, chunk) in enumerate(((0, 0), (E - 1, 3))):
            a = x[first, at : at + 1, 128 * chunk : 128 * chunk + 128]
            b = x[second, at : at + 1, 128 * chunk : 128 * chunk + 128]
            if end == 0:
                b = pltpu.roll(b, 64, 1)
            else:
                a = pltpu.roll(a, 64, 1)
            keep = jnp.where((lane % 64 >= 56) & (own[end] >= -1.5), 0.0, 1.0)
            spot = 8 * end + n
            edges_out[spot : spot + 1] = jnp.where(lane < 64, a, b) * keep


def folded_of(route, target, code, hang, adjoint, fold):
    return pl.pallas_call(
        fold_kernel,
        out_shape=[
            jax.ShapeDtypeStruct((320, 128), F32 if o == 2 else BF16) for o in range(5)
        ]
        + [jax.ShapeDtypeStruct((16, 128), F32), jax.ShapeDtypeStruct((8, 128), F32)],
        in_specs=[HBM] * 6,
        out_specs=[VM] * 7,
        scratch_shapes=[
            pltpu.VMEM((4, 1, E), jnp.int32),
            pltpu.VMEM((5, E, 512), F32),
            pltpu.VMEM((256, 512), BF16),
            pltpu.VMEM((5 * E, 256), BF16),
            pltpu.SemaphoreType.DMA((10,)),
        ],
        compiler_params=pltpu.CompilerParams(vmem_limit_bytes=WHOLE),
        name="fold",
    )(route, target, code, hang, adjoint, fold)


def swap(x):
    return pltpu.roll(x, 64, 1)


def along_first(x, coef, base):
    r3, r2 = swap(x[3]), swap(x[2])
    parity = ((x[0] + r3, x[1] + r2), (x[0] - r3, x[1] - r2))
    sums = []
    for s in range(2):
        kept = (parity[s][0], swap(parity[s][0]), parity[s][1], swap(parity[s][1]))
        for c in range(2):
            at = base + 8 * s + 4 * c
            total = coef[at : at + 1] * kept[0]
            for n in range(1, 4):
                total = total + coef[at + n : at + n + 1] * kept[n]
            sums.append(total)
    p0, p1, q0, q1 = sums
    return [p0 + q0, p1 + q1, swap(q1 - p1), swap(q0 - p0)]


def chunks_of(ref, d):
    return jnp.concatenate([ref[d, :, 128 * c : 128 * c + 128] for c in range(4)], 0)


def two_dims(y, m_first, m_second, v_first, v_second, wf1, wf2, wb1, wb2):
    high, low = parts_of(y)
    g = dot(jnp.concatenate([high, low], 1), wf1[...]) + dot(high, wf2[...])
    high1, low1 = parts_of(m_first * g[:, :128] + v_first * y)
    high2, low2 = parts_of(m_second * g[:, 128:] + v_second * y)
    wide = dot(jnp.concatenate([high1, high2], 1), wb1[...])
    low = dot(jnp.concatenate([low1, low2], 1), wb2[...])
    return wide[:, :128] + wide[:, 128:] + low


def factors_of(met, vel, wb1, wb2, coef, q_out, plane_out, end_q, end_mv):
    lane = iota(1)
    left = lane < 64
    for c in range(4):
        at = slice(128 * c, 128 * c + 128)
        w = met[1, :, at] * coef[32:33] + jnp.where(lane % 64 < 8, vel[1, :, at], 0.0)
        high, low = parts_of(w)
        wide = dot(high, wb1[0:128])
        q_out[:, at] = wide[:, :128] + wide[:, 128:] + dot(low, wb2[0:128])

    for n, (ref, d) in enumerate(((met, 0), (met, 2), (vel, 0), (vel, 2))):
        packed = jnp.zeros((E, 128), F32)
        for c in range(4):
            moved = ref[d, :, 128 * c : 128 * c + 128]
            if c:
                moved = pltpu.roll(moved, 16 * c, 1)
            packed = jnp.where((lane // 16) % 4 == c, moved, packed)
        even = jnp.where(left, packed, swap(packed))
        other = jnp.where(left, swap(packed), packed)
        plane_out[n] = jnp.where(lane % 16 < 8, even, pltpu.roll(other, 8, 1))

    small_left = iota(1, (8, 128)) < 64
    for end in range(2):
        rows = slice((E - 8) * end, (E - 8) * end + 8)
        w = []
        for c in range(4):
            at = slice(128 * c, 128 * c + 128)
            spot = 33 + 4 * end + c
            term = met[0, rows, at] * coef[spot : spot + 1]
            if c == 3 * end:
                term = term + jnp.where(small_left != (end == 1), vel[0, rows, at], 0.0)
            w.append(term)
        back = along_first(w, coef, 16)
        for c in range(4):
            end_q[end, c] = back[c]
        at = slice(384 * end, 384 * end + 128)
        for n, (ref, d) in enumerate(((met, 1), (met, 2), (vel, 1), (vel, 2))):
            end_mv[end, n] = ref[d, rows, at]


def main_kernel(fields, x_ref, met, vel, keep_ref, wf, wb1, wb2, coef, out, *refs):
    factors, (wide_x, xs, wide_in) = refs[:-3], refs[-3:]
    lane, row = iota(1), iota(0)
    keep = keep_ref[...]
    left = lane < 64
    if factors:
        factors_of(met, vel, wb1, wb2, coef, *factors)

    tile = 32
    for n, f in enumerate(fields):
        low_faces = pltpu.roll(swap(x_ref[f, :, 0:128] * keep), E - 1, 0)
        high_faces = pltpu.roll(swap(x_ref[f, :, 384:512] * keep), 1, 0)
        low_faces = jnp.where(left | (row == E - 1), 0.0, low_faces)
        high_faces = jnp.where(left & (row > 0), high_faces, 0.0)
        for r in range(0, E, tile):
            rows = slice(r, r + tile)
            x = [x_ref[f, rows, 128 * c : 128 * c + 128] * keep[rows] for c in range(4)]
            x[0] = x[0] + high_faces[rows]
            x[3] = x[3] + low_faces[rows]
            for c in range(4):
                spot = slice(E * c + r, E * c + r + tile)
                high, low = parts_of(x[c])
                xs[n, spot] = x[c]
                wide_x[n, spot, 0:128] = high
                wide_x[n, spot, 128:256] = low
                wide_x[n, spot, 256:384] = high
            g0 = along_first(x, coef, 0)
            inner0 = []
            for c in range(4):
                at = slice(128 * c, 128 * c + 128)
                inner0.append(met[0, rows, at] * g0[c] + vel[0, rows, at] * x[c])
            back = along_first(inner0, coef, 16)
            for c in range(4):
                out[n, rows, 128 * c : 128 * c + 128] = back[c]
        g = dot(wide_x[n], wf[...])
        for c in range(4):
            at = slice(128 * c, 128 * c + 128)
            for r in range(0, E, tile):
                rows = slice(r, r + tile)
                spot = slice(E * c + r, E * c + r + tile)
                x = xs[n, spot]
                high1, low1 = parts_of(met[1, rows, at] * g[spot, 0:128] + vel[1, rows, at] * x)
                high2, low2 = parts_of(met[2, rows, at] * g[spot, 128:256] + vel[2, rows, at] * x)
                wide_in[n, spot, 0:128] = high1
                wide_in[n, spot, 128:256] = high2
                wide_in[n, spot, 256:384] = low1
                wide_in[n, spot, 384:512] = low2
        wide = dot(wide_in[n, :, 0:256], wb1[...])
        low = dot(wide_in[n, :, 256:512], wb2[...])
        for c in range(4):
            at = slice(128 * c, 128 * c + 128)
            for r in range(0, E, tile):
                rows = slice(r, r + tile)
                spot = slice(E * c + r, E * c + r + tile)
                out[n, rows, at] += wide[spot, 0:128] + wide[spot, 128:256] + low[spot]


def keep_kernel(marks, out):
    kept = jnp.where(iota(0) == iota(1), marks[0:1], 0.0).astype(BF16)
    column = dot(kept, jnp.ones((E, 128), BF16))
    out[...] = jnp.where(iota(1) % 64 >= 56, column, 1.0)


def kept_of(marks):
    return pl.pallas_call(
        keep_kernel,
        out_shape=jax.ShapeDtypeStruct((E, 128), F32),
        in_specs=[VM],
        out_specs=VM,
        compiler_params=pltpu.CompilerParams(vmem_limit_bytes=16 * 1024 * 1024),
        cost_estimate=pl.CostEstimate(
            flops=8_000_000_000, bytes_accessed=30_000_000, transcendentals=0
        ),
        name="keep",
    )(marks)


def main_of(adjoint, metric, velocity, keep, tables, fields, factors):
    def body(*refs):
        main_kernel(fields, *refs)

    return pl.pallas_call(
        body,
        out_shape=[
            jax.ShapeDtypeStruct(shape, F32)
            for shape in [(len(fields), E, 512)]
            + [(E, 512), (4, E, 128), (2, 4, 8, 128), (2, 4, 8, 128)] * factors
        ],
        in_specs=[VM] * 8,
        out_specs=[VM] * (5 if factors else 1),
        scratch_shapes=[
            pltpu.VMEM((len(fields), 4 * E, 384), BF16),
            pltpu.VMEM((len(fields), 4 * E, 128), F32),
            pltpu.VMEM((len(fields), 4 * E, 512), BF16),
        ],
        compiler_params=pltpu.CompilerParams(vmem_limit_bytes=LIMIT),
        cost_estimate=pl.CostEstimate(
            flops=800_000_000 * len(fields), bytes_accessed=5_000_000, transcendentals=0
        ),
        name="inner",
    )(
        adjoint, metric, velocity, keep,
        np.concatenate(tables["forward"], 0), *tables["backward"], tables["coef"],
    )


def odd_device():
    index = lax.axis_index("dom") * lax.axis_size("sub") + lax.axis_index("sub")
    return lax.rem(index, 2) == 1


def line_kernel(a, b, own, c, d, edges, inside, across):
    def rows(start):
        return sum(ref[start : start + 16].astype(F32) for ref in (a, b, own, c, d))

    low = [edges[0:3]]
    high = [edges[8:11]]
    for n, (first, last) in enumerate(((0, 112), (128, 240), (256, 304))):
        low.append(pltpu.roll(rows(first)[0:1], 56, 1))
        line = rows(last)[15:16]
        high.append(pltpu.roll(swap(line) if n == 2 else line, 72, 1))
    zero = jnp.zeros((2, 128), F32)
    low = jnp.concatenate(low + [zero], 0)
    high = jnp.concatenate(high + [zero], 0)
    odd = odd_device()
    across[...] = jnp.where(odd, high, low)
    inside[...] = jnp.where(odd, low, high)


def lines_of(parts, edges):
    return pl.pallas_call(
        line_kernel,
        out_shape=[jax.ShapeDtypeStruct((8, 128), F32)] * 2,
        in_specs=[VM] * 6,
        out_specs=[VM] * 2,
        compiler_params=pltpu.CompilerParams(vmem_limit_bytes=LIMIT),
        name="lines",
    )(*parts, edges)


def post_kernel(
    a, b, own, c2, d, across, inside, base_a, base_b, q_ref, plane, end_q, end_mv,
    wf1, wf2, wb1, wb2, spread, place, out_hbm, out, out_sems,
):
    out_copies = [
        pltpu.make_async_copy(out.at[f], out_hbm.at[f], out_sems.at[f]) for f in range(5)
    ]
    lane, row = iota(1), iota(0)
    left = lane < 64

    small_left = iota(1, (1, 128)) < 64
    halo = []
    odd = odd_device()
    before = jnp.where(odd, inside[...], across[...])
    after = jnp.where(odd, across[...], inside[...])
    for got in (before, after):
        rows = []
        for n in range(3):
            pair = got[n : n + 1]
            turned = pltpu.roll(pair, 64, 1)
            rows.append(jnp.where(small_left, pair, turned))
            rows.append(jnp.where(small_left, turned, pair))
        halo.append(jnp.concatenate(rows + [jnp.zeros((2, 128), F32)], 0))
    u = jnp.concatenate(halo, 0)
    faces = []
    for n in range(3):
        rows = slice(128 * n, min(128 * n + 128, 320))
        m = sum(ref[rows].astype(F32) for ref in (a, b, own, c2, d))
        if n == 2:
            m = jnp.concatenate([m, swap(m)], 0)
        low_lines = pltpu.roll(pltpu.roll(m, 56, 1), E - 1, 0)
        high_lines = pltpu.roll(pltpu.roll(m, 72, 1), 1, 0)
        low_lines = jnp.where(row == E - 1, after[3 + n : 4 + n], low_lines)
        high_lines = jnp.where(row == 0, before[3 + n : 4 + n], high_lines)
        y = m + jnp.where(lane % 64 < 8, high_lines, 0.0)
        y = y + jnp.where(lane % 64 >= 56, low_lines, 0.0)
        faces.append(y)
    stacked = jnp.concatenate(faces + [u], 0)
    factors = [
        jnp.concatenate(
            [plane[at]] * 3
            + [
                jnp.broadcast_to(end_mv[0, n, 0:1], (8, 128)),
                jnp.broadcast_to(end_mv[1, n, 7:8], (8, 128)),
            ],
            0,
        )
        for n, at in enumerate((0, 1, 2, 3))
    ]
    r = two_dims(stacked, *factors, wf1, wf2, wb1, wb2)
    ends = r[3 * E :]
    y_parts = jnp.concatenate(parts_of(stacked[: 3 * E]), 1)
    r_parts = jnp.concatenate(parts_of(r[: 3 * E]), 1)
    for n in range(3):
        rows = slice(E * n, E * n + E)
        for f in range(2 * n, min(2 * n + 2, 5)):
            cols = slice(512 * (f - 2 * n), 512 * (f - 2 * n) + 512)
            out[f] = (
                (base_a[f] if f < 2 else base_b[f - 2])
                + q_ref[...] * dot(y_parts[rows], spread[:, cols])
                + dot(r_parts[rows], place[:, cols])
            )
            for c in range(4):
                at = slice(128 * c, 128 * c + 128)
                first = end_q[0, c, 0:1] * halo[0][f : f + 1]
                final = end_q[1, c, 7:8] * halo[1][f : f + 1]
                if c == 0:
                    first = first + jnp.where(small_left, ends[f : f + 1], 0.0)
                if c == 3:
                    final = final + jnp.where(small_left, 0.0, ends[8 + f : 9 + f])
                out[f, 0:1, at] += first
                out[f, E - 1 : E, at] += final
            out_copies[f].start()
    for copy in out_copies:
        copy.wait()


def post_of(parts, across, inside, local, tables):
    return pl.pallas_call(
        post_kernel,
        out_shape=jax.ShapeDtypeStruct((5, E, 512), F32),
        in_specs=[VM] * 19,
        out_specs=HBM,
        scratch_shapes=[pltpu.VMEM((5, E, 512), F32), pltpu.SemaphoreType.DMA((5,))],
        compiler_params=pltpu.CompilerParams(vmem_limit_bytes=LIMIT),
        name="outer",
    )(
        *parts, across, inside, *local, *tables["forward"], *tables["backward"],
        tables["spread"], tables["place"],
    )


def shards(adjoint_field, metric, velocity, mortar_route, mortar_element, face_code, hanging):
    tables = constants()
    peers = lax.axis_size("dom")
    adjoint = jnp.transpose(adjoint_field, (1, 0, 2))
    met = jnp.transpose(metric, (1, 0, 2))
    vel = jnp.transpose(velocity, (1, 0, 2))
    route, target, code, hang = (
        x.reshape(1, E) for x in (mortar_route, mortar_element, face_code, hanging)
    )
    *parts, edges, marks = folded_of(route, target, code, hang, adjoint, tables["fold"])
    for n in (0, 1, 3, 4):
        pairs = [(i, (i + ORDER[n] - 2) % peers) for i in range(peers)]
        parts[n] = lax.ppermute(parts[n], "dom", pairs)
    kept = kept_of(marks)
    early, *factors = main_of(adjoint, met, vel, kept, tables, (0, 1), True)
    parts, early = lax.optimization_barrier((parts, early))
    lines = lines_of(parts, edges)
    (out_b, out_a), kept = lax.optimization_barrier((lines, kept))
    axes = ("dom", "sub")
    count = lax.axis_size(axes)
    inside = [(i, i ^ 1) for i in range(count)]
    across = [(i, i + 1 if i % 2 else i - 1) for i in range(1, count - 1)]
    inward = lax.ppermute(out_b, axes, inside)
    outward = lax.ppermute(out_a, axes, across)
    (late,) = main_of(adjoint, met, vel, kept, tables, (2, 3, 4), False)
    result = post_of(parts, outward, inward, (early, late, *factors), tables)
    return jnp.transpose(result, (1, 0, 2))


def solution(mesh):
    block = P(("dom", "sub"), None, None)
    flat = P(("dom", "sub"), None)
    return jax.shard_map(
        shards,
        mesh=mesh,
        in_specs=(block, block, block, flat, flat, flat, flat),
        out_specs=block,
        check_vma=False,
    )
```

```python
import jax
import jax.numpy as jnp
import ml_dtypes
import numpy as np
from jax import lax
from jax.experimental import pallas as pl
from jax.experimental.pallas import tpu as pltpu
from jax.sharding import PartitionSpec as P

gll_nodes = np.array(
    [
        -1.0,
        -0.8717401485096066,
        -0.5917001814331423,
        -0.2092992179024789,
        0.2092992179024789,
        0.5917001814331423,
        0.8717401485096066,
        1.0,
    ]
)
viscosity = 0.005
F32, BF16 = jnp.float32, jnp.bfloat16
E = 128
HBM = pl.BlockSpec(memory_space=pltpu.HBM)
VM = pl.BlockSpec(memory_space=pltpu.VMEM)
LIMIT = 32 * 1024 * 1024
ORDER = (3, 4, 2, 1, 0)
WHOLE = 64 * 1024 * 1024


def legendre_seven(points):
    prev = np.ones(points.shape)
    curr = np.array(points)
    for order in range(1, 7):
        nxt = ((2 * order + 1) * points * curr - order * prev) / (order + 1)
        prev, curr = (curr, nxt)
    return curr


def diff_matrix():
    values = legendre_seven(gll_nodes)
    result_mat = np.zeros((8, 8))
    for row in range(8):
        for col in range(8):
            if row != col:
                result_mat[row, col] = values[row] / (
                    values[col] * (gll_nodes[row] - gll_nodes[col])
                )
    result_mat[0, 0] = -14.0
    result_mat[7, 7] = 14.0
    return result_mat


def lagrange_at(points):
    basis = np.ones((8, 8))
    for row in range(8):
        for col in range(8):
            for other in range(8):
                if other != col:
                    basis[row, col] *= (points[row] - gll_nodes[other]) / (
                        gll_nodes[col] - gll_nodes[other]
                    )
    return basis


def face_tables():
    halves = [lagrange_at((gll_nodes - 1.0) / 2.0), lagrange_at((gll_nodes + 1.0) / 2.0)]
    perm_mat = np.zeros((64, 64))
    for col in range(64):
        perm_mat[col % 8 * 8 + col // 8, col] = 1.0
    tables = []
    for code in range(8):
        mat = np.kron(halves[code % 2], halves[code // 2 % 2])
        if code >= 4:
            mat = mat @ perm_mat
        tables.append(mat)
    return np.stack(tables)


def two_parts(mat):
    high = mat.astype(ml_dtypes.bfloat16)
    low = (mat - high.astype(np.float64)).astype(ml_dtypes.bfloat16)
    return high, low


def constants():
    dmat = diff_matrix()
    eye = np.eye(8)
    along_j = np.kron(np.eye(2), np.kron(dmat, eye))
    along_k = np.kron(np.eye(16), dmat)

    def forward(first, second):
        fh, fl = two_parts(viscosity * first.T)
        sh, sl = two_parts(viscosity * second.T)
        top = np.concatenate([fh, sh], 1)
        return np.concatenate([top, top], 0), np.concatenate([fl, sl], 1)

    def backward(first, second):
        fh, fl = two_parts(first)
        sh, sl = two_parts(second)
        return (
            np.concatenate([np.concatenate([fh, fl], 1), np.concatenate([sh, sl], 1)], 0),
            np.concatenate([fh, sh], 0),
        )

    def split_parity(mat):
        vectors = []
        for sign in (1.0, -1.0):
            small = (mat[:4, :4] + sign * mat[:4, ::-1][:, :4]) / 2
            for c in range(2):
                for other in range(2):
                    for swap in (0, 1):
                        vectors.append(
                            np.concatenate(
                                [
                                    np.full(64, small[2 * c + h, 2 * other + (h ^ swap)])
                                    for h in range(2)
                                ]
                            )
                        )
        return np.stack(vectors)

    coef = np.concatenate([split_parity(viscosity * dmat), split_parity(dmat.T)], 0)
    column = np.tile(np.repeat(viscosity * dmat[:, 0], 8), 2)[None]
    ends = [
        np.repeat(viscosity * dmat[2 * c : 2 * c + 2, end], 64)[None]
        for end in (0, 7)
        for c in range(4)
    ]
    coef = np.concatenate([coef, column, *ends, np.zeros((7, 128))], 0).astype(np.float32)

    tables = face_tables()
    fold = np.zeros((256, 512), ml_dtypes.bfloat16)
    for code in range(8):
        high, low = two_parts(tables[code])
        for i in range(8):
            for k in range(8):
                c, h = i // 2, i % 2
                spot = (56 + 64 * h + 16 * c + k) % 128
                cols = slice(64 * code, 64 * code + 64)
                fold[spot, cols] = high[8 * i + k]
                fold[(spot + 8) % 128, cols] = high[8 * i + k]
                fold[128 + spot, cols] = low[8 * i + k]

    spread = np.zeros((64, 512))
    place = np.zeros((64, 512))
    for i in range(8):
        for k in range(8):
            place[8 * i + k, 64 * i + k] = 1.0
            for j in range(8):
                spread[8 * i + k, 64 * i + 8 * j + k] = 1.0
    zero = np.zeros((64, 512))

    def pair(mat):
        one = np.concatenate(
            [np.concatenate([mat, zero], 1), np.concatenate([zero, mat], 1)], 0
        )
        return np.concatenate([one, one], 0).astype(ml_dtypes.bfloat16)

    return {
        "fold": fold,
        "forward": forward(along_j, along_k),
        "backward": backward(along_j, along_k),
        "spread": pair(spread),
        "place": pair(place),
        "coef": coef,
    }


def iota(dim, shape=(E, 128)):
    return lax.broadcasted_iota(jnp.int32, shape, dim)


def down(row):
    spots = jnp.where(iota(0) == iota(1), row, 0).astype(F32).astype(BF16)
    return jnp.dot(spots, jnp.ones((E, 128), BF16), preferred_element_type=F32)


def dot(a, b):
    return jnp.dot(a, b, preferred_element_type=F32)


def parts_of(x):
    high = x.astype(BF16)
    return high, (x - high.astype(F32)).astype(BF16)


def fetch(pairs, sems):
    copies = [
        pltpu.make_async_copy(src, dst, sems.at[n]) for n, (src, dst) in enumerate(pairs)
    ]
    for copy in copies:
        copy.start()
    return copies


def fold_kernel(
    route_hbm, target_hbm, code_hbm, hang_hbm, adj_hbm, fold_hbm, *refs
):
    outs, edges_out, marks_out, ints, x, fold, faces, sems = refs[:5], *refs[5:]
    peers = lax.axis_size("dom")
    copies = fetch(
        [(ref, ints.at[n]) for n, ref in enumerate((route_hbm, target_hbm, code_hbm, hang_hbm))]
        + [(adj_hbm.at[f], x.at[f]) for f in range(5)]
        + [(fold_hbm, fold)],
        sems,
    )
    for copy in copies:
        copy.wait()
    route, target, code, hang = (ints[n] for n in range(4))
    lane = iota(1)
    left = lane < 64
    slot = lax.rem(route - lax.axis_index("dom") + 2 + peers, peers)
    hit = (iota(0, (5 * E, E)) == slot * E + target).astype(F32).astype(BF16)
    marked = down(jnp.where(hang == 1, code, -2)) - (lane // 64).astype(F32)
    odd = lane % 16 >= 8
    group = (lane // 16 + 1) % 4
    def field(f, carry):
        packed = jnp.zeros((E, 128), F32)
        for c in range(4):
            moved = x[f, :, 128 * c : 128 * c + 128]
            if c:
                moved = pltpu.roll(moved, 16 * c, 1)
            packed = jnp.where(odd & (group == c), moved, packed)
        high = packed.astype(BF16)
        high_f = high.astype(F32)
        both = jnp.where(odd, high_f, pltpu.roll(packed - high_f, 8, 1)).astype(BF16)
        mapped = dot(jnp.concatenate([both, high], 1), fold[...])
        total = jnp.zeros((E, 128), F32)
        for q in range(4):
            total = total + jnp.where(
                marked == 2.0 * q, mapped[:, 128 * q : 128 * q + 128], 0.0
            )
        faces[f] = total + pltpu.roll(total, 64, 1)
        return carry

    lax.fori_loop(0, 5, field, 0)
    f01 = jnp.where(left, faces[0], faces[1]).astype(BF16)
    f23 = jnp.where(left, faces[2], faces[3]).astype(BF16)
    sums = dot(hit, jnp.concatenate([f01, f23, faces[4].astype(BF16)], 1))
    for ref, o in zip(outs, ORDER):
        mine = sums[o * E : o * E + E]
        last = jnp.where(left[:64], mine[:64, 256:384], mine[64:, 256:384])
        ref[0:128] = mine[:, 0:128].astype(ref.dtype)
        ref[128:256] = mine[:, 128:256].astype(ref.dtype)
        ref[256:320] = last.astype(ref.dtype)

    marks_out[...] = jnp.broadcast_to(1.0 - hang.astype(F32), (8, E))
    lane = iota(1, (1, 128))
    own = marked[0:1], marked[E - 1 : E]
    edges_out[...] = jnp.zeros((16, 128), F32)
    for n in range(3):
        first, second = 2 * n, min(2 * n + 1, 4)
        for end, (at, chunk) in enumerate(((0, 0), (E - 1, 3))):
            a = x[first, at : at + 1, 128 * chunk : 128 * chunk + 128]
            b = x[second, at : at + 1, 128 * chunk : 128 * chunk + 128]
            if end == 0:
                b = pltpu.roll(b, 64, 1)
            else:
                a = pltpu.roll(a, 64, 1)
            keep = jnp.where((lane % 64 >= 56) & (own[end] >= -1.5), 0.0, 1.0)
            spot = 8 * end + n
            edges_out[spot : spot + 1] = jnp.where(lane < 64, a, b) * keep


def folded_of(route, target, code, hang, adjoint, fold):
    return pl.pallas_call(
        fold_kernel,
        out_shape=[
            jax.ShapeDtypeStruct((320, 128), F32 if o == 2 else BF16) for o in range(5)
        ]
        + [jax.ShapeDtypeStruct((16, 128), F32), jax.ShapeDtypeStruct((8, 128), F32)],
        in_specs=[HBM] * 6,
        out_specs=[VM] * 7,
        scratch_shapes=[
            pltpu.VMEM((4, 1, E), jnp.int32),
            pltpu.VMEM((5, E, 512), F32),
            pltpu.VMEM((256, 512), BF16),
            pltpu.VMEM((5, E, 128), F32),
            pltpu.SemaphoreType.DMA((10,)),
        ],
        compiler_params=pltpu.CompilerParams(vmem_limit_bytes=WHOLE),
        name="fold",
    )(route, target, code, hang, adjoint, fold)


def swap(x):
    return pltpu.roll(x, 64, 1)


def along_first(x, coef, base):
    r3, r2 = swap(x[3]), swap(x[2])
    parity = ((x[0] + r3, x[1] + r2), (x[0] - r3, x[1] - r2))
    sums = []
    for s in range(2):
        kept = (parity[s][0], swap(parity[s][0]), parity[s][1], swap(parity[s][1]))
        for c in range(2):
            at = base + 8 * s + 4 * c
            total = coef[at : at + 1] * kept[0]
            for n in range(1, 4):
                total = total + coef[at + n : at + n + 1] * kept[n]
            sums.append(total)
    p0, p1, q0, q1 = sums
    return [p0 + q0, p1 + q1, swap(q1 - p1), swap(q0 - p0)]


def chunks_of(ref, d):
    return jnp.concatenate([ref[d, :, 128 * c : 128 * c + 128] for c in range(4)], 0)


def two_dims(y, m_first, m_second, v_first, v_second, wf1, wf2, wb1, wb2):
    high, low = parts_of(y)
    g = dot(jnp.concatenate([high, low], 1), wf1[...]) + dot(high, wf2[...])
    high1, low1 = parts_of(m_first * g[:, :128] + v_first * y)
    high2, low2 = parts_of(m_second * g[:, 128:] + v_second * y)
    wide = dot(jnp.concatenate([high1, high2], 1), wb1[...])
    low = dot(jnp.concatenate([low1, low2], 1), wb2[...])
    return wide[:, :128] + wide[:, 128:] + low


def factors_of(met, vel, wb1, wb2, coef, q_out, plane_out, end_q, end_mv):
    lane = iota(1)
    left = lane < 64
    for c in range(4):
        at = slice(128 * c, 128 * c + 128)
        w = met[1, :, at] * coef[32:33] + jnp.where(lane % 64 < 8, vel[1, :, at], 0.0)
        high, low = parts_of(w)
        wide = dot(high, wb1[0:128])
        q_out[:, at] = wide[:, :128] + wide[:, 128:] + dot(low, wb2[0:128])

    for n, (ref, d) in enumerate(((met, 0), (met, 2), (vel, 0), (vel, 2))):
        packed = jnp.zeros((E, 128), F32)
        for c in range(4):
            moved = ref[d, :, 128 * c : 128 * c + 128]
            if c:
                moved = pltpu.roll(moved, 16 * c, 1)
            packed = jnp.where((lane // 16) % 4 == c, moved, packed)
        even = jnp.where(left, packed, swap(packed))
        other = jnp.where(left, swap(packed), packed)
        plane_out[n] = jnp.where(lane % 16 < 8, even, pltpu.roll(other, 8, 1))

    small_left = iota(1, (8, 128)) < 64
    for end in range(2):
        rows = slice((E - 8) * end, (E - 8) * end + 8)
        w = []
        for c in range(4):
            at = slice(128 * c, 128 * c + 128)
            spot = 33 + 4 * end + c
            term = met[0, rows, at] * coef[spot : spot + 1]
            if c == 3 * end:
                term = term + jnp.where(small_left != (end == 1), vel[0, rows, at], 0.0)
            w.append(term)
        back = along_first(w, coef, 16)
        for c in range(4):
            end_q[end, c] = back[c]
        at = slice(384 * end, 384 * end + 128)
        for n, (ref, d) in enumerate(((met, 1), (met, 2), (vel, 1), (vel, 2))):
            end_mv[end, n] = ref[d, rows, at]


def main_kernel(fields, x_ref, met, vel, keep_ref, wf1, wf2, wb1, wb2, coef, out, *factors):
    lane, row = iota(1), iota(0)
    keep = keep_ref[...]
    left = lane < 64
    if factors:
        factors_of(met, vel, wb1, wb2, coef, *factors)

    def field(n, carry):
        f = n + fields[0]
        x = [x_ref[f, :, 128 * c : 128 * c + 128] * keep for c in range(4)]
        low_faces = pltpu.roll(swap(x[0]), E - 1, 0)
        high_faces = pltpu.roll(swap(x[3]), 1, 0)
        x[0] = x[0] + jnp.where(left & (row > 0), high_faces, 0.0)
        x[3] = x[3] + jnp.where(left | (row == E - 1), 0.0, low_faces)
        stacked = jnp.concatenate(x, 0)
        rest = two_dims(
            stacked, chunks_of(met, 1), chunks_of(met, 2), chunks_of(vel, 1), chunks_of(vel, 2),
            wf1, wf2, wb1, wb2,
        )
        g0 = along_first(x, coef, 0)
        inner0 = []
        for c in range(4):
            at = slice(128 * c, 128 * c + 128)
            inner0.append(met[0, :, at] * g0[c] + vel[0, :, at] * x[c])
        back = along_first(inner0, coef, 16)
        for c in range(4):
            out[n, :, 128 * c : 128 * c + 128] = rest[E * c : E * c + E] + back[c]
        return carry

    lax.fori_loop(0, len(fields), field, 0)


def keep_kernel(marks, out):
    kept = jnp.where(iota(0) == iota(1), marks[0:1], 0.0).astype(BF16)
    column = dot(kept, jnp.ones((E, 128), BF16))
    out[...] = jnp.where(iota(1) % 64 >= 56, column, 1.0)


def kept_of(marks):
    return pl.pallas_call(
        keep_kernel,
        out_shape=jax.ShapeDtypeStruct((E, 128), F32),
        in_specs=[VM],
        out_specs=VM,
        compiler_params=pltpu.CompilerParams(vmem_limit_bytes=16 * 1024 * 1024),
        cost_estimate=pl.CostEstimate(
            flops=8_000_000_000, bytes_accessed=30_000_000, transcendentals=0
        ),
        name="keep",
    )(marks)


def main_of(adjoint, metric, velocity, keep, tables, fields, factors):
    def body(*refs):
        main_kernel(fields, *refs)

    return pl.pallas_call(
        body,
        out_shape=[
            jax.ShapeDtypeStruct(shape, F32)
            for shape in [(len(fields), E, 512)]
            + [(E, 512), (4, E, 128), (2, 4, 8, 128), (2, 4, 8, 128)] * factors
        ],
        in_specs=[VM] * 9,
        out_specs=[VM] * (5 if factors else 1),
        compiler_params=pltpu.CompilerParams(vmem_limit_bytes=LIMIT),
        cost_estimate=pl.CostEstimate(
            flops=800_000_000 * len(fields), bytes_accessed=5_000_000, transcendentals=0
        ),
        name="inner",
    )(
        adjoint, metric, velocity, keep,
        *tables["forward"], *tables["backward"], tables["coef"],
    )


def odd_device():
    index = lax.axis_index("dom") * lax.axis_size("sub") + lax.axis_index("sub")
    return lax.rem(index, 2) == 1


def line_kernel(a, b, own, c, d, edges, inside, across):
    def rows(start):
        return sum(ref[start : start + 16].astype(F32) for ref in (a, b, own, c, d))

    low = [edges[0:3]]
    high = [edges[8:11]]
    for n, (first, last) in enumerate(((0, 112), (128, 240), (256, 304))):
        low.append(pltpu.roll(rows(first)[0:1], 56, 1))
        line = rows(last)[15:16]
        high.append(pltpu.roll(swap(line) if n == 2 else line, 72, 1))
    zero = jnp.zeros((2, 128), F32)
    low = jnp.concatenate(low + [zero], 0)
    high = jnp.concatenate(high + [zero], 0)
    odd = odd_device()
    across[...] = jnp.where(odd, high, low)
    inside[...] = jnp.where(odd, low, high)


def lines_of(parts, edges):
    return pl.pallas_call(
        line_kernel,
        out_shape=[jax.ShapeDtypeStruct((8, 128), F32)] * 2,
        in_specs=[VM] * 6,
        out_specs=[VM] * 2,
        compiler_params=pltpu.CompilerParams(vmem_limit_bytes=LIMIT),
        name="lines",
    )(*parts, edges)


def post_kernel(
    a, b, own, c2, d, across, inside, base_a, base_b, q_ref, plane, end_q, end_mv,
    wf1, wf2, wb1, wb2, spread, place, out_hbm, out, out_sems, y_parts, r_parts, rows_of,
):
    out_copies = [
        pltpu.make_async_copy(out.at[f], out_hbm.at[f], out_sems.at[f]) for f in range(5)
    ]
    lane, row = iota(1), iota(0)
    left = lane < 64

    small_left = iota(1, (1, 128)) < 64
    halo = []
    odd = odd_device()
    before = jnp.where(odd, inside[...], across[...])
    after = jnp.where(odd, across[...], inside[...])
    for got in (before, after):
        rows = []
        for n in range(3):
            pair = got[n : n + 1]
            turned = pltpu.roll(pair, 64, 1)
            rows.append(jnp.where(small_left, pair, turned))
            rows.append(jnp.where(small_left, turned, pair))
        halo.append(jnp.concatenate(rows + [jnp.zeros((2, 128), F32)], 0))
    u = jnp.concatenate(halo, 0)
    faces = []
    for n in range(3):
        rows = slice(128 * n, min(128 * n + 128, 320))
        m = sum(ref[rows].astype(F32) for ref in (a, b, own, c2, d))
        if n == 2:
            m = jnp.concatenate([m, swap(m)], 0)
        low_lines = pltpu.roll(pltpu.roll(m, 56, 1), E - 1, 0)
        high_lines = pltpu.roll(pltpu.roll(m, 72, 1), 1, 0)
        low_lines = jnp.where(row == E - 1, after[3 + n : 4 + n], low_lines)
        high_lines = jnp.where(row == 0, before[3 + n : 4 + n], high_lines)
        y = m + jnp.where(lane % 64 < 8, high_lines, 0.0)
        y = y + jnp.where(lane % 64 >= 56, low_lines, 0.0)
        faces.append(y)
    stacked = jnp.concatenate(faces + [u], 0)
    factors = [
        jnp.concatenate(
            [plane[at]] * 3
            + [
                jnp.broadcast_to(end_mv[0, n, 0:1], (8, 128)),
                jnp.broadcast_to(end_mv[1, n, 7:8], (8, 128)),
            ],
            0,
        )
        for n, at in enumerate((0, 1, 2, 3))
    ]
    r = two_dims(stacked, *factors, wf1, wf2, wb1, wb2)
    ends = r[3 * E :]
    y_parts[...] = jnp.concatenate(parts_of(stacked[: 3 * E]), 1)
    r_parts[...] = jnp.concatenate(parts_of(r[: 3 * E]), 1)
    rows_of[0], rows_of[1] = halo
    rows_of[2], rows_of[3] = ends[0:8], ends[8:16]

    def field(base, first_field, n):
        f = first_field + n
        rows = pl.ds(pl.multiple_of(E * lax.div(f, 2), E), E)
        cols = pl.ds(pl.multiple_of(512 * lax.rem(f, 2), 512), 512)
        out[f] = (
            base[n]
            + q_ref[...] * dot(y_parts[rows], spread[:, cols])
            + dot(r_parts[rows], place[:, cols])
        )
        low, high, low_end, high_end = (rows_of[t, pl.ds(f, 1)] for t in range(4))
        for c in range(4):
            at = slice(128 * c, 128 * c + 128)
            first = end_q[0, c, 0:1] * low
            final = end_q[1, c, 7:8] * high
            if c == 0:
                first = first + jnp.where(small_left, low_end, 0.0)
            if c == 3:
                final = final + jnp.where(small_left, 0.0, high_end)
            out[f, 0:1, at] += first
            out[f, E - 1 : E, at] += final
        pltpu.make_async_copy(out.at[f], out_hbm.at[f], out_sems.at[f]).start()

    for base, first_field, count in ((base_a, 0, 2), (base_b, 2, 3)):

        def step(n, carry, base=base, first_field=first_field):
            field(base, first_field, n)
            return carry

        lax.fori_loop(0, count, step, 0)
    for copy in out_copies:
        copy.wait()


def post_of(parts, across, inside, local, tables):
    return pl.pallas_call(
        post_kernel,
        out_shape=jax.ShapeDtypeStruct((5, E, 512), F32),
        in_specs=[VM] * 19,
        out_specs=HBM,
        scratch_shapes=[
            pltpu.VMEM((5, E, 512), F32),
            pltpu.SemaphoreType.DMA((5,)),
            pltpu.VMEM((3 * E, 256), BF16),
            pltpu.VMEM((3 * E, 256), BF16),
            pltpu.VMEM((4, 8, 128), F32),
        ],
        compiler_params=pltpu.CompilerParams(vmem_limit_bytes=LIMIT),
        name="outer",
    )(
        *parts, across, inside, *local, *tables["forward"], *tables["backward"],
        tables["spread"], tables["place"],
    )


def shards(adjoint_field, metric, velocity, mortar_route, mortar_element, face_code, hanging):
    tables = constants()
    peers = lax.axis_size("dom")
    adjoint = jnp.transpose(adjoint_field, (1, 0, 2))
    met = jnp.transpose(metric, (1, 0, 2))
    vel = jnp.transpose(velocity, (1, 0, 2))
    route, target, code, hang = (
        x.reshape(1, E) for x in (mortar_route, mortar_element, face_code, hanging)
    )
    *parts, edges, marks = folded_of(route, target, code, hang, adjoint, tables["fold"])
    for n in (0, 1, 3, 4):
        pairs = [(i, (i + ORDER[n] - 2) % peers) for i in range(peers)]
        parts[n] = lax.ppermute(parts[n], "dom", pairs)
    kept = kept_of(marks)
    early, *factors = main_of(adjoint, met, vel, kept, tables, (0, 1), True)
    parts, early = lax.optimization_barrier((parts, early))
    lines = lines_of(parts, edges)
    (out_b, out_a), kept = lax.optimization_barrier((lines, kept))
    axes = ("dom", "sub")
    count = lax.axis_size(axes)
    inside = [(i, i ^ 1) for i in range(count)]
    across = [(i, i + 1 if i % 2 else i - 1) for i in range(1, count - 1)]
    inward = lax.ppermute(out_b, axes, inside)
    outward = lax.ppermute(out_a, axes, across)
    (late,) = main_of(adjoint, met, vel, kept, tables, (2, 3, 4), False)
    result = post_of(parts, outward, inward, (early, late, *factors), tables)
    return jnp.transpose(result, (1, 0, 2))


def solution(mesh):
    block = P(("dom", "sub"), None, None)
    flat = P(("dom", "sub"), None)
    return jax.shard_map(
        shards,
        mesh=mesh,
        in_specs=(block, block, block, flat, flat, flat, flat),
        out_specs=block,
        check_vma=False,
    )
```

```python
import jax
import jax.numpy as jnp
import ml_dtypes
import numpy as np
from jax import lax
from jax.experimental import pallas as pl
from jax.experimental.pallas import tpu as pltpu
from jax.sharding import PartitionSpec as P

gll_nodes = np.array(
    [
        -1.0,
        -0.8717401485096066,
        -0.5917001814331423,
        -0.2092992179024789,
        0.2092992179024789,
        0.5917001814331423,
        0.8717401485096066,
        1.0,
    ]
)
viscosity = 0.005
F32, BF16 = jnp.float32, jnp.bfloat16
E = 128
HBM = pl.BlockSpec(memory_space=pltpu.HBM)
VM = pl.BlockSpec(memory_space=pltpu.VMEM)
LIMIT = 32 * 1024 * 1024
ORDER = (3, 4, 2, 1, 0)
WHOLE = 64 * 1024 * 1024


def legendre_seven(points):
    prev = np.ones(points.shape)
    curr = np.array(points)
    for order in range(1, 7):
        nxt = ((2 * order + 1) * points * curr - order * prev) / (order + 1)
        prev, curr = (curr, nxt)
    return curr


def diff_matrix():
    values = legendre_seven(gll_nodes)
    result_mat = np.zeros((8, 8))
    for row in range(8):
        for col in range(8):
            if row != col:
                result_mat[row, col] = values[row] / (
                    values[col] * (gll_nodes[row] - gll_nodes[col])
                )
    result_mat[0, 0] = -14.0
    result_mat[7, 7] = 14.0
    return result_mat


def lagrange_at(points):
    basis = np.ones((8, 8))
    for row in range(8):
        for col in range(8):
            for other in range(8):
                if other != col:
                    basis[row, col] *= (points[row] - gll_nodes[other]) / (
                        gll_nodes[col] - gll_nodes[other]
                    )
    return basis


def face_tables():
    halves = [lagrange_at((gll_nodes - 1.0) / 2.0), lagrange_at((gll_nodes + 1.0) / 2.0)]
    perm_mat = np.zeros((64, 64))
    for col in range(64):
        perm_mat[col % 8 * 8 + col // 8, col] = 1.0
    tables = []
    for code in range(8):
        mat = np.kron(halves[code % 2], halves[code // 2 % 2])
        if code >= 4:
            mat = mat @ perm_mat
        tables.append(mat)
    return np.stack(tables)


def two_parts(mat):
    high = mat.astype(ml_dtypes.bfloat16)
    low = (mat - high.astype(np.float64)).astype(ml_dtypes.bfloat16)
    return high, low


def constants():
    dmat = diff_matrix()
    eye = np.eye(8)
    along_j = np.kron(np.eye(2), np.kron(dmat, eye))
    along_k = np.kron(np.eye(16), dmat)

    def forward(first, second):
        fh, fl = two_parts(viscosity * first.T)
        sh, sl = two_parts(viscosity * second.T)
        top = np.concatenate([fh, sh], 1)
        return np.concatenate([top, top], 0), np.concatenate([fl, sl], 1)

    def backward(first, second):
        fh, fl = two_parts(first)
        sh, sl = two_parts(second)
        return (
            np.concatenate([np.concatenate([fh, fl], 1), np.concatenate([sh, sl], 1)], 0),
            np.concatenate([fh, sh], 0),
        )

    def split_parity(mat):
        vectors = []
        for sign in (1.0, -1.0):
            small = (mat[:4, :4] + sign * mat[:4, ::-1][:, :4]) / 2
            for c in range(2):
                for other in range(2):
                    for swap in (0, 1):
                        vectors.append(
                            np.concatenate(
                                [
                                    np.full(64, small[2 * c + h, 2 * other + (h ^ swap)])
                                    for h in range(2)
                                ]
                            )
                        )
        return np.stack(vectors)

    coef = np.concatenate([split_parity(viscosity * dmat), split_parity(dmat.T)], 0)
    column = np.tile(np.repeat(viscosity * dmat[:, 0], 8), 2)[None]
    ends = [
        np.repeat(viscosity * dmat[2 * c : 2 * c + 2, end], 64)[None]
        for end in (0, 7)
        for c in range(4)
    ]
    coef = np.concatenate([coef, column, *ends, np.zeros((7, 128))], 0).astype(np.float32)

    tables = face_tables()
    fold = np.zeros((256, 512), ml_dtypes.bfloat16)
    for code in range(8):
        high, low = two_parts(tables[code])
        for i in range(8):
            for k in range(8):
                c, h = i // 2, i % 2
                spot = (56 + 64 * h + 16 * c + k) % 128
                cols = slice(64 * code, 64 * code + 64)
                fold[spot, cols] = high[8 * i + k]
                fold[(spot + 8) % 128, cols] = high[8 * i + k]
                fold[128 + spot, cols] = low[8 * i + k]

    spread = np.zeros((64, 512))
    place = np.zeros((64, 512))
    for i in range(8):
        for k in range(8):
            place[8 * i + k, 64 * i + k] = 1.0
            for j in range(8):
                spread[8 * i + k, 64 * i + 8 * j + k] = 1.0
    zero = np.zeros((64, 512))

    def pair(mat):
        one = np.concatenate(
            [np.concatenate([mat, zero], 1), np.concatenate([zero, mat], 1)], 0
        )
        return np.concatenate([one, one], 0).astype(ml_dtypes.bfloat16)

    return {
        "fold": fold,
        "forward": forward(along_j, along_k),
        "backward": backward(along_j, along_k),
        "spread": pair(spread),
        "place": pair(place),
        "coef": coef,
    }


def iota(dim, shape=(E, 128)):
    return lax.broadcasted_iota(jnp.int32, shape, dim)


def down(row):
    spots = jnp.where(iota(0) == iota(1), row, 0).astype(F32).astype(BF16)
    return jnp.dot(spots, jnp.ones((E, 128), BF16), preferred_element_type=F32)


def dot(a, b):
    return jnp.dot(a, b, preferred_element_type=F32)


def parts_of(x):
    high = x.astype(BF16)
    return high, (x - high.astype(F32)).astype(BF16)


def fetch(pairs, sems):
    copies = [
        pltpu.make_async_copy(src, dst, sems.at[n]) for n, (src, dst) in enumerate(pairs)
    ]
    for copy in copies:
        copy.start()
    return copies


def fold_kernel(
    route_hbm, target_hbm, code_hbm, hang_hbm, adj_hbm, fold_hbm, *refs
):
    outs, edges_out, marks_out, ints, x, fold, wide, sems = refs[:5], *refs[5:]
    peers = lax.axis_size("dom")
    copies = fetch(
        [(ref, ints.at[n]) for n, ref in enumerate((route_hbm, target_hbm, code_hbm, hang_hbm))]
        + [(adj_hbm.at[f], x.at[f]) for f in range(5)]
        + [(fold_hbm, fold)],
        sems,
    )
    for copy in copies:
        copy.wait()
    route, target, code, hang = (ints[n] for n in range(4))
    lane = iota(1)
    left = lane < 64
    slot = lax.rem(route - lax.axis_index("dom") + 2 + peers, peers)
    hit = (iota(0, (5 * E, E)) == slot * E + target).astype(F32).astype(BF16)
    marked = down(jnp.where(hang == 1, code, -2)) - (lane // 64).astype(F32)
    odd = lane % 16 >= 8
    group = (lane // 16 + 1) % 4
    for f in range(5):
        packed = jnp.zeros((E, 128), F32)
        for c in range(4):
            moved = x[f, :, 128 * c : 128 * c + 128]
            if c:
                moved = pltpu.roll(moved, 16 * c, 1)
            packed = jnp.where(odd & (group == c), moved, packed)
        high = packed.astype(BF16)
        high_f = high.astype(F32)
        both = jnp.where(odd, high_f, pltpu.roll(packed - high_f, 8, 1)).astype(BF16)
        wide[E * f : E * f + E, 0:128] = both
        wide[E * f : E * f + E, 128:256] = high
    mapped = dot(wide[...], fold[...])
    faces = []
    for f in range(5):
        total = jnp.zeros((E, 128), F32)
        for q in range(4):
            total = total + jnp.where(
                marked == 2.0 * q, mapped[E * f : E * f + E, 128 * q : 128 * q + 128], 0.0
            )
        faces.append(total + pltpu.roll(total, 64, 1))
    f01 = jnp.where(left, faces[0], faces[1]).astype(BF16)
    f23 = jnp.where(left, faces[2], faces[3]).astype(BF16)
    sums = dot(hit, jnp.concatenate([f01, f23, faces[4].astype(BF16)], 1))
    for ref, o in zip(outs, ORDER):
        mine = sums[o * E : o * E + E]
        last = jnp.where(left[:64], mine[:64, 256:384], mine[64:, 256:384])
        ref[0:128] = mine[:, 0:128].astype(ref.dtype)
        ref[128:256] = mine[:, 128:256].astype(ref.dtype)
        ref[256:320] = last.astype(ref.dtype)

    marks_out[...] = jnp.broadcast_to(1.0 - hang.astype(F32), (8, E))
    lane = iota(1, (1, 128))
    own = marked[0:1], marked[E - 1 : E]
    edges_out[...] = jnp.zeros((16, 128), F32)
    for n in range(3):
        first, second = 2 * n, min(2 * n + 1, 4)
        for end, (at, chunk) in enumerate(((0, 0), (E - 1, 3))):
            a = x[first, at : at + 1, 128 * chunk : 128 * chunk + 128]
            b = x[second, at : at + 1, 128 * chunk : 128 * chunk + 128]
            if end == 0:
                b = pltpu.roll(b, 64, 1)
            else:
                a = pltpu.roll(a, 64, 1)
            keep = jnp.where((lane % 64 >= 56) & (own[end] >= -1.5), 0.0, 1.0)
            spot = 8 * end + n
            edges_out[spot : spot + 1] = jnp.where(lane < 64, a, b) * keep


def folded_of(route, target, code, hang, adjoint, fold):
    return pl.pallas_call(
        fold_kernel,
        out_shape=[
            jax.ShapeDtypeStruct((320, 128), F32 if o == 2 else BF16) for o in range(5)
        ]
        + [jax.ShapeDtypeStruct((16, 128), F32), jax.ShapeDtypeStruct((8, 128), F32)],
        in_specs=[HBM] * 6,
        out_specs=[VM] * 7,
        scratch_shapes=[
            pltpu.VMEM((4, 1, E), jnp.int32),
            pltpu.VMEM((5, E, 512), F32),
            pltpu.VMEM((256, 512), BF16),
            pltpu.VMEM((5 * E, 256), BF16),
            pltpu.SemaphoreType.DMA((10,)),
        ],
        compiler_params=pltpu.CompilerParams(vmem_limit_bytes=WHOLE),
        name="fold",
    )(route, target, code, hang, adjoint, fold)


def swap(x):
    return pltpu.roll(x, 64, 1)


def along_first(x, coef, base):
    r3, r2 = swap(x[3]), swap(x[2])
    parity = ((x[0] + r3, x[1] + r2), (x[0] - r3, x[1] - r2))
    sums = []
    for s in range(2):
        kept = (parity[s][0], swap(parity[s][0]), parity[s][1], swap(parity[s][1]))
        for c in range(2):
            at = base + 8 * s + 4 * c
            total = coef[at : at + 1] * kept[0]
            for n in range(1, 4):
                total = total + coef[at + n : at + n + 1] * kept[n]
            sums.append(total)
    p0, p1, q0, q1 = sums
    return [p0 + q0, p1 + q1, swap(q1 - p1), swap(q0 - p0)]


def chunks_of(ref, d):
    return jnp.concatenate([ref[d, :, 128 * c : 128 * c + 128] for c in range(4)], 0)


def two_dims(y, m_first, m_second, v_first, v_second, wf1, wf2, wb1, wb2):
    high, low = parts_of(y)
    g = dot(jnp.concatenate([high, low], 1), wf1[...]) + dot(high, wf2[...])
    high1, low1 = parts_of(m_first * g[:, :128] + v_first * y)
    high2, low2 = parts_of(m_second * g[:, 128:] + v_second * y)
    wide = dot(jnp.concatenate([high1, high2], 1), wb1[...])
    low = dot(jnp.concatenate([low1, low2], 1), wb2[...])
    return wide[:, :128] + wide[:, 128:] + low


def factors_of(met, vel, wb1, wb2, coef, q_out, plane_out, end_q, end_mv):
    lane = iota(1)
    left = lane < 64
    for c in range(4):
        at = slice(128 * c, 128 * c + 128)
        w = met[1, :, at] * coef[32:33] + jnp.where(lane % 64 < 8, vel[1, :, at], 0.0)
        high, low = parts_of(w)
        wide = dot(high, wb1[0:128])
        q_out[:, at] = wide[:, :128] + wide[:, 128:] + dot(low, wb2[0:128])

    for n, (ref, d) in enumerate(((met, 0), (met, 2), (vel, 0), (vel, 2))):
        packed = jnp.zeros((E, 128), F32)
        for c in range(4):
            moved = ref[d, :, 128 * c : 128 * c + 128]
            if c:
                moved = pltpu.roll(moved, 16 * c, 1)
            packed = jnp.where((lane // 16) % 4 == c, moved, packed)
        even = jnp.where(left, packed, swap(packed))
        other = jnp.where(left, swap(packed), packed)
        plane_out[n] = jnp.where(lane % 16 < 8, even, pltpu.roll(other, 8, 1))

    small_left = iota(1, (8, 128)) < 64
    for end in range(2):
        rows = slice((E - 8) * end, (E - 8) * end + 8)
        w = []
        for c in range(4):
            at = slice(128 * c, 128 * c + 128)
            spot = 33 + 4 * end + c
            term = met[0, rows, at] * coef[spot : spot + 1]
            if c == 3 * end:
                term = term + jnp.where(small_left != (end == 1), vel[0, rows, at], 0.0)
            w.append(term)
        back = along_first(w, coef, 16)
        for c in range(4):
            end_q[end, c] = back[c]
        at = slice(384 * end, 384 * end + 128)
        for n, (ref, d) in enumerate(((met, 1), (met, 2), (vel, 1), (vel, 2))):
            end_mv[end, n] = ref[d, rows, at]


def main_kernel(fields, x_ref, met, vel, keep_ref, wf1, wf2, wb1, wb2, coef, out, *factors):
    lane, row = iota(1), iota(0)
    keep = keep_ref[...]
    left = lane < 64
    if factors:
        factors_of(met, vel, wb1, wb2, coef, *factors)

    def field(n, carry):
        f = n + fields[0]
        x = [x_ref[f, :, 128 * c : 128 * c + 128] * keep for c in range(4)]
        low_faces = pltpu.roll(swap(x[0]), E - 1, 0)
        high_faces = pltpu.roll(swap(x[3]), 1, 0)
        x[0] = x[0] + jnp.where(left & (row > 0), high_faces, 0.0)
        x[3] = x[3] + jnp.where(left | (row == E - 1), 0.0, low_faces)
        stacked = jnp.concatenate(x, 0)
        rest = two_dims(
            stacked, chunks_of(met, 1), chunks_of(met, 2), chunks_of(vel, 1), chunks_of(vel, 2),
            wf1, wf2, wb1, wb2,
        )
        g0 = along_first(x, coef, 0)
        inner0 = []
        for c in range(4):
            at = slice(128 * c, 128 * c + 128)
            inner0.append(met[0, :, at] * g0[c] + vel[0, :, at] * x[c])
        back = along_first(inner0, coef, 16)
        for c in range(4):
            out[n, :, 128 * c : 128 * c + 128] = rest[E * c : E * c + E] + back[c]
        return carry

    lax.fori_loop(0, len(fields), field, 0)


def keep_kernel(marks, out):
    kept = jnp.where(iota(0) == iota(1), marks[0:1], 0.0).astype(BF16)
    column = dot(kept, jnp.ones((E, 128), BF16))
    out[...] = jnp.where(iota(1) % 64 >= 56, column, 1.0)


def kept_of(marks):
    return pl.pallas_call(
        keep_kernel,
        out_shape=jax.ShapeDtypeStruct((E, 128), F32),
        in_specs=[VM],
        out_specs=VM,
        compiler_params=pltpu.CompilerParams(vmem_limit_bytes=16 * 1024 * 1024),
        cost_estimate=pl.CostEstimate(
            flops=8_000_000_000, bytes_accessed=30_000_000, transcendentals=0
        ),
        name="keep",
    )(marks)


def main_of(adjoint, metric, velocity, keep, tables, fields, factors):
    def body(*refs):
        main_kernel(fields, *refs)

    return pl.pallas_call(
        body,
        out_shape=[
            jax.ShapeDtypeStruct(shape, F32)
            for shape in [(len(fields), E, 512)]
            + [(E, 512), (4, E, 128), (2, 4, 8, 128), (2, 4, 8, 128)] * factors
        ],
        in_specs=[VM] * 9,
        out_specs=[VM] * (5 if factors else 1),
        compiler_params=pltpu.CompilerParams(vmem_limit_bytes=LIMIT),
        cost_estimate=pl.CostEstimate(
            flops=800_000_000 * len(fields), bytes_accessed=5_000_000, transcendentals=0
        ),
        name="inner",
    )(
        adjoint, metric, velocity, keep,
        *tables["forward"], *tables["backward"], tables["coef"],
    )


def odd_device():
    index = lax.axis_index("dom") * lax.axis_size("sub") + lax.axis_index("sub")
    return lax.rem(index, 2) == 1


def line_kernel(a, b, own, c, d, edges, inside, across):
    def rows(start):
        return sum(ref[start : start + 16].astype(F32) for ref in (a, b, own, c, d))

    low = [edges[0:3]]
    high = [edges[8:11]]
    for n, (first, last) in enumerate(((0, 112), (128, 240), (256, 304))):
        low.append(pltpu.roll(rows(first)[0:1], 56, 1))
        line = rows(last)[15:16]
        high.append(pltpu.roll(swap(line) if n == 2 else line, 72, 1))
    zero = jnp.zeros((2, 128), F32)
    low = jnp.concatenate(low + [zero], 0)
    high = jnp.concatenate(high + [zero], 0)
    odd = odd_device()
    across[...] = jnp.where(odd, high, low)
    inside[...] = jnp.where(odd, low, high)


def lines_of(parts, edges):
    return pl.pallas_call(
        line_kernel,
        out_shape=[jax.ShapeDtypeStruct((8, 128), F32)] * 2,
        in_specs=[VM] * 6,
        out_specs=[VM] * 2,
        compiler_params=pltpu.CompilerParams(vmem_limit_bytes=LIMIT),
        name="lines",
    )(*parts, edges)


def post_kernel(
    a, b, own, c2, d, across, inside, base_a, base_b, q_ref, plane, end_q, end_mv,
    wf1, wf2, wb1, wb2, spread, place, out_hbm, out, out_sems,
):
    out_copies = [
        pltpu.make_async_copy(out.at[f], out_hbm.at[f], out_sems.at[f]) for f in range(5)
    ]
    lane, row = iota(1), iota(0)
    left = lane < 64

    small_left = iota(1, (1, 128)) < 64
    halo = []
    odd = odd_device()
    before = jnp.where(odd, inside[...], across[...])
    after = jnp.where(odd, across[...], inside[...])
    for got in (before, after):
        rows = []
        for n in range(3):
            pair = got[n : n + 1]
            turned = pltpu.roll(pair, 64, 1)
            rows.append(jnp.where(small_left, pair, turned))
            rows.append(jnp.where(small_left, turned, pair))
        halo.append(jnp.concatenate(rows + [jnp.zeros((2, 128), F32)], 0))
    u = jnp.concatenate(halo, 0)
    faces = []
    for n in range(3):
        rows = slice(128 * n, min(128 * n + 128, 320))
        m = sum(ref[rows].astype(F32) for ref in (a, b, own, c2, d))
        if n == 2:
            m = jnp.concatenate([m, swap(m)], 0)
        low_lines = pltpu.roll(pltpu.roll(m, 56, 1), E - 1, 0)
        high_lines = pltpu.roll(pltpu.roll(m, 72, 1), 1, 0)
        low_lines = jnp.where(row == E - 1, after[3 + n : 4 + n], low_lines)
        high_lines = jnp.where(row == 0, before[3 + n : 4 + n], high_lines)
        y = m + jnp.where(lane % 64 < 8, high_lines, 0.0)
        y = y + jnp.where(lane % 64 >= 56, low_lines, 0.0)
        faces.append(y)
    stacked = jnp.concatenate(faces + [u], 0)
    factors = [
        jnp.concatenate(
            [plane[at]] * 3
            + [
                jnp.broadcast_to(end_mv[0, n, 0:1], (8, 128)),
                jnp.broadcast_to(end_mv[1, n, 7:8], (8, 128)),
            ],
            0,
        )
        for n, at in enumerate((0, 1, 2, 3))
    ]
    r = two_dims(stacked, *factors, wf1, wf2, wb1, wb2)
    ends = r[3 * E :]
    y_parts = jnp.concatenate(parts_of(stacked[: 3 * E]), 1)
    r_parts = jnp.concatenate(parts_of(r[: 3 * E]), 1)
    for n in range(3):
        rows = slice(E * n, E * n + E)
        for f in range(2 * n, min(2 * n + 2, 5)):
            cols = slice(512 * (f - 2 * n), 512 * (f - 2 * n) + 512)
            out[f] = (
                (base_a[f] if f < 2 else base_b[f - 2])
                + q_ref[...] * dot(y_parts[rows], spread[:, cols])
                + dot(r_parts[rows], place[:, cols])
            )
            for c in range(4):
                at = slice(128 * c, 128 * c + 128)
                first = end_q[0, c, 0:1] * halo[0][f : f + 1]
                final = end_q[1, c, 7:8] * halo[1][f : f + 1]
                if c == 0:
                    first = first + jnp.where(small_left, ends[f : f + 1], 0.0)
                if c == 3:
                    final = final + jnp.where(small_left, 0.0, ends[8 + f : 9 + f])
                out[f, 0:1, at] += first
                out[f, E - 1 : E, at] += final
            out_copies[f].start()
    for copy in out_copies:
        copy.wait()


def post_of(parts, across, inside, local, tables):
    return pl.pallas_call(
        post_kernel,
        out_shape=jax.ShapeDtypeStruct((5, E, 512), F32),
        in_specs=[VM] * 19,
        out_specs=HBM,
        scratch_shapes=[pltpu.VMEM((5, E, 512), F32), pltpu.SemaphoreType.DMA((5,))],
        compiler_params=pltpu.CompilerParams(vmem_limit_bytes=LIMIT),
        name="outer",
    )(
        *parts, across, inside, *local, *tables["forward"], *tables["backward"],
        tables["spread"], tables["place"],
    )


def shards(adjoint_field, metric, velocity, mortar_route, mortar_element, face_code, hanging):
    tables = constants()
    peers = lax.axis_size("dom")
    adjoint = jnp.transpose(adjoint_field, (1, 0, 2))
    met = jnp.transpose(metric, (1, 0, 2))
    vel = jnp.transpose(velocity, (1, 0, 2))
    route, target, code, hang = (
        x.reshape(1, E) for x in (mortar_route, mortar_element, face_code, hanging)
    )
    *parts, edges, marks = folded_of(route, target, code, hang, adjoint, tables["fold"])
    def passed(n):
        pairs = [(i, (i + ORDER[n] - 2) % peers) for i in range(peers)]
        return lax.ppermute(parts[n], "dom", pairs)

    parts[0], parts[1] = passed(0), passed(1)
    kept = kept_of(marks)
    early, *factors = main_of(adjoint, met, vel, kept, tables, (0, 1), True)
    parts[3:], early, kept = lax.optimization_barrier((parts[3:], early, kept))
    parts[3], parts[4] = passed(3), passed(4)
    (late,) = main_of(adjoint, met, vel, kept, tables, (2, 3, 4), False)
    parts, late = lax.optimization_barrier((parts, late))
    out_b, out_a = lines_of(parts, edges)
    axes = ("dom", "sub")
    count = lax.axis_size(axes)
    inside = [(i, i ^ 1) for i in range(count)]
    across = [(i, i + 1 if i % 2 else i - 1) for i in range(1, count - 1)]
    inward = lax.ppermute(out_b, axes, inside)
    outward = lax.ppermute(out_a, axes, across)
    result = post_of(parts, outward, inward, (early, late, *factors), tables)
    return jnp.transpose(result, (1, 0, 2))


def solution(mesh):
    block = P(("dom", "sub"), None, None)
    flat = P(("dom", "sub"), None)
    return jax.shard_map(
        shards,
        mesh=mesh,
        in_specs=(block, block, block, flat, flat, flat, flat),
        out_specs=block,
        check_vma=False,
    )
```

```python
import jax
import jax.numpy as jnp
import ml_dtypes
import numpy as np
from jax import lax
from jax.experimental import pallas as pl
from jax.experimental.pallas import tpu as pltpu
from jax.sharding import PartitionSpec as P

gll_nodes = np.array(
    [
        -1.0,
        -0.8717401485096066,
        -0.5917001814331423,
        -0.2092992179024789,
        0.2092992179024789,
        0.5917001814331423,
        0.8717401485096066,
        1.0,
    ]
)
viscosity = 0.005
F32, BF16 = jnp.float32, jnp.bfloat16
E = 128
HBM = pl.BlockSpec(memory_space=pltpu.HBM)
VM = pl.BlockSpec(memory_space=pltpu.VMEM)
LIMIT = 32 * 1024 * 1024
ORDER = (3, 4, 2, 0, 1)
WHOLE = 64 * 1024 * 1024


def legendre_seven(points):
    prev = np.ones(points.shape)
    curr = np.array(points)
    for order in range(1, 7):
        nxt = ((2 * order + 1) * points * curr - order * prev) / (order + 1)
        prev, curr = (curr, nxt)
    return curr


def diff_matrix():
    values = legendre_seven(gll_nodes)
    result_mat = np.zeros((8, 8))
    for row in range(8):
        for col in range(8):
            if row != col:
                result_mat[row, col] = values[row] / (
                    values[col] * (gll_nodes[row] - gll_nodes[col])
                )
    result_mat[0, 0] = -14.0
    result_mat[7, 7] = 14.0
    return result_mat


def lagrange_at(points):
    basis = np.ones((8, 8))
    for row in range(8):
        for col in range(8):
            for other in range(8):
                if other != col:
                    basis[row, col] *= (points[row] - gll_nodes[other]) / (
                        gll_nodes[col] - gll_nodes[other]
                    )
    return basis


def face_tables():
    halves = [lagrange_at((gll_nodes - 1.0) / 2.0), lagrange_at((gll_nodes + 1.0) / 2.0)]
    perm_mat = np.zeros((64, 64))
    for col in range(64):
        perm_mat[col % 8 * 8 + col // 8, col] = 1.0
    tables = []
    for code in range(8):
        mat = np.kron(halves[code % 2], halves[code // 2 % 2])
        if code >= 4:
            mat = mat @ perm_mat
        tables.append(mat)
    return np.stack(tables)


def two_parts(mat):
    high = mat.astype(ml_dtypes.bfloat16)
    low = (mat - high.astype(np.float64)).astype(ml_dtypes.bfloat16)
    return high, low


def constants():
    dmat = diff_matrix()
    eye = np.eye(8)
    along_j = np.kron(np.eye(2), np.kron(dmat, eye))
    along_k = np.kron(np.eye(16), dmat)

    def forward(first, second):
        fh, fl = two_parts(viscosity * first.T)
        sh, sl = two_parts(viscosity * second.T)
        top = np.concatenate([fh, sh], 1)
        return np.concatenate([top, top], 0), np.concatenate([fl, sl], 1)

    def backward(first, second):
        fh, fl = two_parts(first)
        sh, sl = two_parts(second)
        return (
            np.concatenate([np.concatenate([fh, fl], 1), np.concatenate([sh, sl], 1)], 0),
            np.concatenate([fh, sh], 0),
        )

    def split_parity(mat):
        vectors = []
        for sign in (1.0, -1.0):
            small = (mat[:4, :4] + sign * mat[:4, ::-1][:, :4]) / 2
            for c in range(2):
                for other in range(2):
                    for swap in (0, 1):
                        vectors.append(
                            np.concatenate(
                                [
                                    np.full(64, small[2 * c + h, 2 * other + (h ^ swap)])
                                    for h in range(2)
                                ]
                            )
                        )
        return np.stack(vectors)

    coef = np.concatenate([split_parity(viscosity * dmat), split_parity(dmat.T)], 0)
    column = np.tile(np.repeat(viscosity * dmat[:, 0], 8), 2)[None]
    ends = [
        np.repeat(viscosity * dmat[2 * c : 2 * c + 2, end], 64)[None]
        for end in (0, 7)
        for c in range(4)
    ]
    coef = np.concatenate([coef, column, *ends, np.zeros((7, 128))], 0).astype(np.float32)

    tables = face_tables()
    fold = np.zeros((256, 512), ml_dtypes.bfloat16)
    for code in range(8):
        high, low = two_parts(tables[code])
        for i in range(8):
            for k in range(8):
                c, h = i // 2, i % 2
                spot = (56 + 64 * h + 16 * c + k) % 128
                cols = slice(64 * code, 64 * code + 64)
                fold[spot, cols] = high[8 * i + k]
                fold[(spot + 8) % 128, cols] = high[8 * i + k]
                fold[128 + spot, cols] = low[8 * i + k]

    spread = np.zeros((64, 512))
    place = np.zeros((64, 512))
    for i in range(8):
        for k in range(8):
            place[8 * i + k, 64 * i + k] = 1.0
            for j in range(8):
                spread[8 * i + k, 64 * i + 8 * j + k] = 1.0
    zero = np.zeros((64, 512))

    def pair(mat):
        one = np.concatenate(
            [np.concatenate([mat, zero], 1), np.concatenate([zero, mat], 1)], 0
        )
        return np.concatenate([one, one], 0).astype(ml_dtypes.bfloat16)

    return {
        "fold": fold,
        "forward": forward(along_j, along_k),
        "backward": backward(along_j, along_k),
        "spread": pair(spread),
        "place": pair(place),
        "coef": coef,
    }


def iota(dim, shape=(E, 128)):
    return lax.broadcasted_iota(jnp.int32, shape, dim)


def down(row):
    spots = jnp.where(iota(0) == iota(1), row, 0).astype(F32).astype(BF16)
    return jnp.dot(spots, jnp.ones((E, 128), BF16), preferred_element_type=F32)


def dot(a, b):
    return jnp.dot(a, b, preferred_element_type=F32)


def parts_of(x):
    high = x.astype(BF16)
    return high, (x - high.astype(F32)).astype(BF16)


def fetch(pairs, sems):
    copies = [
        pltpu.make_async_copy(src, dst, sems.at[n]) for n, (src, dst) in enumerate(pairs)
    ]
    for copy in copies:
        copy.start()
    return copies


def fold_kernel(
    route_hbm, target_hbm, code_hbm, hang_hbm, adj_hbm, fold_hbm, *refs
):
    out, ints, x, fold, wide, sems = refs
    faces_out, edges_out = out.at[0:E], out.at[E : E + 32, 0:128]
    peers = lax.axis_size("dom")
    copies = fetch(
        [(ref, ints.at[n]) for n, ref in enumerate((route_hbm, target_hbm, code_hbm, hang_hbm))]
        + [(adj_hbm.at[f], x.at[f]) for f in range(5)]
        + [(fold_hbm, fold)],
        sems,
    )
    for copy in copies[:4]:
        copy.wait()
    route, target, code, hang = (ints[n] for n in range(4))
    lane = iota(1)
    left = lane < 64
    slot = lax.rem(route - lax.axis_index("dom") + 2 + peers, peers)
    marked = down(jnp.where(hang == 1, code, -2)) - (lane // 64).astype(F32)
    odd = lane % 16 >= 8
    group = (lane // 16 + 1) % 4
    for f in range(5):
        copies[4 + f].wait()
        packed = jnp.zeros((E, 128), F32)
        for c in range(4):
            moved = x[f, :, 128 * c : 128 * c + 128]
            if c:
                moved = pltpu.roll(moved, 16 * c, 1)
            packed = jnp.where(odd & (group == c), moved, packed)
        high = packed.astype(BF16)
        high_f = high.astype(F32)
        both = jnp.where(odd, high_f, pltpu.roll(packed - high_f, 8, 1)).astype(BF16)
        wide[E * f : E * f + E, 0:128] = both
        wide[E * f : E * f + E, 128:256] = high
    copies[9].wait()
    mapped = dot(wide[...], fold[...])
    faces = []
    for f in range(5):
        total = jnp.zeros((E, 128), F32)
        for q in range(4):
            total = total + jnp.where(
                marked == 2.0 * q, mapped[E * f : E * f + E, 128 * q : 128 * q + 128], 0.0
            )
        faces.append(total + pltpu.roll(total, 64, 1))
    faces_out[:, 0:128] = jnp.where(left, faces[0], faces[1])
    faces_out[:, 128:256] = jnp.where(left, faces[2], faces[3])
    faces_out[:, 256:384] = faces[4]

    edges_out[...] = jnp.zeros((32, 128), F32)
    edges_out[16:17] = (slot * E + target).astype(F32)
    edges_out[17:18] = 1.0 - hang.astype(F32)
    lane = iota(1, (1, 128))
    own = marked[0:1], marked[E - 1 : E]
    for n in range(3):
        first, second = 2 * n, min(2 * n + 1, 4)
        for end, (at, chunk) in enumerate(((0, 0), (E - 1, 3))):
            a = x[first, at : at + 1, 128 * chunk : 128 * chunk + 128]
            b = x[second, at : at + 1, 128 * chunk : 128 * chunk + 128]
            if end == 0:
                b = pltpu.roll(b, 64, 1)
            else:
                a = pltpu.roll(a, 64, 1)
            keep = jnp.where((lane % 64 >= 56) & (own[end] >= -1.5), 0.0, 1.0)
            spot = 8 * end + n
            edges_out[spot : spot + 1] = jnp.where(lane < 64, a, b) * keep


def folded_of(route, target, code, hang, adjoint, fold):
    return pl.pallas_call(
        fold_kernel,
        out_shape=jax.ShapeDtypeStruct((E + 32, 384), F32),
        in_specs=[HBM] * 6,
        out_specs=VM,
        scratch_shapes=[
            pltpu.VMEM((4, 1, E), jnp.int32),
            pltpu.VMEM((5, E, 512), F32),
            pltpu.VMEM((256, 512), BF16),
            pltpu.VMEM((5 * E, 256), BF16),
            pltpu.SemaphoreType.DMA((10,)),
        ],
        compiler_params=pltpu.CompilerParams(vmem_limit_bytes=WHOLE),
        name="fold",
    )(route, target, code, hang, adjoint, fold)


def swap(x):
    return pltpu.roll(x, 64, 1)


def along_first(x, coef, base):
    r3, r2 = swap(x[3]), swap(x[2])
    parity = ((x[0] + r3, x[1] + r2), (x[0] - r3, x[1] - r2))
    sums = []
    for s in range(2):
        kept = (parity[s][0], swap(parity[s][0]), parity[s][1], swap(parity[s][1]))
        for c in range(2):
            at = base + 8 * s + 4 * c
            total = coef[at : at + 1] * kept[0]
            for n in range(1, 4):
                total = total + coef[at + n : at + n + 1] * kept[n]
            sums.append(total)
    p0, p1, q0, q1 = sums
    return [p0 + q0, p1 + q1, swap(q1 - p1), swap(q0 - p0)]


def chunks_of(ref, d):
    return jnp.concatenate([ref[d, :, 128 * c : 128 * c + 128] for c in range(4)], 0)


def two_dims(y, m_first, m_second, v_first, v_second, wf1, wf2, wb1, wb2):
    high, low = parts_of(y)
    g = dot(jnp.concatenate([high, low], 1), wf1[...]) + dot(high, wf2[...])
    high1, low1 = parts_of(m_first * g[:, :128] + v_first * y)
    high2, low2 = parts_of(m_second * g[:, 128:] + v_second * y)
    wide = dot(jnp.concatenate([high1, high2], 1), wb1[...])
    low = dot(jnp.concatenate([low1, low2], 1), wb2[...])
    return wide[:, :128] + wide[:, 128:] + low


def factors_of(met, vel, wb1, wb2, coef, q_out, plane_out, end_q, end_mv):
    lane = iota(1)
    left = lane < 64
    for c in range(4):
        at = slice(128 * c, 128 * c + 128)
        w = met[1, :, at] * coef[32:33] + jnp.where(lane % 64 < 8, vel[1, :, at], 0.0)
        high, low = parts_of(w)
        wide = dot(high, wb1[0:128])
        q_out[:, at] = wide[:, :128] + wide[:, 128:] + dot(low, wb2[0:128])

    for n, (ref, d) in enumerate(((met, 0), (met, 2), (vel, 0), (vel, 2))):
        packed = jnp.zeros((E, 128), F32)
        for c in range(4):
            moved = ref[d, :, 128 * c : 128 * c + 128]
            if c:
                moved = pltpu.roll(moved, 16 * c, 1)
            packed = jnp.where((lane // 16) % 4 == c, moved, packed)
        even = jnp.where(left, packed, swap(packed))
        other = jnp.where(left, swap(packed), packed)
        plane_out[n] = jnp.where(lane % 16 < 8, even, pltpu.roll(other, 8, 1))

    small_left = iota(1, (8, 128)) < 64
    for end in range(2):
        rows = slice((E - 8) * end, (E - 8) * end + 8)
        w = []
        for c in range(4):
            at = slice(128 * c, 128 * c + 128)
            spot = 33 + 4 * end + c
            term = met[0, rows, at] * coef[spot : spot + 1]
            if c == 3 * end:
                term = term + jnp.where(small_left != (end == 1), vel[0, rows, at], 0.0)
            w.append(term)
        back = along_first(w, coef, 16)
        for c in range(4):
            end_q[end, c] = back[c]
        at = slice(384 * end, 384 * end + 128)
        for n, (ref, d) in enumerate(((met, 1), (met, 2), (vel, 1), (vel, 2))):
            end_mv[end, n] = ref[d, rows, at]


def main_kernel(fields, x_ref, met, vel, keep_ref, wf1, wf2, wb1, wb2, coef, out, *factors):
    lane, row = iota(1), iota(0)
    keep = keep_ref[...]
    left = lane < 64
    if factors:
        factors_of(met, vel, wb1, wb2, coef, *factors)

    def field(n, carry):
        f = n + fields[0]
        x = [x_ref[f, :, 128 * c : 128 * c + 128] * keep for c in range(4)]
        low_faces = pltpu.roll(swap(x[0]), E - 1, 0)
        high_faces = pltpu.roll(swap(x[3]), 1, 0)
        x[0] = x[0] + jnp.where(left & (row > 0), high_faces, 0.0)
        x[3] = x[3] + jnp.where(left | (row == E - 1), 0.0, low_faces)
        stacked = jnp.concatenate(x, 0)
        rest = two_dims(
            stacked, chunks_of(met, 1), chunks_of(met, 2), chunks_of(vel, 1), chunks_of(vel, 2),
            wf1, wf2, wb1, wb2,
        )
        g0 = along_first(x, coef, 0)
        inner0 = []
        for c in range(4):
            at = slice(128 * c, 128 * c + 128)
            inner0.append(met[0, :, at] * g0[c] + vel[0, :, at] * x[c])
        back = along_first(inner0, coef, 16)
        for c in range(4):
            out[n, :, 128 * c : 128 * c + 128] = rest[E * c : E * c + E] + back[c]
        return carry

    lax.fori_loop(0, len(fields), field, 0)


def sum_kernel(both, *outs):
    faces, edges = both.at[0:E], both.at[E : E + 32, 0:128]
    column = jnp.where(iota(0) == iota(1), edges[17:18], 0.0).astype(BF16)
    column = dot(column, jnp.ones((E, 128), BF16))
    outs[5][...] = jnp.where(iota(1) % 64 >= 56, column, 1.0)
    spot = edges[16:17].astype(jnp.int32)
    hit = (iota(0, (5 * E, E)) == spot).astype(F32).astype(BF16)
    sums = dot(hit, faces[...].astype(BF16))
    left = iota(1, (64, 128)) < 64
    for ref, o in zip(outs, ORDER):
        mine = sums[o * E : o * E + E]
        ref[0:128] = mine[:, 0:128].astype(ref.dtype)
        ref[128:256] = mine[:, 128:256].astype(ref.dtype)
        ref[256:320] = jnp.where(left, mine[:64, 256:384], mine[64:, 256:384]).astype(ref.dtype)


def sums_of(both):
    return pl.pallas_call(
        sum_kernel,
        out_shape=[
            jax.ShapeDtypeStruct((320, 128), F32 if o == 2 else BF16) for o in range(5)
        ]
        + [jax.ShapeDtypeStruct((E, 128), F32)],
        in_specs=[VM],
        out_specs=[VM] * 6,
        compiler_params=pltpu.CompilerParams(vmem_limit_bytes=16 * 1024 * 1024),
        cost_estimate=pl.CostEstimate(
            flops=8_000_000_000, bytes_accessed=30_000_000, transcendentals=0
        ),
        name="sums",
    )(both)


def main_of(adjoint, metric, velocity, keep, tables, fields, factors):
    def body(*refs):
        main_kernel(fields, *refs)

    return pl.pallas_call(
        body,
        out_shape=[
            jax.ShapeDtypeStruct(shape, F32)
            for shape in [(len(fields), E, 512)]
            + [(E, 512), (4, E, 128), (2, 4, 8, 128), (2, 4, 8, 128)] * factors
        ],
        in_specs=[VM] * 9,
        out_specs=[VM] * (5 if factors else 1),
        compiler_params=pltpu.CompilerParams(vmem_limit_bytes=LIMIT),
        cost_estimate=pl.CostEstimate(
            flops=800_000_000 * len(fields), bytes_accessed=5_000_000, transcendentals=0
        ),
        name="inner",
    )(
        adjoint, metric, velocity, keep,
        *tables["forward"], *tables["backward"], tables["coef"],
    )


def odd_device():
    index = lax.axis_index("dom") * lax.axis_size("sub") + lax.axis_index("sub")
    return lax.rem(index, 2) == 1


def line_kernel(a, b, own, c, d, both, across, inside):
    edges = both.at[E : E + 32, 0:128]
    def rows(start):
        return sum(ref[start : start + 16].astype(F32) for ref in (a, b, own, c, d))

    low = [edges[0:3]]
    high = [edges[8:11]]
    for n, (first, last) in enumerate(((0, 112), (128, 240), (256, 304))):
        low.append(pltpu.roll(rows(first)[0:1], 56, 1))
        line = rows(last)[15:16]
        high.append(pltpu.roll(swap(line) if n == 2 else line, 72, 1))
    zero = jnp.zeros((2, 128), F32)
    low = jnp.concatenate(low + [zero], 0)
    high = jnp.concatenate(high + [zero], 0)
    odd = odd_device()
    across[...] = jnp.where(odd, high, low)
    inside[...] = jnp.where(odd, low, high)


def lines_of(parts, both):
    return pl.pallas_call(
        line_kernel,
        out_shape=[jax.ShapeDtypeStruct((8, 128), F32)] * 2,
        in_specs=[VM] * 6,
        out_specs=[VM] * 2,
        compiler_params=pltpu.CompilerParams(vmem_limit_bytes=LIMIT),
        name="lines",
    )(*parts, both)


def post_kernel(
    a, b, own, c2, d, across, inside, base_a, base_b, q_ref, plane, end_q, end_mv,
    wf1, wf2, wb1, wb2, spread, place, out_hbm, out, out_sems,
):
    out_copies = [
        pltpu.make_async_copy(out.at[f], out_hbm.at[f], out_sems.at[f]) for f in range(5)
    ]
    lane, row = iota(1), iota(0)
    left = lane < 64

    small_left = iota(1, (1, 128)) < 64
    halo = []
    odd = odd_device()
    before = jnp.where(odd, inside[...], across[...])
    after = jnp.where(odd, across[...], inside[...])
    for got in (before, after):
        rows = []
        for n in range(3):
            pair = got[n : n + 1]
            turned = pltpu.roll(pair, 64, 1)
            rows.append(jnp.where(small_left, pair, turned))
            rows.append(jnp.where(small_left, turned, pair))
        halo.append(jnp.concatenate(rows + [jnp.zeros((2, 128), F32)], 0))
    u = jnp.concatenate(halo, 0)
    faces = []
    for n in range(3):
        rows = slice(128 * n, min(128 * n + 128, 320))
        m = sum(ref[rows].astype(F32) for ref in (a, b, own, c2, d))
        if n == 2:
            m = jnp.concatenate([m, swap(m)], 0)
        low_lines = pltpu.roll(pltpu.roll(m, 56, 1), E - 1, 0)
        high_lines = pltpu.roll(pltpu.roll(m, 72, 1), 1, 0)
        low_lines = jnp.where(row == E - 1, after[3 + n : 4 + n], low_lines)
        high_lines = jnp.where(row == 0, before[3 + n : 4 + n], high_lines)
        y = m + jnp.where(lane % 64 < 8, high_lines, 0.0)
        y = y + jnp.where(lane % 64 >= 56, low_lines, 0.0)
        faces.append(y)
    stacked = jnp.concatenate(faces + [u], 0)
    factors = [
        jnp.concatenate(
            [plane[at]] * 3
            + [
                jnp.broadcast_to(end_mv[0, n, 0:1], (8, 128)),
                jnp.broadcast_to(end_mv[1, n, 7:8], (8, 128)),
            ],
            0,
        )
        for n, at in enumerate((0, 1, 2, 3))
    ]
    r = two_dims(stacked, *factors, wf1, wf2, wb1, wb2)
    ends = r[3 * E :]
    y_parts = jnp.concatenate(parts_of(stacked[: 3 * E]), 1)
    r_parts = jnp.concatenate(parts_of(r[: 3 * E]), 1)
    for n in range(3):
        rows = slice(E * n, E * n + E)
        for f in range(2 * n, min(2 * n + 2, 5)):
            cols = slice(512 * (f - 2 * n), 512 * (f - 2 * n) + 512)
            out[f] = (
                (base_a[f] if f < 2 else base_b[f - 2])
                + q_ref[...] * dot(y_parts[rows], spread[:, cols])
                + dot(r_parts[rows], place[:, cols])
            )
            for c in range(4):
                at = slice(128 * c, 128 * c + 128)
                first = end_q[0, c, 0:1] * halo[0][f : f + 1]
                final = end_q[1, c, 7:8] * halo[1][f : f + 1]
                if c == 0:
                    first = first + jnp.where(small_left, ends[f : f + 1], 0.0)
                if c == 3:
                    final = final + jnp.where(small_left, 0.0, ends[8 + f : 9 + f])
                out[f, 0:1, at] += first
                out[f, E - 1 : E, at] += final
            out_copies[f].start()
    for copy in out_copies:
        copy.wait()


def post_of(parts, across, inside, local, tables):
    return pl.pallas_call(
        post_kernel,
        out_shape=jax.ShapeDtypeStruct((5, E, 512), F32),
        in_specs=[VM] * 19,
        out_specs=HBM,
        scratch_shapes=[pltpu.VMEM((5, E, 512), F32), pltpu.SemaphoreType.DMA((5,))],
        compiler_params=pltpu.CompilerParams(vmem_limit_bytes=LIMIT),
        name="outer",
    )(
        *parts, across, inside, *local, *tables["forward"], *tables["backward"],
        tables["spread"], tables["place"],
    )


def shards(adjoint_field, metric, velocity, mortar_route, mortar_element, face_code, hanging):
    tables = constants()
    peers = lax.axis_size("dom")
    adjoint = jnp.transpose(adjoint_field, (1, 0, 2))
    met = jnp.transpose(metric, (1, 0, 2))
    vel = jnp.transpose(velocity, (1, 0, 2))
    route, target, code, hang = (
        x.reshape(1, E) for x in (mortar_route, mortar_element, face_code, hanging)
    )
    both = folded_of(route, target, code, hang, adjoint, tables["fold"])
    *parts, kept = sums_of(both)
    for n in (0, 1, 3, 4):
        pairs = [(i, (i + ORDER[n] - 2) % peers) for i in range(peers)]
        parts[n] = lax.ppermute(parts[n], "dom", pairs)
    early, *factors = main_of(adjoint, met, vel, kept, tables, (0, 1), True)
    parts, early = lax.optimization_barrier((parts, early))
    lines = lines_of(parts, both)
    (out_a, out_b), kept = lax.optimization_barrier((lines, kept))
    axes = ("dom", "sub")
    count = lax.axis_size(axes)
    inside = [(i, i ^ 1) for i in range(count)]
    across = [(i, i + 1 if i % 2 else i - 1) for i in range(1, count - 1)]
    outward = lax.ppermute(out_a, axes, across)
    inward = lax.ppermute(out_b, axes, inside)
    (late,) = main_of(adjoint, met, vel, kept, tables, (2, 3, 4), False)
    result = post_of(parts, outward, inward, (early, late, *factors), tables)
    return jnp.transpose(result, (1, 0, 2))


def solution(mesh):
    block = P(("dom", "sub"), None, None)
    flat = P(("dom", "sub"), None)
    return jax.shard_map(
        shards,
        mesh=mesh,
        in_specs=(block, block, block, flat, flat, flat, flat),
        out_specs=block,
        check_vma=False,
    )
```

```python
import jax
import jax.numpy as jnp
import ml_dtypes
import numpy as np
from jax import lax
from jax.experimental import pallas as pl
from jax.experimental.pallas import tpu as pltpu
from jax.sharding import PartitionSpec as P

gll_nodes = np.array(
    [
        -1.0,
        -0.8717401485096066,
        -0.5917001814331423,
        -0.2092992179024789,
        0.2092992179024789,
        0.5917001814331423,
        0.8717401485096066,
        1.0,
    ]
)
viscosity = 0.005
F32, BF16 = jnp.float32, jnp.bfloat16
E = 128
HBM = pl.BlockSpec(memory_space=pltpu.HBM)
VM = pl.BlockSpec(memory_space=pltpu.VMEM)
LIMIT = 32 * 1024 * 1024
ORDER = (3, 4, 2, 0, 1)
WHOLE = 64 * 1024 * 1024


def legendre_seven(points):
    prev = np.ones(points.shape)
    curr = np.array(points)
    for order in range(1, 7):
        nxt = ((2 * order + 1) * points * curr - order * prev) / (order + 1)
        prev, curr = (curr, nxt)
    return curr


def diff_matrix():
    values = legendre_seven(gll_nodes)
    result_mat = np.zeros((8, 8))
    for row in range(8):
        for col in range(8):
            if row != col:
                result_mat[row, col] = values[row] / (
                    values[col] * (gll_nodes[row] - gll_nodes[col])
                )
    result_mat[0, 0] = -14.0
    result_mat[7, 7] = 14.0
    return result_mat


def lagrange_at(points):
    basis = np.ones((8, 8))
    for row in range(8):
        for col in range(8):
            for other in range(8):
                if other != col:
                    basis[row, col] *= (points[row] - gll_nodes[other]) / (
                        gll_nodes[col] - gll_nodes[other]
                    )
    return basis


def face_tables():
    halves = [lagrange_at((gll_nodes - 1.0) / 2.0), lagrange_at((gll_nodes + 1.0) / 2.0)]
    perm_mat = np.zeros((64, 64))
    for col in range(64):
        perm_mat[col % 8 * 8 + col // 8, col] = 1.0
    tables = []
    for code in range(8):
        mat = np.kron(halves[code % 2], halves[code // 2 % 2])
        if code >= 4:
            mat = mat @ perm_mat
        tables.append(mat)
    return np.stack(tables)


def two_parts(mat):
    high = mat.astype(ml_dtypes.bfloat16)
    low = (mat - high.astype(np.float64)).astype(ml_dtypes.bfloat16)
    return high, low


def constants():
    dmat = diff_matrix()
    eye = np.eye(8)
    along_j = np.kron(np.eye(2), np.kron(dmat, eye))
    along_k = np.kron(np.eye(16), dmat)

    def forward(first, second):
        fh, fl = two_parts(viscosity * first.T)
        sh, sl = two_parts(viscosity * second.T)
        top = np.concatenate([fh, sh], 1)
        return np.concatenate([top, top], 0), np.concatenate([fl, sl], 1)

    def backward(first, second):
        fh, fl = two_parts(first)
        sh, sl = two_parts(second)
        return (
            np.concatenate([np.concatenate([fh, fl], 1), np.concatenate([sh, sl], 1)], 0),
            np.concatenate([fh, sh], 0),
        )

    def split_parity(mat):
        vectors = []
        for sign in (1.0, -1.0):
            small = (mat[:4, :4] + sign * mat[:4, ::-1][:, :4]) / 2
            for c in range(2):
                for other in range(2):
                    for swap in (0, 1):
                        vectors.append(
                            np.concatenate(
                                [
                                    np.full(64, small[2 * c + h, 2 * other + (h ^ swap)])
                                    for h in range(2)
                                ]
                            )
                        )
        return np.stack(vectors)

    coef = np.concatenate([split_parity(viscosity * dmat), split_parity(dmat.T)], 0)
    column = np.tile(np.repeat(viscosity * dmat[:, 0], 8), 2)[None]
    ends = [
        np.repeat(viscosity * dmat[2 * c : 2 * c + 2, end], 64)[None]
        for end in (0, 7)
        for c in range(4)
    ]
    coef = np.concatenate([coef, column, *ends, np.zeros((7, 128))], 0).astype(np.float32)

    tables = face_tables()
    fold = np.zeros((256, 512), ml_dtypes.bfloat16)
    for code in range(8):
        high, low = two_parts(tables[code])
        for i in range(8):
            for k in range(8):
                c, h = i // 2, i % 2
                spot = (56 + 64 * h + 16 * c + k) % 128
                cols = slice(64 * code, 64 * code + 64)
                fold[spot, cols] = high[8 * i + k]
                fold[(spot + 8) % 128, cols] = high[8 * i + k]
                fold[128 + spot, cols] = low[8 * i + k]

    spread = np.zeros((64, 512))
    place = np.zeros((64, 512))
    for i in range(8):
        for k in range(8):
            place[8 * i + k, 64 * i + k] = 1.0
            for j in range(8):
                spread[8 * i + k, 64 * i + 8 * j + k] = 1.0
    zero = np.zeros((64, 512))

    def pair(mat):
        one = np.concatenate(
            [np.concatenate([mat, zero], 1), np.concatenate([zero, mat], 1)], 0
        )
        return np.concatenate([one, one], 0).astype(ml_dtypes.bfloat16)

    return {
        "fold": fold,
        "forward": forward(along_j, along_k),
        "backward": backward(along_j, along_k),
        "spread": pair(spread),
        "place": pair(place),
        "coef": coef,
    }


def iota(dim, shape=(E, 128)):
    return lax.broadcasted_iota(jnp.int32, shape, dim)


def down(row):
    spots = jnp.where(iota(0) == iota(1), row, 0).astype(F32).astype(BF16)
    return jnp.dot(spots, jnp.ones((E, 128), BF16), preferred_element_type=F32)


def dot(a, b):
    return jnp.dot(a, b, preferred_element_type=F32)


def parts_of(x):
    high = x.astype(BF16)
    return high, (x - high.astype(F32)).astype(BF16)


def fetch(pairs, sems):
    copies = [
        pltpu.make_async_copy(src, dst, sems.at[n]) for n, (src, dst) in enumerate(pairs)
    ]
    for copy in copies:
        copy.start()
    return copies


def fold_kernel(
    route_hbm, target_hbm, code_hbm, hang_hbm, adj_hbm, fold_hbm, *refs
):
    out, ints, x, fold, wide, sems = refs
    faces_out, edges_out = out.at[0:E], out.at[E : E + 32, 0:128]
    peers = lax.axis_size("dom")
    copies = fetch(
        [(ref, ints.at[n]) for n, ref in enumerate((route_hbm, target_hbm, code_hbm, hang_hbm))]
        + [(adj_hbm.at[f], x.at[f]) for f in range(5)]
        + [(fold_hbm, fold)],
        sems,
    )
    for copy in copies[:4]:
        copy.wait()
    route, target, code, hang = (ints[n] for n in range(4))
    lane = iota(1)
    left = lane < 64
    slot = lax.rem(route - lax.axis_index("dom") + 2 + peers, peers)
    marked = down(jnp.where(hang == 1, code, -2)) - (lane // 64).astype(F32)
    odd = lane % 16 >= 8
    group = (lane // 16 + 1) % 4
    for copy in copies[4:]:
        copy.wait()
    for f in range(5):
        packed = jnp.zeros((E, 128), F32)
        for c in range(4):
            moved = x[f, :, 128 * c : 128 * c + 128]
            if c:
                moved = pltpu.roll(moved, 16 * c, 1)
            packed = jnp.where(odd & (group == c), moved, packed)
        high = packed.astype(BF16)
        high_f = high.astype(F32)
        both = jnp.where(odd, high_f, pltpu.roll(packed - high_f, 8, 1)).astype(BF16)
        wide[E * f : E * f + E, 0:128] = both
        wide[E * f : E * f + E, 128:256] = high
    mapped = dot(wide[...], fold[...])
    faces = []
    for f in range(5):
        total = jnp.zeros((E, 128), F32)
        for q in range(4):
            total = total + jnp.where(
                marked == 2.0 * q, mapped[E * f : E * f + E, 128 * q : 128 * q + 128], 0.0
            )
        faces.append(total + pltpu.roll(total, 64, 1))
    faces_out[:, 0:128] = jnp.where(left, faces[0], faces[1])
    faces_out[:, 128:256] = jnp.where(left, faces[2], faces[3])
    faces_out[:, 256:384] = faces[4]

    edges_out[...] = jnp.zeros((32, 128), F32)
    edges_out[16:17] = (slot * E + target).astype(F32)
    edges_out[17:18] = 1.0 - hang.astype(F32)
    lane = iota(1, (1, 128))
    own = marked[0:1], marked[E - 1 : E]
    for n in range(3):
        first, second = 2 * n, min(2 * n + 1, 4)
        for end, (at, chunk) in enumerate(((0, 0), (E - 1, 3))):
            a = x[first, at : at + 1, 128 * chunk : 128 * chunk + 128]
            b = x[second, at : at + 1, 128 * chunk : 128 * chunk + 128]
            if end == 0:
                b = pltpu.roll(b, 64, 1)
            else:
                a = pltpu.roll(a, 64, 1)
            keep = jnp.where((lane % 64 >= 56) & (own[end] >= -1.5), 0.0, 1.0)
            spot = 8 * end + n
            edges_out[spot : spot + 1] = jnp.where(lane < 64, a, b) * keep


def folded_of(route, target, code, hang, adjoint, fold):
    return pl.pallas_call(
        fold_kernel,
        out_shape=jax.ShapeDtypeStruct((E + 32, 384), F32),
        in_specs=[HBM] * 6,
        out_specs=VM,
        scratch_shapes=[
            pltpu.VMEM((4, 1, E), jnp.int32),
            pltpu.VMEM((5, E, 512), F32),
            pltpu.VMEM((256, 512), BF16),
            pltpu.VMEM((5 * E, 256), BF16),
            pltpu.SemaphoreType.DMA((10,)),
        ],
        compiler_params=pltpu.CompilerParams(vmem_limit_bytes=WHOLE),
        name="fold",
    )(route, target, code, hang, adjoint, fold)


def swap(x):
    return pltpu.roll(x, 64, 1)


def along_first(x, coef, base):
    r3, r2 = swap(x[3]), swap(x[2])
    parity = ((x[0] + r3, x[1] + r2), (x[0] - r3, x[1] - r2))
    sums = []
    for s in range(2):
        kept = (parity[s][0], swap(parity[s][0]), parity[s][1], swap(parity[s][1]))
        for c in range(2):
            at = base + 8 * s + 4 * c
            total = coef[at : at + 1] * kept[0]
            for n in range(1, 4):
                total = total + coef[at + n : at + n + 1] * kept[n]
            sums.append(total)
    p0, p1, q0, q1 = sums
    return [p0 + q0, p1 + q1, swap(q1 - p1), swap(q0 - p0)]


def chunks_of(ref, d):
    return jnp.concatenate([ref[d, :, 128 * c : 128 * c + 128] for c in range(4)], 0)


def two_dims(y, m_first, m_second, v_first, v_second, wf1, wf2, wb1, wb2):
    high, low = parts_of(y)
    g = dot(jnp.concatenate([high, low], 1), wf1[...]) + dot(high, wf2[...])
    high1, low1 = parts_of(m_first * g[:, :128] + v_first * y)
    high2, low2 = parts_of(m_second * g[:, 128:] + v_second * y)
    wide = dot(jnp.concatenate([high1, high2], 1), wb1[...])
    low = dot(jnp.concatenate([low1, low2], 1), wb2[...])
    return wide[:, :128] + wide[:, 128:] + low


def factors_of(met, vel, wb1, wb2, coef, q_out, plane_out, end_q, end_mv):
    lane = iota(1)
    left = lane < 64
    for c in range(4):
        at = slice(128 * c, 128 * c + 128)
        w = met[1, :, at] * coef[32:33] + jnp.where(lane % 64 < 8, vel[1, :, at], 0.0)
        high, low = parts_of(w)
        wide = dot(high, wb1[0:128])
        q_out[:, at] = wide[:, :128] + wide[:, 128:] + dot(low, wb2[0:128])

    for n, (ref, d) in enumerate(((met, 0), (met, 2), (vel, 0), (vel, 2))):
        packed = jnp.zeros((E, 128), F32)
        for c in range(4):
            moved = ref[d, :, 128 * c : 128 * c + 128]
            if c:
                moved = pltpu.roll(moved, 16 * c, 1)
            packed = jnp.where((lane // 16) % 4 == c, moved, packed)
        even = jnp.where(left, packed, swap(packed))
        other = jnp.where(left, swap(packed), packed)
        plane_out[n] = jnp.where(lane % 16 < 8, even, pltpu.roll(other, 8, 1))

    small_left = iota(1, (8, 128)) < 64
    for end in range(2):
        rows = slice((E - 8) * end, (E - 8) * end + 8)
        w = []
        for c in range(4):
            at = slice(128 * c, 128 * c + 128)
            spot = 33 + 4 * end + c
            term = met[0, rows, at] * coef[spot : spot + 1]
            if c == 3 * end:
                term = term + jnp.where(small_left != (end == 1), vel[0, rows, at], 0.0)
            w.append(term)
        back = along_first(w, coef, 16)
        for c in range(4):
            end_q[end, c] = back[c]
        at = slice(384 * end, 384 * end + 128)
        for n, (ref, d) in enumerate(((met, 1), (met, 2), (vel, 1), (vel, 2))):
            end_mv[end, n] = ref[d, rows, at]


def main_kernel(fields, x_ref, met, vel, keep_ref, wf1, wf2, wb1, wb2, coef, out, *factors):
    lane, row = iota(1), iota(0)
    keep = keep_ref[...]
    left = lane < 64
    if factors:
        factors_of(met, vel, wb1, wb2, coef, *factors)

    def field(n, carry):
        f = n + fields[0]
        x = [x_ref[f, :, 128 * c : 128 * c + 128] * keep for c in range(4)]
        low_faces = pltpu.roll(swap(x[0]), E - 1, 0)
        high_faces = pltpu.roll(swap(x[3]), 1, 0)
        x[0] = x[0] + jnp.where(left & (row > 0), high_faces, 0.0)
        x[3] = x[3] + jnp.where(left | (row == E - 1), 0.0, low_faces)
        stacked = jnp.concatenate(x, 0)
        rest = two_dims(
            stacked, chunks_of(met, 1), chunks_of(met, 2), chunks_of(vel, 1), chunks_of(vel, 2),
            wf1, wf2, wb1, wb2,
        )
        g0 = along_first(x, coef, 0)
        inner0 = []
        for c in range(4):
            at = slice(128 * c, 128 * c + 128)
            inner0.append(met[0, :, at] * g0[c] + vel[0, :, at] * x[c])
        back = along_first(inner0, coef, 16)
        for c in range(4):
            out[n, :, 128 * c : 128 * c + 128] = rest[E * c : E * c + E] + back[c]
        return carry

    lax.fori_loop(0, len(fields), field, 0)


def sum_kernel(both, *outs):
    faces, edges = both.at[0:E], both.at[E : E + 32, 0:128]
    column = jnp.where(iota(0) == iota(1), edges[17:18], 0.0).astype(BF16)
    column = dot(column, jnp.ones((E, 128), BF16))
    outs[5][...] = jnp.where(iota(1) % 64 >= 56, column, 1.0)
    spot = edges[16:17].astype(jnp.int32)
    hit = (iota(0, (5 * E, E)) == spot).astype(F32).astype(BF16)
    sums = dot(hit, faces[...].astype(BF16))
    left = iota(1, (64, 128)) < 64
    for ref, o in zip(outs, ORDER):
        mine = sums[o * E : o * E + E]
        ref[0:128] = mine[:, 0:128].astype(ref.dtype)
        ref[128:256] = mine[:, 128:256].astype(ref.dtype)
        ref[256:320] = jnp.where(left, mine[:64, 256:384], mine[64:, 256:384]).astype(ref.dtype)


def sums_of(both):
    return pl.pallas_call(
        sum_kernel,
        out_shape=[
            jax.ShapeDtypeStruct((320, 128), F32 if o == 2 else BF16) for o in range(5)
        ]
        + [jax.ShapeDtypeStruct((E, 128), F32)],
        in_specs=[VM],
        out_specs=[VM] * 6,
        compiler_params=pltpu.CompilerParams(vmem_limit_bytes=16 * 1024 * 1024),
        cost_estimate=pl.CostEstimate(
            flops=8_000_000_000, bytes_accessed=30_000_000, transcendentals=0
        ),
        name="sums",
    )(both)


def main_of(adjoint, metric, velocity, keep, tables, fields, factors):
    def body(*refs):
        main_kernel(fields, *refs)

    return pl.pallas_call(
        body,
        out_shape=[
            jax.ShapeDtypeStruct(shape, F32)
            for shape in [(len(fields), E, 512)]
            + [(E, 512), (4, E, 128), (2, 4, 8, 128), (2, 4, 8, 128)] * factors
        ],
        in_specs=[VM] * 9,
        out_specs=[VM] * (5 if factors else 1),
        compiler_params=pltpu.CompilerParams(vmem_limit_bytes=LIMIT),
        cost_estimate=pl.CostEstimate(
            flops=800_000_000 * len(fields), bytes_accessed=5_000_000, transcendentals=0
        ),
        name="inner",
    )(
        adjoint, metric, velocity, keep,
        *tables["forward"], *tables["backward"], tables["coef"],
    )


def odd_device():
    index = lax.axis_index("dom") * lax.axis_size("sub") + lax.axis_index("sub")
    return lax.rem(index, 2) == 1


def line_kernel(a, b, own, c, d, both, across, inside):
    edges = both.at[E : E + 32, 0:128]
    def rows(start):
        return sum(ref[start : start + 16].astype(F32) for ref in (a, b, own, c, d))

    low = [edges[0:3]]
    high = [edges[8:11]]
    for n, (first, last) in enumerate(((0, 112), (128, 240), (256, 304))):
        low.append(pltpu.roll(rows(first)[0:1], 56, 1))
        line = rows(last)[15:16]
        high.append(pltpu.roll(swap(line) if n == 2 else line, 72, 1))
    zero = jnp.zeros((2, 128), F32)
    low = jnp.concatenate(low + [zero], 0)
    high = jnp.concatenate(high + [zero], 0)
    odd = odd_device()
    across[...] = jnp.where(odd, high, low)
    inside[...] = jnp.where(odd, low, high)


def lines_of(parts, both):
    return pl.pallas_call(
        line_kernel,
        out_shape=[jax.ShapeDtypeStruct((8, 128), F32)] * 2,
        in_specs=[VM] * 6,
        out_specs=[VM] * 2,
        compiler_params=pltpu.CompilerParams(vmem_limit_bytes=LIMIT),
        name="lines",
    )(*parts, both)


def post_kernel(
    a, b, own, c2, d, across, inside, base_a, base_b, q_ref, plane, end_q, end_mv,
    wf1, wf2, wb1, wb2, spread, place, out_hbm, out, out_sems,
):
    out_copies = [
        pltpu.make_async_copy(out.at[f], out_hbm.at[f], out_sems.at[f]) for f in range(5)
    ]
    lane, row = iota(1), iota(0)
    left = lane < 64

    small_left = iota(1, (1, 128)) < 64
    halo = []
    odd = odd_device()
    before = jnp.where(odd, inside[...], across[...])
    after = jnp.where(odd, across[...], inside[...])
    for got in (before, after):
        rows = []
        for n in range(3):
            pair = got[n : n + 1]
            turned = pltpu.roll(pair, 64, 1)
            rows.append(jnp.where(small_left, pair, turned))
            rows.append(jnp.where(small_left, turned, pair))
        halo.append(jnp.concatenate(rows + [jnp.zeros((2, 128), F32)], 0))
    u = jnp.concatenate(halo, 0)
    faces = []
    for n in range(3):
        rows = slice(128 * n, min(128 * n + 128, 320))
        m = sum(ref[rows].astype(F32) for ref in (a, b, own, c2, d))
        if n == 2:
            m = jnp.concatenate([m, swap(m)], 0)
        low_lines = pltpu.roll(pltpu.roll(m, 56, 1), E - 1, 0)
        high_lines = pltpu.roll(pltpu.roll(m, 72, 1), 1, 0)
        low_lines = jnp.where(row == E - 1, after[3 + n : 4 + n], low_lines)
        high_lines = jnp.where(row == 0, before[3 + n : 4 + n], high_lines)
        y = m + jnp.where(lane % 64 < 8, high_lines, 0.0)
        y = y + jnp.where(lane % 64 >= 56, low_lines, 0.0)
        faces.append(y)
    stacked = jnp.concatenate(faces + [u], 0)
    factors = [
        jnp.concatenate(
            [plane[at]] * 3
            + [
                jnp.broadcast_to(end_mv[0, n, 0:1], (8, 128)),
                jnp.broadcast_to(end_mv[1, n, 7:8], (8, 128)),
            ],
            0,
        )
        for n, at in enumerate((0, 1, 2, 3))
    ]
    r = two_dims(stacked, *factors, wf1, wf2, wb1, wb2)
    ends = r[3 * E :]
    y_parts = jnp.concatenate(parts_of(stacked[: 3 * E]), 1)
    r_parts = jnp.concatenate(parts_of(r[: 3 * E]), 1)
    for n in range(3):
        rows = slice(E * n, E * n + E)
        for f in range(2 * n, min(2 * n + 2, 5)):
            cols = slice(512 * (f - 2 * n), 512 * (f - 2 * n) + 512)
            out[f] = (
                (base_a[f] if f < 3 else base_b[f - 3])
                + q_ref[...] * dot(y_parts[rows], spread[:, cols])
                + dot(r_parts[rows], place[:, cols])
            )
            for c in range(4):
                at = slice(128 * c, 128 * c + 128)
                first = end_q[0, c, 0:1] * halo[0][f : f + 1]
                final = end_q[1, c, 7:8] * halo[1][f : f + 1]
                if c == 0:
                    first = first + jnp.where(small_left, ends[f : f + 1], 0.0)
                if c == 3:
                    final = final + jnp.where(small_left, 0.0, ends[8 + f : 9 + f])
                out[f, 0:1, at] += first
                out[f, E - 1 : E, at] += final
            out_copies[f].start()
    for copy in out_copies:
        copy.wait()


def post_of(parts, across, inside, local, tables):
    return pl.pallas_call(
        post_kernel,
        out_shape=jax.ShapeDtypeStruct((5, E, 512), F32),
        in_specs=[VM] * 19,
        out_specs=HBM,
        scratch_shapes=[pltpu.VMEM((5, E, 512), F32), pltpu.SemaphoreType.DMA((5,))],
        compiler_params=pltpu.CompilerParams(vmem_limit_bytes=LIMIT),
        name="outer",
    )(
        *parts, across, inside, *local, *tables["forward"], *tables["backward"],
        tables["spread"], tables["place"],
    )


def shards(adjoint_field, metric, velocity, mortar_route, mortar_element, face_code, hanging):
    tables = constants()
    peers = lax.axis_size("dom")
    adjoint = jnp.transpose(adjoint_field, (1, 0, 2))
    met = jnp.transpose(metric, (1, 0, 2))
    vel = jnp.transpose(velocity, (1, 0, 2))
    route, target, code, hang = (
        x.reshape(1, E) for x in (mortar_route, mortar_element, face_code, hanging)
    )
    both = folded_of(route, target, code, hang, adjoint, tables["fold"])
    *parts, kept = sums_of(both)
    for n in (0, 1, 3, 4):
        pairs = [(i, (i + ORDER[n] - 2) % peers) for i in range(peers)]
        parts[n] = lax.ppermute(parts[n], "dom", pairs)
    early, *factors = main_of(adjoint, met, vel, kept, tables, (0, 1, 2), True)
    parts, early = lax.optimization_barrier((parts, early))
    lines = lines_of(parts, both)
    (out_a, out_b), kept = lax.optimization_barrier((lines, kept))
    axes = ("dom", "sub")
    count = lax.axis_size(axes)
    inside = [(i, i ^ 1) for i in range(count)]
    across = [(i, i + 1 if i % 2 else i - 1) for i in range(1, count - 1)]
    outward = lax.ppermute(out_a, axes, across)
    inward = lax.ppermute(out_b, axes, inside)
    (late,) = main_of(adjoint, met, vel, kept, tables, (3, 4), False)
    result = post_of(parts, outward, inward, (early, late, *factors), tables)
    return jnp.transpose(result, (1, 0, 2))


def solution(mesh):
    block = P(("dom", "sub"), None, None)
    flat = P(("dom", "sub"), None)
    return jax.shard_map(
        shards,
        mesh=mesh,
        in_specs=(block, block, block, flat, flat, flat, flat),
        out_specs=block,
        check_vma=False,
    )
```

```python
import jax
import jax.numpy as jnp
import ml_dtypes
import numpy as np
from jax import lax
from jax.experimental import pallas as pl
from jax.experimental.pallas import tpu as pltpu
from jax.sharding import PartitionSpec as P

gll_nodes = np.array(
    [
        -1.0,
        -0.8717401485096066,
        -0.5917001814331423,
        -0.2092992179024789,
        0.2092992179024789,
        0.5917001814331423,
        0.8717401485096066,
        1.0,
    ]
)
viscosity = 0.005
F32, BF16 = jnp.float32, jnp.bfloat16
E = 128
HBM = pl.BlockSpec(memory_space=pltpu.HBM)
VM = pl.BlockSpec(memory_space=pltpu.VMEM)
LIMIT = 32 * 1024 * 1024
ORDER = (3, 4, 2, 0, 1)
WHOLE = 64 * 1024 * 1024


def legendre_seven(points):
    prev = np.ones(points.shape)
    curr = np.array(points)
    for order in range(1, 7):
        nxt = ((2 * order + 1) * points * curr - order * prev) / (order + 1)
        prev, curr = (curr, nxt)
    return curr


def diff_matrix():
    values = legendre_seven(gll_nodes)
    result_mat = np.zeros((8, 8))
    for row in range(8):
        for col in range(8):
            if row != col:
                result_mat[row, col] = values[row] / (
                    values[col] * (gll_nodes[row] - gll_nodes[col])
                )
    result_mat[0, 0] = -14.0
    result_mat[7, 7] = 14.0
    return result_mat


def lagrange_at(points):
    basis = np.ones((8, 8))
    for row in range(8):
        for col in range(8):
            for other in range(8):
                if other != col:
                    basis[row, col] *= (points[row] - gll_nodes[other]) / (
                        gll_nodes[col] - gll_nodes[other]
                    )
    return basis


def face_tables():
    halves = [lagrange_at((gll_nodes - 1.0) / 2.0), lagrange_at((gll_nodes + 1.0) / 2.0)]
    perm_mat = np.zeros((64, 64))
    for col in range(64):
        perm_mat[col % 8 * 8 + col // 8, col] = 1.0
    tables = []
    for code in range(8):
        mat = np.kron(halves[code % 2], halves[code // 2 % 2])
        if code >= 4:
            mat = mat @ perm_mat
        tables.append(mat)
    return np.stack(tables)


def two_parts(mat):
    high = mat.astype(ml_dtypes.bfloat16)
    low = (mat - high.astype(np.float64)).astype(ml_dtypes.bfloat16)
    return high, low


def constants():
    dmat = diff_matrix()
    eye = np.eye(8)
    along_j = np.kron(np.eye(2), np.kron(dmat, eye))
    along_k = np.kron(np.eye(16), dmat)

    def forward(first, second):
        fh, fl = two_parts(viscosity * first.T)
        sh, sl = two_parts(viscosity * second.T)
        top = np.concatenate([fh, sh], 1)
        return np.concatenate([top, top], 0), np.concatenate([fl, sl], 1)

    def backward(first, second):
        fh, fl = two_parts(first)
        sh, sl = two_parts(second)
        return (
            np.concatenate([np.concatenate([fh, fl], 1), np.concatenate([sh, sl], 1)], 0),
            np.concatenate([fh, sh], 0),
        )

    def split_parity(mat):
        vectors = []
        for sign in (1.0, -1.0):
            small = (mat[:4, :4] + sign * mat[:4, ::-1][:, :4]) / 2
            for c in range(2):
                for other in range(2):
                    for swap in (0, 1):
                        vectors.append(
                            np.concatenate(
                                [
                                    np.full(64, small[2 * c + h, 2 * other + (h ^ swap)])
                                    for h in range(2)
                                ]
                            )
                        )
        return np.stack(vectors)

    coef = np.concatenate([split_parity(viscosity * dmat), split_parity(dmat.T)], 0)
    column = np.tile(np.repeat(viscosity * dmat[:, 0], 8), 2)[None]
    ends = [
        np.repeat(viscosity * dmat[2 * c : 2 * c + 2, end], 64)[None]
        for end in (0, 7)
        for c in range(4)
    ]
    coef = np.concatenate([coef, column, *ends, np.zeros((7, 128))], 0).astype(np.float32)

    tables = face_tables()
    fold = np.zeros((256, 512), ml_dtypes.bfloat16)
    for code in range(8):
        high, low = two_parts(tables[code])
        for i in range(8):
            for k in range(8):
                c, h = i // 2, i % 2
                spot = (56 + 64 * h + 16 * c + k) % 128
                cols = slice(64 * code, 64 * code + 64)
                fold[spot, cols] = high[8 * i + k]
                fold[(spot + 8) % 128, cols] = high[8 * i + k]
                fold[128 + spot, cols] = low[8 * i + k]

    spread = np.zeros((64, 512))
    place = np.zeros((64, 512))
    for i in range(8):
        for k in range(8):
            place[8 * i + k, 64 * i + k] = 1.0
            for j in range(8):
                spread[8 * i + k, 64 * i + 8 * j + k] = 1.0
    zero = np.zeros((64, 512))

    def pair(mat):
        one = np.concatenate(
            [np.concatenate([mat, zero], 1), np.concatenate([zero, mat], 1)], 0
        )
        return np.concatenate([one, one], 0).astype(ml_dtypes.bfloat16)

    return {
        "fold": fold,
        "forward": forward(along_j, along_k),
        "backward": backward(along_j, along_k),
        "spread": pair(spread),
        "place": pair(place),
        "coef": coef,
    }


def iota(dim, shape=(E, 128)):
    return lax.broadcasted_iota(jnp.int32, shape, dim)


def down(row):
    spots = jnp.where(iota(0) == iota(1), row, 0).astype(F32).astype(BF16)
    return jnp.dot(spots, jnp.ones((E, 128), BF16), preferred_element_type=F32)


def dot(a, b):
    return jnp.dot(a, b, preferred_element_type=F32)


def parts_of(x):
    high = x.astype(BF16)
    return high, (x - high.astype(F32)).astype(BF16)


def fetch(pairs, sems):
    copies = [
        pltpu.make_async_copy(src, dst, sems.at[n]) for n, (src, dst) in enumerate(pairs)
    ]
    for copy in copies:
        copy.start()
    return copies


def fold_kernel(
    route_hbm, target_hbm, code_hbm, hang_hbm, adj_hbm, fold_hbm, *refs
):
    out, ints, x, fold, wide, sems = refs
    faces_out, edges_out = out.at[0:E], out.at[E : E + 32, 0:128]
    peers = lax.axis_size("dom")
    copies = fetch(
        [(ref, ints.at[n]) for n, ref in enumerate((route_hbm, target_hbm, code_hbm, hang_hbm))]
        + [(adj_hbm.at[f], x.at[f]) for f in range(5)]
        + [(fold_hbm, fold)],
        sems,
    )
    for copy in copies[:4]:
        copy.wait()
    route, target, code, hang = (ints[n] for n in range(4))
    lane = iota(1)
    left = lane < 64
    slot = lax.rem(route - lax.axis_index("dom") + 2 + peers, peers)
    marked = down(jnp.where(hang == 1, code, -2)) - (lane // 64).astype(F32)
    odd = lane % 16 >= 8
    group = (lane // 16 + 1) % 4
    for copy in copies[4:]:
        copy.wait()
    for f in range(5):
        packed = jnp.zeros((E, 128), F32)
        for c in range(4):
            moved = x[f, :, 128 * c : 128 * c + 128]
            if c:
                moved = pltpu.roll(moved, 16 * c, 1)
            packed = jnp.where(odd & (group == c), moved, packed)
        high = packed.astype(BF16)
        high_f = high.astype(F32)
        both = jnp.where(odd, high_f, pltpu.roll(packed - high_f, 8, 1)).astype(BF16)
        wide[E * f : E * f + E, 0:128] = both
        wide[E * f : E * f + E, 128:256] = high
    mapped = dot(wide[...], fold[...])
    faces = []
    for f in range(5):
        total = jnp.zeros((E, 128), F32)
        for q in range(4):
            total = total + jnp.where(
                marked == 2.0 * q, mapped[E * f : E * f + E, 128 * q : 128 * q + 128], 0.0
            )
        faces.append(total + pltpu.roll(total, 64, 1))
    faces_out[:, 0:128] = jnp.where(left, faces[0], faces[1])
    faces_out[:, 128:256] = jnp.where(left, faces[2], faces[3])
    faces_out[:, 256:384] = faces[4]

    edges_out[...] = jnp.zeros((32, 128), F32)
    edges_out[16:17] = (slot * E + target).astype(F32)
    edges_out[17:18] = 1.0 - hang.astype(F32)
    lane = iota(1, (1, 128))
    own = marked[0:1], marked[E - 1 : E]
    for n in range(3):
        first, second = 2 * n, min(2 * n + 1, 4)
        for end, (at, chunk) in enumerate(((0, 0), (E - 1, 3))):
            a = x[first, at : at + 1, 128 * chunk : 128 * chunk + 128]
            b = x[second, at : at + 1, 128 * chunk : 128 * chunk + 128]
            if end == 0:
                b = pltpu.roll(b, 64, 1)
            else:
                a = pltpu.roll(a, 64, 1)
            keep = jnp.where((lane % 64 >= 56) & (own[end] >= -1.5), 0.0, 1.0)
            spot = 8 * end + n
            edges_out[spot : spot + 1] = jnp.where(lane < 64, a, b) * keep


def folded_of(route, target, code, hang, adjoint, fold):
    return pl.pallas_call(
        fold_kernel,
        out_shape=jax.ShapeDtypeStruct((E + 32, 384), F32),
        in_specs=[HBM] * 6,
        out_specs=VM,
        scratch_shapes=[
            pltpu.VMEM((4, 1, E), jnp.int32),
            pltpu.VMEM((5, E, 512), F32),
            pltpu.VMEM((256, 512), BF16),
            pltpu.VMEM((5 * E, 256), BF16),
            pltpu.SemaphoreType.DMA((10,)),
        ],
        compiler_params=pltpu.CompilerParams(vmem_limit_bytes=WHOLE),
        name="fold",
    )(route, target, code, hang, adjoint, fold)


def swap(x):
    return pltpu.roll(x, 64, 1)


def along_first(x, coef, base):
    r3, r2 = swap(x[3]), swap(x[2])
    parity = ((x[0] + r3, x[1] + r2), (x[0] - r3, x[1] - r2))
    sums = []
    for s in range(2):
        kept = (parity[s][0], swap(parity[s][0]), parity[s][1], swap(parity[s][1]))
        for c in range(2):
            at = base + 8 * s + 4 * c
            total = coef[at : at + 1] * kept[0]
            for n in range(1, 4):
                total = total + coef[at + n : at + n + 1] * kept[n]
            sums.append(total)
    p0, p1, q0, q1 = sums
    return [p0 + q0, p1 + q1, swap(q1 - p1), swap(q0 - p0)]


def chunks_of(ref, d):
    return jnp.concatenate([ref[d, :, 128 * c : 128 * c + 128] for c in range(4)], 0)


def two_dims(y, m_first, m_second, v_first, v_second, wf1, wf2, wb1, wb2):
    high, low = parts_of(y)
    g = dot(jnp.concatenate([high, low], 1), wf1[...]) + dot(high, wf2[...])
    high1, low1 = parts_of(m_first * g[:, :128] + v_first * y)
    high2, low2 = parts_of(m_second * g[:, 128:] + v_second * y)
    wide = dot(jnp.concatenate([high1, high2], 1), wb1[...])
    low = dot(jnp.concatenate([low1, low2], 1), wb2[...])
    return wide[:, :128] + wide[:, 128:] + low


def factors_of(met, vel, wb1, wb2, coef, q_out, plane_out, end_q, end_mv):
    lane = iota(1)
    left = lane < 64
    for c in range(4):
        at = slice(128 * c, 128 * c + 128)
        w = met[1, :, at] * coef[32:33] + jnp.where(lane % 64 < 8, vel[1, :, at], 0.0)
        high, low = parts_of(w)
        wide = dot(high, wb1[0:128])
        q_out[:, at] = wide[:, :128] + wide[:, 128:] + dot(low, wb2[0:128])

    for n, (ref, d) in enumerate(((met, 0), (met, 2), (vel, 0), (vel, 2))):
        packed = jnp.zeros((E, 128), F32)
        for c in range(4):
            moved = ref[d, :, 128 * c : 128 * c + 128]
            if c:
                moved = pltpu.roll(moved, 16 * c, 1)
            packed = jnp.where((lane // 16) % 4 == c, moved, packed)
        even = jnp.where(left, packed, swap(packed))
        other = jnp.where(left, swap(packed), packed)
        plane_out[n] = jnp.where(lane % 16 < 8, even, pltpu.roll(other, 8, 1))

    small_left = iota(1, (8, 128)) < 64
    for end in range(2):
        rows = slice((E - 8) * end, (E - 8) * end + 8)
        w = []
        for c in range(4):
            at = slice(128 * c, 128 * c + 128)
            spot = 33 + 4 * end + c
            term = met[0, rows, at] * coef[spot : spot + 1]
            if c == 3 * end:
                term = term + jnp.where(small_left != (end == 1), vel[0, rows, at], 0.0)
            w.append(term)
        back = along_first(w, coef, 16)
        for c in range(4):
            end_q[end, c] = back[c]
        at = slice(384 * end, 384 * end + 128)
        for n, (ref, d) in enumerate(((met, 1), (met, 2), (vel, 1), (vel, 2))):
            end_mv[end, n] = ref[d, rows, at]


def main_kernel(fields, x_ref, met, vel, keep_ref, wf1, wf2, wb1, wb2, coef, out, *factors):
    lane, row = iota(1), iota(0)
    keep = keep_ref[...]
    left = lane < 64
    if factors:
        factors_of(met, vel, wb1, wb2, coef, *factors)

    xs = []
    for f in fields:
        x = [x_ref[f, :, 128 * c : 128 * c + 128] * keep for c in range(4)]
        low_faces = pltpu.roll(swap(x[0]), E - 1, 0)
        high_faces = pltpu.roll(swap(x[3]), 1, 0)
        x[0] = x[0] + jnp.where(left & (row > 0), high_faces, 0.0)
        x[3] = x[3] + jnp.where(left | (row == E - 1), 0.0, low_faces)
        xs.append(x)
    count = len(fields)
    rest = two_dims(
        jnp.concatenate(sum(xs, []), 0),
        jnp.concatenate([chunks_of(met, 1)] * count, 0),
        jnp.concatenate([chunks_of(met, 2)] * count, 0),
        jnp.concatenate([chunks_of(vel, 1)] * count, 0),
        jnp.concatenate([chunks_of(vel, 2)] * count, 0),
        wf1, wf2, wb1, wb2,
    )
    for n, x in enumerate(xs):
        g0 = along_first(x, coef, 0)
        inner0 = []
        for c in range(4):
            at = slice(128 * c, 128 * c + 128)
            inner0.append(met[0, :, at] * g0[c] + vel[0, :, at] * x[c])
        back = along_first(inner0, coef, 16)
        for c in range(4):
            start = E * (4 * n + c)
            out[n, :, 128 * c : 128 * c + 128] = rest[start : start + E] + back[c]


def sum_kernel(both, *outs):
    faces, edges = both.at[0:E], both.at[E : E + 32, 0:128]
    column = jnp.where(iota(0) == iota(1), edges[17:18], 0.0).astype(BF16)
    column = dot(column, jnp.ones((E, 128), BF16))
    outs[5][...] = jnp.where(iota(1) % 64 >= 56, column, 1.0)
    spot = edges[16:17].astype(jnp.int32)
    hit = (iota(0, (5 * E, E)) == spot).astype(F32).astype(BF16)
    sums = dot(hit, faces[...].astype(BF16))
    left = iota(1, (64, 128)) < 64
    for ref, o in zip(outs, ORDER):
        mine = sums[o * E : o * E + E]
        ref[0:128] = mine[:, 0:128].astype(ref.dtype)
        ref[128:256] = mine[:, 128:256].astype(ref.dtype)
        ref[256:320] = jnp.where(left, mine[:64, 256:384], mine[64:, 256:384]).astype(ref.dtype)


def sums_of(both):
    return pl.pallas_call(
        sum_kernel,
        out_shape=[
            jax.ShapeDtypeStruct((320, 128), F32 if o == 2 else BF16) for o in range(5)
        ]
        + [jax.ShapeDtypeStruct((E, 128), F32)],
        in_specs=[VM],
        out_specs=[VM] * 6,
        compiler_params=pltpu.CompilerParams(vmem_limit_bytes=16 * 1024 * 1024),
        cost_estimate=pl.CostEstimate(
            flops=8_000_000_000, bytes_accessed=30_000_000, transcendentals=0
        ),
        name="sums",
    )(both)


def main_of(adjoint, metric, velocity, keep, tables, fields, factors):
    def body(*refs):
        main_kernel(fields, *refs)

    return pl.pallas_call(
        body,
        out_shape=[
            jax.ShapeDtypeStruct(shape, F32)
            for shape in [(len(fields), E, 512)]
            + [(E, 512), (4, E, 128), (2, 4, 8, 128), (2, 4, 8, 128)] * factors
        ],
        in_specs=[VM] * 9,
        out_specs=[VM] * (5 if factors else 1),
        compiler_params=pltpu.CompilerParams(vmem_limit_bytes=LIMIT),
        cost_estimate=pl.CostEstimate(
            flops=800_000_000 * len(fields), bytes_accessed=5_000_000, transcendentals=0
        ),
        name="inner",
    )(
        adjoint, metric, velocity, keep,
        *tables["forward"], *tables["backward"], tables["coef"],
    )


def odd_device():
    index = lax.axis_index("dom") * lax.axis_size("sub") + lax.axis_index("sub")
    return lax.rem(index, 2) == 1


def line_kernel(a, b, own, c, d, both, across, inside):
    edges = both.at[E : E + 32, 0:128]
    def rows(start):
        return sum(ref[start : start + 16].astype(F32) for ref in (a, b, own, c, d))

    low = [edges[0:3]]
    high = [edges[8:11]]
    for n, (first, last) in enumerate(((0, 112), (128, 240), (256, 304))):
        low.append(pltpu.roll(rows(first)[0:1], 56, 1))
        line = rows(last)[15:16]
        high.append(pltpu.roll(swap(line) if n == 2 else line, 72, 1))
    zero = jnp.zeros((2, 128), F32)
    low = jnp.concatenate(low + [zero], 0)
    high = jnp.concatenate(high + [zero], 0)
    odd = odd_device()
    across[...] = jnp.where(odd, high, low)
    inside[...] = jnp.where(odd, low, high)


def lines_of(parts, both):
    return pl.pallas_call(
        line_kernel,
        out_shape=[jax.ShapeDtypeStruct((8, 128), F32)] * 2,
        in_specs=[VM] * 6,
        out_specs=[VM] * 2,
        compiler_params=pltpu.CompilerParams(vmem_limit_bytes=LIMIT),
        name="lines",
    )(*parts, both)


def post_kernel(
    a, b, own, c2, d, across, inside, base_a, base_b, q_ref, plane, end_q, end_mv,
    wf1, wf2, wb1, wb2, spread, place, out_hbm, out, out_sems,
):
    out_copies = [
        pltpu.make_async_copy(out.at[f], out_hbm.at[f], out_sems.at[f]) for f in range(5)
    ]
    lane, row = iota(1), iota(0)
    left = lane < 64

    small_left = iota(1, (1, 128)) < 64
    halo = []
    odd = odd_device()
    before = jnp.where(odd, inside[...], across[...])
    after = jnp.where(odd, across[...], inside[...])
    for got in (before, after):
        rows = []
        for n in range(3):
            pair = got[n : n + 1]
            turned = pltpu.roll(pair, 64, 1)
            rows.append(jnp.where(small_left, pair, turned))
            rows.append(jnp.where(small_left, turned, pair))
        halo.append(jnp.concatenate(rows + [jnp.zeros((2, 128), F32)], 0))
    u = jnp.concatenate(halo, 0)
    faces = []
    for n in range(3):
        rows = slice(128 * n, min(128 * n + 128, 320))
        m = sum(ref[rows].astype(F32) for ref in (a, b, own, c2, d))
        if n == 2:
            m = jnp.concatenate([m, swap(m)], 0)
        low_lines = pltpu.roll(pltpu.roll(m, 56, 1), E - 1, 0)
        high_lines = pltpu.roll(pltpu.roll(m, 72, 1), 1, 0)
        low_lines = jnp.where(row == E - 1, after[3 + n : 4 + n], low_lines)
        high_lines = jnp.where(row == 0, before[3 + n : 4 + n], high_lines)
        y = m + jnp.where(lane % 64 < 8, high_lines, 0.0)
        y = y + jnp.where(lane % 64 >= 56, low_lines, 0.0)
        faces.append(y)
    stacked = jnp.concatenate(faces + [u], 0)
    factors = [
        jnp.concatenate(
            [plane[at]] * 3
            + [
                jnp.broadcast_to(end_mv[0, n, 0:1], (8, 128)),
                jnp.broadcast_to(end_mv[1, n, 7:8], (8, 128)),
            ],
            0,
        )
        for n, at in enumerate((0, 1, 2, 3))
    ]
    r = two_dims(stacked, *factors, wf1, wf2, wb1, wb2)
    ends = r[3 * E :]
    y_parts = jnp.concatenate(parts_of(stacked[: 3 * E]), 1)
    r_parts = jnp.concatenate(parts_of(r[: 3 * E]), 1)
    for n in range(3):
        rows = slice(E * n, E * n + E)
        for f in range(2 * n, min(2 * n + 2, 5)):
            cols = slice(512 * (f - 2 * n), 512 * (f - 2 * n) + 512)
            out[f] = (
                (base_a[f] if f < 3 else base_b[f - 3])
                + q_ref[...] * dot(y_parts[rows], spread[:, cols])
                + dot(r_parts[rows], place[:, cols])
            )
            for c in range(4):
                at = slice(128 * c, 128 * c + 128)
                first = end_q[0, c, 0:1] * halo[0][f : f + 1]
                final = end_q[1, c, 7:8] * halo[1][f : f + 1]
                if c == 0:
                    first = first + jnp.where(small_left, ends[f : f + 1], 0.0)
                if c == 3:
                    final = final + jnp.where(small_left, 0.0, ends[8 + f : 9 + f])
                out[f, 0:1, at] += first
                out[f, E - 1 : E, at] += final
            out_copies[f].start()
    for copy in out_copies:
        copy.wait()


def post_of(parts, across, inside, local, tables):
    return pl.pallas_call(
        post_kernel,
        out_shape=jax.ShapeDtypeStruct((5, E, 512), F32),
        in_specs=[VM] * 19,
        out_specs=HBM,
        scratch_shapes=[pltpu.VMEM((5, E, 512), F32), pltpu.SemaphoreType.DMA((5,))],
        compiler_params=pltpu.CompilerParams(vmem_limit_bytes=LIMIT),
        name="outer",
    )(
        *parts, across, inside, *local, *tables["forward"], *tables["backward"],
        tables["spread"], tables["place"],
    )


def shards(adjoint_field, metric, velocity, mortar_route, mortar_element, face_code, hanging):
    tables = constants()
    peers = lax.axis_size("dom")
    adjoint = jnp.transpose(adjoint_field, (1, 0, 2))
    met = jnp.transpose(metric, (1, 0, 2))
    vel = jnp.transpose(velocity, (1, 0, 2))
    route, target, code, hang = (
        x.reshape(1, E) for x in (mortar_route, mortar_element, face_code, hanging)
    )
    both = folded_of(route, target, code, hang, adjoint, tables["fold"])
    *parts, kept = sums_of(both)
    for n in (0, 1, 3, 4):
        pairs = [(i, (i + ORDER[n] - 2) % peers) for i in range(peers)]
        parts[n] = lax.ppermute(parts[n], "dom", pairs)
    early, *factors = main_of(adjoint, met, vel, kept, tables, (0, 1, 2), True)
    parts, early = lax.optimization_barrier((parts, early))
    lines = lines_of(parts, both)
    (out_a, out_b), kept = lax.optimization_barrier((lines, kept))
    axes = ("dom", "sub")
    count = lax.axis_size(axes)
    inside = [(i, i ^ 1) for i in range(count)]
    across = [(i, i + 1 if i % 2 else i - 1) for i in range(1, count - 1)]
    outward = lax.ppermute(out_a, axes, across)
    inward = lax.ppermute(out_b, axes, inside)
    (late,) = main_of(adjoint, met, vel, kept, tables, (3, 4), False)
    result = post_of(parts, outward, inward, (early, late, *factors), tables)
    return jnp.transpose(result, (1, 0, 2))


def solution(mesh):
    block = P(("dom", "sub"), None, None)
    flat = P(("dom", "sub"), None)
    return jax.shard_map(
        shards,
        mesh=mesh,
        in_specs=(block, block, block, flat, flat, flat, flat),
        out_specs=block,
        check_vma=False,
    )
```

```python
import jax
import jax.numpy as jnp
import ml_dtypes
import numpy as np
from jax import lax
from jax.experimental import pallas as pl
from jax.experimental.pallas import tpu as pltpu
from jax.sharding import PartitionSpec as P

gll_nodes = np.array(
    [
        -1.0,
        -0.8717401485096066,
        -0.5917001814331423,
        -0.2092992179024789,
        0.2092992179024789,
        0.5917001814331423,
        0.8717401485096066,
        1.0,
    ]
)
viscosity = 0.005
F32, BF16 = jnp.float32, jnp.bfloat16
E = 128
HBM = pl.BlockSpec(memory_space=pltpu.HBM)
VM = pl.BlockSpec(memory_space=pltpu.VMEM)
LIMIT = 32 * 1024 * 1024
ORDER = (3, 0, 2, 1, 4)
WHOLE = 64 * 1024 * 1024


def legendre_seven(points):
    prev = np.ones(points.shape)
    curr = np.array(points)
    for order in range(1, 7):
        nxt = ((2 * order + 1) * points * curr - order * prev) / (order + 1)
        prev, curr = (curr, nxt)
    return curr


def diff_matrix():
    values = legendre_seven(gll_nodes)
    result_mat = np.zeros((8, 8))
    for row in range(8):
        for col in range(8):
            if row != col:
                result_mat[row, col] = values[row] / (
                    values[col] * (gll_nodes[row] - gll_nodes[col])
                )
    result_mat[0, 0] = -14.0
    result_mat[7, 7] = 14.0
    return result_mat


def lagrange_at(points):
    basis = np.ones((8, 8))
    for row in range(8):
        for col in range(8):
            for other in range(8):
                if other != col:
                    basis[row, col] *= (points[row] - gll_nodes[other]) / (
                        gll_nodes[col] - gll_nodes[other]
                    )
    return basis


def face_tables():
    halves = [lagrange_at((gll_nodes - 1.0) / 2.0), lagrange_at((gll_nodes + 1.0) / 2.0)]
    perm_mat = np.zeros((64, 64))
    for col in range(64):
        perm_mat[col % 8 * 8 + col // 8, col] = 1.0
    tables = []
    for code in range(8):
        mat = np.kron(halves[code % 2], halves[code // 2 % 2])
        if code >= 4:
            mat = mat @ perm_mat
        tables.append(mat)
    return np.stack(tables)


def two_parts(mat):
    high = mat.astype(ml_dtypes.bfloat16)
    low = (mat - high.astype(np.float64)).astype(ml_dtypes.bfloat16)
    return high, low


def constants():
    dmat = diff_matrix()
    eye = np.eye(8)
    along_j = np.kron(np.eye(2), np.kron(dmat, eye))
    along_k = np.kron(np.eye(16), dmat)

    def forward(first, second):
        fh, fl = two_parts(viscosity * first.T)
        sh, sl = two_parts(viscosity * second.T)
        top = np.concatenate([fh, sh], 1)
        return np.concatenate([top, top, np.concatenate([fl, sl], 1)], 0)

    def backward(first, second):
        fh, fl = two_parts(first)
        sh, sl = two_parts(second)
        return np.concatenate([fh, sh, fh, sh, fl, sl], 0)

    def split_parity(mat):
        vectors = []
        for sign in (1.0, -1.0):
            small = (mat[:4, :4] + sign * mat[:4, ::-1][:, :4]) / 2
            for c in range(2):
                for other in range(2):
                    for swap in (0, 1):
                        vectors.append(
                            np.concatenate(
                                [
                                    np.full(64, small[2 * c + h, 2 * other + (h ^ swap)])
                                    for h in range(2)
                                ]
                            )
                        )
        return np.stack(vectors)

    coef = np.concatenate([split_parity(viscosity * dmat), split_parity(dmat.T)], 0)
    column = np.tile(np.repeat(viscosity * dmat[:, 0], 8), 2)[None]
    ends = [
        np.repeat(viscosity * dmat[2 * c : 2 * c + 2, end], 64)[None]
        for end in (0, 7)
        for c in range(4)
    ]
    coef = np.concatenate([coef, column, *ends, np.zeros((7, 128))], 0).astype(np.float32)

    tables = face_tables()
    fold = np.zeros((256, 512), ml_dtypes.bfloat16)
    for code in range(8):
        high, low = two_parts(tables[code])
        for i in range(8):
            for k in range(8):
                c, h = i // 2, i % 2
                spot = (56 + 64 * h + 16 * c + k) % 128
                cols = slice(64 * code, 64 * code + 64)
                fold[spot, cols] = high[8 * i + k]
                fold[(spot + 8) % 128, cols] = high[8 * i + k]
                fold[128 + spot, cols] = low[8 * i + k]

    spread = np.zeros((64, 512))
    place = np.zeros((64, 512))
    for i in range(8):
        for k in range(8):
            place[8 * i + k, 64 * i + k] = 1.0
            for j in range(8):
                spread[8 * i + k, 64 * i + 8 * j + k] = 1.0
    zero = np.zeros((64, 512))

    def pair(mat):
        one = np.concatenate(
            [np.concatenate([mat, zero], 1), np.concatenate([zero, mat], 1)], 0
        )
        return np.concatenate([one, one], 0).astype(ml_dtypes.bfloat16)

    return {
        "fold": fold,
        "forward": forward(along_j, along_k),
        "backward": backward(along_j, along_k),
        "spread": pair(spread),
        "place": pair(place),
        "coef": coef,
    }


def iota(dim, shape=(E, 128)):
    return lax.broadcasted_iota(jnp.int32, shape, dim)


def down(row):
    spots = jnp.where(iota(0) == iota(1), row, 0).astype(F32).astype(BF16)
    return jnp.dot(spots, jnp.ones((E, 128), BF16), preferred_element_type=F32)


def dot(a, b):
    return jnp.dot(a, b, preferred_element_type=F32)


def parts_of(x):
    high = x.astype(BF16)
    return high, (x - high.astype(F32)).astype(BF16)


def fetch(pairs, sems):
    copies = [
        pltpu.make_async_copy(src, dst, sems.at[n]) for n, (src, dst) in enumerate(pairs)
    ]
    for copy in copies:
        copy.start()
    return copies


def fold_kernel(
    route_hbm, target_hbm, code_hbm, hang_hbm, adj_hbm, fold_hbm, *refs
):
    out, ints, x, fold, wide, sems = refs
    faces_out, edges_out = out.at[0:E], out.at[E : E + 32, 0:128]
    peers = lax.axis_size("dom")
    copies = fetch(
        [(ref, ints.at[n]) for n, ref in enumerate((route_hbm, target_hbm, code_hbm, hang_hbm))]
        + [(adj_hbm.at[f], x.at[f]) for f in range(5)]
        + [(fold_hbm, fold)],
        sems,
    )
    for copy in copies[:4]:
        copy.wait()
    route, target, code, hang = (ints[n] for n in range(4))
    lane = iota(1)
    left = lane < 64
    slot = lax.rem(route - lax.axis_index("dom") + 2 + peers, peers)
    marked = down(jnp.where(hang == 1, code, -2)) - (lane // 64).astype(F32)
    odd = lane % 16 >= 8
    group = (lane // 16 + 1) % 4
    for copy in copies[4:]:
        copy.wait()
    for f in range(5):
        packed = jnp.zeros((E, 128), F32)
        for c in range(4):
            moved = x[f, :, 128 * c : 128 * c + 128]
            if c:
                moved = pltpu.roll(moved, 16 * c, 1)
            packed = jnp.where(odd & (group == c), moved, packed)
        high = packed.astype(BF16)
        high_f = high.astype(F32)
        both = jnp.where(odd, high_f, pltpu.roll(packed - high_f, 8, 1)).astype(BF16)
        wide[E * f : E * f + E, 0:128] = both
        wide[E * f : E * f + E, 128:256] = high
    mapped = dot(wide[...], fold[...])
    faces = []
    for f in range(5):
        total = jnp.zeros((E, 128), F32)
        for q in range(4):
            total = total + jnp.where(
                marked == 2.0 * q, mapped[E * f : E * f + E, 128 * q : 128 * q + 128], 0.0
            )
        faces.append(total + pltpu.roll(total, 64, 1))
    faces_out[:, 0:128] = jnp.where(left, faces[0], faces[1])
    faces_out[:, 128:256] = jnp.where(left, faces[2], faces[3])
    faces_out[:, 256:384] = faces[4]

    edges_out[...] = jnp.zeros((32, 128), F32)
    edges_out[16:17] = (slot * E + target).astype(F32)
    edges_out[17:18] = 1.0 - hang.astype(F32)
    lane = iota(1, (1, 128))
    own = marked[0:1], marked[E - 1 : E]
    for n in range(3):
        first, second = 2 * n, min(2 * n + 1, 4)
        for end, (at, chunk) in enumerate(((0, 0), (E - 1, 3))):
            a = x[first, at : at + 1, 128 * chunk : 128 * chunk + 128]
            b = x[second, at : at + 1, 128 * chunk : 128 * chunk + 128]
            if end == 0:
                b = pltpu.roll(b, 64, 1)
            else:
                a = pltpu.roll(a, 64, 1)
            keep = jnp.where((lane % 64 >= 56) & (own[end] >= -1.5), 0.0, 1.0)
            spot = 8 * end + n
            edges_out[spot : spot + 1] = jnp.where(lane < 64, a, b) * keep


def folded_of(route, target, code, hang, adjoint, fold):
    return pl.pallas_call(
        fold_kernel,
        out_shape=jax.ShapeDtypeStruct((E + 32, 384), F32),
        in_specs=[HBM] * 6,
        out_specs=VM,
        scratch_shapes=[
            pltpu.VMEM((4, 1, E), jnp.int32),
            pltpu.VMEM((5, E, 512), F32),
            pltpu.VMEM((256, 512), BF16),
            pltpu.VMEM((5 * E, 256), BF16),
            pltpu.SemaphoreType.DMA((10,)),
        ],
        compiler_params=pltpu.CompilerParams(vmem_limit_bytes=WHOLE),
        name="fold",
    )(route, target, code, hang, adjoint, fold)


def swap(x):
    return pltpu.roll(x, 64, 1)


def along_first(x, coef, base):
    r3, r2 = swap(x[3]), swap(x[2])
    parity = ((x[0] + r3, x[1] + r2), (x[0] - r3, x[1] - r2))
    sums = []
    for s in range(2):
        kept = (parity[s][0], swap(parity[s][0]), parity[s][1], swap(parity[s][1]))
        for c in range(2):
            at = base + 8 * s + 4 * c
            total = coef[at : at + 1] * kept[0]
            for n in range(1, 4):
                total = total + coef[at + n : at + n + 1] * kept[n]
            sums.append(total)
    p0, p1, q0, q1 = sums
    return [p0 + q0, p1 + q1, swap(q1 - p1), swap(q0 - p0)]


def chunks_of(ref, d):
    return jnp.concatenate([ref[d, :, 128 * c : 128 * c + 128] for c in range(4)], 0)


def two_dims(y, m_first, m_second, v_first, v_second, wf, wb):
    high, low = parts_of(y)
    g = dot(jnp.concatenate([high, low, high], 1), wf[...])
    high1, low1 = parts_of(m_first * g[:, :128] + v_first * y)
    high2, low2 = parts_of(m_second * g[:, 128:] + v_second * y)
    return dot(jnp.concatenate([high1, high2, low1, low2, high1, high2], 1), wb[...])


def factors_of(met, vel, wb, coef, q_out, plane_out, end_q, end_mv):
    lane = iota(1)
    left = lane < 64
    for c in range(4):
        at = slice(128 * c, 128 * c + 128)
        w = met[1, :, at] * coef[32:33] + jnp.where(lane % 64 < 8, vel[1, :, at], 0.0)
        high, low = parts_of(w)
        along = [wb[start : start + 128] for start in (0, 256, 512)]
        q_out[:, at] = dot(jnp.concatenate([high, low, high], 1), jnp.concatenate(along, 0))

    for n, (ref, d) in enumerate(((met, 0), (met, 2), (vel, 0), (vel, 2))):
        packed = jnp.zeros((E, 128), F32)
        for c in range(4):
            moved = ref[d, :, 128 * c : 128 * c + 128]
            if c:
                moved = pltpu.roll(moved, 16 * c, 1)
            packed = jnp.where((lane // 16) % 4 == c, moved, packed)
        even = jnp.where(left, packed, swap(packed))
        other = jnp.where(left, swap(packed), packed)
        plane_out[n] = jnp.where(lane % 16 < 8, even, pltpu.roll(other, 8, 1))

    small_left = iota(1, (8, 128)) < 64
    for end in range(2):
        rows = slice((E - 8) * end, (E - 8) * end + 8)
        w = []
        for c in range(4):
            at = slice(128 * c, 128 * c + 128)
            spot = 33 + 4 * end + c
            term = met[0, rows, at] * coef[spot : spot + 1]
            if c == 3 * end:
                term = term + jnp.where(small_left != (end == 1), vel[0, rows, at], 0.0)
            w.append(term)
        back = along_first(w, coef, 16)
        for c in range(4):
            end_q[end, c] = back[c]
        at = slice(384 * end, 384 * end + 128)
        for n, (ref, d) in enumerate(((met, 1), (met, 2), (vel, 1), (vel, 2))):
            end_mv[end, n] = ref[d, rows, at]


def main_kernel(fields, x_ref, met, vel, keep_ref, wf, wb, coef, out, *factors):
    lane, row = iota(1), iota(0)
    keep = keep_ref[...]
    left = lane < 64
    if factors:
        factors_of(met, vel, wb, coef, *factors)

    xs = []
    for f in fields:
        x = [x_ref[f, :, 128 * c : 128 * c + 128] * keep for c in range(4)]
        low_faces = pltpu.roll(swap(x[0]), E - 1, 0)
        high_faces = pltpu.roll(swap(x[3]), 1, 0)
        x[0] = x[0] + jnp.where(left & (row > 0), high_faces, 0.0)
        x[3] = x[3] + jnp.where(left | (row == E - 1), 0.0, low_faces)
        xs.append(x)
    count = len(fields)
    rest = two_dims(
        jnp.concatenate(sum(xs, []), 0),
        jnp.concatenate([chunks_of(met, 1)] * count, 0),
        jnp.concatenate([chunks_of(met, 2)] * count, 0),
        jnp.concatenate([chunks_of(vel, 1)] * count, 0),
        jnp.concatenate([chunks_of(vel, 2)] * count, 0),
        wf, wb,
    )
    for n, x in enumerate(xs):
        g0 = along_first(x, coef, 0)
        inner0 = []
        for c in range(4):
            at = slice(128 * c, 128 * c + 128)
            inner0.append(met[0, :, at] * g0[c] + vel[0, :, at] * x[c])
        back = along_first(inner0, coef, 16)
        for c in range(4):
            start = E * (4 * n + c)
            out[n, :, 128 * c : 128 * c + 128] = rest[start : start + E] + back[c]


def sum_kernel(both, *outs):
    faces, edges = both.at[0:E], both.at[E : E + 32, 0:128]
    column = jnp.where(iota(0) == iota(1), edges[17:18], 0.0).astype(BF16)
    column = dot(column, jnp.ones((E, 128), BF16))
    outs[5][...] = jnp.where(iota(1) % 64 >= 56, column, 1.0)
    spot = edges[16:17].astype(jnp.int32)
    hit = (iota(0, (5 * E, E)) == spot).astype(F32).astype(BF16)
    sums = dot(hit, faces[...].astype(BF16))
    left = iota(1, (64, 128)) < 64
    for ref, o in zip(outs, ORDER):
        mine = sums[o * E : o * E + E]
        ref[0:128] = mine[:, 0:128].astype(ref.dtype)
        ref[128:256] = mine[:, 128:256].astype(ref.dtype)
        ref[256:320] = jnp.where(left, mine[:64, 256:384], mine[64:, 256:384]).astype(ref.dtype)


def sums_of(both):
    return pl.pallas_call(
        sum_kernel,
        out_shape=[
            jax.ShapeDtypeStruct((320, 128), F32 if o == 2 else BF16) for o in range(5)
        ]
        + [jax.ShapeDtypeStruct((E, 128), F32)],
        in_specs=[VM],
        out_specs=[VM] * 6,
        compiler_params=pltpu.CompilerParams(vmem_limit_bytes=16 * 1024 * 1024),
        cost_estimate=pl.CostEstimate(
            flops=8_000_000_000, bytes_accessed=30_000_000, transcendentals=0
        ),
        name="sums",
    )(both)


def main_of(adjoint, metric, velocity, keep, tables, fields, factors):
    def body(*refs):
        main_kernel(fields, *refs)

    return pl.pallas_call(
        body,
        out_shape=[
            jax.ShapeDtypeStruct(shape, F32)
            for shape in [(len(fields), E, 512)]
            + [(E, 512), (4, E, 128), (2, 4, 8, 128), (2, 4, 8, 128)] * factors
        ],
        in_specs=[VM] * 7,
        out_specs=[VM] * (5 if factors else 1),
        compiler_params=pltpu.CompilerParams(vmem_limit_bytes=LIMIT),
        cost_estimate=pl.CostEstimate(
            flops=800_000_000 * len(fields), bytes_accessed=5_000_000, transcendentals=0
        ),
        name="inner",
    )(
        adjoint, metric, velocity, keep,
        tables["forward"], tables["backward"], tables["coef"],
    )


def odd_device():
    index = lax.axis_index("dom") * lax.axis_size("sub") + lax.axis_index("sub")
    return lax.rem(index, 2) == 1


def line_kernel(a, b, own, c, d, both, across, inside):
    edges = both.at[E : E + 32, 0:128]
    def rows(start):
        return sum(ref[start : start + 16].astype(F32) for ref in (a, b, own, c, d))

    low = [edges[0:3]]
    high = [edges[8:11]]
    for n, (first, last) in enumerate(((0, 112), (128, 240), (256, 304))):
        low.append(pltpu.roll(rows(first)[0:1], 56, 1))
        line = rows(last)[15:16]
        high.append(pltpu.roll(swap(line) if n == 2 else line, 72, 1))
    zero = jnp.zeros((2, 128), F32)
    low = jnp.concatenate(low + [zero], 0)
    high = jnp.concatenate(high + [zero], 0)
    odd = odd_device()
    across[...] = jnp.where(odd, high, low)
    inside[...] = jnp.where(odd, low, high)


def lines_of(parts, both):
    return pl.pallas_call(
        line_kernel,
        out_shape=[jax.ShapeDtypeStruct((8, 128), F32)] * 2,
        in_specs=[VM] * 6,
        out_specs=[VM] * 2,
        compiler_params=pltpu.CompilerParams(vmem_limit_bytes=LIMIT),
        name="lines",
    )(*parts, both)


def post_kernel(
    a, b, own, c2, d, across, inside, base_a, base_b, q_ref, plane, end_q, end_mv,
    wf, wb, spread, place, out_hbm, out, out_sems,
):
    out_copies = [
        pltpu.make_async_copy(out.at[f], out_hbm.at[f], out_sems.at[f]) for f in range(5)
    ]
    lane, row = iota(1), iota(0)
    left = lane < 64

    small_left = iota(1, (1, 128)) < 64
    halo = []
    odd = odd_device()
    before = jnp.where(odd, inside[...], across[...])
    after = jnp.where(odd, across[...], inside[...])
    for got in (before, after):
        rows = []
        for n in range(3):
            pair = got[n : n + 1]
            turned = pltpu.roll(pair, 64, 1)
            rows.append(jnp.where(small_left, pair, turned))
            rows.append(jnp.where(small_left, turned, pair))
        halo.append(jnp.concatenate(rows + [jnp.zeros((2, 128), F32)], 0))
    u = jnp.concatenate(halo, 0)
    faces = []
    for n in range(3):
        rows = slice(128 * n, min(128 * n + 128, 320))
        m = sum(ref[rows].astype(F32) for ref in (a, b, own, c2, d))
        if n == 2:
            m = jnp.concatenate([m, swap(m)], 0)
        low_lines = pltpu.roll(pltpu.roll(m, 56, 1), E - 1, 0)
        high_lines = pltpu.roll(pltpu.roll(m, 72, 1), 1, 0)
        low_lines = jnp.where(row == E - 1, after[3 + n : 4 + n], low_lines)
        high_lines = jnp.where(row == 0, before[3 + n : 4 + n], high_lines)
        y = m + jnp.where(lane % 64 < 8, high_lines, 0.0)
        y = y + jnp.where(lane % 64 >= 56, low_lines, 0.0)
        faces.append(y)
    stacked = jnp.concatenate(faces + [u], 0)
    factors = [
        jnp.concatenate(
            [plane[at]] * 3
            + [
                jnp.broadcast_to(end_mv[0, n, 0:1], (8, 128)),
                jnp.broadcast_to(end_mv[1, n, 7:8], (8, 128)),
            ],
            0,
        )
        for n, at in enumerate((0, 1, 2, 3))
    ]
    r = two_dims(stacked, *factors, wf, wb)
    ends = r[3 * E :]
    y_parts = jnp.concatenate(parts_of(stacked[: 3 * E]), 1)
    r_parts = jnp.concatenate(parts_of(r[: 3 * E]), 1)
    for n in range(3):
        rows = slice(E * n, E * n + E)
        for f in range(2 * n, min(2 * n + 2, 5)):
            cols = slice(512 * (f - 2 * n), 512 * (f - 2 * n) + 512)
            out[f] = (
                (base_a[f] if f < 3 else base_b[f - 3])
                + q_ref[...] * dot(y_parts[rows], spread[:, cols])
                + dot(r_parts[rows], place[:, cols])
            )
            for c in range(4):
                at = slice(128 * c, 128 * c + 128)
                first = end_q[0, c, 0:1] * halo[0][f : f + 1]
                final = end_q[1, c, 7:8] * halo[1][f : f + 1]
                if c == 0:
                    first = first + jnp.where(small_left, ends[f : f + 1], 0.0)
                if c == 3:
                    final = final + jnp.where(small_left, 0.0, ends[8 + f : 9 + f])
                out[f, 0:1, at] += first
                out[f, E - 1 : E, at] += final
            out_copies[f].start()
    for copy in out_copies:
        copy.wait()


def post_of(parts, across, inside, local, tables):
    return pl.pallas_call(
        post_kernel,
        out_shape=jax.ShapeDtypeStruct((5, E, 512), F32),
        in_specs=[VM] * 17,
        out_specs=HBM,
        scratch_shapes=[pltpu.VMEM((5, E, 512), F32), pltpu.SemaphoreType.DMA((5,))],
        compiler_params=pltpu.CompilerParams(vmem_limit_bytes=LIMIT),
        name="outer",
    )(
        *parts, across, inside, *local, tables["forward"], tables["backward"],
        tables["spread"], tables["place"],
    )


def shards(adjoint_field, metric, velocity, mortar_route, mortar_element, face_code, hanging):
    tables = constants()
    peers = lax.axis_size("dom")
    adjoint = jnp.transpose(adjoint_field, (1, 0, 2))
    met = jnp.transpose(metric, (1, 0, 2))
    vel = jnp.transpose(velocity, (1, 0, 2))
    route, target, code, hang = (
        x.reshape(1, E) for x in (mortar_route, mortar_element, face_code, hanging)
    )
    both = folded_of(route, target, code, hang, adjoint, tables["fold"])
    *parts, kept = sums_of(both)
    for n in (0, 1, 3, 4):
        pairs = [(i, (i + ORDER[n] - 2) % peers) for i in range(peers)]
        parts[n] = lax.ppermute(parts[n], "dom", pairs)
    early, *factors = main_of(adjoint, met, vel, kept, tables, (0, 1, 2), True)
    parts, early = lax.optimization_barrier((parts, early))
    lines = lines_of(parts, both)
    (out_a, out_b), kept = lax.optimization_barrier((lines, kept))
    axes = ("dom", "sub")
    count = lax.axis_size(axes)
    inside = [(i, i ^ 1) for i in range(count)]
    across = [(i, i + 1 if i % 2 else i - 1) for i in range(1, count - 1)]
    outward = lax.ppermute(out_a, axes, across)
    inward = lax.ppermute(out_b, axes, inside)
    (late,) = main_of(adjoint, met, vel, kept, tables, (3, 4), False)
    result = post_of(parts, outward, inward, (early, late, *factors), tables)
    return jnp.transpose(result, (1, 0, 2))


def solution(mesh):
    block = P(("dom", "sub"), None, None)
    flat = P(("dom", "sub"), None)
    return jax.shard_map(
        shards,
        mesh=mesh,
        in_specs=(block, block, block, flat, flat, flat, flat),
        out_specs=block,
        check_vma=False,
    )
```

```python
import jax
import jax.numpy as jnp
import ml_dtypes
import numpy as np
from jax import lax
from jax.experimental import pallas as pl
from jax.experimental.pallas import tpu as pltpu
from jax.sharding import PartitionSpec as P

gll_nodes = np.array(
    [
        -1.0,
        -0.8717401485096066,
        -0.5917001814331423,
        -0.2092992179024789,
        0.2092992179024789,
        0.5917001814331423,
        0.8717401485096066,
        1.0,
    ]
)
viscosity = 0.005
F32, BF16 = jnp.float32, jnp.bfloat16
E = 128
HBM = pl.BlockSpec(memory_space=pltpu.HBM)
VM = pl.BlockSpec(memory_space=pltpu.VMEM)
LIMIT = 32 * 1024 * 1024
ORDER = (3, 4, 2, 0, 1)
WHOLE = 64 * 1024 * 1024


def legendre_seven(points):
    prev = np.ones(points.shape)
    curr = np.array(points)
    for order in range(1, 7):
        nxt = ((2 * order + 1) * points * curr - order * prev) / (order + 1)
        prev, curr = (curr, nxt)
    return curr


def diff_matrix():
    values = legendre_seven(gll_nodes)
    result_mat = np.zeros((8, 8))
    for row in range(8):
        for col in range(8):
            if row != col:
                result_mat[row, col] = values[row] / (
                    values[col] * (gll_nodes[row] - gll_nodes[col])
                )
    result_mat[0, 0] = -14.0
    result_mat[7, 7] = 14.0
    return result_mat


def lagrange_at(points):
    basis = np.ones((8, 8))
    for row in range(8):
        for col in range(8):
            for other in range(8):
                if other != col:
                    basis[row, col] *= (points[row] - gll_nodes[other]) / (
                        gll_nodes[col] - gll_nodes[other]
                    )
    return basis


def face_tables():
    halves = [lagrange_at((gll_nodes - 1.0) / 2.0), lagrange_at((gll_nodes + 1.0) / 2.0)]
    perm_mat = np.zeros((64, 64))
    for col in range(64):
        perm_mat[col % 8 * 8 + col // 8, col] = 1.0
    tables = []
    for code in range(8):
        mat = np.kron(halves[code % 2], halves[code // 2 % 2])
        if code >= 4:
            mat = mat @ perm_mat
        tables.append(mat)
    return np.stack(tables)


def two_parts(mat):
    high = mat.astype(ml_dtypes.bfloat16)
    low = (mat - high.astype(np.float64)).astype(ml_dtypes.bfloat16)
    return high, low


def constants():
    dmat = diff_matrix()
    eye = np.eye(8)
    along_j = np.kron(np.eye(2), np.kron(dmat, eye))
    along_k = np.kron(np.eye(16), dmat)

    def forward(first, second):
        fh, fl = two_parts(viscosity * first.T)
        sh, sl = two_parts(viscosity * second.T)
        top = np.concatenate([fh, sh], 1)
        return np.concatenate([top, top], 0), np.concatenate([fl, sl], 1)

    def backward(first, second):
        fh, fl = two_parts(first)
        sh, sl = two_parts(second)
        return (
            np.concatenate([np.concatenate([fh, fl], 1), np.concatenate([sh, sl], 1)], 0),
            np.concatenate([fh, sh], 0),
        )

    def split_parity(mat):
        vectors = []
        for sign in (1.0, -1.0):
            small = (mat[:4, :4] + sign * mat[:4, ::-1][:, :4]) / 2
            for c in range(2):
                for other in range(2):
                    for swap in (0, 1):
                        vectors.append(
                            np.concatenate(
                                [
                                    np.full(64, small[2 * c + h, 2 * other + (h ^ swap)])
                                    for h in range(2)
                                ]
                            )
                        )
        return np.stack(vectors)

    coef = np.concatenate([split_parity(viscosity * dmat), split_parity(dmat.T)], 0)
    column = np.tile(np.repeat(viscosity * dmat[:, 0], 8), 2)[None]
    ends = [
        np.repeat(viscosity * dmat[2 * c : 2 * c + 2, end], 64)[None]
        for end in (0, 7)
        for c in range(4)
    ]
    coef = np.concatenate([coef, column, *ends, np.zeros((7, 128))], 0).astype(np.float32)

    tables = face_tables()
    fold = np.zeros((256, 512), ml_dtypes.bfloat16)
    for code in range(8):
        high, low = two_parts(tables[code])
        for i in range(8):
            for k in range(8):
                c, h = i // 2, i % 2
                spot = (56 + 64 * h + 16 * c + k) % 128
                cols = slice(64 * code, 64 * code + 64)
                fold[spot, cols] = high[8 * i + k]
                fold[(spot + 8) % 128, cols] = high[8 * i + k]
                fold[128 + spot, cols] = low[8 * i + k]

    spread = np.zeros((64, 512))
    place = np.zeros((64, 512))
    for i in range(8):
        for k in range(8):
            place[8 * i + k, 64 * i + k] = 1.0
            for j in range(8):
                spread[8 * i + k, 64 * i + 8 * j + k] = 1.0
    zero = np.zeros((64, 512))

    def pair(mat):
        one = np.concatenate(
            [np.concatenate([mat, zero], 1), np.concatenate([zero, mat], 1)], 0
        )
        return np.concatenate([one, one], 0).astype(ml_dtypes.bfloat16)

    return {
        "fold": fold,
        "forward": forward(along_j, along_k),
        "backward": backward(along_j, along_k),
        "spread": pair(spread),
        "place": pair(place),
        "coef": coef,
    }


def iota(dim, shape=(E, 128)):
    return lax.broadcasted_iota(jnp.int32, shape, dim)


def down(row):
    spots = jnp.where(iota(0) == iota(1), row, 0).astype(F32).astype(BF16)
    return jnp.dot(spots, jnp.ones((E, 128), BF16), preferred_element_type=F32)


def dot(a, b):
    return jnp.dot(a, b, preferred_element_type=F32)


def parts_of(x):
    high = x.astype(BF16)
    return high, (x - high.astype(F32)).astype(BF16)


def fetch(pairs, sems):
    copies = [
        pltpu.make_async_copy(src, dst, sems.at[n]) for n, (src, dst) in enumerate(pairs)
    ]
    for copy in copies:
        copy.start()
    return copies


def fold_kernel(
    route_hbm, target_hbm, code_hbm, hang_hbm, adj_hbm, fold_hbm, *refs
):
    out, ints, x, fold, wide, sems = refs
    faces_out, edges_out = out.at[0:E], out.at[E : E + 32, 0:128]
    peers = lax.axis_size("dom")
    copies = fetch(
        [(ref, ints.at[n]) for n, ref in enumerate((route_hbm, target_hbm, code_hbm, hang_hbm))]
        + [(adj_hbm.at[f], x.at[f]) for f in range(5)]
        + [(fold_hbm, fold)],
        sems,
    )
    for copy in copies[:4]:
        copy.wait()
    route, target, code, hang = (ints[n] for n in range(4))
    lane = iota(1)
    left = lane < 64
    slot = lax.rem(route - lax.axis_index("dom") + 2 + peers, peers)
    marked = down(jnp.where(hang == 1, code, -2)) - (lane // 64).astype(F32)
    odd = lane % 16 >= 8
    group = (lane // 16 + 1) % 4
    for copy in copies[4:]:
        copy.wait()
    for f in range(5):
        packed = jnp.zeros((E, 128), F32)
        for c in range(4):
            moved = x[f, :, 128 * c : 128 * c + 128]
            if c:
                moved = pltpu.roll(moved, 16 * c, 1)
            packed = jnp.where(odd & (group == c), moved, packed)
        high = packed.astype(BF16)
        high_f = high.astype(F32)
        both = jnp.where(odd, high_f, pltpu.roll(packed - high_f, 8, 1)).astype(BF16)
        wide[E * f : E * f + E, 0:128] = both
        wide[E * f : E * f + E, 128:256] = high
    mapped = dot(wide[...], fold[...])
    faces = []
    for f in range(5):
        total = jnp.zeros((E, 128), F32)
        for q in range(4):
            total = total + jnp.where(
                marked == 2.0 * q, mapped[E * f : E * f + E, 128 * q : 128 * q + 128], 0.0
            )
        faces.append(total + pltpu.roll(total, 64, 1))
    faces_out[:, 0:128] = jnp.where(left, faces[0], faces[1])
    faces_out[:, 128:256] = jnp.where(left, faces[2], faces[3])
    faces_out[:, 256:384] = faces[4]

    edges_out[...] = jnp.zeros((32, 128), F32)
    edges_out[16:17] = (slot * E + target).astype(F32)
    edges_out[17:18] = 1.0 - hang.astype(F32)
    lane = iota(1, (1, 128))
    own = marked[0:1], marked[E - 1 : E]
    for n in range(3):
        first, second = 2 * n, min(2 * n + 1, 4)
        for end, (at, chunk) in enumerate(((0, 0), (E - 1, 3))):
            a = x[first, at : at + 1, 128 * chunk : 128 * chunk + 128]
            b = x[second, at : at + 1, 128 * chunk : 128 * chunk + 128]
            if end == 0:
                b = pltpu.roll(b, 64, 1)
            else:
                a = pltpu.roll(a, 64, 1)
            keep = jnp.where((lane % 64 >= 56) & (own[end] >= -1.5), 0.0, 1.0)
            spot = 8 * end + n
            edges_out[spot : spot + 1] = jnp.where(lane < 64, a, b) * keep


def folded_of(route, target, code, hang, adjoint, fold):
    return pl.pallas_call(
        fold_kernel,
        out_shape=jax.ShapeDtypeStruct((E + 32, 384), F32),
        in_specs=[HBM] * 6,
        out_specs=VM,
        scratch_shapes=[
            pltpu.VMEM((4, 1, E), jnp.int32),
            pltpu.VMEM((5, E, 512), F32),
            pltpu.VMEM((256, 512), BF16),
            pltpu.VMEM((5 * E, 256), BF16),
            pltpu.SemaphoreType.DMA((10,)),
        ],
        compiler_params=pltpu.CompilerParams(vmem_limit_bytes=WHOLE),
        name="fold",
    )(route, target, code, hang, adjoint, fold)


def swap(x):
    return pltpu.roll(x, 64, 1)


def along_first(x, coef, base):
    r3, r2 = swap(x[3]), swap(x[2])
    parity = ((x[0] + r3, x[1] + r2), (x[0] - r3, x[1] - r2))
    sums = []
    for s in range(2):
        kept = (parity[s][0], swap(parity[s][0]), parity[s][1], swap(parity[s][1]))
        for c in range(2):
            at = base + 8 * s + 4 * c
            total = coef[at : at + 1] * kept[0]
            for n in range(1, 4):
                total = total + coef[at + n : at + n + 1] * kept[n]
            sums.append(total)
    p0, p1, q0, q1 = sums
    return [p0 + q0, p1 + q1, swap(q1 - p1), swap(q0 - p0)]


def chunks_of(ref, d):
    return jnp.concatenate([ref[d, :, 128 * c : 128 * c + 128] for c in range(4)], 0)


def two_dims(y, m_first, m_second, v_first, v_second, wf1, wf2, wb1, wb2):
    high, low = parts_of(y)
    g = dot(jnp.concatenate([high, low], 1), wf1[...]) + dot(high, wf2[...])
    high1, low1 = parts_of(m_first * g[:, :128] + v_first * y)
    high2, low2 = parts_of(m_second * g[:, 128:] + v_second * y)
    wide = dot(jnp.concatenate([high1, high2], 1), wb1[...])
    low = dot(jnp.concatenate([low1, low2], 1), wb2[...])
    return wide[:, :128] + wide[:, 128:] + low


def factors_of(met, vel, wb1, wb2, coef, q_out, plane_out, end_q, end_mv):
    lane = iota(1)
    left = lane < 64
    for c in range(4):
        at = slice(128 * c, 128 * c + 128)
        w = met[1, :, at] * coef[32:33] + jnp.where(lane % 64 < 8, vel[1, :, at], 0.0)
        high, low = parts_of(w)
        wide = dot(high, wb1[0:128])
        q_out[:, at] = wide[:, :128] + wide[:, 128:] + dot(low, wb2[0:128])

    for n, (ref, d) in enumerate(((met, 0), (met, 2), (vel, 0), (vel, 2))):
        packed = jnp.zeros((E, 128), F32)
        for c in range(4):
            moved = ref[d, :, 128 * c : 128 * c + 128]
            if c:
                moved = pltpu.roll(moved, 16 * c, 1)
            packed = jnp.where((lane // 16) % 4 == c, moved, packed)
        even = jnp.where(left, packed, swap(packed))
        other = jnp.where(left, swap(packed), packed)
        plane_out[n] = jnp.where(lane % 16 < 8, even, pltpu.roll(other, 8, 1))

    small_left = iota(1, (8, 128)) < 64
    for end in range(2):
        rows = slice((E - 8) * end, (E - 8) * end + 8)
        w = []
        for c in range(4):
            at = slice(128 * c, 128 * c + 128)
            spot = 33 + 4 * end + c
            term = met[0, rows, at] * coef[spot : spot + 1]
            if c == 3 * end:
                term = term + jnp.where(small_left != (end == 1), vel[0, rows, at], 0.0)
            w.append(term)
        back = along_first(w, coef, 16)
        for c in range(4):
            end_q[end, c] = back[c]
        at = slice(384 * end, 384 * end + 128)
        for n, (ref, d) in enumerate(((met, 1), (met, 2), (vel, 1), (vel, 2))):
            end_mv[end, n] = ref[d, rows, at]


def main_kernel(fields, x_ref, met, vel, keep_ref, wf1, wf2, wb1, wb2, coef, out, *factors):
    lane, row = iota(1), iota(0)
    keep = keep_ref[...]
    left = lane < 64
    if factors:
        factors_of(met, vel, wb1, wb2, coef, *factors)

    xs = []
    for f in fields:
        x = [x_ref[f, :, 128 * c : 128 * c + 128] * keep for c in range(4)]
        low_faces = pltpu.roll(swap(x[0]), E - 1, 0)
        high_faces = pltpu.roll(swap(x[3]), 1, 0)
        x[0] = x[0] + jnp.where(left & (row > 0), high_faces, 0.0)
        x[3] = x[3] + jnp.where(left | (row == E - 1), 0.0, low_faces)
        xs.append(x)
    count = len(fields)
    rest = two_dims(
        jnp.concatenate(sum(xs, []), 0),
        jnp.concatenate([chunks_of(met, 1)] * count, 0),
        jnp.concatenate([chunks_of(met, 2)] * count, 0),
        jnp.concatenate([chunks_of(vel, 1)] * count, 0),
        jnp.concatenate([chunks_of(vel, 2)] * count, 0),
        wf1, wf2, wb1, wb2,
    )
    for n, x in enumerate(xs):
        g0 = along_first(x, coef, 0)
        inner0 = []
        for c in range(4):
            at = slice(128 * c, 128 * c + 128)
            inner0.append(met[0, :, at] * g0[c] + vel[0, :, at] * x[c])
        back = along_first(inner0, coef, 16)
        for c in range(4):
            start = E * (4 * n + c)
            out[n, :, 128 * c : 128 * c + 128] = rest[start : start + E] + back[c]


def sum_kernel(both, *outs):
    faces, edges = both.at[0:E], both.at[E : E + 32, 0:128]
    column = jnp.where(iota(0) == iota(1), edges[17:18], 0.0).astype(BF16)
    column = dot(column, jnp.ones((E, 128), BF16))
    outs[5][...] = jnp.where(iota(1) % 64 >= 56, column, 1.0)
    spot = edges[16:17].astype(jnp.int32)
    hit = (iota(0, (5 * E, E)) == spot).astype(F32).astype(BF16)
    sums = dot(hit, faces[...].astype(BF16))
    left = iota(1, (64, 128)) < 64
    for ref, o in zip(outs, ORDER):
        mine = sums[o * E : o * E + E]
        ref[0:128] = mine[:, 0:128].astype(ref.dtype)
        ref[128:256] = mine[:, 128:256].astype(ref.dtype)
        ref[256:320] = jnp.where(left, mine[:64, 256:384], mine[64:, 256:384]).astype(ref.dtype)


def sums_of(both):
    return pl.pallas_call(
        sum_kernel,
        out_shape=[
            jax.ShapeDtypeStruct((320, 128), F32 if o == 2 else BF16) for o in range(5)
        ]
        + [jax.ShapeDtypeStruct((E, 128), F32)],
        in_specs=[VM],
        out_specs=[VM] * 6,
        compiler_params=pltpu.CompilerParams(vmem_limit_bytes=16 * 1024 * 1024),
        cost_estimate=pl.CostEstimate(
            flops=8_000_000_000, bytes_accessed=30_000_000, transcendentals=0
        ),
        name="sums",
    )(both)


def main_of(adjoint, metric, velocity, keep, tables, fields, factors):
    def body(*refs):
        main_kernel(fields, *refs)

    return pl.pallas_call(
        body,
        out_shape=[
            jax.ShapeDtypeStruct(shape, F32)
            for shape in [(len(fields), E, 512)]
            + [(E, 512), (4, E, 128), (2, 4, 8, 128), (2, 4, 8, 128)] * factors
        ],
        in_specs=[VM] * 9,
        out_specs=[VM] * (5 if factors else 1),
        compiler_params=pltpu.CompilerParams(vmem_limit_bytes=LIMIT),
        cost_estimate=pl.CostEstimate(
            flops=800_000_000 * len(fields), bytes_accessed=5_000_000, transcendentals=0
        ),
        name="inner",
    )(
        adjoint, metric, velocity, keep,
        *tables["forward"], *tables["backward"], tables["coef"],
    )


def odd_device():
    index = lax.axis_index("dom") * lax.axis_size("sub") + lax.axis_index("sub")
    return lax.rem(index, 2) == 1


def line_kernel(a, b, own, c, d, both, across, inside):
    edges = both.at[E : E + 32, 0:128]
    def rows(start):
        return sum(ref[start : start + 16].astype(F32) for ref in (a, b, own, c, d))

    low = [edges[0:3]]
    high = [edges[8:11]]
    for n, (first, last) in enumerate(((0, 112), (128, 240), (256, 304))):
        low.append(pltpu.roll(rows(first)[0:1], 56, 1))
        line = rows(last)[15:16]
        high.append(pltpu.roll(swap(line) if n == 2 else line, 72, 1))
    zero = jnp.zeros((2, 128), F32)
    low = jnp.concatenate(low + [zero], 0)
    high = jnp.concatenate(high + [zero], 0)
    odd = odd_device()
    across[...] = jnp.where(odd, high, low)
    inside[...] = jnp.where(odd, low, high)


def lines_of(parts, both):
    return pl.pallas_call(
        line_kernel,
        out_shape=[jax.ShapeDtypeStruct((8, 128), F32)] * 2,
        in_specs=[VM] * 6,
        out_specs=[VM] * 2,
        compiler_params=pltpu.CompilerParams(vmem_limit_bytes=LIMIT),
        name="lines",
    )(*parts, both)


def post_kernel(
    a, b, own, c2, d, across, inside, base_a, base_b, q_ref, plane, end_q, end_mv,
    wf1, wf2, wb1, wb2, spread, place, out_hbm, out, out_sems,
):
    out_copies = [
        pltpu.make_async_copy(out.at[f], out_hbm.at[f], out_sems.at[f]) for f in range(5)
    ]
    lane, row = iota(1), iota(0)
    left = lane < 64

    small_left = iota(1, (1, 128)) < 64
    halo = []
    odd = odd_device()
    before = jnp.where(odd, inside[...], across[...])
    after = jnp.where(odd, across[...], inside[...])
    for got in (before, after):
        rows = []
        for n in range(3):
            pair = got[n : n + 1]
            turned = pltpu.roll(pair, 64, 1)
            rows.append(jnp.where(small_left, pair, turned))
            rows.append(jnp.where(small_left, turned, pair))
        halo.append(jnp.concatenate(rows + [jnp.zeros((2, 128), F32)], 0))
    u = jnp.concatenate(halo, 0)
    faces = []
    for n in range(3):
        rows = slice(128 * n, min(128 * n + 128, 320))
        m = sum(ref[rows].astype(F32) for ref in (a, b, own, c2, d))
        if n == 2:
            m = jnp.concatenate([m, swap(m)], 0)
        low_lines = pltpu.roll(pltpu.roll(m, 56, 1), E - 1, 0)
        high_lines = pltpu.roll(pltpu.roll(m, 72, 1), 1, 0)
        low_lines = jnp.where(row == E - 1, after[3 + n : 4 + n], low_lines)
        high_lines = jnp.where(row == 0, before[3 + n : 4 + n], high_lines)
        y = m + jnp.where(lane % 64 < 8, high_lines, 0.0)
        y = y + jnp.where(lane % 64 >= 56, low_lines, 0.0)
        faces.append(y)
    stacked = jnp.concatenate(faces + [u], 0)
    factors = [
        jnp.concatenate(
            [plane[at]] * 3
            + [
                jnp.broadcast_to(end_mv[0, n, 0:1], (8, 128)),
                jnp.broadcast_to(end_mv[1, n, 7:8], (8, 128)),
            ],
            0,
        )
        for n, at in enumerate((0, 1, 2, 3))
    ]
    r = two_dims(stacked, *factors, wf1, wf2, wb1, wb2)
    ends = r[3 * E :]
    y_parts = jnp.concatenate(parts_of(stacked[: 3 * E]), 1)
    r_parts = jnp.concatenate(parts_of(r[: 3 * E]), 1)
    for odd_field in range(2):
        fields = range(odd_field, 5, 2)
        rows = slice(0, E * len(fields))
        cols = slice(512 * odd_field, 512 * odd_field + 512)
        spread_y = dot(y_parts[rows], spread[:, cols])
        placed_r = dot(r_parts[rows], place[:, cols])
        for n, f in enumerate(fields):
            rows = slice(E * n, E * n + E)
            out[f] = (
                (base_a[f] if f < 3 else base_b[f - 3])
                + q_ref[...] * spread_y[rows]
                + placed_r[rows]
            )
            for c in range(4):
                at = slice(128 * c, 128 * c + 128)
                first = end_q[0, c, 0:1] * halo[0][f : f + 1]
                final = end_q[1, c, 7:8] * halo[1][f : f + 1]
                if c == 0:
                    first = first + jnp.where(small_left, ends[f : f + 1], 0.0)
                if c == 3:
                    final = final + jnp.where(small_left, 0.0, ends[8 + f : 9 + f])
                out[f, 0:1, at] += first
                out[f, E - 1 : E, at] += final
            out_copies[f].start()
    for copy in out_copies:
        copy.wait()


def post_of(parts, across, inside, local, tables):
    return pl.pallas_call(
        post_kernel,
        out_shape=jax.ShapeDtypeStruct((5, E, 512), F32),
        in_specs=[VM] * 19,
        out_specs=HBM,
        scratch_shapes=[pltpu.VMEM((5, E, 512), F32), pltpu.SemaphoreType.DMA((5,))],
        compiler_params=pltpu.CompilerParams(vmem_limit_bytes=LIMIT),
        name="outer",
    )(
        *parts, across, inside, *local, *tables["forward"], *tables["backward"],
        tables["spread"], tables["place"],
    )


def shards(adjoint_field, metric, velocity, mortar_route, mortar_element, face_code, hanging):
    tables = constants()
    peers = lax.axis_size("dom")
    adjoint = jnp.transpose(adjoint_field, (1, 0, 2))
    met = jnp.transpose(metric, (1, 0, 2))
    vel = jnp.transpose(velocity, (1, 0, 2))
    route, target, code, hang = (
        x.reshape(1, E) for x in (mortar_route, mortar_element, face_code, hanging)
    )
    both = folded_of(route, target, code, hang, adjoint, tables["fold"])
    *parts, kept = sums_of(both)
    for n in (0, 1, 3, 4):
        pairs = [(i, (i + ORDER[n] - 2) % peers) for i in range(peers)]
        parts[n] = lax.ppermute(parts[n], "dom", pairs)
    early, *factors = main_of(adjoint, met, vel, kept, tables, (0, 1, 2), True)
    parts, early = lax.optimization_barrier((parts, early))
    lines = lines_of(parts, both)
    (out_a, out_b), kept = lax.optimization_barrier((lines, kept))
    axes = ("dom", "sub")
    count = lax.axis_size(axes)
    inside = [(i, i ^ 1) for i in range(count)]
    across = [(i, i + 1 if i % 2 else i - 1) for i in range(1, count - 1)]
    outward = lax.ppermute(out_a, axes, across)
    inward = lax.ppermute(out_b, axes, inside)
    (late,) = main_of(adjoint, met, vel, kept, tables, (3, 4), False)
    result = post_of(parts, outward, inward, (early, late, *factors), tables)
    return jnp.transpose(result, (1, 0, 2))


def solution(mesh):
    block = P(("dom", "sub"), None, None)
    flat = P(("dom", "sub"), None)
    return jax.shard_map(
        shards,
        mesh=mesh,
        in_specs=(block, block, block, flat, flat, flat, flat),
        out_specs=block,
        check_vma=False,
    )
```

```python
import jax
import jax.numpy as jnp
import ml_dtypes
import numpy as np
from jax import lax
from jax.experimental import pallas as pl
from jax.experimental.pallas import tpu as pltpu
from jax.sharding import PartitionSpec as P

gll_nodes = np.array(
    [
        -1.0,
        -0.8717401485096066,
        -0.5917001814331423,
        -0.2092992179024789,
        0.2092992179024789,
        0.5917001814331423,
        0.8717401485096066,
        1.0,
    ]
)
viscosity = 0.005
F32, BF16 = jnp.float32, jnp.bfloat16
E = 128
HBM = pl.BlockSpec(memory_space=pltpu.HBM)
VM = pl.BlockSpec(memory_space=pltpu.VMEM)
LIMIT = 32 * 1024 * 1024
ORDER = (4, 3, 2, 0, 1)
WHOLE = 64 * 1024 * 1024


def legendre_seven(points):
    prev = np.ones(points.shape)
    curr = np.array(points)
    for order in range(1, 7):
        nxt = ((2 * order + 1) * points * curr - order * prev) / (order + 1)
        prev, curr = (curr, nxt)
    return curr


def diff_matrix():
    values = legendre_seven(gll_nodes)
    result_mat = np.zeros((8, 8))
    for row in range(8):
        for col in range(8):
            if row != col:
                result_mat[row, col] = values[row] / (
                    values[col] * (gll_nodes[row] - gll_nodes[col])
                )
    result_mat[0, 0] = -14.0
    result_mat[7, 7] = 14.0
    return result_mat


def lagrange_at(points):
    basis = np.ones((8, 8))
    for row in range(8):
        for col in range(8):
            for other in range(8):
                if other != col:
                    basis[row, col] *= (points[row] - gll_nodes[other]) / (
                        gll_nodes[col] - gll_nodes[other]
                    )
    return basis


def face_tables():
    halves = [lagrange_at((gll_nodes - 1.0) / 2.0), lagrange_at((gll_nodes + 1.0) / 2.0)]
    perm_mat = np.zeros((64, 64))
    for col in range(64):
        perm_mat[col % 8 * 8 + col // 8, col] = 1.0
    tables = []
    for code in range(8):
        mat = np.kron(halves[code % 2], halves[code // 2 % 2])
        if code >= 4:
            mat = mat @ perm_mat
        tables.append(mat)
    return np.stack(tables)


def two_parts(mat):
    high = mat.astype(ml_dtypes.bfloat16)
    low = (mat - high.astype(np.float64)).astype(ml_dtypes.bfloat16)
    return high, low


def constants():
    dmat = diff_matrix()
    eye = np.eye(8)
    along_j = np.kron(np.eye(2), np.kron(dmat, eye))
    along_k = np.kron(np.eye(16), dmat)

    def forward(first, second):
        fh, fl = two_parts(viscosity * first.T)
        sh, sl = two_parts(viscosity * second.T)
        top = np.concatenate([fh, sh], 1)
        return np.concatenate([top, top], 0), np.concatenate([fl, sl], 1)

    def backward(first, second):
        fh, fl = two_parts(first)
        sh, sl = two_parts(second)
        return (
            np.concatenate([np.concatenate([fh, fl], 1), np.concatenate([sh, sl], 1)], 0),
            np.concatenate([fh, sh], 0),
        )

    def split_parity(mat):
        vectors = []
        for sign in (1.0, -1.0):
            small = (mat[:4, :4] + sign * mat[:4, ::-1][:, :4]) / 2
            for c in range(2):
                for other in range(2):
                    for swap in (0, 1):
                        vectors.append(
                            np.concatenate(
                                [
                                    np.full(64, small[2 * c + h, 2 * other + (h ^ swap)])
                                    for h in range(2)
                                ]
                            )
                        )
        return np.stack(vectors)

    coef = np.concatenate([split_parity(viscosity * dmat), split_parity(dmat.T)], 0)
    column = np.tile(np.repeat(viscosity * dmat[:, 0], 8), 2)[None]
    ends = [
        np.repeat(viscosity * dmat[2 * c : 2 * c + 2, end], 64)[None]
        for end in (0, 7)
        for c in range(4)
    ]
    coef = np.concatenate([coef, column, *ends, np.zeros((7, 128))], 0).astype(np.float32)

    tables = face_tables()
    fold = np.zeros((256, 512), ml_dtypes.bfloat16)
    for code in range(8):
        high, low = two_parts(tables[code])
        for i in range(8):
            for k in range(8):
                c, h = i // 2, i % 2
                spot = (56 + 64 * h + 16 * c + k) % 128
                cols = slice(64 * code, 64 * code + 64)
                fold[spot, cols] = high[8 * i + k]
                fold[(spot + 8) % 128, cols] = high[8 * i + k]
                fold[128 + spot, cols] = low[8 * i + k]

    spread = np.zeros((64, 512))
    place = np.zeros((64, 512))
    for i in range(8):
        for k in range(8):
            place[8 * i + k, 64 * i + k] = 1.0
            for j in range(8):
                spread[8 * i + k, 64 * i + 8 * j + k] = 1.0
    zero = np.zeros((64, 512))

    def pair(mat):
        one = np.concatenate(
            [np.concatenate([mat, zero], 1), np.concatenate([zero, mat], 1)], 0
        )
        return np.concatenate([one, one], 0).astype(ml_dtypes.bfloat16)

    return {
        "fold": fold,
        "forward": forward(along_j, along_k),
        "backward": backward(along_j, along_k),
        "spread": pair(spread),
        "place": pair(place),
        "coef": coef,
    }


def iota(dim, shape=(E, 128)):
    return lax.broadcasted_iota(jnp.int32, shape, dim)


def down(row):
    spots = jnp.where(iota(0) == iota(1), row, 0).astype(F32).astype(BF16)
    return jnp.dot(spots, jnp.ones((E, 128), BF16), preferred_element_type=F32)


def dot(a, b):
    return jnp.dot(a, b, preferred_element_type=F32)


def parts_of(x):
    high = x.astype(BF16)
    return high, (x - high.astype(F32)).astype(BF16)


def fetch(pairs, sems):
    copies = [
        pltpu.make_async_copy(src, dst, sems.at[n]) for n, (src, dst) in enumerate(pairs)
    ]
    for copy in copies:
        copy.start()
    return copies


def fold_kernel(
    route_hbm, target_hbm, code_hbm, hang_hbm, adj_hbm, fold_hbm, *refs
):
    out, ints, x, fold, wide, sems = refs
    faces_out, edges_out = out.at[0:E], out.at[E : E + 32, 0:128]
    peers = lax.axis_size("dom")
    copies = fetch(
        [(ref, ints.at[n]) for n, ref in enumerate((route_hbm, target_hbm, code_hbm, hang_hbm))]
        + [(adj_hbm.at[f], x.at[f]) for f in range(5)]
        + [(fold_hbm, fold)],
        sems,
    )
    for copy in copies[:4]:
        copy.wait()
    route, target, code, hang = (ints[n] for n in range(4))
    lane = iota(1)
    left = lane < 64
    slot = lax.rem(route - lax.axis_index("dom") + 2 + peers, peers)
    marked = down(jnp.where(hang == 1, code, -2)) - (lane // 64).astype(F32)
    odd = lane % 16 >= 8
    group = (lane // 16 + 1) % 4
    for copy in copies[4:]:
        copy.wait()
    for f in range(5):
        packed = jnp.zeros((E, 128), F32)
        for c in range(4):
            moved = x[f, :, 128 * c : 128 * c + 128]
            if c:
                moved = pltpu.roll(moved, 16 * c, 1)
            packed = jnp.where(odd & (group == c), moved, packed)
        high = packed.astype(BF16)
        high_f = high.astype(F32)
        both = jnp.where(odd, high_f, pltpu.roll(packed - high_f, 8, 1)).astype(BF16)
        wide[E * f : E * f + E, 0:128] = both
        wide[E * f : E * f + E, 128:256] = high
    mapped = dot(wide[...], fold[...])
    faces = []
    for f in range(5):
        total = jnp.zeros((E, 128), F32)
        for q in range(4):
            total = total + jnp.where(
                marked == 2.0 * q, mapped[E * f : E * f + E, 128 * q : 128 * q + 128], 0.0
            )
        faces.append(total + pltpu.roll(total, 64, 1))
    faces_out[:, 0:128] = jnp.where(left, faces[0], faces[1])
    faces_out[:, 128:256] = jnp.where(left, faces[2], faces[3])
    faces_out[:, 256:384] = faces[4]

    edges_out[...] = jnp.zeros((32, 128), F32)
    edges_out[16:17] = (slot * E + target).astype(F32)
    edges_out[17:18] = 1.0 - hang.astype(F32)
    lane = iota(1, (1, 128))
    own = marked[0:1], marked[E - 1 : E]
    for n in range(3):
        first, second = 2 * n, min(2 * n + 1, 4)
        for end, (at, chunk) in enumerate(((0, 0), (E - 1, 3))):
            a = x[first, at : at + 1, 128 * chunk : 128 * chunk + 128]
            b = x[second, at : at + 1, 128 * chunk : 128 * chunk + 128]
            if end == 0:
                b = pltpu.roll(b, 64, 1)
            else:
                a = pltpu.roll(a, 64, 1)
            keep = jnp.where((lane % 64 >= 56) & (own[end] >= -1.5), 0.0, 1.0)
            spot = 8 * end + n
            edges_out[spot : spot + 1] = jnp.where(lane < 64, a, b) * keep


def folded_of(route, target, code, hang, adjoint, fold):
    return pl.pallas_call(
        fold_kernel,
        out_shape=jax.ShapeDtypeStruct((E + 32, 384), F32),
        in_specs=[HBM] * 6,
        out_specs=VM,
        scratch_shapes=[
            pltpu.VMEM((4, 1, E), jnp.int32),
            pltpu.VMEM((5, E, 512), F32),
            pltpu.VMEM((256, 512), BF16),
            pltpu.VMEM((5 * E, 256), BF16),
            pltpu.SemaphoreType.DMA((10,)),
        ],
        compiler_params=pltpu.CompilerParams(vmem_limit_bytes=WHOLE),
        name="fold",
    )(route, target, code, hang, adjoint, fold)


def swap(x):
    return pltpu.roll(x, 64, 1)


def along_first(x, coef, base):
    r3, r2 = swap(x[3]), swap(x[2])
    parity = ((x[0] + r3, x[1] + r2), (x[0] - r3, x[1] - r2))
    sums = []
    for s in range(2):
        kept = (parity[s][0], swap(parity[s][0]), parity[s][1], swap(parity[s][1]))
        for c in range(2):
            at = base + 8 * s + 4 * c
            total = coef[at : at + 1] * kept[0]
            for n in range(1, 4):
                total = total + coef[at + n : at + n + 1] * kept[n]
            sums.append(total)
    p0, p1, q0, q1 = sums
    return [p0 + q0, p1 + q1, swap(q1 - p1), swap(q0 - p0)]


def chunks_of(ref, d):
    return jnp.concatenate([ref[d, :, 128 * c : 128 * c + 128] for c in range(4)], 0)


def two_dims(y, m_first, m_second, v_first, v_second, wf1, wf2, wb1, wb2):
    high, low = parts_of(y)
    g = dot(jnp.concatenate([high, low], 1), wf1[...]) + dot(high, wf2[...])
    high1, low1 = parts_of(m_first * g[:, :128] + v_first * y)
    high2, low2 = parts_of(m_second * g[:, 128:] + v_second * y)
    wide = dot(jnp.concatenate([high1, high2], 1), wb1[...])
    low = dot(jnp.concatenate([low1, low2], 1), wb2[...])
    return wide[:, :128] + wide[:, 128:] + low


def factors_of(met, vel, wb1, wb2, coef, q_out, plane_out, end_q, end_mv):
    lane = iota(1)
    left = lane < 64
    for c in range(4):
        at = slice(128 * c, 128 * c + 128)
        w = met[1, :, at] * coef[32:33] + jnp.where(lane % 64 < 8, vel[1, :, at], 0.0)
        high, low = parts_of(w)
        wide = dot(high, wb1[0:128])
        q_out[:, at] = wide[:, :128] + wide[:, 128:] + dot(low, wb2[0:128])

    for n, (ref, d) in enumerate(((met, 0), (met, 2), (vel, 0), (vel, 2))):
        packed = jnp.zeros((E, 128), F32)
        for c in range(4):
            moved = ref[d, :, 128 * c : 128 * c + 128]
            if c:
                moved = pltpu.roll(moved, 16 * c, 1)
            packed = jnp.where((lane // 16) % 4 == c, moved, packed)
        even = jnp.where(left, packed, swap(packed))
        other = jnp.where(left, swap(packed), packed)
        plane_out[n] = jnp.where(lane % 16 < 8, even, pltpu.roll(other, 8, 1))

    small_left = iota(1, (8, 128)) < 64
    for end in range(2):
        rows = slice((E - 8) * end, (E - 8) * end + 8)
        w = []
        for c in range(4):
            at = slice(128 * c, 128 * c + 128)
            spot = 33 + 4 * end + c
            term = met[0, rows, at] * coef[spot : spot + 1]
            if c == 3 * end:
                term = term + jnp.where(small_left != (end == 1), vel[0, rows, at], 0.0)
            w.append(term)
        back = along_first(w, coef, 16)
        for c in range(4):
            end_q[end, c] = back[c]
        at = slice(384 * end, 384 * end + 128)
        for n, (ref, d) in enumerate(((met, 1), (met, 2), (vel, 1), (vel, 2))):
            end_mv[end, n] = ref[d, rows, at]


def main_kernel(fields, x_ref, met, vel, keep_ref, wf1, wf2, wb1, wb2, coef, out, *factors):
    lane, row = iota(1), iota(0)
    keep = keep_ref[...]
    left = lane < 64
    if factors:
        factors_of(met, vel, wb1, wb2, coef, *factors)

    xs = []
    for f in fields:
        x = [x_ref[f, :, 128 * c : 128 * c + 128] * keep for c in range(4)]
        low_faces = pltpu.roll(swap(x[0]), E - 1, 0)
        high_faces = pltpu.roll(swap(x[3]), 1, 0)
        x[0] = x[0] + jnp.where(left & (row > 0), high_faces, 0.0)
        x[3] = x[3] + jnp.where(left | (row == E - 1), 0.0, low_faces)
        xs.append(x)
    count = len(fields)
    rest = two_dims(
        jnp.concatenate(sum(xs, []), 0),
        jnp.concatenate([chunks_of(met, 1)] * count, 0),
        jnp.concatenate([chunks_of(met, 2)] * count, 0),
        jnp.concatenate([chunks_of(vel, 1)] * count, 0),
        jnp.concatenate([chunks_of(vel, 2)] * count, 0),
        wf1, wf2, wb1, wb2,
    )
    for n, x in enumerate(xs):
        g0 = along_first(x, coef, 0)
        inner0 = []
        for c in range(4):
            at = slice(128 * c, 128 * c + 128)
            inner0.append(met[0, :, at] * g0[c] + vel[0, :, at] * x[c])
        back = along_first(inner0, coef, 16)
        for c in range(4):
            start = E * (4 * n + c)
            out[n, :, 128 * c : 128 * c + 128] = rest[start : start + E] + back[c]


def sum_kernel(both, *outs):
    faces, edges = both.at[0:E], both.at[E : E + 32, 0:128]
    column = jnp.where(iota(0) == iota(1), edges[17:18], 0.0).astype(BF16)
    column = dot(column, jnp.ones((E, 128), BF16))
    outs[5][...] = jnp.where(iota(1) % 64 >= 56, column, 1.0)
    spot = edges[16:17].astype(jnp.int32)
    hit = (iota(0, (5 * E, E)) == spot).astype(F32).astype(BF16)
    sums = dot(hit, faces[...].astype(BF16))
    left = iota(1, (64, 128)) < 64
    for ref, o in zip(outs, ORDER):
        mine = sums[o * E : o * E + E]
        ref[0:128] = mine[:, 0:128].astype(ref.dtype)
        ref[128:256] = mine[:, 128:256].astype(ref.dtype)
        ref[256:320] = jnp.where(left, mine[:64, 256:384], mine[64:, 256:384]).astype(ref.dtype)


def sums_of(both):
    return pl.pallas_call(
        sum_kernel,
        out_shape=[
            jax.ShapeDtypeStruct((320, 128), F32 if o == 2 else BF16) for o in range(5)
        ]
        + [jax.ShapeDtypeStruct((E, 128), F32)],
        in_specs=[VM],
        out_specs=[VM] * 6,
        compiler_params=pltpu.CompilerParams(vmem_limit_bytes=16 * 1024 * 1024),
        cost_estimate=pl.CostEstimate(
            flops=8_000_000_000, bytes_accessed=30_000_000, transcendentals=0
        ),
        name="sums",
    )(both)


def main_of(adjoint, metric, velocity, keep, tables, fields, factors):
    def body(*refs):
        main_kernel(fields, *refs)

    return pl.pallas_call(
        body,
        out_shape=[
            jax.ShapeDtypeStruct(shape, F32)
            for shape in [(len(fields), E, 512)]
            + [(E, 512), (4, E, 128), (2, 4, 8, 128), (2, 4, 8, 128)] * factors
        ],
        in_specs=[VM] * 9,
        out_specs=[VM] * (5 if factors else 1),
        compiler_params=pltpu.CompilerParams(vmem_limit_bytes=LIMIT),
        cost_estimate=pl.CostEstimate(
            flops=800_000_000 * len(fields), bytes_accessed=5_000_000, transcendentals=0
        ),
        name="inner",
    )(
        adjoint, metric, velocity, keep,
        *tables["forward"], *tables["backward"], tables["coef"],
    )


def odd_device():
    index = lax.axis_index("dom") * lax.axis_size("sub") + lax.axis_index("sub")
    return lax.rem(index, 2) == 1


def line_kernel(a, b, own, c, d, both, across, inside):
    edges = both.at[E : E + 32, 0:128]
    def rows(start):
        return sum(ref[start : start + 16].astype(F32) for ref in (a, b, own, c, d))

    low = [edges[0:3]]
    high = [edges[8:11]]
    for n, (first, last) in enumerate(((0, 112), (128, 240), (256, 304))):
        low.append(pltpu.roll(rows(first)[0:1], 56, 1))
        line = rows(last)[15:16]
        high.append(pltpu.roll(swap(line) if n == 2 else line, 72, 1))
    zero = jnp.zeros((2, 128), F32)
    low = jnp.concatenate(low + [zero], 0)
    high = jnp.concatenate(high + [zero], 0)
    odd = odd_device()
    across[...] = jnp.where(odd, high, low)
    inside[...] = jnp.where(odd, low, high)


def lines_of(parts, both):
    return pl.pallas_call(
        line_kernel,
        out_shape=[jax.ShapeDtypeStruct((8, 128), F32)] * 2,
        in_specs=[VM] * 6,
        out_specs=[VM] * 2,
        compiler_params=pltpu.CompilerParams(vmem_limit_bytes=LIMIT),
        name="lines",
    )(*parts, both)


def post_kernel(
    a, b, own, c2, d, across, inside, base_a, base_b, q_ref, plane, end_q, end_mv,
    wf1, wf2, wb1, wb2, spread, place, out_hbm, out, out_sems,
):
    out_copies = [
        pltpu.make_async_copy(out.at[f], out_hbm.at[f], out_sems.at[f]) for f in range(5)
    ]
    lane, row = iota(1), iota(0)
    left = lane < 64

    small_left = iota(1, (1, 128)) < 64
    halo = []
    odd = odd_device()
    before = jnp.where(odd, inside[...], across[...])
    after = jnp.where(odd, across[...], inside[...])
    for got in (before, after):
        rows = []
        for n in range(3):
            pair = got[n : n + 1]
            turned = pltpu.roll(pair, 64, 1)
            rows.append(jnp.where(small_left, pair, turned))
            rows.append(jnp.where(small_left, turned, pair))
        halo.append(jnp.concatenate(rows + [jnp.zeros((2, 128), F32)], 0))
    u = jnp.concatenate(halo, 0)
    faces = []
    for n in range(3):
        rows = slice(128 * n, min(128 * n + 128, 320))
        m = sum(ref[rows].astype(F32) for ref in (a, b, own, c2, d))
        if n == 2:
            m = jnp.concatenate([m, swap(m)], 0)
        low_lines = pltpu.roll(pltpu.roll(m, 56, 1), E - 1, 0)
        high_lines = pltpu.roll(pltpu.roll(m, 72, 1), 1, 0)
        low_lines = jnp.where(row == E - 1, after[3 + n : 4 + n], low_lines)
        high_lines = jnp.where(row == 0, before[3 + n : 4 + n], high_lines)
        y = m + jnp.where(lane % 64 < 8, high_lines, 0.0)
        y = y + jnp.where(lane % 64 >= 56, low_lines, 0.0)
        faces.append(y)
    stacked = jnp.concatenate(faces + [u], 0)
    factors = [
        jnp.concatenate(
            [plane[at]] * 3
            + [
                jnp.broadcast_to(end_mv[0, n, 0:1], (8, 128)),
                jnp.broadcast_to(end_mv[1, n, 7:8], (8, 128)),
            ],
            0,
        )
        for n, at in enumerate((0, 1, 2, 3))
    ]
    r = two_dims(stacked, *factors, wf1, wf2, wb1, wb2)
    ends = r[3 * E :]
    y_parts = jnp.concatenate(parts_of(stacked[: 3 * E]), 1)
    r_parts = jnp.concatenate(parts_of(r[: 3 * E]), 1)
    for n in range(3):
        rows = slice(E * n, E * n + E)
        for f in range(2 * n, min(2 * n + 2, 5)):
            cols = slice(512 * (f - 2 * n), 512 * (f - 2 * n) + 512)
            out[f] = (
                (base_a[f] if f < 3 else base_b[f - 3])
                + q_ref[...] * dot(y_parts[rows], spread[:, cols])
                + dot(r_parts[rows], place[:, cols])
            )
            for c in range(4):
                at = slice(128 * c, 128 * c + 128)
                first = end_q[0, c, 0:1] * halo[0][f : f + 1]
                final = end_q[1, c, 7:8] * halo[1][f : f + 1]
                if c == 0:
                    first = first + jnp.where(small_left, ends[f : f + 1], 0.0)
                if c == 3:
                    final = final + jnp.where(small_left, 0.0, ends[8 + f : 9 + f])
                out[f, 0:1, at] += first
                out[f, E - 1 : E, at] += final
            out_copies[f].start()
    for copy in out_copies:
        copy.wait()


def post_of(parts, across, inside, local, tables):
    return pl.pallas_call(
        post_kernel,
        out_shape=jax.ShapeDtypeStruct((5, E, 512), F32),
        in_specs=[VM] * 19,
        out_specs=HBM,
        scratch_shapes=[pltpu.VMEM((5, E, 512), F32), pltpu.SemaphoreType.DMA((5,))],
        compiler_params=pltpu.CompilerParams(vmem_limit_bytes=LIMIT),
        name="outer",
    )(
        *parts, across, inside, *local, *tables["forward"], *tables["backward"],
        tables["spread"], tables["place"],
    )


def shards(adjoint_field, metric, velocity, mortar_route, mortar_element, face_code, hanging):
    tables = constants()
    peers = lax.axis_size("dom")
    adjoint = jnp.transpose(adjoint_field, (1, 0, 2))
    met = jnp.transpose(metric, (1, 0, 2))
    vel = jnp.transpose(velocity, (1, 0, 2))
    route, target, code, hang = (
        x.reshape(1, E) for x in (mortar_route, mortar_element, face_code, hanging)
    )
    both = folded_of(route, target, code, hang, adjoint, tables["fold"])
    *parts, kept = sums_of(both)
    for n in (0, 1, 3, 4):
        pairs = [(i, (i + ORDER[n] - 2) % peers) for i in range(peers)]
        parts[n] = lax.ppermute(parts[n], "dom", pairs)
    early, *factors = main_of(adjoint, met, vel, kept, tables, (0, 1, 2), True)
    parts, early = lax.optimization_barrier((parts, early))
    lines = lines_of(parts, both)
    (out_a, out_b), kept = lax.optimization_barrier((lines, kept))
    axes = ("dom", "sub")
    count = lax.axis_size(axes)
    inside = [(i, i ^ 1) for i in range(count)]
    across = [(i, i + 1 if i % 2 else i - 1) for i in range(1, count - 1)]
    outward = lax.ppermute(out_a, axes, across)
    inward = lax.ppermute(out_b, axes, inside)
    (late,) = main_of(adjoint, met, vel, kept, tables, (3, 4), False)
    result = post_of(parts, outward, inward, (early, late, *factors), tables)
    return jnp.transpose(result, (1, 0, 2))


def solution(mesh):
    block = P(("dom", "sub"), None, None)
    flat = P(("dom", "sub"), None)
    return jax.shard_map(
        shards,
        mesh=mesh,
        in_specs=(block, block, block, flat, flat, flat, flat),
        out_specs=block,
        check_vma=False,
    )
```

```python
import jax
import jax.numpy as jnp
import ml_dtypes
import numpy as np
from jax import lax
from jax.experimental import pallas as pl
from jax.experimental.pallas import tpu as pltpu
from jax.sharding import PartitionSpec as P

gll_nodes = np.array(
    [
        -1.0,
        -0.8717401485096066,
        -0.5917001814331423,
        -0.2092992179024789,
        0.2092992179024789,
        0.5917001814331423,
        0.8717401485096066,
        1.0,
    ]
)
viscosity = 0.005
F32, BF16 = jnp.float32, jnp.bfloat16
E = 128
HBM = pl.BlockSpec(memory_space=pltpu.HBM)
VM = pl.BlockSpec(memory_space=pltpu.VMEM)
LIMIT = 32 * 1024 * 1024
ORDER = (3, 4, 2, 0, 1)
WHOLE = 64 * 1024 * 1024


def legendre_seven(points):
    prev = np.ones(points.shape)
    curr = np.array(points)
    for order in range(1, 7):
        nxt = ((2 * order + 1) * points * curr - order * prev) / (order + 1)
        prev, curr = (curr, nxt)
    return curr


def diff_matrix():
    values = legendre_seven(gll_nodes)
    result_mat = np.zeros((8, 8))
    for row in range(8):
        for col in range(8):
            if row != col:
                result_mat[row, col] = values[row] / (
                    values[col] * (gll_nodes[row] - gll_nodes[col])
                )
    result_mat[0, 0] = -14.0
    result_mat[7, 7] = 14.0
    return result_mat


def lagrange_at(points):
    basis = np.ones((8, 8))
    for row in range(8):
        for col in range(8):
            for other in range(8):
                if other != col:
                    basis[row, col] *= (points[row] - gll_nodes[other]) / (
                        gll_nodes[col] - gll_nodes[other]
                    )
    return basis


def face_tables():
    halves = [lagrange_at((gll_nodes - 1.0) / 2.0), lagrange_at((gll_nodes + 1.0) / 2.0)]
    perm_mat = np.zeros((64, 64))
    for col in range(64):
        perm_mat[col % 8 * 8 + col // 8, col] = 1.0
    tables = []
    for code in range(8):
        mat = np.kron(halves[code % 2], halves[code // 2 % 2])
        if code >= 4:
            mat = mat @ perm_mat
        tables.append(mat)
    return np.stack(tables)


def two_parts(mat):
    high = mat.astype(ml_dtypes.bfloat16)
    low = (mat - high.astype(np.float64)).astype(ml_dtypes.bfloat16)
    return high, low


def constants():
    dmat = diff_matrix()
    eye = np.eye(8)
    along_j = np.kron(np.eye(2), np.kron(dmat, eye))
    along_k = np.kron(np.eye(16), dmat)

    def forward(first, second):
        fh, fl = two_parts(viscosity * first.T)
        sh, sl = two_parts(viscosity * second.T)
        top = np.concatenate([fh, sh], 1)
        return np.concatenate([top, top], 0), np.concatenate([fl, sl], 1)

    def backward(first, second):
        fh, fl = two_parts(first)
        sh, sl = two_parts(second)
        return (
            np.concatenate([np.concatenate([fh, fl], 1), np.concatenate([sh, sl], 1)], 0),
            np.concatenate([fh, sh], 0),
        )

    def split_parity(mat):
        vectors = []
        for sign in (1.0, -1.0):
            small = (mat[:4, :4] + sign * mat[:4, ::-1][:, :4]) / 2
            for c in range(2):
                for other in range(2):
                    for swap in (0, 1):
                        vectors.append(
                            np.concatenate(
                                [
                                    np.full(64, small[2 * c + h, 2 * other + (h ^ swap)])
                                    for h in range(2)
                                ]
                            )
                        )
        return np.stack(vectors)

    coef = np.concatenate([split_parity(viscosity * dmat), split_parity(dmat.T)], 0)
    column = np.tile(np.repeat(viscosity * dmat[:, 0], 8), 2)[None]
    ends = [
        np.repeat(viscosity * dmat[2 * c : 2 * c + 2, end], 64)[None]
        for end in (0, 7)
        for c in range(4)
    ]
    coef = np.concatenate([coef, column, *ends, np.zeros((7, 128))], 0).astype(np.float32)

    tables = face_tables()
    fold = np.zeros((256, 512), ml_dtypes.bfloat16)
    for code in range(8):
        high, low = two_parts(tables[code])
        for i in range(8):
            for k in range(8):
                c, h = i // 2, i % 2
                spot = (56 + 64 * h + 16 * c + k) % 128
                cols = slice(64 * code, 64 * code + 64)
                fold[spot, cols] = high[8 * i + k]
                fold[(spot + 8) % 128, cols] = high[8 * i + k]
                fold[128 + spot, cols] = low[8 * i + k]

    spread = np.zeros((64, 512))
    place = np.zeros((64, 512))
    for i in range(8):
        for k in range(8):
            place[8 * i + k, 64 * i + k] = 1.0
            for j in range(8):
                spread[8 * i + k, 64 * i + 8 * j + k] = 1.0
    zero = np.zeros((64, 512))

    def pair(mat):
        one = np.concatenate(
            [np.concatenate([mat, zero], 1), np.concatenate([zero, mat], 1)], 0
        )
        return np.concatenate([one, one], 0).astype(ml_dtypes.bfloat16)

    return {
        "fold": fold,
        "forward": forward(along_j, along_k),
        "backward": backward(along_j, along_k),
        "spread": pair(spread),
        "place": pair(place),
        "coef": coef,
    }


def iota(dim, shape=(E, 128)):
    return lax.broadcasted_iota(jnp.int32, shape, dim)


def down(row):
    spots = jnp.where(iota(0) == iota(1), row, 0).astype(F32).astype(BF16)
    return jnp.dot(spots, jnp.ones((E, 128), BF16), preferred_element_type=F32)


def dot(a, b):
    return jnp.dot(a, b, preferred_element_type=F32)


def parts_of(x):
    high = x.astype(BF16)
    return high, (x - high.astype(F32)).astype(BF16)


def fetch(pairs, sems):
    copies = [
        pltpu.make_async_copy(src, dst, sems.at[n]) for n, (src, dst) in enumerate(pairs)
    ]
    for copy in copies:
        copy.start()
    return copies


def fold_kernel(
    route_hbm, target_hbm, code_hbm, hang_hbm, adj_hbm, fold_hbm, *refs
):
    out, ints, x, fold, wide, sems = refs
    edges_out = out.at[320:352]
    peers = lax.axis_size("dom")
    copies = fetch(
        [(ref, ints.at[n]) for n, ref in enumerate((route_hbm, target_hbm, code_hbm, hang_hbm))]
        + [(adj_hbm.at[f], x.at[f]) for f in range(5)]
        + [(fold_hbm, fold)],
        sems,
    )
    for copy in copies[:4]:
        copy.wait()
    route, target, code, hang = (ints[n] for n in range(4))
    lane = iota(1)
    left = lane < 64
    slot = lax.rem(route - lax.axis_index("dom") + 2 + peers, peers)
    marked = down(jnp.where(hang == 1, code, -2)) - (lane // 64).astype(F32)
    odd = lane % 16 >= 8
    group = (lane // 16 + 1) % 4
    for copy in copies[4:]:
        copy.wait()
    for f in range(5):
        packed = jnp.zeros((E, 128), F32)
        for c in range(4):
            moved = x[f, :, 128 * c : 128 * c + 128]
            if c:
                moved = pltpu.roll(moved, 16 * c, 1)
            packed = jnp.where(odd & (group == c), moved, packed)
        high = packed.astype(BF16)
        high_f = high.astype(F32)
        both = jnp.where(odd, high_f, pltpu.roll(packed - high_f, 8, 1)).astype(BF16)
        wide[E * f : E * f + E, 0:128] = both
        wide[E * f : E * f + E, 128:256] = high
    mapped = dot(wide[...], fold[...])
    faces = []
    for f in range(5):
        total = jnp.zeros((E, 128), F32)
        for q in range(4):
            total = total + jnp.where(
                marked == 2.0 * q, mapped[E * f : E * f + E, 128 * q : 128 * q + 128], 0.0
            )
        faces.append(total + pltpu.roll(total, 64, 1))
    out[0:128] = jnp.where(left, faces[0], faces[1])
    out[128:256] = jnp.where(left, faces[2], faces[3])
    out[256:320] = jnp.where(left[:64], faces[4][:64], faces[4][64:])

    edges_out[...] = jnp.zeros((32, 128), F32)
    edges_out[16:17] = (slot * E + target).astype(F32)
    edges_out[17:18] = 1.0 - hang.astype(F32)
    lane = iota(1, (1, 128))
    own = marked[0:1], marked[E - 1 : E]
    for n in range(3):
        first, second = 2 * n, min(2 * n + 1, 4)
        for end, (at, chunk) in enumerate(((0, 0), (E - 1, 3))):
            a = x[first, at : at + 1, 128 * chunk : 128 * chunk + 128]
            b = x[second, at : at + 1, 128 * chunk : 128 * chunk + 128]
            if end == 0:
                b = pltpu.roll(b, 64, 1)
            else:
                a = pltpu.roll(a, 64, 1)
            keep = jnp.where((lane % 64 >= 56) & (own[end] >= -1.5), 0.0, 1.0)
            spot = 8 * end + n
            edges_out[spot : spot + 1] = jnp.where(lane < 64, a, b) * keep


def folded_of(route, target, code, hang, adjoint, fold):
    return pl.pallas_call(
        fold_kernel,
        out_shape=jax.ShapeDtypeStruct((352, 128), F32),
        in_specs=[HBM] * 6,
        out_specs=VM,
        scratch_shapes=[
            pltpu.VMEM((4, 1, E), jnp.int32),
            pltpu.VMEM((5, E, 512), F32),
            pltpu.VMEM((256, 512), BF16),
            pltpu.VMEM((5 * E, 256), BF16),
            pltpu.SemaphoreType.DMA((10,)),
        ],
        compiler_params=pltpu.CompilerParams(vmem_limit_bytes=WHOLE),
        name="fold",
    )(route, target, code, hang, adjoint, fold)


def swap(x):
    return pltpu.roll(x, 64, 1)


def along_first(x, coef, base):
    r3, r2 = swap(x[3]), swap(x[2])
    parity = ((x[0] + r3, x[1] + r2), (x[0] - r3, x[1] - r2))
    sums = []
    for s in range(2):
        kept = (parity[s][0], swap(parity[s][0]), parity[s][1], swap(parity[s][1]))
        for c in range(2):
            at = base + 8 * s + 4 * c
            total = coef[at : at + 1] * kept[0]
            for n in range(1, 4):
                total = total + coef[at + n : at + n + 1] * kept[n]
            sums.append(total)
    p0, p1, q0, q1 = sums
    return [p0 + q0, p1 + q1, swap(q1 - p1), swap(q0 - p0)]


def chunks_of(ref, d):
    return jnp.concatenate([ref[d, :, 128 * c : 128 * c + 128] for c in range(4)], 0)


def two_dims(y, m_first, m_second, v_first, v_second, wf1, wf2, wb1, wb2):
    high, low = parts_of(y)
    g = dot(jnp.concatenate([high, low], 1), wf1[...]) + dot(high, wf2[...])
    high1, low1 = parts_of(m_first * g[:, :128] + v_first * y)
    high2, low2 = parts_of(m_second * g[:, 128:] + v_second * y)
    wide = dot(jnp.concatenate([high1, high2], 1), wb1[...])
    low = dot(jnp.concatenate([low1, low2], 1), wb2[...])
    return wide[:, :128] + wide[:, 128:] + low


def factors_of(met, vel, wb1, wb2, coef, q_out, plane_out, end_q, end_mv):
    lane = iota(1)
    left = lane < 64
    for c in range(4):
        at = slice(128 * c, 128 * c + 128)
        w = met[1, :, at] * coef[32:33] + jnp.where(lane % 64 < 8, vel[1, :, at], 0.0)
        high, low = parts_of(w)
        wide = dot(high, wb1[0:128])
        q_out[:, at] = wide[:, :128] + wide[:, 128:] + dot(low, wb2[0:128])

    for n, (ref, d) in enumerate(((met, 0), (met, 2), (vel, 0), (vel, 2))):
        packed = jnp.zeros((E, 128), F32)
        for c in range(4):
            moved = ref[d, :, 128 * c : 128 * c + 128]
            if c:
                moved = pltpu.roll(moved, 16 * c, 1)
            packed = jnp.where((lane // 16) % 4 == c, moved, packed)
        even = jnp.where(left, packed, swap(packed))
        other = jnp.where(left, swap(packed), packed)
        plane_out[n] = jnp.where(lane % 16 < 8, even, pltpu.roll(other, 8, 1))

    small_left = iota(1, (8, 128)) < 64
    for end in range(2):
        rows = slice((E - 8) * end, (E - 8) * end + 8)
        w = []
        for c in range(4):
            at = slice(128 * c, 128 * c + 128)
            spot = 33 + 4 * end + c
            term = met[0, rows, at] * coef[spot : spot + 1]
            if c == 3 * end:
                term = term + jnp.where(small_left != (end == 1), vel[0, rows, at], 0.0)
            w.append(term)
        back = along_first(w, coef, 16)
        for c in range(4):
            end_q[end, c] = back[c]
        at = slice(384 * end, 384 * end + 128)
        for n, (ref, d) in enumerate(((met, 1), (met, 2), (vel, 1), (vel, 2))):
            end_mv[end, n] = ref[d, rows, at]


def main_kernel(fields, x_ref, met, vel, keep_ref, wf1, wf2, wb1, wb2, coef, out, *factors):
    lane, row = iota(1), iota(0)
    keep = keep_ref[...]
    left = lane < 64
    if factors:
        factors_of(met, vel, wb1, wb2, coef, *factors)

    xs = []
    for f in fields:
        x = [x_ref[f, :, 128 * c : 128 * c + 128] * keep for c in range(4)]
        low_faces = pltpu.roll(swap(x[0]), E - 1, 0)
        high_faces = pltpu.roll(swap(x[3]), 1, 0)
        x[0] = x[0] + jnp.where(left & (row > 0), high_faces, 0.0)
        x[3] = x[3] + jnp.where(left | (row == E - 1), 0.0, low_faces)
        xs.append(x)
    count = len(fields)
    rest = two_dims(
        jnp.concatenate(sum(xs, []), 0),
        jnp.concatenate([chunks_of(met, 1)] * count, 0),
        jnp.concatenate([chunks_of(met, 2)] * count, 0),
        jnp.concatenate([chunks_of(vel, 1)] * count, 0),
        jnp.concatenate([chunks_of(vel, 2)] * count, 0),
        wf1, wf2, wb1, wb2,
    )
    for n, x in enumerate(xs):
        g0 = along_first(x, coef, 0)
        inner0 = []
        for c in range(4):
            at = slice(128 * c, 128 * c + 128)
            inner0.append(met[0, :, at] * g0[c] + vel[0, :, at] * x[c])
        back = along_first(inner0, coef, 16)
        for c in range(4):
            start = E * (4 * n + c)
            out[n, :, 128 * c : 128 * c + 128] = rest[start : start + E] + back[c]


def sum_kernel(both, *outs):
    edges = both.at[320:352]
    last = both[256:320]
    last = jnp.concatenate([last, swap(last)], 0)
    last = jnp.where(iota(1) < 64, last, swap(last))
    faces = jnp.concatenate([both[0:128], both[128:256], last], 1).astype(BF16)
    column = jnp.where(iota(0) == iota(1), edges[17:18], 0.0).astype(BF16)
    column = dot(column, jnp.ones((E, 128), BF16))
    outs[5][...] = jnp.where(iota(1) % 64 >= 56, column, 1.0)
    spot = edges[16:17].astype(jnp.int32)
    hit = (iota(0, (5 * E, E)) == spot).astype(F32).astype(BF16)
    sums = dot(hit, faces)
    left = iota(1, (64, 128)) < 64
    for ref, o in zip(outs, ORDER):
        mine = sums[o * E : o * E + E]
        ref[0:128] = mine[:, 0:128].astype(ref.dtype)
        ref[128:256] = mine[:, 128:256].astype(ref.dtype)
        ref[256:320] = jnp.where(left, mine[:64, 256:384], mine[64:, 256:384]).astype(ref.dtype)


def sums_of(both):
    return pl.pallas_call(
        sum_kernel,
        out_shape=[
            jax.ShapeDtypeStruct((320, 128), F32 if o == 2 else BF16) for o in range(5)
        ]
        + [jax.ShapeDtypeStruct((E, 128), F32)],
        in_specs=[VM],
        out_specs=[VM] * 6,
        compiler_params=pltpu.CompilerParams(vmem_limit_bytes=16 * 1024 * 1024),
        cost_estimate=pl.CostEstimate(
            flops=8_000_000_000, bytes_accessed=30_000_000, transcendentals=0
        ),
        name="sums",
    )(both)


def main_of(adjoint, metric, velocity, keep, tables, fields, factors):
    def body(*refs):
        main_kernel(fields, *refs)

    return pl.pallas_call(
        body,
        out_shape=[
            jax.ShapeDtypeStruct(shape, F32)
            for shape in [(len(fields), E, 512)]
            + [(E, 512), (4, E, 128), (2, 4, 8, 128), (2, 4, 8, 128)] * factors
        ],
        in_specs=[VM] * 9,
        out_specs=[VM] * (5 if factors else 1),
        compiler_params=pltpu.CompilerParams(vmem_limit_bytes=LIMIT),
        cost_estimate=pl.CostEstimate(
            flops=800_000_000 * len(fields), bytes_accessed=5_000_000, transcendentals=0
        ),
        name="inner",
    )(
        adjoint, metric, velocity, keep,
        *tables["forward"], *tables["backward"], tables["coef"],
    )


def odd_device():
    index = lax.axis_index("dom") * lax.axis_size("sub") + lax.axis_index("sub")
    return lax.rem(index, 2) == 1


def line_kernel(a, b, own, c, d, both, across, inside):
    edges = both.at[320:352]
    def rows(start):
        return sum(ref[start : start + 16].astype(F32) for ref in (a, b, own, c, d))

    low = [edges[0:3]]
    high = [edges[8:11]]
    for n, (first, last) in enumerate(((0, 112), (128, 240), (256, 304))):
        low.append(pltpu.roll(rows(first)[0:1], 56, 1))
        line = rows(last)[15:16]
        high.append(pltpu.roll(swap(line) if n == 2 else line, 72, 1))
    zero = jnp.zeros((2, 128), F32)
    low = jnp.concatenate(low + [zero], 0)
    high = jnp.concatenate(high + [zero], 0)
    odd = odd_device()
    across[...] = jnp.where(odd, high, low)
    inside[...] = jnp.where(odd, low, high)


def lines_of(parts, both):
    return pl.pallas_call(
        line_kernel,
        out_shape=[jax.ShapeDtypeStruct((8, 128), F32)] * 2,
        in_specs=[VM] * 6,
        out_specs=[VM] * 2,
        compiler_params=pltpu.CompilerParams(vmem_limit_bytes=LIMIT),
        name="lines",
    )(*parts, both)


def post_kernel(
    a, b, own, c2, d, across, inside, base_a, base_b, q_ref, plane, end_q, end_mv,
    wf1, wf2, wb1, wb2, spread, place, out_hbm, out, out_sems,
):
    out_copies = [
        pltpu.make_async_copy(out.at[f], out_hbm.at[f], out_sems.at[f]) for f in range(5)
    ]
    lane, row = iota(1), iota(0)
    left = lane < 64

    small_left = iota(1, (1, 128)) < 64
    halo = []
    odd = odd_device()
    before = jnp.where(odd, inside[...], across[...])
    after = jnp.where(odd, across[...], inside[...])
    for got in (before, after):
        rows = []
        for n in range(3):
            pair = got[n : n + 1]
            turned = pltpu.roll(pair, 64, 1)
            rows.append(jnp.where(small_left, pair, turned))
            rows.append(jnp.where(small_left, turned, pair))
        halo.append(jnp.concatenate(rows + [jnp.zeros((2, 128), F32)], 0))
    u = jnp.concatenate(halo, 0)
    faces = []
    for n in range(3):
        rows = slice(128 * n, min(128 * n + 128, 320))
        m = sum(ref[rows].astype(F32) for ref in (a, b, own, c2, d))
        if n == 2:
            m = jnp.concatenate([m, swap(m)], 0)
        low_lines = pltpu.roll(pltpu.roll(m, 56, 1), E - 1, 0)
        high_lines = pltpu.roll(pltpu.roll(m, 72, 1), 1, 0)
        low_lines = jnp.where(row == E - 1, after[3 + n : 4 + n], low_lines)
        high_lines = jnp.where(row == 0, before[3 + n : 4 + n], high_lines)
        y = m + jnp.where(lane % 64 < 8, high_lines, 0.0)
        y = y + jnp.where(lane % 64 >= 56, low_lines, 0.0)
        faces.append(y)
    stacked = jnp.concatenate(faces + [u], 0)
    factors = [
        jnp.concatenate(
            [plane[at]] * 3
            + [
                jnp.broadcast_to(end_mv[0, n, 0:1], (8, 128)),
                jnp.broadcast_to(end_mv[1, n, 7:8], (8, 128)),
            ],
            0,
        )
        for n, at in enumerate((0, 1, 2, 3))
    ]
    r = two_dims(stacked, *factors, wf1, wf2, wb1, wb2)
    ends = r[3 * E :]
    y_parts = jnp.concatenate(parts_of(stacked[: 3 * E]), 1)
    r_parts = jnp.concatenate(parts_of(r[: 3 * E]), 1)
    for n in range(3):
        rows = slice(E * n, E * n + E)
        for f in range(2 * n, min(2 * n + 2, 5)):
            cols = slice(512 * (f - 2 * n), 512 * (f - 2 * n) + 512)
            out[f] = (
                (base_a[f] if f < 3 else base_b[f - 3])
                + q_ref[...] * dot(y_parts[rows], spread[:, cols])
                + dot(r_parts[rows], place[:, cols])
            )
            for c in range(4):
                at = slice(128 * c, 128 * c + 128)
                first = end_q[0, c, 0:1] * halo[0][f : f + 1]
                final = end_q[1, c, 7:8] * halo[1][f : f + 1]
                if c == 0:
                    first = first + jnp.where(small_left, ends[f : f + 1], 0.0)
                if c == 3:
                    final = final + jnp.where(small_left, 0.0, ends[8 + f : 9 + f])
                out[f, 0:1, at] += first
                out[f, E - 1 : E, at] += final
            out_copies[f].start()
    for copy in out_copies:
        copy.wait()


def post_of(parts, across, inside, local, tables):
    return pl.pallas_call(
        post_kernel,
        out_shape=jax.ShapeDtypeStruct((5, E, 512), F32),
        in_specs=[VM] * 19,
        out_specs=HBM,
        scratch_shapes=[pltpu.VMEM((5, E, 512), F32), pltpu.SemaphoreType.DMA((5,))],
        compiler_params=pltpu.CompilerParams(vmem_limit_bytes=LIMIT),
        name="outer",
    )(
        *parts, across, inside, *local, *tables["forward"], *tables["backward"],
        tables["spread"], tables["place"],
    )


def shards(adjoint_field, metric, velocity, mortar_route, mortar_element, face_code, hanging):
    tables = constants()
    peers = lax.axis_size("dom")
    adjoint = jnp.transpose(adjoint_field, (1, 0, 2))
    met = jnp.transpose(metric, (1, 0, 2))
    vel = jnp.transpose(velocity, (1, 0, 2))
    route, target, code, hang = (
        x.reshape(1, E) for x in (mortar_route, mortar_element, face_code, hanging)
    )
    both = folded_of(route, target, code, hang, adjoint, tables["fold"])
    *parts, kept = sums_of(both)
    for n in (0, 1, 3, 4):
        pairs = [(i, (i + ORDER[n] - 2) % peers) for i in range(peers)]
        parts[n] = lax.ppermute(parts[n], "dom", pairs)
    early, *factors = main_of(adjoint, met, vel, kept, tables, (0, 1, 2), True)
    parts, early = lax.optimization_barrier((parts, early))
    lines = lines_of(parts, both)
    (out_a, out_b), kept = lax.optimization_barrier((lines, kept))
    axes = ("dom", "sub")
    count = lax.axis_size(axes)
    inside = [(i, i ^ 1) for i in range(count)]
    across = [(i, i + 1 if i % 2 else i - 1) for i in range(1, count - 1)]
    outward = lax.ppermute(out_a, axes, across)
    inward = lax.ppermute(out_b, axes, inside)
    (late,) = main_of(adjoint, met, vel, kept, tables, (3, 4), False)
    result = post_of(parts, outward, inward, (early, late, *factors), tables)
    return jnp.transpose(result, (1, 0, 2))


def solution(mesh):
    block = P(("dom", "sub"), None, None)
    flat = P(("dom", "sub"), None)
    return jax.shard_map(
        shards,
        mesh=mesh,
        in_specs=(block, block, block, flat, flat, flat, flat),
        out_specs=block,
        check_vma=False,
    )
```

```python
import jax
import jax.numpy as jnp
import ml_dtypes
import numpy as np
from jax import lax
from jax.experimental import pallas as pl
from jax.experimental.pallas import tpu as pltpu
from jax.sharding import PartitionSpec as P

gll_nodes = np.array(
    [
        -1.0,
        -0.8717401485096066,
        -0.5917001814331423,
        -0.2092992179024789,
        0.2092992179024789,
        0.5917001814331423,
        0.8717401485096066,
        1.0,
    ]
)
viscosity = 0.005
F32, BF16 = jnp.float32, jnp.bfloat16
E = 128
HBM = pl.BlockSpec(memory_space=pltpu.HBM)
VM = pl.BlockSpec(memory_space=pltpu.VMEM)
LIMIT = 32 * 1024 * 1024
ORDER = (3, 4, 2, 0, 1)
WHOLE = 64 * 1024 * 1024


def legendre_seven(points):
    prev = np.ones(points.shape)
    curr = np.array(points)
    for order in range(1, 7):
        nxt = ((2 * order + 1) * points * curr - order * prev) / (order + 1)
        prev, curr = (curr, nxt)
    return curr


def diff_matrix():
    values = legendre_seven(gll_nodes)
    result_mat = np.zeros((8, 8))
    for row in range(8):
        for col in range(8):
            if row != col:
                result_mat[row, col] = values[row] / (
                    values[col] * (gll_nodes[row] - gll_nodes[col])
                )
    result_mat[0, 0] = -14.0
    result_mat[7, 7] = 14.0
    return result_mat


def lagrange_at(points):
    basis = np.ones((8, 8))
    for row in range(8):
        for col in range(8):
            for other in range(8):
                if other != col:
                    basis[row, col] *= (points[row] - gll_nodes[other]) / (
                        gll_nodes[col] - gll_nodes[other]
                    )
    return basis


def face_tables():
    halves = [lagrange_at((gll_nodes - 1.0) / 2.0), lagrange_at((gll_nodes + 1.0) / 2.0)]
    perm_mat = np.zeros((64, 64))
    for col in range(64):
        perm_mat[col % 8 * 8 + col // 8, col] = 1.0
    tables = []
    for code in range(8):
        mat = np.kron(halves[code % 2], halves[code // 2 % 2])
        if code >= 4:
            mat = mat @ perm_mat
        tables.append(mat)
    return np.stack(tables)


def two_parts(mat):
    high = mat.astype(ml_dtypes.bfloat16)
    low = (mat - high.astype(np.float64)).astype(ml_dtypes.bfloat16)
    return high, low


def constants():
    dmat = diff_matrix()
    eye = np.eye(8)
    along_j = np.kron(np.eye(2), np.kron(dmat, eye))
    along_k = np.kron(np.eye(16), dmat)

    def forward(first, second):
        fh, fl = two_parts(viscosity * first.T)
        sh, sl = two_parts(viscosity * second.T)
        top = np.concatenate([fh, sh], 1)
        return np.concatenate([top, top], 0), np.concatenate([fl, sl], 1)

    def backward(first, second):
        fh, fl = two_parts(first)
        sh, sl = two_parts(second)
        return (
            np.concatenate([np.concatenate([fh, fl], 1), np.concatenate([sh, sl], 1)], 0),
            np.concatenate([fh, sh], 0),
        )

    def split_parity(mat):
        vectors = []
        for sign in (1.0, -1.0):
            small = (mat[:4, :4] + sign * mat[:4, ::-1][:, :4]) / 2
            for c in range(2):
                for other in range(2):
                    for swap in (0, 1):
                        vectors.append(
                            np.concatenate(
                                [
                                    np.full(64, small[2 * c + h, 2 * other + (h ^ swap)])
                                    for h in range(2)
                                ]
                            )
                        )
        return np.stack(vectors)

    coef = np.concatenate([split_parity(viscosity * dmat), split_parity(dmat.T)], 0)
    column = np.tile(np.repeat(viscosity * dmat[:, 0], 8), 2)[None]
    ends = [
        np.repeat(viscosity * dmat[2 * c : 2 * c + 2, end], 64)[None]
        for end in (0, 7)
        for c in range(4)
    ]
    coef = np.concatenate([coef, column, *ends, np.zeros((7, 128))], 0).astype(np.float32)

    tables = face_tables()
    fold = np.zeros((256, 512), ml_dtypes.bfloat16)
    for code in range(8):
        high, low = two_parts(tables[code])
        for i in range(8):
            for k in range(8):
                c, h = i // 2, i % 2
                spot = (56 + 64 * h + 16 * c + k) % 128
                cols = slice(64 * code, 64 * code + 64)
                fold[spot, cols] = high[8 * i + k]
                fold[(spot + 8) % 128, cols] = high[8 * i + k]
                fold[128 + spot, cols] = low[8 * i + k]

    spread = np.zeros((64, 512))
    place = np.zeros((64, 512))
    for i in range(8):
        for k in range(8):
            place[8 * i + k, 64 * i + k] = 1.0
            for j in range(8):
                spread[8 * i + k, 64 * i + 8 * j + k] = 1.0
    zero = np.zeros((64, 512))

    def pair(mat):
        one = np.concatenate(
            [np.concatenate([mat, zero], 1), np.concatenate([zero, mat], 1)], 0
        )
        return np.concatenate([one, one], 0).astype(ml_dtypes.bfloat16)

    return {
        "fold": fold,
        "forward": forward(along_j, along_k),
        "backward": backward(along_j, along_k),
        "spread": pair(spread),
        "place": pair(place),
        "coef": coef,
    }


def iota(dim, shape=(E, 128)):
    return lax.broadcasted_iota(jnp.int32, shape, dim)


def down(row):
    spots = jnp.where(iota(0) == iota(1), row, 0).astype(F32).astype(BF16)
    return jnp.dot(spots, jnp.ones((E, 128), BF16), preferred_element_type=F32)


def dot(a, b):
    return jnp.dot(a, b, preferred_element_type=F32)


def parts_of(x):
    high = x.astype(BF16)
    return high, (x - high.astype(F32)).astype(BF16)


def fetch(pairs, sems):
    copies = [
        pltpu.make_async_copy(src, dst, sems.at[n]) for n, (src, dst) in enumerate(pairs)
    ]
    for copy in copies:
        copy.start()
    return copies


def fold_kernel(
    route_hbm, target_hbm, code_hbm, hang_hbm, adj_hbm, fold_hbm, *refs
):
    out, ints, x, fold, wide, sems = refs
    edges_out = out.at[320:352]
    peers = lax.axis_size("dom")
    copies = fetch(
        [(adj_hbm, x), (fold_hbm, fold)]
        + [(ref, ints.at[n]) for n, ref in enumerate((route_hbm, target_hbm, code_hbm, hang_hbm))],
        sems,
    )
    for copy in copies[2:]:
        copy.wait()
    route, target, code, hang = (ints[n] for n in range(4))
    lane = iota(1)
    left = lane < 64
    slot = lax.rem(route - lax.axis_index("dom") + 2 + peers, peers)
    marked = down(jnp.where(hang == 1, code, -2)) - (lane // 64).astype(F32)
    odd = lane % 16 >= 8
    group = (lane // 16 + 1) % 4
    for copy in copies[:2]:
        copy.wait()
    for f in range(5):
        packed = jnp.zeros((E, 128), F32)
        for c in range(4):
            moved = x[f, :, 128 * c : 128 * c + 128]
            if c:
                moved = pltpu.roll(moved, 16 * c, 1)
            packed = jnp.where(odd & (group == c), moved, packed)
        high = packed.astype(BF16)
        high_f = high.astype(F32)
        both = jnp.where(odd, high_f, pltpu.roll(packed - high_f, 8, 1)).astype(BF16)
        wide[E * f : E * f + E, 0:128] = both
        wide[E * f : E * f + E, 128:256] = high
    mapped = dot(wide[...], fold[...])
    faces = []
    for f in range(5):
        total = jnp.zeros((E, 128), F32)
        for q in range(4):
            total = total + jnp.where(
                marked == 2.0 * q, mapped[E * f : E * f + E, 128 * q : 128 * q + 128], 0.0
            )
        faces.append(total + pltpu.roll(total, 64, 1))
    out[0:128] = jnp.where(left, faces[0], faces[1])
    out[128:256] = jnp.where(left, faces[2], faces[3])
    out[256:320] = jnp.where(left[:64], faces[4][:64], faces[4][64:])

    edges_out[...] = jnp.zeros((32, 128), F32)
    edges_out[16:17] = (slot * E + target).astype(F32)
    edges_out[17:18] = 1.0 - hang.astype(F32)
    lane = iota(1, (1, 128))
    own = marked[0:1], marked[E - 1 : E]
    for n in range(3):
        first, second = 2 * n, min(2 * n + 1, 4)
        for end, (at, chunk) in enumerate(((0, 0), (E - 1, 3))):
            a = x[first, at : at + 1, 128 * chunk : 128 * chunk + 128]
            b = x[second, at : at + 1, 128 * chunk : 128 * chunk + 128]
            if end == 0:
                b = pltpu.roll(b, 64, 1)
            else:
                a = pltpu.roll(a, 64, 1)
            keep = jnp.where((lane % 64 >= 56) & (own[end] >= -1.5), 0.0, 1.0)
            spot = 8 * end + n
            edges_out[spot : spot + 1] = jnp.where(lane < 64, a, b) * keep


def folded_of(route, target, code, hang, adjoint, fold):
    return pl.pallas_call(
        fold_kernel,
        out_shape=jax.ShapeDtypeStruct((352, 128), F32),
        in_specs=[HBM] * 6,
        out_specs=VM,
        scratch_shapes=[
            pltpu.VMEM((4, 1, E), jnp.int32),
            pltpu.VMEM((5, E, 512), F32),
            pltpu.VMEM((256, 512), BF16),
            pltpu.VMEM((5 * E, 256), BF16),
            pltpu.SemaphoreType.DMA((10,)),
        ],
        compiler_params=pltpu.CompilerParams(vmem_limit_bytes=WHOLE),
        name="fold",
    )(route, target, code, hang, adjoint, fold)


def swap(x):
    return pltpu.roll(x, 64, 1)


def along_first(x, coef, base):
    r3, r2 = swap(x[3]), swap(x[2])
    parity = ((x[0] + r3, x[1] + r2), (x[0] - r3, x[1] - r2))
    sums = []
    for s in range(2):
        kept = (parity[s][0], swap(parity[s][0]), parity[s][1], swap(parity[s][1]))
        for c in range(2):
            at = base + 8 * s + 4 * c
            total = coef[at : at + 1] * kept[0]
            for n in range(1, 4):
                total = total + coef[at + n : at + n + 1] * kept[n]
            sums.append(total)
    p0, p1, q0, q1 = sums
    return [p0 + q0, p1 + q1, swap(q1 - p1), swap(q0 - p0)]


def chunks_of(ref, d):
    return jnp.concatenate([ref[d, :, 128 * c : 128 * c + 128] for c in range(4)], 0)


def two_dims(y, m_first, m_second, v_first, v_second, wf1, wf2, wb1, wb2):
    high, low = parts_of(y)
    g = dot(jnp.concatenate([high, low], 1), wf1[...]) + dot(high, wf2[...])
    high1, low1 = parts_of(m_first * g[:, :128] + v_first * y)
    high2, low2 = parts_of(m_second * g[:, 128:] + v_second * y)
    wide = dot(jnp.concatenate([high1, high2], 1), wb1[...])
    low = dot(jnp.concatenate([low1, low2], 1), wb2[...])
    return wide[:, :128] + wide[:, 128:] + low


def factors_of(met, vel, wb1, wb2, coef, q_out, plane_out, end_q, end_mv):
    lane = iota(1)
    left = lane < 64
    for c in range(4):
        at = slice(128 * c, 128 * c + 128)
        w = met[1, :, at] * coef[32:33] + jnp.where(lane % 64 < 8, vel[1, :, at], 0.0)
        high, low = parts_of(w)
        wide = dot(high, wb1[0:128])
        q_out[:, at] = wide[:, :128] + wide[:, 128:] + dot(low, wb2[0:128])

    for n, (ref, d) in enumerate(((met, 0), (met, 2), (vel, 0), (vel, 2))):
        packed = jnp.zeros((E, 128), F32)
        for c in range(4):
            moved = ref[d, :, 128 * c : 128 * c + 128]
            if c:
                moved = pltpu.roll(moved, 16 * c, 1)
            packed = jnp.where((lane // 16) % 4 == c, moved, packed)
        even = jnp.where(left, packed, swap(packed))
        other = jnp.where(left, swap(packed), packed)
        plane_out[n] = jnp.where(lane % 16 < 8, even, pltpu.roll(other, 8, 1))

    small_left = iota(1, (8, 128)) < 64
    for end in range(2):
        rows = slice((E - 8) * end, (E - 8) * end + 8)
        w = []
        for c in range(4):
            at = slice(128 * c, 128 * c + 128)
            spot = 33 + 4 * end + c
            term = met[0, rows, at] * coef[spot : spot + 1]
            if c == 3 * end:
                term = term + jnp.where(small_left != (end == 1), vel[0, rows, at], 0.0)
            w.append(term)
        back = along_first(w, coef, 16)
        for c in range(4):
            end_q[end, c] = back[c]
        at = slice(384 * end, 384 * end + 128)
        for n, (ref, d) in enumerate(((met, 1), (met, 2), (vel, 1), (vel, 2))):
            end_mv[end, n] = ref[d, rows, at]


def main_kernel(fields, x_ref, met, vel, keep_ref, wf1, wf2, wb1, wb2, coef, out, *factors):
    lane, row = iota(1), iota(0)
    keep = keep_ref[...]
    left = lane < 64
    if factors:
        factors_of(met, vel, wb1, wb2, coef, *factors)

    xs = []
    for f in fields:
        x = [x_ref[f, :, 128 * c : 128 * c + 128] * keep for c in range(4)]
        low_faces = pltpu.roll(swap(x[0]), E - 1, 0)
        high_faces = pltpu.roll(swap(x[3]), 1, 0)
        x[0] = x[0] + jnp.where(left & (row > 0), high_faces, 0.0)
        x[3] = x[3] + jnp.where(left | (row == E - 1), 0.0, low_faces)
        xs.append(x)
    count = len(fields)
    rest = two_dims(
        jnp.concatenate(sum(xs, []), 0),
        jnp.concatenate([chunks_of(met, 1)] * count, 0),
        jnp.concatenate([chunks_of(met, 2)] * count, 0),
        jnp.concatenate([chunks_of(vel, 1)] * count, 0),
        jnp.concatenate([chunks_of(vel, 2)] * count, 0),
        wf1, wf2, wb1, wb2,
    )
    for n, x in enumerate(xs):
        g0 = along_first(x, coef, 0)
        inner0 = []
        for c in range(4):
            at = slice(128 * c, 128 * c + 128)
            inner0.append(met[0, :, at] * g0[c] + vel[0, :, at] * x[c])
        back = along_first(inner0, coef, 16)
        for c in range(4):
            start = E * (4 * n + c)
            out[n, :, 128 * c : 128 * c + 128] = rest[start : start + E] + back[c]


def sum_kernel(both, *outs):
    edges = both.at[320:352]
    last = both[256:320]
    last = jnp.concatenate([last, swap(last)], 0)
    last = jnp.where(iota(1) < 64, last, swap(last))
    faces = jnp.concatenate([both[0:128], both[128:256], last], 1).astype(BF16)
    column = jnp.where(iota(0) == iota(1), edges[17:18], 0.0).astype(BF16)
    column = dot(column, jnp.ones((E, 128), BF16))
    outs[5][...] = jnp.where(iota(1) % 64 >= 56, column, 1.0)
    spot = edges[16:17].astype(jnp.int32)
    hit = (iota(0, (5 * E, E)) == spot).astype(F32).astype(BF16)
    sums = dot(hit, faces)
    left = iota(1, (64, 128)) < 64
    for ref, o in zip(outs, ORDER):
        mine = sums[o * E : o * E + E]
        ref[0:128] = mine[:, 0:128].astype(ref.dtype)
        ref[128:256] = mine[:, 128:256].astype(ref.dtype)
        ref[256:320] = jnp.where(left, mine[:64, 256:384], mine[64:, 256:384]).astype(ref.dtype)


def sums_of(both):
    return pl.pallas_call(
        sum_kernel,
        out_shape=[
            jax.ShapeDtypeStruct((320, 128), F32 if o == 2 else BF16) for o in range(5)
        ]
        + [jax.ShapeDtypeStruct((E, 128), F32)],
        in_specs=[VM],
        out_specs=[VM] * 6,
        compiler_params=pltpu.CompilerParams(vmem_limit_bytes=16 * 1024 * 1024),
        cost_estimate=pl.CostEstimate(
            flops=8_000_000_000, bytes_accessed=30_000_000, transcendentals=0
        ),
        name="sums",
    )(both)


def main_of(adjoint, metric, velocity, keep, tables, fields, factors):
    def body(*refs):
        main_kernel(fields, *refs)

    return pl.pallas_call(
        body,
        out_shape=[
            jax.ShapeDtypeStruct(shape, F32)
            for shape in [(len(fields), E, 512)]
            + [(E, 512), (4, E, 128), (2, 4, 8, 128), (2, 4, 8, 128)] * factors
        ],
        in_specs=[VM] * 9,
        out_specs=[VM] * (5 if factors else 1),
        compiler_params=pltpu.CompilerParams(vmem_limit_bytes=LIMIT),
        cost_estimate=pl.CostEstimate(
            flops=800_000_000 * len(fields), bytes_accessed=5_000_000, transcendentals=0
        ),
        name="inner",
    )(
        adjoint, metric, velocity, keep,
        *tables["forward"], *tables["backward"], tables["coef"],
    )


def odd_device():
    index = lax.axis_index("dom") * lax.axis_size("sub") + lax.axis_index("sub")
    return lax.rem(index, 2) == 1


def line_kernel(a, b, own, c, d, both, across, inside):
    edges = both.at[320:352]
    def rows(start):
        return sum(ref[start : start + 16].astype(F32) for ref in (a, b, own, c, d))

    low = [edges[0:3]]
    high = [edges[8:11]]
    for n, (first, last) in enumerate(((0, 112), (128, 240), (256, 304))):
        low.append(pltpu.roll(rows(first)[0:1], 56, 1))
        line = rows(last)[15:16]
        high.append(pltpu.roll(swap(line) if n == 2 else line, 72, 1))
    zero = jnp.zeros((2, 128), F32)
    low = jnp.concatenate(low + [zero], 0)
    high = jnp.concatenate(high + [zero], 0)
    odd = odd_device()
    across[...] = jnp.where(odd, high, low)
    inside[...] = jnp.where(odd, low, high)


def lines_of(parts, both):
    return pl.pallas_call(
        line_kernel,
        out_shape=[jax.ShapeDtypeStruct((8, 128), F32)] * 2,
        in_specs=[VM] * 6,
        out_specs=[VM] * 2,
        compiler_params=pltpu.CompilerParams(vmem_limit_bytes=LIMIT),
        name="lines",
    )(*parts, both)


def post_kernel(
    a, b, own, c2, d, across, inside, base_a, base_b, q_ref, plane, end_q, end_mv,
    wf1, wf2, wb1, wb2, spread, place, out_hbm, out, out_sems,
):
    out_copies = [
        pltpu.make_async_copy(out.at[f], out_hbm.at[f], out_sems.at[f]) for f in range(5)
    ]
    lane, row = iota(1), iota(0)
    left = lane < 64

    small_left = iota(1, (1, 128)) < 64
    halo = []
    odd = odd_device()
    before = jnp.where(odd, inside[...], across[...])
    after = jnp.where(odd, across[...], inside[...])
    for got in (before, after):
        rows = []
        for n in range(3):
            pair = got[n : n + 1]
            turned = pltpu.roll(pair, 64, 1)
            rows.append(jnp.where(small_left, pair, turned))
            rows.append(jnp.where(small_left, turned, pair))
        halo.append(jnp.concatenate(rows + [jnp.zeros((2, 128), F32)], 0))
    u = jnp.concatenate(halo, 0)
    faces = []
    for n in range(3):
        rows = slice(128 * n, min(128 * n + 128, 320))
        m = sum(ref[rows].astype(F32) for ref in (a, b, own, c2, d))
        if n == 2:
            m = jnp.concatenate([m, swap(m)], 0)
        low_lines = pltpu.roll(pltpu.roll(m, 56, 1), E - 1, 0)
        high_lines = pltpu.roll(pltpu.roll(m, 72, 1), 1, 0)
        low_lines = jnp.where(row == E - 1, after[3 + n : 4 + n], low_lines)
        high_lines = jnp.where(row == 0, before[3 + n : 4 + n], high_lines)
        y = m + jnp.where(lane % 64 < 8, high_lines, 0.0)
        y = y + jnp.where(lane % 64 >= 56, low_lines, 0.0)
        faces.append(y)
    stacked = jnp.concatenate(faces + [u], 0)
    factors = [
        jnp.concatenate(
            [plane[at]] * 3
            + [
                jnp.broadcast_to(end_mv[0, n, 0:1], (8, 128)),
                jnp.broadcast_to(end_mv[1, n, 7:8], (8, 128)),
            ],
            0,
        )
        for n, at in enumerate((0, 1, 2, 3))
    ]
    r = two_dims(stacked, *factors, wf1, wf2, wb1, wb2)
    ends = r[3 * E :]
    y_parts = jnp.concatenate(parts_of(stacked[: 3 * E]), 1)
    r_parts = jnp.concatenate(parts_of(r[: 3 * E]), 1)
    for n in range(3):
        rows = slice(E * n, E * n + E)
        for f in range(2 * n, min(2 * n + 2, 5)):
            cols = slice(512 * (f - 2 * n), 512 * (f - 2 * n) + 512)
            out[f] = (
                (base_a[f] if f < 3 else base_b[f - 3])
                + q_ref[...] * dot(y_parts[rows], spread[:, cols])
                + dot(r_parts[rows], place[:, cols])
            )
            for c in range(4):
                at = slice(128 * c, 128 * c + 128)
                first = end_q[0, c, 0:1] * halo[0][f : f + 1]
                final = end_q[1, c, 7:8] * halo[1][f : f + 1]
                if c == 0:
                    first = first + jnp.where(small_left, ends[f : f + 1], 0.0)
                if c == 3:
                    final = final + jnp.where(small_left, 0.0, ends[8 + f : 9 + f])
                out[f, 0:1, at] += first
                out[f, E - 1 : E, at] += final
            out_copies[f].start()
    for copy in out_copies:
        copy.wait()


def post_of(parts, across, inside, local, tables):
    return pl.pallas_call(
        post_kernel,
        out_shape=jax.ShapeDtypeStruct((5, E, 512), F32),
        in_specs=[VM] * 19,
        out_specs=HBM,
        scratch_shapes=[pltpu.VMEM((5, E, 512), F32), pltpu.SemaphoreType.DMA((5,))],
        compiler_params=pltpu.CompilerParams(vmem_limit_bytes=LIMIT),
        name="outer",
    )(
        *parts, across, inside, *local, *tables["forward"], *tables["backward"],
        tables["spread"], tables["place"],
    )


def shards(adjoint_field, metric, velocity, mortar_route, mortar_element, face_code, hanging):
    tables = constants()
    peers = lax.axis_size("dom")
    adjoint = jnp.transpose(adjoint_field, (1, 0, 2))
    met = jnp.transpose(metric, (1, 0, 2))
    vel = jnp.transpose(velocity, (1, 0, 2))
    route, target, code, hang = (
        x.reshape(1, E) for x in (mortar_route, mortar_element, face_code, hanging)
    )
    both = folded_of(route, target, code, hang, adjoint, tables["fold"])
    *parts, kept = sums_of(both)
    for n in (0, 1, 3, 4):
        pairs = [(i, (i + ORDER[n] - 2) % peers) for i in range(peers)]
        parts[n] = lax.ppermute(parts[n], "dom", pairs)
    early, *factors = main_of(adjoint, met, vel, kept, tables, (0, 1, 2), True)
    parts, early = lax.optimization_barrier((parts, early))
    lines = lines_of(parts, both)
    (out_a, out_b), kept = lax.optimization_barrier((lines, kept))
    axes = ("dom", "sub")
    count = lax.axis_size(axes)
    inside = [(i, i ^ 1) for i in range(count)]
    across = [(i, i + 1 if i % 2 else i - 1) for i in range(1, count - 1)]
    outward = lax.ppermute(out_a, axes, across)
    inward = lax.ppermute(out_b, axes, inside)
    (late,) = main_of(adjoint, met, vel, kept, tables, (3, 4), False)
    result = post_of(parts, outward, inward, (early, late, *factors), tables)
    return jnp.transpose(result, (1, 0, 2))


def solution(mesh):
    block = P(("dom", "sub"), None, None)
    flat = P(("dom", "sub"), None)
    return jax.shard_map(
        shards,
        mesh=mesh,
        in_specs=(block, block, block, flat, flat, flat, flat),
        out_specs=block,
        check_vma=False,
    )
```
